32 devices in a mesh: ka: 4 (over y, core), ga: 8 (over z, x).
Axes of the slice: x: 2, y: 2, z: 4, core: 2. Of those that a mesh axis runs over, the one named last changes fastest.
Arguments:
- bands: bfloat16 [8, 2, 512, 16384], P('ka', None, None, 'ga'), may hold values from -1.75 to 1.75
- nbr_slot: int32 [8], P('ka'), may hold values from 0 to 1, as said below
- gshift: int32 [8], P('ka'), may hold values from -1 to 1
Outputs:
- margin: float32 [512, 8, 2, 512], P('ga', 'ka')
The draws below stay inside these ranges and needn't reach their ends.
Inputs may be any that keep to these rules, and one draw needn't show every extreme that they name: `nbr_slot`: for the 2 k-points of one group the entries are a permutation of 0 to 1.
All inputs are finite; a program needn't handle non-finite values.
Results may differ from the reference program's by a relative error of at most 0.0028.
Values may be sent and summed in bfloat16 or wider, within the bound.
No kernel may reach another device: no remote copies, remote signals or barrier semaphores. Data moves between devices by JAX's collectives and lax.ppermute only.
A program may use at most 128 MiB of HBM per device.

```python
import math
import jax
import jax.numpy as jnp
from jax import lax

NB = 512
K_DEV = 2
NKB = 4
X_DEV = 2
PLANE = 1024
NX = 16
NPTS = 16384
KPTS = 8
N_KA = 4
N_GA = 8


def draw_nbr_slot(key, part):
    key = jax.random.fold_in(key, 7)
    group_keys = jax.random.split(key, KPTS // K_DEV)
    orders = jax.vmap(lambda single: jax.random.permutation(single, K_DEV))(group_keys)
    return orders.reshape(KPTS).astype(jnp.int32)


def with_ends(values, key, smallest, top_value):
    longest = values.shape.index(max(values.shape))
    spots = []
    for shift in (0, 1):
        where = [jax.random.randint(jax.random.fold_in(key, axis), (), 0, length) for axis, length in enumerate(values.shape)]
        where[longest] = (where[longest] + shift) % values.shape[longest]
        spots.append(tuple(where))
    return values.at[spots[0]].set(smallest).at[spots[1]].set(top_value)


def with_spikes(values, stream_key, source, target, shards_of, factor):
    def block_of(position):
        return (jnp.arange(values.shape[position]) // (values.shape[position] // shards_of)).reshape((-1,) + (1,) * (values.ndim - 1 - position))

    one_side = jax.random.permutation(stream_key, shards_of)[block_of(target)]
    far = (block_of(target) + shards_of // 2) % shards_of
    return jnp.where((block_of(source) == one_side) | (block_of(source) == far), factor * values, values)


def level_of(stream_key, shape, pieces, least, high):
    def one(position, blocks):
        heights = jax.random.uniform(jax.random.fold_in(jax.random.fold_in(stream_key, 6), position), (blocks,), jnp.float32, least / len(pieces), high / len(pieces))
        return jnp.repeat(jnp.exp(heights), shape[position] // blocks).reshape((-1,) + (1,) * (len(shape) - position - 1))

    gain = one(*pieces[0])
    for cut in pieces[1:]:
        gain = gain * one(*cut)
    return gain


def gaussian_with(own_key, dims, deviation, bound, cuts, heavy, held_as=jnp.bfloat16):
    values = deviation * jax.random.normal(own_key, dims, jnp.float32)
    if cuts:
        values = values * level_of(own_key, dims, cuts, -0.22, 0.18)
    return jnp.clip(with_spikes(values, jax.random.fold_in(own_key, 3), *heavy), -bound, bound).astype(held_as)


def setup_inputs(seed: int = 0) -> dict:
    splits = jax.random.split(jax.random.key(seed), 4)
    return {
        "bands": gaussian_with(splits[0], (KPTS, 2, NB, NPTS), (1.0 / (X_DEV * PLANE * N_GA) ** 0.25), 1.75, ((0, 4), (3, 8)), (3, 2, 8, 2.0)),
        "nbr_slot": draw_nbr_slot(jax.random.fold_in(splits[3], 71), 0),
        "gshift": with_ends(jax.random.randint(splits[2], (KPTS,), -1, 2), jax.random.fold_in(splits[2], 1), -1, 1).astype(jnp.int32),
    }


def phase_field(slab, shift_g):
    planes = jnp.arange(NPTS, dtype=jnp.int32) // PLANE
    turns = ((1 + NKB * shift_g) * planes) % (NKB * NX)
    angle = (2.0 * math.pi / (NKB * NX)) * turns.astype(jnp.float32)
    cosine = jnp.cos(angle)
    sine = jnp.sin(angle)
    real_part = slab[0].astype(jnp.float32)
    imag_part = slab[1].astype(jnp.float32)
    near_re = real_part * cosine + imag_part * sine
    near_im = imag_part * cosine - real_part * sine
    return jnp.stack([near_re, near_im]).astype(jnp.bfloat16)


def margin_one(conj_side, near):
    terms = jnp.einsum("cmx,dnx->cdmn", conj_side.astype(jnp.float32), near.astype(jnp.float32))
    real_part = terms[0, 0] + terms[1, 1]
    imag_part = terms[0, 1] - terms[1, 0]
    return jnp.stack([real_part, imag_part])


def reference(bands, nbr_slot, gshift):
    def one_point(kidx):
        group = kidx // K_DEV
        slot = lax.dynamic_index_in_dim(nbr_slot, kidx, 0, keepdims=False)
        other = (((group + 1) % N_KA) * K_DEV + slot).astype(jnp.int32)
        conj_side = lax.dynamic_index_in_dim(bands, kidx, 0, keepdims=False)
        partner = lax.dynamic_index_in_dim(bands, other, 0, keepdims=False)
        shift_g = lax.dynamic_index_in_dim(gshift, kidx, 0, keepdims=False)
        return margin_one(conj_side, phase_field(partner, shift_g))

    result = lax.map(one_point, jnp.arange(KPTS, dtype=jnp.int32))
    return jnp.transpose(result, (2, 0, 1, 3))
```

```python
import functools
import math

import jax
import jax.numpy as jnp
from jax import lax
from jax.experimental import pallas as pl
from jax.experimental.pallas import tpu as pltpu
from jax.sharding import PartitionSpec as P

NKB = 4
PLANE = 1024
WIDTH = 128
DEPTH = 512


def shifted(block, axis, distance):
    count = lax.axis_size(axis)
    route = [((i - distance) % count, i) for i in range(count)]
    return lax.ppermute(block, axis, route)


def margin_kernel(slot, order_ref, cos_ref, sin_ref, own_ref, there_ref, out_ref, acc_ref):
    step = pl.program_id(0)
    point = order_ref[slot]
    plane = step * DEPTH // PLANE
    cosine = cos_ref[point, plane]
    sine = sin_ref[point, plane]
    real_part = there_ref[0].astype(jnp.float32)
    imag_part = there_ref[1].astype(jnp.float32)
    near_re = (real_part * cosine + imag_part * sine).astype(jnp.bfloat16)
    near_im = (imag_part * cosine - real_part * sine).astype(jnp.bfloat16)
    dims = (((1,), (1,)), ((), ()))
    with_re = jnp.concatenate([near_re, near_im], axis=0)
    with_im = jnp.concatenate([near_im, -near_re], axis=0)
    terms = lax.dot_general(own_ref[0, 0], with_re, dims, preferred_element_type=jnp.float32)
    terms += lax.dot_general(own_ref[0, 1], with_im, dims, preferred_element_type=jnp.float32)

    @pl.when(step == 0)
    def _():
        acc_ref[...] = terms

    @pl.when(step > 0)
    def _():
        acc_ref[...] += terms

    @pl.when(step == pl.num_programs(0) - 1)
    def _():
        out_ref[...] = acc_ref[...].astype(out_ref.dtype)


def margin_part(slot, order, cosine, sine, bands, there):
    _, _, nbands, points = bands.shape
    width = there.shape[1]
    flops = 2 * nbands * 2 * width * 2 * points
    return pl.pallas_call(
        functools.partial(margin_kernel, slot),
        grid_spec=pltpu.PrefetchScalarGridSpec(
            num_scalar_prefetch=3,
            grid=(points // DEPTH,),
            in_specs=[
                pl.BlockSpec((1, 2, nbands, DEPTH), lambda t, order, c, s: (order[slot], 0, 0, t)),
                pl.BlockSpec((2, width, DEPTH), lambda t, order, c, s: (0, 0, t)),
            ],
            out_specs=pl.BlockSpec((nbands, 2 * width), lambda t, order, c, s: (0, 0)),
            scratch_shapes=[pltpu.VMEM((nbands, 2 * width), jnp.float32)],
        ),
        out_shape=jax.ShapeDtypeStruct((nbands, 2 * width), jnp.bfloat16),
        compiler_params=pltpu.CompilerParams(
            dimension_semantics=("arbitrary",), vmem_limit_bytes=32 * 1024 * 1024
        ),
        cost_estimate=pl.CostEstimate(
            flops=flops, bytes_accessed=4 * nbands * points + 4 * width * points, transcendentals=0
        ),
        name="margin_part",
    )(order, cosine, sine, bands, there)


def gather_kernel(order_ref, parts_ref, *rest):
    out_ref = rest[-1]
    total = parts_ref[0].astype(jnp.float32)
    for source in range(1, parts_ref.shape[0]):
        total = total + parts_ref[source].astype(jnp.float32)
    width = out_ref.shape[3]
    out_ref[:, 0, 0, :] = total[:, :width]
    out_ref[:, 0, 1, :] = total[:, width:]


def add_part(slot, block, order, parts, result, shape):
    count, rows, wide = parts.shape
    width = wide // 2
    operands = (order, parts) if result is None else (order, parts, result)
    in_specs = [pl.BlockSpec((count, rows, wide), lambda i, order: (0, 0, 0))]
    if result is not None:
        in_specs.append(pl.BlockSpec(memory_space=pl.ANY))
    return pl.pallas_call(
        gather_kernel,
        grid_spec=pltpu.PrefetchScalarGridSpec(
            num_scalar_prefetch=1,
            grid=(1,),
            in_specs=in_specs,
            out_specs=pl.BlockSpec((rows, 1, 2, width), lambda i, order: (0, order[slot], 0, block)),
        ),
        out_shape=jax.ShapeDtypeStruct(shape, jnp.float32),
        input_output_aliases={} if result is None else {2: 0},
        cost_estimate=pl.CostEstimate(
            flops=count * rows * wide, bytes_accessed=2 * count * rows * wide, transcendentals=0
        ),
        name="add_part",
    )(*operands)


def body(bands, nbr_slot, gshift):
    grid_index = lax.axis_index("ga")
    grid_count = lax.axis_size("ga")
    k_dev, _, nbands, points = bands.shape
    rows = nbands // grid_count
    own_planes = points // PLANE
    total_planes = own_planes * grid_count
    planes = grid_index * own_planes + jnp.arange(own_planes, dtype=jnp.int32)
    turns = (1 + NKB * gshift[:, None]) * planes[None, :] % (NKB * total_planes)
    angle = 2.0 * math.pi / (NKB * total_planes) * turns.astype(jnp.float32)
    cosine = jnp.cos(angle)
    sine = jnp.sin(angle)
    slots = jnp.arange(k_dev, dtype=jnp.int32)
    order = jnp.sum(jnp.where(nbr_slot[None, :] == slots[:, None], slots[None, :], 0), axis=1)
    result = None
    for slot in range(k_dev):
        for block in range(nbands // WIDTH):
            piece = bands[slot, :, block * WIDTH : (block + 1) * WIDTH, :]
            there = shifted(piece, "ka", -1)
            part = margin_part(slot, order, cosine, sine, bands, there)
            part = part.reshape(grid_count, rows, 2 * WIDTH)
            parts = lax.all_to_all(part, "ga", 0, 0)
            result = add_part(slot, block, order, parts, result, (rows, k_dev, 2, nbands))
    return result


def solution(mesh):
    placed = (P("ka", None, None, "ga"), P("ka"), P("ka"))
    return jax.shard_map(
        body, mesh=mesh, in_specs=placed, out_specs=P("ga", "ka", None, None), check_vma=False
    )
```

```python
import functools
import math

import jax
import jax.numpy as jnp
from jax import lax
from jax.experimental import pallas as pl
from jax.experimental.pallas import tpu as pltpu
from jax.sharding import PartitionSpec as P

NKB = 4
PLANE = 1024
DEPTH = 512
VMEM_BYTES = 60 * 1024 * 1024


def shifted(block, axis, distance):
    count = lax.axis_size(axis)
    route = [((i - distance) % count, i) for i in range(count)]
    return lax.ppermute(block, axis, route)


def margin_kernel(slot, order_ref, cos_ref, sin_ref, own_ref, there_ref, *rest):
    out_ref, acc_ref = rest[-2:]
    step = pl.program_id(0)
    point = order_ref[slot]
    plane = step * DEPTH // PLANE
    cosine = cos_ref[point, plane]
    sine = sin_ref[point, plane]
    real_part = there_ref[0].astype(jnp.float32)
    imag_part = there_ref[1].astype(jnp.float32)
    near_re = (real_part * cosine + imag_part * sine).astype(jnp.bfloat16)
    near_im = (imag_part * cosine - real_part * sine).astype(jnp.bfloat16)
    dims = (((1,), (1,)), ((), ()))
    with_re = jnp.concatenate([near_re, near_im], axis=0)
    with_im = jnp.concatenate([near_im, -near_re], axis=0)
    terms = lax.dot_general(own_ref[0, 0], with_re, dims, preferred_element_type=jnp.float32)
    terms += lax.dot_general(own_ref[0, 1], with_im, dims, preferred_element_type=jnp.float32)

    @pl.when(step == 0)
    def _():
        acc_ref[...] = terms

    @pl.when(step > 0)
    def _():
        acc_ref[...] += terms

    @pl.when(step == pl.num_programs(0) - 1)
    def _():
        out_ref[...] = acc_ref[...].astype(out_ref.dtype)


def margin_part(slot, order, cosine, sine, bands, there, after):
    _, _, nbands, points = bands.shape
    width = there.shape[1]
    flops = 2 * nbands * 2 * width * 2 * points
    return pl.pallas_call(
        functools.partial(margin_kernel, slot),
        grid_spec=pltpu.PrefetchScalarGridSpec(
            num_scalar_prefetch=3,
            grid=(points // DEPTH,),
            in_specs=[
                pl.BlockSpec((1, 2, nbands, DEPTH), lambda t, order, c, s: (order[slot], 0, 0, t)),
                pl.BlockSpec((2, width, DEPTH), lambda t, order, c, s: (0, 0, t)),
            ]
            + [pl.BlockSpec(memory_space=pl.ANY)] * len(after),
            out_specs=pl.BlockSpec((nbands, 2 * width), lambda t, order, c, s: (0, 0)),
            scratch_shapes=[pltpu.VMEM((nbands, 2 * width), jnp.float32)],
        ),
        out_shape=jax.ShapeDtypeStruct((nbands, 2 * width), jnp.bfloat16),
        compiler_params=pltpu.CompilerParams(
            dimension_semantics=("arbitrary",), vmem_limit_bytes=VMEM_BYTES
        ),
        cost_estimate=pl.CostEstimate(
            flops=flops, bytes_accessed=4 * nbands * points + 4 * width * points, transcendentals=0
        ),
        name="margin_part",
    )(order, cosine, sine, bands, there, *after)


def gather_kernel(order_ref, parts_ref, *rest):
    out_ref, done_ref = rest[-2:]
    done_ref[...] = jnp.zeros_like(done_ref)
    total = parts_ref[0].astype(jnp.float32)
    for source in range(1, parts_ref.shape[0]):
        total = total + parts_ref[source].astype(jnp.float32)
    width = out_ref.shape[3]
    out_ref[:, 0, 0, :] = total[:, :width]
    out_ref[:, 0, 1, :] = total[:, width:]


def add_part(slot, block, order, parts, result, shape):
    count, rows, wide = parts.shape
    width = wide // 2
    operands = (order, parts) if result is None else (order, parts, result)
    in_specs = [pl.BlockSpec((count, rows, wide), lambda i, order: (0, 0, 0))]
    if result is not None:
        in_specs.append(pl.BlockSpec(memory_space=pl.ANY))
    return pl.pallas_call(
        gather_kernel,
        grid_spec=pltpu.PrefetchScalarGridSpec(
            num_scalar_prefetch=1,
            grid=(1,),
            in_specs=in_specs,
            out_specs=[
                pl.BlockSpec((rows, 1, 2, width), lambda i, order: (0, order[slot], 0, block)),
                pl.BlockSpec((8, 128), lambda i, order: (0, 0)),
            ],
        ),
        out_shape=[
            jax.ShapeDtypeStruct(shape, jnp.float32),
            jax.ShapeDtypeStruct((8, 128), jnp.float32),
        ],
        input_output_aliases={} if result is None else {2: 0},
        cost_estimate=pl.CostEstimate(
            flops=count * rows * wide, bytes_accessed=2 * count * rows * wide, transcendentals=0
        ),
        name="add_part",
    )(*operands)


def cuts(nbands, last):
    half, quarter = nbands // 2, nbands // 4
    if not last:
        return [(0, half), (half, half)]
    return [(0, half), (half, quarter), (half + quarter, quarter)]


def body(bands, nbr_slot, gshift):
    grid_index = lax.axis_index("ga")
    grid_count = lax.axis_size("ga")
    k_dev, _, nbands, points = bands.shape
    rows = nbands // grid_count
    own_planes = points // PLANE
    total_planes = own_planes * grid_count
    planes = grid_index * own_planes + jnp.arange(own_planes, dtype=jnp.int32)
    turns = (1 + NKB * gshift[:, None]) * planes[None, :] % (NKB * total_planes)
    angle = 2.0 * math.pi / (NKB * total_planes) * turns.astype(jnp.float32)
    cosine = jnp.cos(angle)
    sine = jnp.sin(angle)
    slots = jnp.arange(k_dev, dtype=jnp.int32)
    order = jnp.sum(jnp.where(nbr_slot[None, :] == slots[:, None], slots[None, :], 0), axis=1)
    parts = []
    for slot in range(k_dev):
        last = slot == k_dev - 1
        for start, width in cuts(nbands, last):
            parts.append((slot, start, width))
    sources = bands
    theres = []
    for slot, start, width in parts:
        piece = sources[slot, :, start : start + width, :]
        piece, sources = lax.optimization_barrier((piece, sources))
        theres.append(shifted(piece, "ka", -1))
    result = None
    done = []
    for (slot, start, width), there in zip(parts, theres):
        part = margin_part(slot, order, cosine, sine, bands, there, done[-2:-1])
        part = part.reshape(grid_count, rows, 2 * width)
        arrived = lax.all_to_all(part, "ga", 0, 0)
        shape = (rows, k_dev, 2, nbands)
        result, token = add_part(slot, start // width, order, arrived, result, shape)
        done.append(token)
    return result


def solution(mesh):
    placed = (P("ka", None, None, "ga"), P("ka"), P("ka"))
    return jax.shard_map(
        body, mesh=mesh, in_specs=placed, out_specs=P("ga", "ka", None, None), check_vma=False
    )
```

```python
import functools
import math

import jax
import jax.numpy as jnp
from jax import lax
from jax.experimental import pallas as pl
from jax.experimental.pallas import tpu as pltpu
from jax.sharding import PartitionSpec as P

NKB = 4
PLANE = 1024
DEPTH = 512
AHEAD = 3
VMEM_BYTES = 60 * 1024 * 1024


def shifted(block, axis, distance):
    count = lax.axis_size(axis)
    route = [((i - distance) % count, i) for i in range(count)]
    return lax.ppermute(block, axis, route)


def piece_kernel(slot, start, bands_ref, *rest):
    out_ref, sems = rest[-2:]
    half = out_ref.shape[1] // 2
    copies = []
    for part in range(2):
        for side in range(2):
            rows = pl.ds(start + side * half, half)
            copies.append(
                pltpu.make_async_copy(
                    bands_ref.at[slot, part, rows, :],
                    out_ref.at[part, pl.ds(side * half, half), :],
                    sems.at[part, side],
                )
            )
    for copy in copies:
        copy.start()
    for copy in copies:
        copy.wait()


def piece_of(slot, start, width, bands, after):
    points = bands.shape[3]
    return pl.pallas_call(
        functools.partial(piece_kernel, slot, start),
        in_specs=[pl.BlockSpec(memory_space=pl.ANY)] * (1 + len(after)),
        out_specs=pl.BlockSpec(memory_space=pl.ANY),
        scratch_shapes=[pltpu.SemaphoreType.DMA((2, 2))],
        out_shape=jax.ShapeDtypeStruct((2, width, points), bands.dtype),
        compiler_params=pltpu.CompilerParams(vmem_limit_bytes=VMEM_BYTES),
        cost_estimate=pl.CostEstimate(
            flops=0, bytes_accessed=8 * width * points, transcendentals=0
        ),
        name="piece_of",
    )(bands, *after)


def margin_kernel(slot, k_dev, table_ref, bands_ref, there_ref, *rest):
    out_ref, own_buf, there_buf, sems = rest[-4:]
    pieces = own_buf.shape[0]
    planes = (table_ref.shape[0] // k_dev - 1) // 2
    base = slot * (1 + 2 * planes)
    point = table_ref[base].astype(jnp.int32)

    def copies(piece):
        columns = pl.ds(piece * DEPTH, DEPTH)
        own = pltpu.make_async_copy(
            bands_ref.at[point, :, :, columns], own_buf.at[piece], sems.at[0, piece]
        )
        there = pltpu.make_async_copy(
            there_ref.at[:, :, columns], there_buf.at[piece], sems.at[1, piece]
        )
        return there, own

    for piece in range(pieces):
        for copy in copies(piece):
            copy.start()
    for piece in range(pieces):
        plane = piece * DEPTH // PLANE
        cosine = table_ref[base + 1 + plane]
        sine = table_ref[base + 1 + planes + plane]
        there, own = copies(piece)
        there.wait()
        real_part = there_buf[piece, 0].astype(jnp.float32)
        imag_part = there_buf[piece, 1].astype(jnp.float32)
        near_re = (real_part * cosine + imag_part * sine).astype(jnp.bfloat16)
        near_im = (imag_part * cosine - real_part * sine).astype(jnp.bfloat16)
        with_re = jnp.concatenate([near_re, near_im], axis=0)
        with_im = jnp.concatenate([near_im, -near_re], axis=0)
        right = jnp.concatenate([with_re, with_im], axis=1)
        own.wait()
        left = jnp.concatenate([own_buf[piece, 0], own_buf[piece, 1]], axis=1)
        dims = (((1,), (1,)), ((), ()))
        terms = lax.dot_general(left, right, dims, preferred_element_type=jnp.float32)
        if piece == 0:
            out_ref[...] = terms
        else:
            out_ref[...] += terms


def margin_part(slot, table, bands, there, after):
    k_dev, _, nbands, points = bands.shape
    width = there.shape[1]
    pieces = points // DEPTH
    return pl.pallas_call(
        functools.partial(margin_kernel, slot, k_dev),
        in_specs=[
            pl.BlockSpec(memory_space=pltpu.SMEM),
            pl.BlockSpec(memory_space=pl.ANY),
            pl.BlockSpec(memory_space=pl.ANY),
        ]
        + [pl.BlockSpec(memory_space=pl.ANY)] * len(after),
        out_specs=pl.BlockSpec(memory_space=pltpu.VMEM),
        scratch_shapes=[
            pltpu.VMEM((pieces, 2, nbands, DEPTH), jnp.bfloat16),
            pltpu.VMEM((pieces, 2, width, DEPTH), jnp.bfloat16),
            pltpu.SemaphoreType.DMA((2, pieces)),
        ],
        out_shape=jax.ShapeDtypeStruct((nbands, 2 * width), jnp.float32),
        compiler_params=pltpu.CompilerParams(vmem_limit_bytes=VMEM_BYTES),
        cost_estimate=pl.CostEstimate(
            flops=8 * nbands * width * points,
            bytes_accessed=4 * (nbands + width) * points + 8 * nbands * width,
            transcendentals=0,
        ),
        name="margin_part",
    )(table, bands, there, *after)


def layout_kernel(parts, stride, table_ref, *refs):
    count = len(parts)
    totals, out_ref, bufs, sems = refs[:count], refs[count], refs[count + 1 : -1], refs[-1]
    copies = [
        pltpu.make_async_copy(totals[i], bufs[i], sems.at[i]) for i in range(count)
    ]
    for copy in copies:
        copy.start()
    for copy, (slot, start, width), buf in zip(copies, parts, bufs):
        copy.wait()
        point = table_ref[slot * stride].astype(jnp.int32)
        out_ref[:, point, 0, start : start + width] = buf[:, :width]
        out_ref[:, point, 1, start : start + width] = buf[:, width:]


def laid_out(parts, table, totals, shape):
    return pl.pallas_call(
        functools.partial(layout_kernel, parts, table.shape[0] // shape[1]),
        in_specs=[pl.BlockSpec(memory_space=pltpu.SMEM)]
        + [pl.BlockSpec(memory_space=pl.ANY)] * len(totals),
        out_specs=pl.BlockSpec(memory_space=pltpu.VMEM),
        scratch_shapes=[pltpu.VMEM(total.shape, total.dtype) for total in totals]
        + [pltpu.SemaphoreType.DMA((len(totals),))],
        out_shape=jax.ShapeDtypeStruct(shape, jnp.float32),
        compiler_params=pltpu.CompilerParams(vmem_limit_bytes=VMEM_BYTES),
        cost_estimate=pl.CostEstimate(
            flops=0, bytes_accessed=8 * math.prod(shape), transcendentals=0
        ),
        name="laid_out",
    )(table, *totals)


def cuts(nbands, first, last):
    half, quarter, eighth = nbands // 2, nbands // 4, nbands // 8
    widths = [half, quarter, quarter]
    if first:
        widths = [quarter, quarter, half]
    if last:
        widths = [half, quarter, eighth, eighth]
    starts = [sum(widths[:i]) for i in range(len(widths))]
    return list(zip(starts, widths))


def body(bands, nbr_slot, gshift):
    grid_index = lax.axis_index("ga")
    grid_count = lax.axis_size("ga")
    k_dev, _, nbands, points = bands.shape
    rows = nbands // grid_count
    own_planes = points // PLANE
    total_planes = own_planes * grid_count
    planes = grid_index * own_planes + jnp.arange(own_planes, dtype=jnp.int32)
    slots = jnp.arange(k_dev, dtype=jnp.int32)
    chosen = nbr_slot[None, :] == slots[:, None]
    order = jnp.sum(jnp.where(chosen, slots[None, :], 0), axis=1)
    shifts = jnp.sum(jnp.where(chosen, gshift[None, :], 0), axis=1)
    turns = (1 + NKB * shifts[:, None]) * planes[None, :] % (NKB * total_planes)
    angle = 2.0 * math.pi / (NKB * total_planes) * turns.astype(jnp.float32)
    columns = [order[:, None].astype(jnp.float32), jnp.cos(angle), jnp.sin(angle)]
    table = jnp.concatenate(columns, axis=1).reshape(-1)
    parts = []
    for slot in range(k_dev):
        for start, width in cuts(nbands, slot == 0, slot == k_dev - 1):
            parts.append((slot, start, width))
    theres = []
    piece = None
    for index, (slot, start, width) in enumerate(parts):
        after = [] if piece is None else [piece]
        if index >= AHEAD:
            after.append(theres[index - AHEAD])
        piece = piece_of(slot, start, width, bands, after)
        theres.append(shifted(piece, "ka", -1))
    totals = []
    part = None
    for (slot, start, width), there in zip(parts, theres):
        part = margin_part(slot, table, bands, there, [] if part is None else [part])
        totals.append(lax.psum_scatter(part, "ga", scatter_dimension=0, tiled=True))
    return laid_out(parts, table, totals, (rows, k_dev, 2, nbands))


def solution(mesh):
    placed = (P("ka", None, None, "ga"), P("ka"), P("ka"))
    return jax.shard_map(
        body, mesh=mesh, in_specs=placed, out_specs=P("ga", "ka", None, None), check_vma=False
    )
```

```python
import functools
import math

import jax
import jax.numpy as jnp
from jax import lax
from jax.experimental import pallas as pl
from jax.experimental.pallas import tpu as pltpu
from jax.sharding import PartitionSpec as P

NKB = 4
PLANE = 1024
ROWS = 256
STRIP = 32
DEPTH = 512
LAG = 2
AHEAD = 3
VMEM_BYTES = 58 * 1024 * 1024


def shifted(block, axis, distance):
    count = lax.axis_size(axis)
    route = [((i - distance) % count, i) for i in range(count)]
    return lax.ppermute(block, axis, route)


def piece_kernel(slot, start, bands_ref, *rest):
    out_ref, piece_buf, sems = rest[-3:]
    width = piece_buf.shape[1]
    rows = pl.ds(start, width)
    loads = [
        pltpu.make_async_copy(bands_ref.at[slot, part, rows, :], piece_buf.at[part], sems.at[0, part])
        for part in range(2)
    ]
    stores = [
        pltpu.make_async_copy(piece_buf.at[part], out_ref.at[part], sems.at[1, part])
        for part in range(2)
    ]
    for load in loads:
        load.start()
    for load, store in zip(loads, stores):
        load.wait()
        store.start()
    for store in stores:
        store.wait()


def piece_of(slot, start, width, bands, after):
    points = bands.shape[3]
    return pl.pallas_call(
        functools.partial(piece_kernel, slot, start),
        in_specs=[pl.BlockSpec(memory_space=pl.ANY)] * (1 + len(after)),
        out_specs=pl.BlockSpec(memory_space=pl.ANY),
        scratch_shapes=[
            pltpu.VMEM((2, width, points), bands.dtype),
            pltpu.SemaphoreType.DMA((2, 2)),
        ],
        out_shape=jax.ShapeDtypeStruct((2, width, points), bands.dtype),
        compiler_params=pltpu.CompilerParams(vmem_limit_bytes=VMEM_BYTES),
        cost_estimate=pl.CostEstimate(
            flops=0, bytes_accessed=8 * width * points, transcendentals=0
        ),
        name="piece_of",
    )(bands, *after)


def near_into(near_buf, there_buf, table_ref, base, planes):
    width, points = there_buf.shape[1:]

    @pl.loop(0, width // STRIP)
    def _(strip):
        rows = pl.ds(strip * STRIP, STRIP)
        mirror = pl.ds(width + strip * STRIP, STRIP)
        for start in range(0, points, DEPTH):
            plane = start // PLANE
            cosine = table_ref[base + 1 + plane]
            sine = table_ref[base + 1 + planes + plane]
            columns = pl.ds(start, DEPTH)
            later = pl.ds(points + start, DEPTH)
            real_part = there_buf[0, rows, columns].astype(jnp.float32)
            imag_part = there_buf[1, rows, columns].astype(jnp.float32)
            near_re = (real_part * cosine + imag_part * sine).astype(jnp.bfloat16)
            near_im = (imag_part * cosine - real_part * sine).astype(jnp.bfloat16)
            near_buf[rows, columns] = near_re
            near_buf[rows, later] = near_im
            near_buf[mirror, columns] = near_im
            near_buf[mirror, later] = -near_re


def add_into(sum_buf, arrived_buf):
    width = arrived_buf.shape[2] // 2
    total = arrived_buf[0].astype(jnp.float32)
    for source in range(1, arrived_buf.shape[0]):
        total = total + arrived_buf[source].astype(jnp.float32)
    sum_buf[:, 0, :] = total[:, :width]
    sum_buf[:, 1, :] = total[:, width:]


def step_kernel(slot, k_dev, adding, first, later, table_ref, bands_ref, there_ref, *rest):
    stride = table_ref.shape[0] // k_dev
    planes = (stride - 1) // 2
    base = slot * stride
    point = table_ref[base].astype(jnp.int32)
    rest = list(rest)
    arrived_ref = rest.pop(0) if adding else None
    if adding and not first:
        rest.pop(0)
    out_ref = rest.pop(0)
    result_ref = rest.pop(0) if adding else None
    piece_ref = rest.pop(0) if later else None
    own_buf, there_buf, near_buf, sems = rest[:4]
    if later:
        piece_buf, piece_sems = rest[4:6]
        del rest[4:6]
        later_slot, later_start, later_width = later
        loads = [
            pltpu.make_async_copy(
                bands_ref.at[later_slot, part, pl.ds(later_start, later_width), :],
                piece_buf.at[part],
                piece_sems.at[0, part],
            )
            for part in range(2)
        ]
        stores = [
            pltpu.make_async_copy(piece_buf.at[part], piece_ref.at[part], piece_sems.at[1, part])
            for part in range(2)
        ]
    points = there_buf.shape[2]
    blocks = own_buf.shape[0]
    if adding:
        arrived_buf, sum_buf, add_sems = rest[4:]
        arrival = pltpu.make_async_copy(arrived_ref, arrived_buf, add_sems.at[0])
        arrival.start()
    there = [
        pltpu.make_async_copy(there_ref.at[part], there_buf.at[part], sems.at[0, part])
        for part in range(2)
    ]
    own = [
        pltpu.make_async_copy(
            bands_ref.at[point, part, pl.ds(block * ROWS, ROWS), :],
            own_buf.at[block, :, pl.ds(part * points, points)],
            sems.at[1 + block, part],
        )
        for block in range(blocks)
        for part in range(2)
    ]
    for copy in there + (loads if later else []) + own:
        copy.start()
    if adding:
        add_slot, start, width = adding
        add_point = table_ref[add_slot * stride].astype(jnp.int32)
        arrival.wait()
        add_into(sum_buf, arrived_buf)
        placing = pltpu.make_async_copy(
            sum_buf, result_ref.at[:, add_point, :, pl.ds(start, width)], add_sems.at[1]
        )
        placing.start()
    for copy in there:
        copy.wait()
    near_into(near_buf, there_buf, table_ref, base, planes)
    if later:
        for load, store in zip(loads, stores):
            load.wait()
            store.start()
    for block in range(blocks):
        own[2 * block].wait()
        own[2 * block + 1].wait()
        out_ref[pl.ds(block * ROWS, ROWS), :] = lax.dot_general(
            own_buf[block],
            near_buf[...],
            (((1,), (1,)), ((), ())),
            preferred_element_type=jnp.float32,
        ).astype(out_ref.dtype)
    if adding:
        placing.wait()
    if later:
        for store in stores:
            store.wait()


def step(slot, table, bands, there, adding, arrived, result, shape, later):
    k_dev, _, nbands, points = bands.shape
    width = there.shape[1]
    blocks = nbands // ROWS
    operands = [table, bands, there]
    out_shape = [jax.ShapeDtypeStruct((nbands, 2 * width), jnp.bfloat16)]
    out_specs = [pl.BlockSpec(memory_space=pltpu.VMEM)]
    scratch = [
        pltpu.VMEM((blocks, ROWS, 2 * points), jnp.bfloat16),
        pltpu.VMEM((2, width, points), jnp.bfloat16),
        pltpu.VMEM((2 * width, 2 * points), jnp.bfloat16),
        pltpu.SemaphoreType.DMA((1 + blocks, 2)),
    ]
    aliases = {}
    if later:
        scratch += [
            pltpu.VMEM((2, later[2], points), bands.dtype),
            pltpu.SemaphoreType.DMA((2, 2)),
        ]
    if adding:
        operands.append(arrived)
        if result is not None:
            aliases = {len(operands): 1}
            operands.append(result)
        out_shape.append(jax.ShapeDtypeStruct(shape, jnp.float32))
        out_specs.append(pl.BlockSpec(memory_space=pl.ANY))
        scratch += [
            pltpu.VMEM(arrived.shape, arrived.dtype),
            pltpu.VMEM((shape[0], 2, adding[2]), jnp.float32),
            pltpu.SemaphoreType.DMA((2,)),
        ]
    if later:
        out_shape.append(jax.ShapeDtypeStruct((2, later[2], points), bands.dtype))
        out_specs.append(pl.BlockSpec(memory_space=pl.ANY))
    outs = pl.pallas_call(
        functools.partial(step_kernel, slot, k_dev, adding, result is None, later),
        in_specs=[pl.BlockSpec(memory_space=pltpu.SMEM)]
        + [pl.BlockSpec(memory_space=pl.ANY)] * (len(operands) - 1),
        out_specs=out_specs,
        scratch_shapes=scratch,
        out_shape=out_shape,
        input_output_aliases=aliases,
        compiler_params=pltpu.CompilerParams(vmem_limit_bytes=VMEM_BYTES),
        cost_estimate=pl.CostEstimate(
            flops=8 * nbands * width * points,
            bytes_accessed=4 * (nbands + width) * points + 8 * nbands * width,
            transcendentals=0,
        ),
        name="step",
    )(*operands)
    return outs[0], outs[1] if adding else result, outs[-1] if later else None


def finish_kernel(parts, stride, table_ref, *refs):
    count = len(parts)
    arrived, result_ref = refs[:count], refs[count + 1]
    bufs, sums, sems = refs[count + 2 : -1 - count], refs[-1 - count : -1], refs[-1]
    copies = [pltpu.make_async_copy(arrived[i], bufs[i], sems.at[0, i]) for i in range(count)]
    for copy in copies:
        copy.start()
    placing = []
    for i, (slot, start, width) in enumerate(parts):
        point = table_ref[slot * stride].astype(jnp.int32)
        copies[i].wait()
        add_into(sums[i], bufs[i])
        columns = pl.ds(start, width)
        placing.append(
            pltpu.make_async_copy(sums[i], result_ref.at[:, point, :, columns], sems.at[1, i])
        )
        placing[-1].start()
    for copy in placing:
        copy.wait()


def finish(parts, table, arrived, result):
    rows, k_dev = result.shape[:2]
    return pl.pallas_call(
        functools.partial(finish_kernel, parts, table.shape[0] // k_dev),
        in_specs=[pl.BlockSpec(memory_space=pltpu.SMEM)]
        + [pl.BlockSpec(memory_space=pl.ANY)] * (len(parts) + 1),
        out_specs=pl.BlockSpec(memory_space=pl.ANY),
        scratch_shapes=[pltpu.VMEM(array.shape, array.dtype) for array in arrived]
        + [pltpu.VMEM((rows, 2, width), jnp.float32) for _, _, width in parts]
        + [pltpu.SemaphoreType.DMA((2, len(parts)))],
        out_shape=jax.ShapeDtypeStruct(result.shape, jnp.float32),
        input_output_aliases={1 + len(parts): 0},
        compiler_params=pltpu.CompilerParams(vmem_limit_bytes=VMEM_BYTES),
        cost_estimate=pl.CostEstimate(
            flops=0, bytes_accessed=4 * math.prod(result.shape), transcendentals=0
        ),
        name="finish",
    )(table, *arrived, result)


def cuts(nbands, first):
    half, quarter = nbands // 2, nbands // 4
    widths = [quarter, half + quarter] if first else [half, quarter, quarter]
    starts = [sum(widths[:i]) for i in range(len(widths))]
    return list(zip(starts, widths))


def body(bands, nbr_slot, gshift):
    grid_index = lax.axis_index("ga")
    grid_count = lax.axis_size("ga")
    k_dev, _, nbands, points = bands.shape
    rows = nbands // grid_count
    own_planes = points // PLANE
    total_planes = own_planes * grid_count
    planes = grid_index * own_planes + jnp.arange(own_planes, dtype=jnp.int32)
    slots = jnp.arange(k_dev, dtype=jnp.int32)
    chosen = nbr_slot[None, :] == slots[:, None]
    order = jnp.sum(jnp.where(chosen, slots[None, :], 0), axis=1)
    shifts = jnp.sum(jnp.where(chosen, gshift[None, :], 0), axis=1)
    turns = (1 + NKB * shifts[:, None]) * planes[None, :] % (NKB * total_planes)
    angle = 2.0 * math.pi / (NKB * total_planes) * turns.astype(jnp.float32)
    columns = [order[:, None].astype(jnp.float32), jnp.cos(angle), jnp.sin(angle)]
    table = jnp.concatenate(columns, axis=1).reshape(-1)
    parts = []
    for slot in range(k_dev):
        for start, width in cuts(nbands, slot == 0):
            parts.append((slot, start, width))
    theres = []
    piece = None
    for slot, start, width in parts[:AHEAD]:
        piece = piece_of(slot, start, width, bands, [] if piece is None else [piece])
        theres.append(shifted(piece, "ka", -1))
    arrived = []
    result = None
    shape = (rows, k_dev, 2, nbands)
    for index, part in enumerate(parts):
        adding = parts[index - LAG] if index >= LAG else None
        ready = arrived[index - LAG] if index >= LAG else None
        later = parts[index + AHEAD] if index + AHEAD < len(parts) else None
        terms, result, piece = step(
            part[0], table, bands, theres[index], adding, ready, result, shape, later
        )
        if later:
            theres.append(shifted(piece, "ka", -1))
        terms = terms.reshape(grid_count, rows, 2 * part[2])
        arrived.append(lax.all_to_all(terms, "ga", 0, 0))
    return finish(parts[-LAG:], table, arrived[-LAG:], result)


def solution(mesh):
    placed = (P("ka", None, None, "ga"), P("ka"), P("ka"))
    return jax.shard_map(
        body, mesh=mesh, in_specs=placed, out_specs=P("ga", "ka", None, None), check_vma=False
    )
```

```python
import functools
import math

import jax
import jax.numpy as jnp
from jax import lax
from jax.experimental import pallas as pl
from jax.experimental.pallas import tpu as pltpu
from jax.sharding import PartitionSpec as P

NKB = 4
PLANE = 1024
STRIP = 32
DEPTH = 512
LAG = 2
AHEAD = 2
VMEM_BYTES = 56 * 1024 * 1024


def shifted(block, axis, distance):
    count = lax.axis_size(axis)
    route = [((i - distance) % count, i) for i in range(count)]
    return lax.ppermute(block, axis, route)


def piece_kernel(slot, start, bands_ref, *rest):
    out_ref, piece_buf, sems = rest[-3:]
    width = piece_buf.shape[1]
    rows = pl.ds(start, width)
    loads = [
        pltpu.make_async_copy(bands_ref.at[slot, part, rows, :], piece_buf.at[part], sems.at[0, part])
        for part in range(2)
    ]
    stores = [
        pltpu.make_async_copy(piece_buf.at[part], out_ref.at[part], sems.at[1, part])
        for part in range(2)
    ]
    for load in loads:
        load.start()
    for load, store in zip(loads, stores):
        load.wait()
        store.start()
    for store in stores:
        store.wait()


def piece_of(slot, start, width, bands, after):
    points = bands.shape[3]
    return pl.pallas_call(
        functools.partial(piece_kernel, slot, start),
        in_specs=[pl.BlockSpec(memory_space=pl.ANY)] * (1 + len(after)),
        out_specs=pl.BlockSpec(memory_space=pl.ANY),
        scratch_shapes=[
            pltpu.VMEM((2, width, points), bands.dtype),
            pltpu.SemaphoreType.DMA((2, 2)),
        ],
        out_shape=jax.ShapeDtypeStruct((2, width, points), bands.dtype),
        compiler_params=pltpu.CompilerParams(vmem_limit_bytes=VMEM_BYTES),
        cost_estimate=pl.CostEstimate(
            flops=0, bytes_accessed=8 * width * points, transcendentals=0
        ),
        name="piece_of",
    )(bands, *after)


def near_into(near_buf, there_ref, table_ref, base, planes):
    width, points = there_ref.shape[1:]

    @pl.loop(0, width // STRIP)
    def _(strip):
        rows = pl.ds(strip * STRIP, STRIP)
        mirror = pl.ds(width + strip * STRIP, STRIP)
        for start in range(0, points, DEPTH):
            plane = start // PLANE
            cosine = table_ref[base + 1 + plane]
            sine = table_ref[base + 1 + planes + plane]
            columns = pl.ds(start, DEPTH)
            real_part = there_ref[0, rows, columns].astype(jnp.float32)
            imag_part = there_ref[1, rows, columns].astype(jnp.float32)
            near_re = real_part * cosine + imag_part * sine
            near_im = imag_part * cosine - real_part * sine
            near_buf[rows, columns] = near_re.astype(jnp.bfloat16)
            near_buf[mirror, columns] = near_im.astype(jnp.bfloat16)


def add_into(sum_buf, arrived_buf):
    width = arrived_buf.shape[2] // 2
    total = arrived_buf[0].astype(jnp.float32)
    for source in range(1, arrived_buf.shape[0]):
        total = total + arrived_buf[source].astype(jnp.float32)
    sum_buf[:, 0, :] = total[:, :width]
    sum_buf[:, 1, :] = total[:, width:]


def step_kernel(slot, k_dev, adding, first, later, table_ref, bands_ref, there_ref, *rest):
    stride = table_ref.shape[0] // k_dev
    planes = (stride - 1) // 2
    base = slot * stride
    point = table_ref[base].astype(jnp.int32)
    rest = list(rest)
    arrived_ref = rest.pop(0) if adding else None
    if adding and not first:
        rest.pop(0)
    out_ref = rest.pop(0)
    result_ref = rest.pop(0) if adding else None
    piece_ref = rest.pop(0) if later else None
    own_buf, near_buf, own_sems = rest[:3]
    del rest[:3]
    if later:
        piece_buf, piece_sems = rest[:2]
        del rest[:2]
        later_slot, later_start, later_width = later
        loads = [
            pltpu.make_async_copy(
                bands_ref.at[later_slot, part, pl.ds(later_start, later_width), :],
                piece_buf.at[part],
                piece_sems.at[0, part],
            )
            for part in range(2)
        ]
        stores = [
            pltpu.make_async_copy(piece_buf.at[part], piece_ref.at[part], piece_sems.at[1, part])
            for part in range(2)
        ]
    if adding:
        sum_buf, placed_sem = rest
    own = [
        pltpu.make_async_copy(bands_ref.at[point, part], own_buf.at[part], own_sems.at[part])
        for part in range(2)
    ]
    for copy in own + (loads if later else []):
        copy.start()
    if adding:
        add_slot, start, width = adding
        add_point = table_ref[add_slot * stride].astype(jnp.int32)
        add_into(sum_buf, arrived_ref)
        placing = pltpu.make_async_copy(
            sum_buf, result_ref.at[:, add_point, :, pl.ds(start, width)], placed_sem
        )
        placing.start()
    near_into(near_buf, there_ref, table_ref, base, planes)
    if later:
        for load, store in zip(loads, stores):
            load.wait()
            store.start()
    for copy in own:
        copy.wait()
    dims = (((1,), (1,)), ((), ()))
    width = there_ref.shape[1]
    of_re, of_im = [
        lax.dot_general(own_buf[part], near_buf[...], dims, preferred_element_type=jnp.float32)
        for part in range(2)
    ]
    out_ref[:, :width] = (of_re[:, :width] + of_im[:, width:]).astype(out_ref.dtype)
    out_ref[:, width:] = (of_re[:, width:] - of_im[:, :width]).astype(out_ref.dtype)
    if adding:
        placing.wait()
    if later:
        for store in stores:
            store.wait()


def step(slot, table, bands, there, adding, arrived, result, shape, later):
    k_dev, _, nbands, points = bands.shape
    width = there.shape[1]
    operands = [table, bands, there]
    spaces = [pltpu.SMEM, pl.ANY, pltpu.VMEM]
    out_shape = [jax.ShapeDtypeStruct((nbands, 2 * width), jnp.bfloat16)]
    out_specs = [pl.BlockSpec(memory_space=pltpu.VMEM)]
    scratch = [
        pltpu.VMEM((2, nbands, points), jnp.bfloat16),
        pltpu.VMEM((2 * width, points), jnp.bfloat16),
        pltpu.SemaphoreType.DMA((2,)),
    ]
    aliases = {}
    if later:
        scratch += [
            pltpu.VMEM((2, later[2], points), bands.dtype),
            pltpu.SemaphoreType.DMA((2, 2)),
        ]
    if adding:
        operands.append(arrived)
        spaces.append(pltpu.VMEM)
        if result is not None:
            aliases = {len(operands): 1}
            operands.append(result)
            spaces.append(pl.ANY)
        out_shape.append(jax.ShapeDtypeStruct(shape, jnp.float32))
        out_specs.append(pl.BlockSpec(memory_space=pl.ANY))
        scratch += [
            pltpu.VMEM((shape[0], 2, adding[2]), jnp.float32),
            pltpu.SemaphoreType.DMA,
        ]
    if later:
        out_shape.append(jax.ShapeDtypeStruct((2, later[2], points), bands.dtype))
        out_specs.append(pl.BlockSpec(memory_space=pl.ANY))
    outs = pl.pallas_call(
        functools.partial(step_kernel, slot, k_dev, adding, result is None, later),
        in_specs=[pl.BlockSpec(memory_space=space) for space in spaces],
        out_specs=out_specs,
        scratch_shapes=scratch,
        out_shape=out_shape,
        input_output_aliases=aliases,
        compiler_params=pltpu.CompilerParams(vmem_limit_bytes=VMEM_BYTES),
        cost_estimate=pl.CostEstimate(
            flops=8 * nbands * width * points,
            bytes_accessed=4 * (nbands + width) * points + 8 * nbands * width,
            transcendentals=0,
        ),
        name="step",
    )(*operands)
    return outs[0], outs[1] if adding else result, outs[-1] if later else None


def finish_kernel(parts, stride, table_ref, *refs):
    count = len(parts)
    arrived, result_ref = refs[:count], refs[count + 1]
    sums, sems = refs[count + 2 : -1], refs[-1]
    placing = []
    for i, (slot, start, width) in enumerate(parts):
        point = table_ref[slot * stride].astype(jnp.int32)
        add_into(sums[i], arrived[i])
        columns = pl.ds(start, width)
        placing.append(
            pltpu.make_async_copy(sums[i], result_ref.at[:, point, :, columns], sems.at[i])
        )
        placing[-1].start()
    for copy in placing:
        copy.wait()


def finish(parts, table, arrived, result):
    rows, k_dev = result.shape[:2]
    return pl.pallas_call(
        functools.partial(finish_kernel, parts, table.shape[0] // k_dev),
        in_specs=[pl.BlockSpec(memory_space=pltpu.SMEM)]
        + [pl.BlockSpec(memory_space=pltpu.VMEM)] * len(parts)
        + [pl.BlockSpec(memory_space=pl.ANY)],
        out_specs=pl.BlockSpec(memory_space=pl.ANY),
        scratch_shapes=[pltpu.VMEM((rows, 2, width), jnp.float32) for _, _, width in parts]
        + [pltpu.SemaphoreType.DMA((len(parts),))],
        out_shape=jax.ShapeDtypeStruct(result.shape, jnp.float32),
        input_output_aliases={1 + len(parts): 0},
        compiler_params=pltpu.CompilerParams(vmem_limit_bytes=VMEM_BYTES),
        cost_estimate=pl.CostEstimate(
            flops=0, bytes_accessed=4 * math.prod(result.shape), transcendentals=0
        ),
        name="finish",
    )(table, *arrived, result)


def cuts(nbands, first):
    half, quarter = nbands // 2, nbands // 4
    widths = [quarter, quarter, half] if first else [half, quarter, quarter]
    starts = [sum(widths[:i]) for i in range(len(widths))]
    return list(zip(starts, widths))


def body(bands, nbr_slot, gshift):
    grid_index = lax.axis_index("ga")
    grid_count = lax.axis_size("ga")
    k_dev, _, nbands, points = bands.shape
    rows = nbands // grid_count
    own_planes = points // PLANE
    total_planes = own_planes * grid_count
    planes = grid_index * own_planes + jnp.arange(own_planes, dtype=jnp.int32)
    slots = jnp.arange(k_dev, dtype=jnp.int32)
    chosen = nbr_slot[None, :] == slots[:, None]
    order = jnp.sum(jnp.where(chosen, slots[None, :], 0), axis=1)
    shifts = jnp.sum(jnp.where(chosen, gshift[None, :], 0), axis=1)
    turns = (1 + NKB * shifts[:, None]) * planes[None, :] % (NKB * total_planes)
    angle = 2.0 * math.pi / (NKB * total_planes) * turns.astype(jnp.float32)
    columns = [order[:, None].astype(jnp.float32), jnp.cos(angle), jnp.sin(angle)]
    table = jnp.concatenate(columns, axis=1).reshape(-1)
    parts = []
    for slot in range(k_dev):
        for start, width in cuts(nbands, slot == 0):
            parts.append((slot, start, width))
    theres = []
    piece = None
    for slot, start, width in parts[:AHEAD]:
        piece = piece_of(slot, start, width, bands, [] if piece is None else [piece])
        theres.append(shifted(piece, "ka", -1))
    arrived = []
    result = None
    shape = (rows, k_dev, 2, nbands)
    for index, part in enumerate(parts):
        adding = parts[index - LAG] if index >= LAG else None
        ready = arrived[index - LAG] if index >= LAG else None
        later = parts[index + AHEAD] if index + AHEAD < len(parts) else None
        terms, result, piece = step(
            part[0], table, bands, theres[index], adding, ready, result, shape, later
        )
        if later:
            theres.append(shifted(piece, "ka", -1))
        terms = terms.reshape(grid_count, rows, 2 * part[2])
        arrived.append(lax.all_to_all(terms, "ga", 0, 0))
    return finish(parts[-LAG:], table, arrived[-LAG:], result)


def solution(mesh):
    placed = (P("ka", None, None, "ga"), P("ka"), P("ka"))
    return jax.shard_map(
        body, mesh=mesh, in_specs=placed, out_specs=P("ga", "ka", None, None), check_vma=False
    )
```

```python
import functools
import math

import jax
import jax.numpy as jnp
from jax import lax
from jax.experimental import pallas as pl
from jax.experimental.pallas import tpu as pltpu
from jax.sharding import PartitionSpec as P

NKB = 4
PLANE = 1024
STRIP = 32
DEPTH = 512
LAG = 2
AHEAD = 2
BLOCK = 256
VMEM_BYTES = 48 * 1024 * 1024


def shifted(block, axis, distance):
    count = lax.axis_size(axis)
    route = [((i - distance) % count, i) for i in range(count)]
    return lax.ppermute(block, axis, route)


def piece_kernel(slot, start, bands_ref, *rest):
    out_ref, piece_buf, sems = rest[-3:]
    width = piece_buf.shape[1]
    rows = pl.ds(start, width)
    loads = [
        pltpu.make_async_copy(bands_ref.at[slot, part, rows, :], piece_buf.at[part], sems.at[0, part])
        for part in range(2)
    ]
    stores = [
        pltpu.make_async_copy(piece_buf.at[part], out_ref.at[part], sems.at[1, part])
        for part in range(2)
    ]
    for load in loads:
        load.start()
    for load, store in zip(loads, stores):
        load.wait()
        store.start()
    for store in stores:
        store.wait()


def piece_of(slot, start, width, bands, after):
    points = bands.shape[3]
    return pl.pallas_call(
        functools.partial(piece_kernel, slot, start),
        in_specs=[pl.BlockSpec(memory_space=pl.ANY)] * (1 + len(after)),
        out_specs=pl.BlockSpec(memory_space=pl.ANY),
        scratch_shapes=[
            pltpu.VMEM((2, width, points), bands.dtype),
            pltpu.SemaphoreType.DMA((2, 2)),
        ],
        out_shape=jax.ShapeDtypeStruct((2, width, points), bands.dtype),
        compiler_params=pltpu.CompilerParams(vmem_limit_bytes=VMEM_BYTES),
        cost_estimate=pl.CostEstimate(flops=1000, bytes_accessed=1000, transcendentals=0),
        name="piece_of",
    )(bands, *after)


def near_into(near_buf, there_ref, table_ref, base, planes):
    width, points = there_ref.shape[1:]

    @pl.loop(0, width // STRIP)
    def _(strip):
        rows = pl.ds(strip * STRIP, STRIP)
        mirror = pl.ds(width + strip * STRIP, STRIP)
        for start in range(0, points, DEPTH):
            plane = start // PLANE
            cosine = table_ref[base + 1 + plane]
            sine = table_ref[base + 1 + planes + plane]
            columns = pl.ds(start, DEPTH)
            real_part = there_ref[0, rows, columns].astype(jnp.float32)
            imag_part = there_ref[1, rows, columns].astype(jnp.float32)
            near_re = real_part * cosine + imag_part * sine
            near_im = imag_part * cosine - real_part * sine
            near_buf[rows, columns] = near_re.astype(jnp.bfloat16)
            near_buf[mirror, columns] = near_im.astype(jnp.bfloat16)


def add_into(sum_buf, arrived_buf):
    width = arrived_buf.shape[2] // 2
    total = arrived_buf[0].astype(jnp.float32)
    for source in range(1, arrived_buf.shape[0]):
        total = total + arrived_buf[source].astype(jnp.float32)
    sum_buf[:, 0, :] = total[:, :width]
    sum_buf[:, 1, :] = total[:, width:]


def step_kernel(slot, k_dev, adding, first, later, table_ref, bands_ref, there_ref, *rest):
    stride = table_ref.shape[0] // k_dev
    planes = (stride - 1) // 2
    base = slot * stride
    point = table_ref[base].astype(jnp.int32)
    rest = list(rest)
    arrived_ref = rest.pop(0) if adding else None
    if adding and not first:
        rest.pop(0)
    out_ref = rest.pop(0)
    result_ref = rest.pop(0) if adding else None
    piece_ref = rest.pop(0) if later else None
    own_buf, near_buf, own_sems = rest[:3]
    del rest[:3]
    if later:
        piece_buf, piece_sems = rest[:2]
        del rest[:2]
        later_slot, later_start, later_width = later
        loads = [
            pltpu.make_async_copy(
                bands_ref.at[later_slot, part, pl.ds(later_start, later_width), :],
                piece_buf.at[part],
                piece_sems.at[0, part],
            )
            for part in range(2)
        ]
        stores = [
            pltpu.make_async_copy(piece_buf.at[part], piece_ref.at[part], piece_sems.at[1, part])
            for part in range(2)
        ]
    if adding:
        sum_buf, placed_sem = rest
    width = there_ref.shape[1]
    blocks = own_buf.shape[1] // BLOCK
    own = [
        pltpu.make_async_copy(
            bands_ref.at[point, part, pl.ds(block * BLOCK, BLOCK), :],
            own_buf.at[part, pl.ds(block * BLOCK, BLOCK), :],
            own_sems.at[block, part],
        )
        for block in range(blocks)
        for part in range(2)
    ]
    for copy in own + (loads if later else []):
        copy.start()
    if adding:
        add_slot, add_start, add_width = adding
        add_point = table_ref[add_slot * stride].astype(jnp.int32)
        add_into(sum_buf, arrived_ref)
        placing = pltpu.make_async_copy(
            sum_buf, result_ref.at[:, add_point, :, pl.ds(add_start, add_width)], placed_sem
        )
        placing.start()
    near_into(near_buf, there_ref, table_ref, base, planes)
    dims = (((1,), (1,)), ((), ()))
    half = there_ref.shape[2] // 2
    for block in range(blocks):
        lines = pl.ds(block * BLOCK, BLOCK)
        products = []
        for part in range(2):
            own[2 * block + part].wait()
            for first_column in (0, half):
                columns = pl.ds(first_column, half)
                products.append(
                    lax.dot_general(
                        own_buf[part, lines, columns],
                        near_buf[:, columns],
                        dims,
                        preferred_element_type=jnp.float32,
                    )
                )
        of_re = products[0] + products[1]
        of_im = products[2] + products[3]
        out_ref[lines, :width] = (of_re[:, :width] + of_im[:, width:]).astype(out_ref.dtype)
        out_ref[lines, width:] = (of_re[:, width:] - of_im[:, :width]).astype(out_ref.dtype)
        if later and block == 0:
            for load, store in zip(loads, stores):
                load.wait()
                store.start()
    if adding:
        placing.wait()
    if later:
        for store in stores:
            store.wait()


def step(slot, table, bands, there, adding, arrived, result, shape, later):
    k_dev, _, nbands, points = bands.shape
    width = there.shape[1]
    operands = [table, bands, there]
    spaces = [pltpu.SMEM, pl.ANY, pltpu.VMEM]
    out_shape = [jax.ShapeDtypeStruct((nbands, 2 * width), jnp.bfloat16)]
    out_specs = [pl.BlockSpec(memory_space=pltpu.VMEM)]
    scratch = [
        pltpu.VMEM((2, nbands, points), jnp.bfloat16),
        pltpu.VMEM((2 * width, points), jnp.bfloat16),
        pltpu.SemaphoreType.DMA((nbands // BLOCK, 2)),
    ]
    aliases = {}
    if later:
        scratch += [
            pltpu.VMEM((2, later[2], points), bands.dtype),
            pltpu.SemaphoreType.DMA((2, 2)),
        ]
    if adding:
        operands.append(arrived)
        spaces.append(pltpu.VMEM)
        if result is not None:
            aliases = {len(operands): 1}
            operands.append(result)
            spaces.append(pl.ANY)
        out_shape.append(jax.ShapeDtypeStruct(shape, jnp.float32))
        out_specs.append(pl.BlockSpec(memory_space=pl.ANY))
        scratch += [
            pltpu.VMEM((shape[0], 2, adding[2]), jnp.float32),
            pltpu.SemaphoreType.DMA,
        ]
    if later:
        out_shape.append(jax.ShapeDtypeStruct((2, later[2], points), bands.dtype))
        out_specs.append(pl.BlockSpec(memory_space=pl.ANY))
    outs = pl.pallas_call(
        functools.partial(step_kernel, slot, k_dev, adding, result is None, later),
        in_specs=[pl.BlockSpec(memory_space=space) for space in spaces],
        out_specs=out_specs,
        scratch_shapes=scratch,
        out_shape=out_shape,
        input_output_aliases=aliases,
        compiler_params=pltpu.CompilerParams(vmem_limit_bytes=VMEM_BYTES),
        cost_estimate=pl.CostEstimate(flops=1000, bytes_accessed=1000, transcendentals=0),
        name="step",
    )(*operands)
    return outs[0], outs[1] if adding else result, outs[-1] if later else None


def finish_kernel(parts, stride, table_ref, *refs):
    count = len(parts)
    arrived, result_ref = refs[:count], refs[count + 1]
    sums, sems = refs[count + 2 : -1], refs[-1]
    placing = []
    for i, (slot, start, width) in enumerate(parts):
        point = table_ref[slot * stride].astype(jnp.int32)
        add_into(sums[i], arrived[i])
        columns = pl.ds(start, width)
        placing.append(
            pltpu.make_async_copy(sums[i], result_ref.at[:, point, :, columns], sems.at[i])
        )
        placing[-1].start()
    for copy in placing:
        copy.wait()


def finish(parts, table, arrived, result):
    rows, k_dev = result.shape[:2]
    return pl.pallas_call(
        functools.partial(finish_kernel, parts, table.shape[0] // k_dev),
        in_specs=[pl.BlockSpec(memory_space=pltpu.SMEM)]
        + [pl.BlockSpec(memory_space=pltpu.VMEM)] * len(parts)
        + [pl.BlockSpec(memory_space=pl.ANY)],
        out_specs=pl.BlockSpec(memory_space=pl.ANY),
        scratch_shapes=[pltpu.VMEM((rows, 2, width), jnp.float32) for _, _, width in parts]
        + [pltpu.SemaphoreType.DMA((len(parts),))],
        out_shape=jax.ShapeDtypeStruct(result.shape, jnp.float32),
        input_output_aliases={1 + len(parts): 0},
        compiler_params=pltpu.CompilerParams(vmem_limit_bytes=VMEM_BYTES),
        cost_estimate=pl.CostEstimate(flops=1000, bytes_accessed=1000, transcendentals=0),
        name="finish",
    )(table, *arrived, result)


def cuts(nbands, first):
    half, quarter = nbands // 2, nbands // 4
    widths = [quarter, quarter, half] if first else [half, quarter, quarter]
    starts = [sum(widths[:i]) for i in range(len(widths))]
    return list(zip(starts, widths))


def body(bands, nbr_slot, gshift):
    grid_index = lax.axis_index("ga")
    grid_count = lax.axis_size("ga")
    k_dev, _, nbands, points = bands.shape
    rows = nbands // grid_count
    own_planes = points // PLANE
    total_planes = own_planes * grid_count
    planes = grid_index * own_planes + jnp.arange(own_planes, dtype=jnp.int32)
    slots = jnp.arange(k_dev, dtype=jnp.int32)
    chosen = nbr_slot[None, :] == slots[:, None]
    order = jnp.sum(jnp.where(chosen, slots[None, :], 0), axis=1)
    shifts = jnp.sum(jnp.where(chosen, gshift[None, :], 0), axis=1)
    turns = (1 + NKB * shifts[:, None]) * planes[None, :] % (NKB * total_planes)
    angle = 2.0 * math.pi / (NKB * total_planes) * turns.astype(jnp.float32)
    columns = [order[:, None].astype(jnp.float32), jnp.cos(angle), jnp.sin(angle)]
    table = jnp.concatenate(columns, axis=1).reshape(-1)
    parts = []
    for slot in range(k_dev):
        for start, width in cuts(nbands, slot == 0):
            parts.append((slot, start, width))
    theres = []
    piece = None
    for slot, start, width in parts[:AHEAD]:
        piece = piece_of(slot, start, width, bands, [] if piece is None else [piece])
        theres.append(shifted(piece, "ka", -1))
    arrived = []
    result = None
    shape = (rows, k_dev, 2, nbands)
    for index, part in enumerate(parts):
        adding = parts[index - LAG] if index >= LAG else None
        ready = arrived[index - LAG] if index >= LAG else None
        later = parts[index + AHEAD] if index + AHEAD < len(parts) else None
        terms, result, piece = step(
            part[0], table, bands, theres[index], adding, ready, result, shape, later
        )
        if later:
            theres.append(shifted(piece, "ka", -1))
        terms = terms.reshape(grid_count, rows, 2 * part[2])
        arrived.append(lax.all_to_all(terms, "ga", 0, 0))
    return finish(parts[-LAG:], table, arrived[-LAG:], result)


def solution(mesh):
    placed = (P("ka", None, None, "ga"), P("ka"), P("ka"))
    return jax.shard_map(
        body, mesh=mesh, in_specs=placed, out_specs=P("ga", "ka", None, None), check_vma=False
    )
```

```python
import functools
import math
from typing import NamedTuple

import jax
import jax.numpy as jnp
from jax import lax
from jax.experimental import pallas as pl
from jax.experimental.pallas import tpu as pltpu
from jax.sharding import PartitionSpec as P

NKB = 4
PLANE = 1024
STRIP = 32
DEPTH = 512
AHEAD = 2
OUTER = 4
SPLIT = 128
LANES = 128
BLOCK = 256
VMEM_BYTES = 48 * 1024 * 1024


def shifted(block, axis, distance, fold=1, inner=False):
    count = lax.axis_size(axis)
    route = []
    for i in range(count):
        outer, place = divmod(i, fold)
        if inner:
            route.append((i, outer * fold + (place + distance) % fold))
        else:
            route.append((i, (outer + distance) % (count // fold) * fold + place))
    return lax.ppermute(block, axis, route)


def piece_kernel(slot, start, bands_ref, *rest):
    out_ref, piece_buf, sems = rest[-3:]
    width = piece_buf.shape[1]
    rows = pl.ds(start, width)
    loads = [
        pltpu.make_async_copy(bands_ref.at[slot, part, rows, :], piece_buf.at[part], sems.at[0, part])
        for part in range(2)
    ]
    stores = [
        pltpu.make_async_copy(piece_buf.at[part], out_ref.at[part], sems.at[1, part])
        for part in range(2)
    ]
    for load in loads:
        load.start()
    for load, store in zip(loads, stores):
        load.wait()
        store.start()
    for store in stores:
        store.wait()


def piece_of(slot, start, width, bands, after):
    points = bands.shape[3]
    return pl.pallas_call(
        functools.partial(piece_kernel, slot, start),
        in_specs=[pl.BlockSpec(memory_space=pl.ANY)] * (1 + len(after)),
        out_specs=pl.BlockSpec(memory_space=pl.ANY),
        scratch_shapes=[
            pltpu.VMEM((2, width, points), bands.dtype),
            pltpu.SemaphoreType.DMA((2, 2)),
        ],
        out_shape=jax.ShapeDtypeStruct((2, width, points), bands.dtype),
        compiler_params=pltpu.CompilerParams(vmem_limit_bytes=VMEM_BYTES),
        cost_estimate=pl.CostEstimate(flops=1000, bytes_accessed=1000, transcendentals=0),
        name="piece_of",
    )(bands, *after)


def near_into(near_buf, there_ref, table_ref, base, planes):
    width, points = there_ref.shape[1:]

    @pl.loop(0, width // STRIP)
    def _(strip):
        rows = pl.ds(strip * STRIP, STRIP)
        mirror = pl.ds(width + strip * STRIP, STRIP)
        for start in range(0, points, DEPTH):
            plane = start // PLANE
            cosine = table_ref[base + 1 + plane]
            sine = table_ref[base + 1 + planes + plane]
            columns = pl.ds(start, DEPTH)
            real_part = there_ref[0, rows, columns].astype(jnp.float32)
            imag_part = there_ref[1, rows, columns].astype(jnp.float32)
            near_re = real_part * cosine + imag_part * sine
            near_im = imag_part * cosine - real_part * sine
            near_buf[rows, columns] = near_re.astype(jnp.bfloat16)
            near_buf[mirror, columns] = near_im.astype(jnp.bfloat16)


def put_sum(sum_buf, lane, total):
    width = total.shape[1] // 2
    sum_buf[:, 0, lane : lane + width] = total[:, :width]
    sum_buf[:, 1, lane : lane + width] = total[:, width:]


def step_kernel(plan, table_ref, *refs):
    rows, k_dev, _, nbands = plan.shape
    fold, depth = plan.fold, plan.depth
    refs = list(refs)

    def take(count):
        taken = refs[:count]
        del refs[:count]
        return taken

    stride = (table_ref.shape[0] - 1) // k_dev
    planes = (stride - 1) // 2
    me = table_ref[k_dev * stride].astype(jnp.int32)
    place, outer = lax.rem(me, fold), lax.div(me, fold)
    if plan.part:
        bands_ref, there_ref = take(2)
    folded = take(fold) if plan.folding else None
    arrived = [take(depth) for _ in plan.adding]
    if plan.adding and plan.placed:
        take(1)
    outs = take(fold) if plan.part else None
    sends = take(depth) if plan.folding else None
    result_ref = take(1)[0] if plan.adding else None
    piece_ref = take(1)[0] if plan.later else None
    if plan.part:
        own_buf, near_buf, terms_buf, own_sems = take(4)
        slot = plan.part[0]
        base = slot * stride
        point = table_ref[base].astype(jnp.int32)
        width = there_ref.shape[1]
        blocks = nbands // BLOCK
        own = [
            pltpu.make_async_copy(
                bands_ref.at[point, part, pl.ds(block * BLOCK, BLOCK), :],
                own_buf.at[part, pl.ds(block * BLOCK, BLOCK), :],
                own_sems.at[block, part],
            )
            for block in range(blocks)
            for part in range(2)
        ]
        for copy in own:
            copy.start()
    if plan.later:
        piece_buf, piece_sems = take(2)
        later_slot, later_start, later_width = plan.later
        loads = [
            pltpu.make_async_copy(
                bands_ref.at[later_slot, part, pl.ds(later_start, later_width), :],
                piece_buf.at[part],
                piece_sems.at[0, part],
            )
            for part in range(2)
        ]
        stores = [
            pltpu.make_async_copy(piece_buf.at[part], piece_ref.at[part], piece_sems.at[1, part])
            for part in range(2)
        ]
        for copy in loads:
            copy.start()
    if plan.adding:
        sum_buf, placed_sem = take(2)
        add_slot, add_start, _ = plan.adding[0]
        for (_, start, _), arrays in zip(plan.adding, arrived):
            total = arrays[0][...]
            for array in arrays[1:]:
                total = total + array[...].astype(jnp.float32)
            put_sum(sum_buf, start - add_start, total)
        add_point = table_ref[add_slot * stride].astype(jnp.int32)
        columns = pl.ds(add_start, sum_buf.shape[2])
        placing = pltpu.make_async_copy(
            sum_buf, result_ref.at[:, add_point, :, columns], placed_sem
        )
        placing.start()
    if plan.folding:
        for distance, send_ref in enumerate(sends):
            target = lax.rem(outer + distance, depth)
            total = folded[0][target]
            for array in folded[1:]:
                total = total + array[target].astype(jnp.float32)
            send_ref[...] = total.astype(send_ref.dtype)
    if plan.part:
        near_into(near_buf, there_ref, table_ref, base, planes)
        dims = (((1,), (1,)), ((), ()))
        points = there_ref.shape[2]
        run = points // 2 if width <= SPLIT else points
        for block in range(blocks):
            lines = pl.ds(block * BLOCK, BLOCK)
            of_both = []
            for part in range(2):
                own[2 * block + part].wait()
                products = [
                    lax.dot_general(
                        own_buf[part, lines, pl.ds(first, run)],
                        near_buf[:, pl.ds(first, run)],
                        dims,
                        preferred_element_type=jnp.float32,
                    )
                    for first in range(0, points, run)
                ]
                of_both.append(sum(products[1:], products[0]))
            of_re, of_im = of_both
            terms_buf[lines, :width] = of_re[:, :width] + of_im[:, width:]
            terms_buf[lines, width:] = of_re[:, width:] - of_im[:, :width]
            if plan.later and block == 0:
                for load, store in zip(loads, stores):
                    load.wait()
                    store.start()
        for distance, out_ref in enumerate(outs):
            target = lax.rem(place + distance, fold)
            for level in range(depth):
                first = pl.multiple_of((level * fold + target) * rows, rows)
                out_ref[level] = terms_buf[pl.ds(first, rows), :].astype(out_ref.dtype)
    if plan.adding:
        placing.wait()
    if plan.later:
        for store in stores:
            store.wait()


class Plan(NamedTuple):
    shape: tuple
    fold: int
    depth: int
    part: tuple
    folding: tuple
    adding: tuple
    placed: bool
    later: tuple


def step(plan, table, bands, there, folded, arrived, result):
    rows, _, _, nbands = plan.shape
    fold, depth = plan.fold, plan.depth
    points = bands.shape[3]
    vmem = pl.BlockSpec(memory_space=pltpu.VMEM)
    hbm = pl.BlockSpec(memory_space=pltpu.HBM)
    operands, in_specs = [table], [pl.BlockSpec(memory_space=pltpu.SMEM)]
    out_shape, out_specs, scratch, aliases = [], [], [], {}

    def kind(index):
        return jnp.bfloat16 if index else jnp.float32

    if plan.part:
        width = plan.part[2]
        operands += [bands, there]
        in_specs += [hbm, vmem]
        out_shape += [
            jax.ShapeDtypeStruct((depth, rows, 2 * width), kind(i)) for i in range(fold)
        ]
        out_specs += [vmem] * fold
        scratch += [
            pltpu.VMEM((2, nbands, points), jnp.bfloat16),
            pltpu.VMEM((2 * width, points), jnp.bfloat16),
            pltpu.VMEM((nbands, 2 * width), jnp.float32),
            pltpu.SemaphoreType.DMA((nbands // BLOCK, 2)),
        ]
    if plan.folding:
        operands += folded
        in_specs += [vmem] * fold
        out_shape += [
            jax.ShapeDtypeStruct((rows, 2 * plan.folding[2]), kind(i)) for i in range(depth)
        ]
        out_specs += [vmem] * depth
    if plan.later:
        scratch += [
            pltpu.VMEM((2, plan.later[2], points), bands.dtype),
            pltpu.SemaphoreType.DMA((2, 2)),
        ]
    if plan.adding:
        for arrays in arrived:
            operands += arrays
            in_specs += [vmem] * depth
        if plan.placed:
            aliases = {len(operands): len(out_shape)}
            operands.append(result)
            in_specs.append(hbm)
        out_shape.append(jax.ShapeDtypeStruct(plan.shape, jnp.float32))
        out_specs.append(hbm)
        lanes = sum(width for _, _, width in plan.adding)
        scratch += [pltpu.VMEM((rows, 2, lanes), jnp.float32), pltpu.SemaphoreType.DMA]
    if plan.later:
        out_shape.append(jax.ShapeDtypeStruct((2, plan.later[2], points), bands.dtype))
        out_specs.append(hbm)
    outs = list(
        pl.pallas_call(
            functools.partial(step_kernel, plan),
            in_specs=in_specs,
            out_specs=out_specs,
            scratch_shapes=scratch,
            out_shape=out_shape,
            input_output_aliases=aliases,
            compiler_params=pltpu.CompilerParams(vmem_limit_bytes=VMEM_BYTES),
            cost_estimate=pl.CostEstimate(flops=1000, bytes_accessed=1000, transcendentals=0),
            name="step",
        )(*operands)
    )
    piece = outs.pop() if plan.later else None
    result = outs.pop() if plan.adding else result
    terms = outs[:fold] if plan.part else None
    sends = outs[-depth:] if plan.folding else None
    return terms, sends, result, piece


def cuts(nbands, first):
    half, quarter = nbands // 2, nbands // 4
    widths = [quarter, quarter, half] if first else [half, quarter, quarter]
    starts = [sum(widths[:i]) for i in range(len(widths))]
    return list(zip(starts, widths))


def adding_jobs(parts):
    jobs = {}
    group = ()
    for index, part in enumerate(parts):
        group += (part,)
        if sum(width for _, _, width in group) % LANES == 0:
            jobs[index] = group
            group = ()
    return jobs


def body(bands, nbr_slot, gshift):
    grid_index = lax.axis_index("ga")
    grid_count = lax.axis_size("ga")
    k_dev, _, nbands, points = bands.shape
    rows = nbands // grid_count
    own_planes = points // PLANE
    total_planes = own_planes * grid_count
    planes = grid_index * own_planes + jnp.arange(own_planes, dtype=jnp.int32)
    slots = jnp.arange(k_dev, dtype=jnp.int32)
    chosen = nbr_slot[None, :] == slots[:, None]
    order = jnp.sum(jnp.where(chosen, slots[None, :], 0), axis=1)
    shifts = jnp.sum(jnp.where(chosen, gshift[None, :], 0), axis=1)
    turns = (1 + NKB * shifts[:, None]) * planes[None, :] % (NKB * total_planes)
    angle = 2.0 * math.pi / (NKB * total_planes) * turns.astype(jnp.float32)
    columns = [order[:, None].astype(jnp.float32), jnp.cos(angle), jnp.sin(angle)]
    table = jnp.concatenate(columns, axis=1).reshape(-1)
    table = jnp.append(table, grid_index.astype(jnp.float32))
    parts = []
    for slot in range(k_dev):
        for start, width in cuts(nbands, slot == 0):
            parts.append((slot, start, width))
    theres = []
    piece = None
    for slot, start, width in parts[:AHEAD]:
        piece = piece_of(slot, start, width, bands, [] if piece is None else [piece])
        theres.append(shifted(piece, "ka", -1))
    shape = (rows, k_dev, 2, nbands)
    depth = min(OUTER, grid_count)
    fold = grid_count // depth
    jobs = adding_jobs(parts)
    folded, arrived = {}, {}
    result = None
    for index in range(len(parts) + 2):
        part = parts[index] if index < len(parts) else None
        folding = parts[index - 1] if 0 <= index - 1 < len(parts) else None
        adding = jobs.get(index - 2, ())
        later = parts[index + AHEAD] if index + AHEAD < len(parts) else None
        plan = Plan(shape, fold, depth, part, folding, adding, result is not None, later)
        terms, sends, result, piece = step(
            plan,
            table,
            bands,
            theres[index] if part else None,
            folded.pop(folding, None),
            [arrived.pop(done) for done in adding],
            result,
        )
        if later:
            theres.append(shifted(piece, "ka", -1))
        if part:
            folded[part] = [terms[0]] + [
                shifted(terms[i], "ga", i, fold, True) for i in range(1, fold)
            ]
        if folding:
            arrived[folding] = [sends[0]] + [
                shifted(sends[i], "ga", i, fold) for i in range(1, depth)
            ]
    return result


def solution(mesh):
    placed = (P("ka", None, None, "ga"), P("ka"), P("ka"))
    return jax.shard_map(
        body, mesh=mesh, in_specs=placed, out_specs=P("ga", "ka", None, None), check_vma=False
    )
```

```python
import functools
import math
from typing import NamedTuple

import jax
import jax.numpy as jnp
from jax import lax
from jax.experimental import pallas as pl
from jax.experimental.pallas import tpu as pltpu
from jax.sharding import PartitionSpec as P

NKB = 4
PLANE = 1024
STRIP = 32
DEPTH = 512
AHEAD = 2
OUTER = 4
SPLIT = 128
LANES = 128
BLOCK = 256
VMEM_BYTES = 48 * 1024 * 1024


def shifted(block, axis, distance, fold=1, inner=False):
    count = lax.axis_size(axis)
    route = []
    for i in range(count):
        outer, place = divmod(i, fold)
        if inner:
            route.append((i, outer * fold + (place + distance) % fold))
        else:
            route.append((i, (outer + distance) % (count // fold) * fold + place))
    return lax.ppermute(block, axis, route)


def piece_kernel(slot, start, bands_ref, *rest):
    out_ref, piece_buf, sems = rest[-3:]
    width = piece_buf.shape[1]
    rows = pl.ds(start, width)
    loads = [
        pltpu.make_async_copy(bands_ref.at[slot, part, rows, :], piece_buf.at[part], sems.at[0, part])
        for part in range(2)
    ]
    stores = [
        pltpu.make_async_copy(piece_buf.at[part], out_ref.at[part], sems.at[1, part])
        for part in range(2)
    ]
    for load in loads:
        load.start()
    for load, store in zip(loads, stores):
        load.wait()
        store.start()
    for store in stores:
        store.wait()


def piece_of(slot, start, width, bands, after):
    points = bands.shape[3]
    return pl.pallas_call(
        functools.partial(piece_kernel, slot, start),
        in_specs=[pl.BlockSpec(memory_space=pl.ANY)] * (1 + len(after)),
        out_specs=pl.BlockSpec(memory_space=pl.ANY),
        scratch_shapes=[
            pltpu.VMEM((2, width, points), bands.dtype),
            pltpu.SemaphoreType.DMA((2, 2)),
        ],
        out_shape=jax.ShapeDtypeStruct((2, width, points), bands.dtype),
        compiler_params=pltpu.CompilerParams(vmem_limit_bytes=VMEM_BYTES),
        cost_estimate=pl.CostEstimate(flops=1000, bytes_accessed=1000, transcendentals=0),
        name="piece_of",
    )(bands, *after)


def near_into(near_buf, there_ref, table_ref, base, planes):
    width, points = there_ref.shape[1:]

    @pl.loop(0, width // STRIP)
    def _(strip):
        rows = pl.ds(strip * STRIP, STRIP)
        mirror = pl.ds(width + strip * STRIP, STRIP)
        for start in range(0, points, DEPTH):
            plane = start // PLANE
            cosine = table_ref[base + 1 + plane]
            sine = table_ref[base + 1 + planes + plane]
            columns = pl.ds(start, DEPTH)
            real_part = there_ref[0, rows, columns].astype(jnp.float32)
            imag_part = there_ref[1, rows, columns].astype(jnp.float32)
            near_re = real_part * cosine + imag_part * sine
            near_im = imag_part * cosine - real_part * sine
            near_buf[rows, columns] = near_re.astype(jnp.bfloat16)
            near_buf[mirror, columns] = near_im.astype(jnp.bfloat16)


def put_sum(sum_buf, lane, total):
    width = total.shape[1] // 2
    sum_buf[:, 0, lane : lane + width] = total[:, :width]
    sum_buf[:, 1, lane : lane + width] = total[:, width:]


def step_kernel(plan, table_ref, *refs):
    rows, k_dev, _, nbands = plan.shape
    fold, depth = plan.fold, plan.depth
    refs = list(refs)

    def take(count):
        taken = refs[:count]
        del refs[:count]
        return taken

    stride = (table_ref.shape[0] - 1) // k_dev
    planes = (stride - 1) // 2
    me = table_ref[k_dev * stride].astype(jnp.int32)
    place, outer = lax.rem(me, fold), lax.div(me, fold)
    if plan.part:
        bands_ref, there_ref = take(2)
    folded = [take(fold) for _ in plan.folding]
    arrived = [take(depth) for _ in plan.adding]
    if plan.adding and plan.placed:
        take(1)
    take(plan.after)
    outs = take(fold) if plan.part else None
    sends = take(depth) if plan.folding else None
    result_ref = take(1)[0] if plan.adding else None
    piece_ref = take(1)[0] if plan.later else None
    if plan.part:
        own_buf, near_buf, terms_buf, own_sems = take(4)
        slot = plan.part[0]
        base = slot * stride
        point = table_ref[base].astype(jnp.int32)
        width = there_ref.shape[1]
        blocks = nbands // BLOCK
        own = [
            pltpu.make_async_copy(
                bands_ref.at[point, part, pl.ds(block * BLOCK, BLOCK), :],
                own_buf.at[part, pl.ds(block * BLOCK, BLOCK), :],
                own_sems.at[block, part],
            )
            for block in range(blocks)
            for part in range(2)
        ]
        for copy in own:
            copy.start()
    if plan.later:
        piece_buf, piece_sems = take(2)
        later_slot, later_start, later_width = plan.later
        loads = [
            pltpu.make_async_copy(
                bands_ref.at[later_slot, part, pl.ds(later_start, later_width), :],
                piece_buf.at[part],
                piece_sems.at[0, part],
            )
            for part in range(2)
        ]
        stores = [
            pltpu.make_async_copy(piece_buf.at[part], piece_ref.at[part], piece_sems.at[1, part])
            for part in range(2)
        ]
        for copy in loads:
            copy.start()
    if plan.adding:
        sum_buf, placed_sem = take(2)
        add_slot, add_start, _ = plan.adding[0][0]
        for batch, arrays in zip(plan.adding, arrived):
            total = arrays[0][...]
            for array in arrays[1:]:
                total = total + array[...].astype(jnp.float32)
            column = 0
            for _, start, width in batch:
                put_sum(sum_buf, start - add_start, total[:, column : column + 2 * width])
                column += 2 * width
        add_point = table_ref[add_slot * stride].astype(jnp.int32)
        columns = pl.ds(add_start, sum_buf.shape[2])
        placing = pltpu.make_async_copy(
            sum_buf, result_ref.at[:, add_point, :, columns], placed_sem
        )
        placing.start()
    if plan.folding:
        for distance, send_ref in enumerate(sends):
            target = lax.rem(outer + distance, depth)
            column = 0
            for arrays in folded:
                total = arrays[0][target]
                for array in arrays[1:]:
                    total = total + array[target].astype(jnp.float32)
                columns = slice(column, column + total.shape[1])
                send_ref[:, columns] = total.astype(send_ref.dtype)
                column += total.shape[1]
    if plan.part:
        near_into(near_buf, there_ref, table_ref, base, planes)
        dims = (((1,), (1,)), ((), ()))
        points = there_ref.shape[2]
        run = points // 2 if width <= SPLIT else points
        for block in range(blocks):
            lines = pl.ds(block * BLOCK, BLOCK)
            of_both = []
            for part in range(2):
                own[2 * block + part].wait()
                products = [
                    lax.dot_general(
                        own_buf[part, lines, pl.ds(first, run)],
                        near_buf[:, pl.ds(first, run)],
                        dims,
                        preferred_element_type=jnp.float32,
                    )
                    for first in range(0, points, run)
                ]
                of_both.append(sum(products[1:], products[0]))
            of_re, of_im = of_both
            terms_buf[lines, :width] = of_re[:, :width] + of_im[:, width:]
            terms_buf[lines, width:] = of_re[:, width:] - of_im[:, :width]
            if plan.later and block == 0:
                for load, store in zip(loads, stores):
                    load.wait()
                    store.start()
        for distance, out_ref in enumerate(outs):
            target = lax.rem(place + distance, fold)
            for level in range(depth):
                first = pl.multiple_of((level * fold + target) * rows, rows)
                out_ref[level] = terms_buf[pl.ds(first, rows), :].astype(out_ref.dtype)
    if plan.adding:
        placing.wait()
    if plan.later:
        for store in stores:
            store.wait()


class Plan(NamedTuple):
    shape: tuple
    fold: int
    depth: int
    part: tuple
    folding: tuple
    adding: tuple
    placed: bool
    later: tuple
    after: int


def step(plan, table, bands, there, folded, arrived, result, after):
    rows, _, _, nbands = plan.shape
    fold, depth = plan.fold, plan.depth
    points = bands.shape[3]
    vmem = pl.BlockSpec(memory_space=pltpu.VMEM)
    hbm = pl.BlockSpec(memory_space=pltpu.HBM)
    operands, in_specs = [table], [pl.BlockSpec(memory_space=pltpu.SMEM)]
    out_shape, out_specs, scratch, aliases = [], [], [], {}

    def kind(index):
        return jnp.bfloat16 if index else jnp.float32

    if plan.part:
        width = plan.part[2]
        operands += [bands, there]
        in_specs += [hbm, vmem]
        out_shape += [
            jax.ShapeDtypeStruct((depth, rows, 2 * width), kind(i)) for i in range(fold)
        ]
        out_specs += [vmem] * fold
        scratch += [
            pltpu.VMEM((2, nbands, points), jnp.bfloat16),
            pltpu.VMEM((2 * width, points), jnp.bfloat16),
            pltpu.VMEM((nbands, 2 * width), jnp.float32),
            pltpu.SemaphoreType.DMA((nbands // BLOCK, 2)),
        ]
    if plan.folding:
        for arrays in folded:
            operands += arrays
            in_specs += [vmem] * fold
        wide = sum(2 * width for _, _, width in plan.folding)
        out_shape += [jax.ShapeDtypeStruct((rows, wide), kind(i)) for i in range(depth)]
        out_specs += [vmem] * depth
    if plan.later:
        scratch += [
            pltpu.VMEM((2, plan.later[2], points), bands.dtype),
            pltpu.SemaphoreType.DMA((2, 2)),
        ]
    if plan.adding:
        for arrays in arrived:
            operands += arrays
            in_specs += [vmem] * depth
        if plan.placed:
            aliases = {len(operands): len(out_shape)}
            operands.append(result)
            in_specs.append(hbm)
        out_shape.append(jax.ShapeDtypeStruct(plan.shape, jnp.float32))
        out_specs.append(hbm)
        lanes = sum(width for batch in plan.adding for _, _, width in batch)
        scratch += [pltpu.VMEM((rows, 2, lanes), jnp.float32), pltpu.SemaphoreType.DMA]
    operands += after
    in_specs += [pl.BlockSpec(memory_space=pl.ANY)] * len(after)
    if plan.later:
        out_shape.append(jax.ShapeDtypeStruct((2, plan.later[2], points), bands.dtype))
        out_specs.append(hbm)
    outs = list(
        pl.pallas_call(
            functools.partial(step_kernel, plan),
            in_specs=in_specs,
            out_specs=out_specs,
            scratch_shapes=scratch,
            out_shape=out_shape,
            input_output_aliases=aliases,
            compiler_params=pltpu.CompilerParams(vmem_limit_bytes=VMEM_BYTES),
            cost_estimate=pl.CostEstimate(flops=1000, bytes_accessed=1000, transcendentals=0),
            name="step",
        )(*operands)
    )
    piece = outs.pop() if plan.later else None
    result = outs.pop() if plan.adding else result
    terms = outs[:fold] if plan.part else None
    sends = outs[-depth:] if plan.folding else None
    return terms, sends, result, piece


def cuts(nbands, first):
    eighth = nbands // 8
    widths = [4 * eighth, 4 * eighth] if first else [3 * eighth, 3 * eighth, 2 * eighth]
    starts = [sum(widths[:i]) for i in range(len(widths))]
    return list(zip(starts, widths))


def schedule(parts):
    kernels = []
    waiting = []
    for part in parts[:-2]:
        kernels.append((part, (), ()))
        ready = waiting_block(waiting)
        for batch in ready:
            waiting.remove(batch)
        kernels.append((None, (part,), ready))
        waiting.append((part,))
    kernels.append((parts[-2], (), ()))
    kernels.append((parts[-1], (), ()))
    kernels.append((None, tuple(parts[-2:]), ()))
    kernels.append((None, (), tuple(waiting) + (tuple(parts[-2:]),)))
    return kernels


def waiting_block(waiting):
    total = 0
    for count, batch in enumerate(waiting, 1):
        total += sum(width for _, _, width in batch)
        if total % LANES == 0:
            return tuple(waiting[:count])
    return ()


def body(bands, nbr_slot, gshift):
    grid_index = lax.axis_index("ga")
    grid_count = lax.axis_size("ga")
    k_dev, _, nbands, points = bands.shape
    rows = nbands // grid_count
    own_planes = points // PLANE
    total_planes = own_planes * grid_count
    planes = grid_index * own_planes + jnp.arange(own_planes, dtype=jnp.int32)
    slots = jnp.arange(k_dev, dtype=jnp.int32)
    chosen = nbr_slot[None, :] == slots[:, None]
    order = jnp.sum(jnp.where(chosen, slots[None, :], 0), axis=1)
    shifts = jnp.sum(jnp.where(chosen, gshift[None, :], 0), axis=1)
    turns = (1 + NKB * shifts[:, None]) * planes[None, :] % (NKB * total_planes)
    angle = 2.0 * math.pi / (NKB * total_planes) * turns.astype(jnp.float32)
    columns = [order[:, None].astype(jnp.float32), jnp.cos(angle), jnp.sin(angle)]
    table = jnp.concatenate(columns, axis=1).reshape(-1)
    table = jnp.append(table, grid_index.astype(jnp.float32))
    parts = []
    for slot in range(k_dev):
        for start, width in cuts(nbands, slot == 0):
            parts.append((slot, start, width))
    theres = []
    piece = None
    for slot, start, width in parts[:AHEAD]:
        piece = piece_of(slot, start, width, bands, [] if piece is None else [piece])
        theres.append(shifted(piece, "ka", -1))
    shape = (rows, k_dev, 2, nbands)
    depth = min(OUTER, grid_count)
    fold = grid_count // depth
    folded, arrived = {}, {}
    result = None
    after = []
    for part, folding, adding in schedule(parts):
        index = parts.index(part) + AHEAD if part else len(parts)
        later = parts[index] if index < len(parts) else None
        plan = Plan(
            shape, fold, depth, part, folding, adding, result is not None, later, len(after)
        )
        terms, sends, result, piece = step(
            plan,
            table,
            bands,
            theres[parts.index(part)] if part else None,
            [folded.pop(done) for done in folding],
            [arrived.pop(batch) for batch in adding],
            result,
            after,
        )
        after = []
        if later:
            theres.append(shifted(piece, "ka", -1))
        if part:
            folded[part] = [terms[0]] + [
                shifted(terms[i], "ga", i, fold, True) for i in range(1, fold)
            ]
        if folding:
            arrived[folding] = [sends[0]] + [
                shifted(sends[i], "ga", i, fold) for i in range(1, depth)
            ]
            after = [sends[1]]
    return result


def solution(mesh):
    placed = (P("ka", None, None, "ga"), P("ka"), P("ka"))
    return jax.shard_map(
        body, mesh=mesh, in_specs=placed, out_specs=P("ga", "ka", None, None), check_vma=False
    )
```

```python
import functools
import math
from typing import NamedTuple

import jax
import jax.numpy as jnp
from jax import lax
from jax.experimental import pallas as pl
from jax.experimental.pallas import tpu as pltpu
from jax.sharding import PartitionSpec as P

NKB = 4
PLANE = 1024
STRIP = 32
DEPTH = 512
AHEAD = 2
OUTER = 4
SPLIT = 128
LANES = 128
BLOCK = 256
VMEM_BYTES = 48 * 1024 * 1024


def shifted(block, axis, distance, fold=1, inner=False):
    count = lax.axis_size(axis)
    route = []
    for i in range(count):
        outer, place = divmod(i, fold)
        if inner:
            route.append((i, outer * fold + (place + distance) % fold))
        else:
            route.append((i, (outer + distance) % (count // fold) * fold + place))
    return lax.ppermute(block, axis, route)


def piece_kernel(slot, start, bands_ref, *rest):
    out_ref, piece_buf, sems = rest[-3:]
    width = piece_buf.shape[1]
    rows = pl.ds(start, width)
    loads = [
        pltpu.make_async_copy(bands_ref.at[slot, part, rows, :], piece_buf.at[part], sems.at[0, part])
        for part in range(2)
    ]
    stores = [
        pltpu.make_async_copy(piece_buf.at[part], out_ref.at[part], sems.at[1, part])
        for part in range(2)
    ]
    for load in loads:
        load.start()
    for load, store in zip(loads, stores):
        load.wait()
        store.start()
    for store in stores:
        store.wait()


def piece_of(slot, start, width, bands, after):
    points = bands.shape[3]
    return pl.pallas_call(
        functools.partial(piece_kernel, slot, start),
        in_specs=[pl.BlockSpec(memory_space=pl.ANY)] * (1 + len(after)),
        out_specs=pl.BlockSpec(memory_space=pl.ANY),
        scratch_shapes=[
            pltpu.VMEM((2, width, points), bands.dtype),
            pltpu.SemaphoreType.DMA((2, 2)),
        ],
        out_shape=jax.ShapeDtypeStruct((2, width, points), bands.dtype),
        compiler_params=pltpu.CompilerParams(vmem_limit_bytes=VMEM_BYTES),
        cost_estimate=pl.CostEstimate(flops=1000, bytes_accessed=1000, transcendentals=0),
        name="piece_of",
    )(bands, *after)


def near_into(near_buf, there_ref, table_ref, base, planes):
    width, points = there_ref.shape[1:]

    @pl.loop(0, width // STRIP)
    def _(strip):
        rows = pl.ds(strip * STRIP, STRIP)
        mirror = pl.ds(width + strip * STRIP, STRIP)
        for start in range(0, points, DEPTH):
            plane = start // PLANE
            cosine = table_ref[base + 1 + plane]
            sine = table_ref[base + 1 + planes + plane]
            columns = pl.ds(start, DEPTH)
            real_part = there_ref[0, rows, columns].astype(jnp.float32)
            imag_part = there_ref[1, rows, columns].astype(jnp.float32)
            near_re = real_part * cosine + imag_part * sine
            near_im = imag_part * cosine - real_part * sine
            near_buf[rows, columns] = near_re.astype(jnp.bfloat16)
            near_buf[mirror, columns] = near_im.astype(jnp.bfloat16)


def put_sum(sum_buf, lane, total):
    width = total.shape[1] // 2
    sum_buf[:, 0, lane : lane + width] = total[:, :width]
    sum_buf[:, 1, lane : lane + width] = total[:, width:]


def step_kernel(plan, table_ref, *refs):
    rows, k_dev, _, nbands = plan.shape
    fold, depth = plan.fold, plan.depth
    refs = list(refs)

    def take(count):
        taken = refs[:count]
        del refs[:count]
        return taken

    stride = (table_ref.shape[0] - 1) // k_dev
    planes = (stride - 1) // 2
    me = table_ref[k_dev * stride].astype(jnp.int32)
    place, outer = lax.rem(me, fold), lax.div(me, fold)
    if plan.part:
        bands_ref, there_ref = take(2)
    folded = [take(fold) for _ in plan.folding]
    arrived = [take(depth) for _ in plan.adding]
    if plan.adding and plan.placed:
        take(1)
    outs = take(fold) if plan.part else None
    sends = take(depth) if plan.folding else None
    result_ref = take(1)[0] if plan.adding else None
    piece_ref = take(1)[0] if plan.later else None
    if plan.part:
        own_buf, near_buf, terms_buf, own_sems = take(4)
        slot = plan.part[0]
        base = slot * stride
        point = table_ref[base].astype(jnp.int32)
        width = there_ref.shape[1]
        blocks = nbands // BLOCK
        own = [
            pltpu.make_async_copy(
                bands_ref.at[point, part, pl.ds(block * BLOCK, BLOCK), :],
                own_buf.at[part, pl.ds(block * BLOCK, BLOCK), :],
                own_sems.at[block, part],
            )
            for block in range(blocks)
            for part in range(2)
        ]
        for copy in own:
            copy.start()
    if plan.later:
        piece_buf, piece_sems = take(2)
        later_slot, later_start, later_width = plan.later
        loads = [
            pltpu.make_async_copy(
                bands_ref.at[later_slot, part, pl.ds(later_start, later_width), :],
                piece_buf.at[part],
                piece_sems.at[0, part],
            )
            for part in range(2)
        ]
        stores = [
            pltpu.make_async_copy(piece_buf.at[part], piece_ref.at[part], piece_sems.at[1, part])
            for part in range(2)
        ]
        for copy in loads:
            copy.start()
    if plan.adding:
        sum_buf, placed_sem = take(2)
        add_slot, add_start, _ = plan.adding[0][0]
        for batch, arrays in zip(plan.adding, arrived):
            total = arrays[0][...]
            for array in arrays[1:]:
                total = total + array[...].astype(jnp.float32)
            column = 0
            for _, start, span in batch:
                put_sum(sum_buf, start - add_start, total[:, column : column + 2 * span])
                column += 2 * span
        add_point = table_ref[add_slot * stride].astype(jnp.int32)
        columns = pl.ds(add_start, sum_buf.shape[2])
        placing = pltpu.make_async_copy(
            sum_buf, result_ref.at[:, add_point, :, columns], placed_sem
        )
        placing.start()
    if plan.folding:
        for distance, send_ref in enumerate(sends):
            target = lax.rem(outer + distance, depth)
            column = 0
            for arrays in folded:
                total = arrays[0][target]
                for array in arrays[1:]:
                    total = total + array[target].astype(jnp.float32)
                columns = slice(column, column + total.shape[1])
                send_ref[:, columns] = total.astype(send_ref.dtype)
                column += total.shape[1]
    if plan.part:
        near_into(near_buf, there_ref, table_ref, base, planes)
        dims = (((1,), (1,)), ((), ()))
        points = there_ref.shape[2]
        run = points // 2 if width <= SPLIT else points
        for block in range(blocks):
            lines = pl.ds(block * BLOCK, BLOCK)
            of_both = []
            for part in range(2):
                own[2 * block + part].wait()
                products = [
                    lax.dot_general(
                        own_buf[part, lines, pl.ds(first, run)],
                        near_buf[:, pl.ds(first, run)],
                        dims,
                        preferred_element_type=jnp.float32,
                    )
                    for first in range(0, points, run)
                ]
                of_both.append(sum(products[1:], products[0]))
            of_re, of_im = of_both
            terms_buf[lines, :width] = of_re[:, :width] + of_im[:, width:]
            terms_buf[lines, width:] = of_re[:, width:] - of_im[:, :width]
            if plan.later and block == 0:
                for load, store in zip(loads, stores):
                    load.wait()
                    store.start()
        for distance, out_ref in enumerate(outs):
            target = lax.rem(place + distance, fold)
            for level in range(depth):
                first = pl.multiple_of((level * fold + target) * rows, rows)
                out_ref[level] = terms_buf[pl.ds(first, rows), :].astype(out_ref.dtype)
    if plan.adding:
        placing.wait()
    if plan.later:
        for store in stores:
            store.wait()


class Plan(NamedTuple):
    shape: tuple
    fold: int
    depth: int
    part: tuple
    folding: tuple
    adding: tuple
    placed: bool
    later: tuple


def step(plan, table, bands, there, folded, arrived, result):
    rows, _, _, nbands = plan.shape
    fold, depth = plan.fold, plan.depth
    points = bands.shape[3]
    vmem = pl.BlockSpec(memory_space=pltpu.VMEM)
    hbm = pl.BlockSpec(memory_space=pltpu.HBM)
    operands, in_specs = [table], [pl.BlockSpec(memory_space=pltpu.SMEM)]
    out_shape, out_specs, scratch, aliases = [], [], [], {}

    def kind(index):
        return jnp.bfloat16 if index else jnp.float32

    if plan.part:
        width = plan.part[2]
        operands += [bands, there]
        in_specs += [hbm, vmem]
        out_shape += [
            jax.ShapeDtypeStruct((depth, rows, 2 * width), kind(i)) for i in range(fold)
        ]
        out_specs += [vmem] * fold
        scratch += [
            pltpu.VMEM((2, nbands, points), jnp.bfloat16),
            pltpu.VMEM((2 * width, points), jnp.bfloat16),
            pltpu.VMEM((nbands, 2 * width), jnp.float32),
            pltpu.SemaphoreType.DMA((nbands // BLOCK, 2)),
        ]
    if plan.folding:
        for arrays in folded:
            operands += arrays
            in_specs += [vmem] * fold
        wide = sum(2 * width for _, _, width in plan.folding)
        out_shape += [jax.ShapeDtypeStruct((rows, wide), kind(i)) for i in range(depth)]
        out_specs += [vmem] * depth
    if plan.later:
        scratch += [
            pltpu.VMEM((2, plan.later[2], points), bands.dtype),
            pltpu.SemaphoreType.DMA((2, 2)),
        ]
    if plan.adding:
        for arrays in arrived:
            operands += arrays
            in_specs += [vmem] * depth
        if plan.placed:
            aliases = {len(operands): len(out_shape)}
            operands.append(result)
            in_specs.append(hbm)
        out_shape.append(jax.ShapeDtypeStruct(plan.shape, jnp.float32))
        out_specs.append(hbm)
        lanes = sum(width for batch in plan.adding for _, _, width in batch)
        scratch += [pltpu.VMEM((rows, 2, lanes), jnp.float32), pltpu.SemaphoreType.DMA]
    if plan.later:
        out_shape.append(jax.ShapeDtypeStruct((2, plan.later[2], points), bands.dtype))
        out_specs.append(hbm)
    outs = list(
        pl.pallas_call(
            functools.partial(step_kernel, plan),
            in_specs=in_specs,
            out_specs=out_specs,
            scratch_shapes=scratch,
            out_shape=out_shape,
            input_output_aliases=aliases,
            compiler_params=pltpu.CompilerParams(vmem_limit_bytes=VMEM_BYTES),
            cost_estimate=pl.CostEstimate(flops=1000, bytes_accessed=1000, transcendentals=0),
            name="step",
        )(*operands)
    )
    piece = outs.pop() if plan.later else None
    result = outs.pop() if plan.adding else result
    terms = outs[:fold] if plan.part else None
    sends = outs[-depth:] if plan.folding else None
    return terms, sends, result, piece


def cuts(nbands, first):
    eighth = nbands // 8
    widths = [4 * eighth, 4 * eighth] if first else [3 * eighth, 3 * eighth, 2 * eighth]
    starts = [sum(widths[:i]) for i in range(len(widths))]
    return list(zip(starts, widths))


def schedule(parts):
    kernels = []
    waiting = []
    for index, part in enumerate(parts[:-1]):
        folding = (parts[index - 1],) if index else ()
        ready = ready_batches(waiting)
        waiting = waiting[len(ready) :]
        kernels.append((part, folding, ready))
        if folding:
            waiting.append(folding)
    last = tuple(parts[-2:])
    kernels.append((parts[-1], (), ()))
    kernels.append((None, last, ()))
    kernels.append((None, (), tuple(waiting) + (last,)))
    return kernels


def ready_batches(waiting):
    total = 0
    for count, batch in enumerate(waiting, 1):
        total += sum(width for _, _, width in batch)
        if total % LANES == 0:
            return tuple(waiting[:count])
    return ()


def body(bands, nbr_slot, gshift):
    grid_index = lax.axis_index("ga")
    grid_count = lax.axis_size("ga")
    k_dev, _, nbands, points = bands.shape
    rows = nbands // grid_count
    own_planes = points // PLANE
    total_planes = own_planes * grid_count
    planes = grid_index * own_planes + jnp.arange(own_planes, dtype=jnp.int32)
    slots = jnp.arange(k_dev, dtype=jnp.int32)
    chosen = nbr_slot[None, :] == slots[:, None]
    order = jnp.sum(jnp.where(chosen, slots[None, :], 0), axis=1)
    shifts = jnp.sum(jnp.where(chosen, gshift[None, :], 0), axis=1)
    turns = (1 + NKB * shifts[:, None]) * planes[None, :] % (NKB * total_planes)
    angle = 2.0 * math.pi / (NKB * total_planes) * turns.astype(jnp.float32)
    columns = [order[:, None].astype(jnp.float32), jnp.cos(angle), jnp.sin(angle)]
    table = jnp.concatenate(columns, axis=1).reshape(-1)
    table = jnp.append(table, grid_index.astype(jnp.float32))
    parts = []
    for slot in range(k_dev):
        for start, width in cuts(nbands, slot == 0):
            parts.append((slot, start, width))
    theres = []
    piece = None
    for slot, start, width in parts[:AHEAD]:
        piece = piece_of(slot, start, width, bands, [] if piece is None else [piece])
        theres.append(shifted(piece, "ka", -1))
    shape = (rows, k_dev, 2, nbands)
    depth = min(OUTER, grid_count)
    fold = grid_count // depth
    folded, arrived = {}, {}
    result = None
    for part, folding, adding in schedule(parts):
        place = parts.index(part) if part else len(parts)
        later = parts[place + AHEAD] if place + AHEAD < len(parts) else None
        plan = Plan(shape, fold, depth, part, folding, adding, result is not None, later)
        terms, sends, result, piece = step(
            plan,
            table,
            bands,
            theres[place] if part else None,
            [folded.pop(done) for done in folding],
            [arrived.pop(batch) for batch in adding],
            result,
        )
        if later:
            theres.append(shifted(piece, "ka", -1))
        if part:
            folded[part] = [terms[0]] + [
                shifted(terms[i], "ga", i, fold, True) for i in range(1, fold)
            ]
        if folding:
            arrived[folding] = [sends[0]] + [
                shifted(sends[i], "ga", i, fold) for i in range(1, depth)
            ]
    return result


def solution(mesh):
    placed = (P("ka", None, None, "ga"), P("ka"), P("ka"))
    return jax.shard_map(
        body, mesh=mesh, in_specs=placed, out_specs=P("ga", "ka", None, None), check_vma=False
    )
```

```python
import functools
import math
from typing import NamedTuple

import jax
import jax.numpy as jnp
from jax import lax
from jax.experimental import pallas as pl
from jax.experimental.pallas import tpu as pltpu
from jax.sharding import PartitionSpec as P

NKB = 4
PLANE = 1024
STRIP = 32
DEPTH = 512
AHEAD = 2
OUTER = 4
SPLIT = 128
LANES = 128
BLOCK = 256
VMEM_BYTES = 48 * 1024 * 1024


def shifted(block, axis, distance, fold=1, inner=False):
    count = lax.axis_size(axis)
    route = []
    for i in range(count):
        outer, place = divmod(i, fold)
        if inner:
            route.append((i, outer * fold + (place + distance) % fold))
        else:
            route.append((i, (outer + distance) % (count // fold) * fold + place))
    return lax.ppermute(block, axis, route)


def swapped(block, axis, distance):
    count = lax.axis_size(axis)
    return lax.ppermute(block, axis, [(i, i ^ distance) for i in range(count)])


def piece_kernel(slot, start, bands_ref, *rest):
    out_ref, piece_buf, sems = rest[-3:]
    width = piece_buf.shape[1]
    rows = pl.ds(start, width)
    loads = [
        pltpu.make_async_copy(bands_ref.at[slot, part, rows, :], piece_buf.at[part], sems.at[0, part])
        for part in range(2)
    ]
    stores = [
        pltpu.make_async_copy(piece_buf.at[part], out_ref.at[part], sems.at[1, part])
        for part in range(2)
    ]
    for load in loads:
        load.start()
    for load, store in zip(loads, stores):
        load.wait()
        store.start()
    for store in stores:
        store.wait()


def piece_of(slot, start, width, bands, after):
    points = bands.shape[3]
    return pl.pallas_call(
        functools.partial(piece_kernel, slot, start),
        in_specs=[pl.BlockSpec(memory_space=pl.ANY)] * (1 + len(after)),
        out_specs=pl.BlockSpec(memory_space=pl.ANY),
        scratch_shapes=[
            pltpu.VMEM((2, width, points), bands.dtype),
            pltpu.SemaphoreType.DMA((2, 2)),
        ],
        out_shape=jax.ShapeDtypeStruct((2, width, points), bands.dtype),
        compiler_params=pltpu.CompilerParams(vmem_limit_bytes=VMEM_BYTES),
        cost_estimate=pl.CostEstimate(flops=1000, bytes_accessed=1000, transcendentals=0),
        name="piece_of",
    )(bands, *after)


def near_into(near_buf, there_ref, table_ref, base, planes):
    width, points = there_ref.shape[1:]

    @pl.loop(0, width // STRIP)
    def _(strip):
        rows = pl.ds(strip * STRIP, STRIP)
        mirror = pl.ds(width + strip * STRIP, STRIP)
        for start in range(0, points, DEPTH):
            plane = start // PLANE
            cosine = table_ref[base + 1 + plane]
            sine = table_ref[base + 1 + planes + plane]
            columns = pl.ds(start, DEPTH)
            real_part = there_ref[0, rows, columns].astype(jnp.float32)
            imag_part = there_ref[1, rows, columns].astype(jnp.float32)
            near_re = real_part * cosine + imag_part * sine
            near_im = imag_part * cosine - real_part * sine
            near_buf[rows, columns] = near_re.astype(jnp.bfloat16)
            near_buf[mirror, columns] = near_im.astype(jnp.bfloat16)


def put_sum(sum_buf, lane, total):
    width = total.shape[1] // 2
    sum_buf[:, 0, lane : lane + width] = total[:, :width]
    sum_buf[:, 1, lane : lane + width] = total[:, width:]


def step_kernel(plan, table_ref, *refs):
    rows, k_dev, _, nbands = plan.shape
    fold, depth = plan.fold, plan.depth
    refs = list(refs)

    def take(count):
        taken = refs[:count]
        del refs[:count]
        return taken

    stride = (table_ref.shape[0] - 1) // k_dev
    planes = (stride - 1) // 2
    me = table_ref[k_dev * stride].astype(jnp.int32)
    place, outer = lax.rem(me, fold), lax.div(me, fold)
    if plan.part:
        bands_ref, there_ref = take(2)
    sources = [take(count) for count in plan.takes]
    arrived = [take(count) for count in plan.adds]
    if plan.adding and plan.placed:
        take(1)
    outs = take(fold) if plan.part else None
    targets = [take(task.count) for task in plan.tasks]
    result_ref = take(1)[0] if plan.adding else None
    piece_ref = take(1)[0] if plan.later else None
    if plan.part:
        own_buf, near_buf, terms_buf, own_sems = take(4)
        slot = plan.part[0]
        base = slot * stride
        point = table_ref[base].astype(jnp.int32)
        width = there_ref.shape[1]
        blocks = nbands // BLOCK
        own = [
            pltpu.make_async_copy(
                bands_ref.at[point, part, pl.ds(block * BLOCK, BLOCK), :],
                own_buf.at[part, pl.ds(block * BLOCK, BLOCK), :],
                own_sems.at[block, part],
            )
            for block in range(blocks)
            for part in range(2)
        ]
        for copy in own:
            copy.start()
    if plan.later:
        piece_buf, piece_sems = take(2)
        later_slot, later_start, later_width = plan.later
        loads = [
            pltpu.make_async_copy(
                bands_ref.at[later_slot, part, pl.ds(later_start, later_width), :],
                piece_buf.at[part],
                piece_sems.at[0, part],
            )
            for part in range(2)
        ]
        stores = [
            pltpu.make_async_copy(piece_buf.at[part], piece_ref.at[part], piece_sems.at[1, part])
            for part in range(2)
        ]
        for copy in loads:
            copy.start()
    if plan.adding:
        sum_buf, placed_sem = take(2)
        add_slot, add_start, _ = plan.adding[0][0]
        for batch, arrays in zip(plan.adding, arrived):
            total = summed(arrays, 0)
            column = 0
            for _, start, span in batch:
                put_sum(sum_buf, start - add_start, total[:, column : column + 2 * span])
                column += 2 * span
        add_point = table_ref[add_slot * stride].astype(jnp.int32)
        columns = pl.ds(add_start, sum_buf.shape[2])
        placing = pltpu.make_async_copy(
            sum_buf, result_ref.at[:, add_point, :, columns], placed_sem
        )
        placing.start()
    for task, arrays, outputs in zip(plan.tasks, sources, targets):
        groups = [arrays[i : i + task.each] for i in range(0, len(arrays), task.each)]
        bit = lax.rem(lax.div(outer, 1 << task.stage), 2)
        for index, out_ref in enumerate(outputs):
            for level in range(out_ref.shape[0]):
                if task.count == 1:
                    source = 0
                elif task.direct:
                    source = lax.rem(outer + index, depth)
                else:
                    source = 2 * level + (1 - bit if index else bit)
                column = 0
                for group in groups:
                    total = summed(group, source)
                    columns = slice(column, column + total.shape[1])
                    out_ref[level, :, columns] = total.astype(out_ref.dtype)
                    column += total.shape[1]
    if plan.part:
        near_into(near_buf, there_ref, table_ref, base, planes)
        dims = (((1,), (1,)), ((), ()))
        points = there_ref.shape[2]
        run = points // 2 if width <= SPLIT else points
        for block in range(blocks):
            lines = pl.ds(block * BLOCK, BLOCK)
            of_both = []
            for part in range(2):
                own[2 * block + part].wait()
                products = [
                    lax.dot_general(
                        own_buf[part, lines, pl.ds(first, run)],
                        near_buf[:, pl.ds(first, run)],
                        dims,
                        preferred_element_type=jnp.float32,
                    )
                    for first in range(0, points, run)
                ]
                of_both.append(sum(products[1:], products[0]))
            of_re, of_im = of_both
            terms_buf[lines, :width] = of_re[:, :width] + of_im[:, width:]
            terms_buf[lines, width:] = of_re[:, width:] - of_im[:, :width]
            if plan.later and block == 0:
                for load, store in zip(loads, stores):
                    load.wait()
                    store.start()
        for distance, out_ref in enumerate(outs):
            target = lax.rem(place + distance, fold)
            for level in range(depth):
                first = pl.multiple_of((level * fold + target) * rows, rows)
                out_ref[level] = terms_buf[pl.ds(first, rows), :].astype(out_ref.dtype)
    if plan.adding:
        placing.wait()
    if plan.later:
        for store in stores:
            store.wait()


def summed(arrays, level):
    total = arrays[0][level]
    for array in arrays[1:]:
        total = total + array[level].astype(jnp.float32)
    return total


class Task(NamedTuple):
    batch: tuple
    stage: int
    direct: bool
    each: int
    count: int


class Plan(NamedTuple):
    shape: tuple
    fold: int
    depth: int
    part: tuple
    tasks: tuple
    takes: tuple
    adding: tuple
    adds: tuple
    placed: bool
    later: tuple


def step(plan, table, bands, there, sources, arrived, result):
    rows, _, _, nbands = plan.shape
    fold, depth = plan.fold, plan.depth
    points = bands.shape[3]
    vmem = pl.BlockSpec(memory_space=pltpu.VMEM)
    hbm = pl.BlockSpec(memory_space=pltpu.HBM)
    operands, in_specs = [table], [pl.BlockSpec(memory_space=pltpu.SMEM)]
    out_shape, out_specs, scratch, aliases = [], [], [], {}

    def kind(index):
        return jnp.bfloat16 if index else jnp.float32

    if plan.part:
        width = plan.part[2]
        operands += [bands, there]
        in_specs += [hbm, vmem]
        out_shape += [
            jax.ShapeDtypeStruct((depth, rows, 2 * width), kind(i)) for i in range(fold)
        ]
        scratch += [
            pltpu.VMEM((2, nbands, points), jnp.bfloat16),
            pltpu.VMEM((2 * width, points), jnp.bfloat16),
            pltpu.VMEM((nbands, 2 * width), jnp.float32),
            pltpu.SemaphoreType.DMA((nbands // BLOCK, 2)),
        ]
    for arrays in sources + arrived:
        operands += arrays
        in_specs += [vmem] * len(arrays)
    for task in plan.tasks:
        wide = sum(2 * width for _, _, width in task.batch)
        levels = 1 if task.direct else depth >> (task.stage + 1)
        out_shape += [
            jax.ShapeDtypeStruct((levels, rows, wide), kind(i)) for i in range(task.count)
        ]
    out_specs += [vmem] * len(out_shape)
    if plan.later:
        scratch += [
            pltpu.VMEM((2, plan.later[2], points), bands.dtype),
            pltpu.SemaphoreType.DMA((2, 2)),
        ]
    if plan.adding:
        if plan.placed:
            aliases = {len(operands): len(out_shape)}
            operands.append(result)
            in_specs.append(hbm)
        out_shape.append(jax.ShapeDtypeStruct(plan.shape, jnp.float32))
        out_specs.append(hbm)
        lanes = sum(width for batch in plan.adding for _, _, width in batch)
        scratch += [pltpu.VMEM((rows, 2, lanes), jnp.float32), pltpu.SemaphoreType.DMA]
    if plan.later:
        out_shape.append(jax.ShapeDtypeStruct((2, plan.later[2], points), bands.dtype))
        out_specs.append(hbm)
    outs = list(
        pl.pallas_call(
            functools.partial(step_kernel, plan),
            in_specs=in_specs,
            out_specs=out_specs,
            scratch_shapes=scratch,
            out_shape=out_shape,
            input_output_aliases=aliases,
            compiler_params=pltpu.CompilerParams(vmem_limit_bytes=VMEM_BYTES),
            cost_estimate=pl.CostEstimate(flops=1000, bytes_accessed=1000, transcendentals=0),
            name="step",
        )(*operands)
    )
    piece = outs.pop() if plan.later else None
    result = outs.pop() if plan.adding else result
    terms = outs[:fold] if plan.part else None
    handed = outs[fold if plan.part else 0 :]
    sends = []
    for task in plan.tasks:
        sends.append(handed[: task.count])
        handed = handed[task.count :]
    return terms, sends, result, piece


def cuts(nbands, first):
    eighth = nbands // 8
    widths = [4 * eighth, 4 * eighth] if first else [3 * eighth, 3 * eighth, 2 * eighth]
    starts = [sum(widths[:i]) for i in range(len(widths))]
    return list(zip(starts, widths))


def schedule(parts, fold, depth):
    stages = depth.bit_length() - 1
    kernels = []
    waiting = []
    moving = []
    for index, part in enumerate(parts):
        ready = ready_batches(waiting)
        waiting = waiting[len(ready) :]
        tasks = [Task(batch, stage, False, 2, 2) for batch, stage in moving]
        if 0 < index < len(parts) - 1:
            tasks.append(Task((parts[index - 1],), 0, False, fold, 2))
        kernels.append((part, tuple(tasks), ready))
        ended = [task.batch for task in tasks if task.stage + 1 == stages]
        waiting += ended
        moving = [(task.batch, task.stage + 1) for task in tasks if task.stage + 1 < stages]
    last = tuple(parts[-2:])
    tasks = [Task(batch, 0, True, 2, 1) for batch in ended]
    kernels.append((None, (Task(last, 0, True, fold, depth), *tasks), ()))
    kernels.append((None, (), tuple(waiting) + (last,)))
    return kernels


def ready_batches(waiting):
    total = 0
    for count, batch in enumerate(waiting, 1):
        total += sum(width for _, _, width in batch)
        if total % LANES == 0:
            return tuple(waiting[:count])
    return ()


def body(bands, nbr_slot, gshift):
    grid_index = lax.axis_index("ga")
    grid_count = lax.axis_size("ga")
    k_dev, _, nbands, points = bands.shape
    rows = nbands // grid_count
    own_planes = points // PLANE
    total_planes = own_planes * grid_count
    planes = grid_index * own_planes + jnp.arange(own_planes, dtype=jnp.int32)
    slots = jnp.arange(k_dev, dtype=jnp.int32)
    chosen = nbr_slot[None, :] == slots[:, None]
    order = jnp.sum(jnp.where(chosen, slots[None, :], 0), axis=1)
    shifts = jnp.sum(jnp.where(chosen, gshift[None, :], 0), axis=1)
    turns = (1 + NKB * shifts[:, None]) * planes[None, :] % (NKB * total_planes)
    angle = 2.0 * math.pi / (NKB * total_planes) * turns.astype(jnp.float32)
    columns = [order[:, None].astype(jnp.float32), jnp.cos(angle), jnp.sin(angle)]
    table = jnp.concatenate(columns, axis=1).reshape(-1)
    table = jnp.append(table, grid_index.astype(jnp.float32))
    parts = []
    for slot in range(k_dev):
        for start, width in cuts(nbands, slot == 0):
            parts.append((slot, start, width))
    theres = []
    piece = None
    for slot, start, width in parts[:AHEAD]:
        piece = piece_of(slot, start, width, bands, [] if piece is None else [piece])
        theres.append(shifted(piece, "ka", -1))
    shape = (rows, k_dev, 2, nbands)
    depth = min(OUTER, grid_count)
    fold = grid_count // depth
    held = {}
    result = None
    for part, tasks, adding in schedule(parts, fold, depth):
        place = parts.index(part) if part else len(parts)
        later = parts[place + AHEAD] if place + AHEAD < len(parts) else None
        sources = []
        for task in tasks:
            whole = task.stage or task.count == 1
            keys = [task.batch] if whole else [(done,) for done in task.batch]
            sources.append([array for key in keys for array in held.pop(key)])
        arrived = [held.pop(batch) for batch in adding]
        plan = Plan(
            shape,
            fold,
            depth,
            part,
            tasks,
            tuple(len(arrays) for arrays in sources),
            adding,
            tuple(len(arrays) for arrays in arrived),
            result is not None,
            later,
        )
        terms, sends, result, piece = step(
            plan, table, bands, theres[place] if part else None, sources, arrived, result
        )
        if later:
            theres.append(shifted(piece, "ka", -1))
        if part:
            held[(part,)] = [terms[0]] + [
                shifted(terms[i], "ga", i, fold, True) for i in range(1, fold)
            ]
        for task, arrays in zip(tasks, sends):
            if task.direct:
                held[task.batch] = [arrays[0]] + [
                    shifted(arrays[i], "ga", i, fold) for i in range(1, task.count)
                ]
            else:
                held[task.batch] = [arrays[0], swapped(arrays[1], "ga", fold << task.stage)]
    return result


def solution(mesh):
    placed = (P("ka", None, None, "ga"), P("ka"), P("ka"))
    return jax.shard_map(
        body, mesh=mesh, in_specs=placed, out_specs=P("ga", "ka", None, None), check_vma=False
    )
```

```python
import functools
import math
from typing import NamedTuple

import jax
import jax.numpy as jnp
from jax import lax
from jax.experimental import pallas as pl
from jax.experimental.pallas import tpu as pltpu
from jax.sharding import PartitionSpec as P

NKB = 4
PLANE = 1024
STRIP = 32
DEPTH = 512
AHEAD = 2
OUTER = 4
SPLIT = 128
LANES = 128
BLOCK = 256
VMEM_BYTES = 48 * 1024 * 1024


def shifted(block, axis, distance, fold=1, inner=False):
    count = lax.axis_size(axis)
    route = []
    for i in range(count):
        outer, place = divmod(i, fold)
        if inner:
            route.append((i, outer * fold + (place + distance) % fold))
        else:
            route.append((i, (outer + distance) % (count // fold) * fold + place))
    return lax.ppermute(block, axis, route)


def swapped(block, axis, distance):
    count = lax.axis_size(axis)
    return lax.ppermute(block, axis, [(i, i ^ distance) for i in range(count)])


def piece_kernel(slot, start, bands_ref, *rest):
    out_ref, piece_buf, sems = rest[-3:]
    width = piece_buf.shape[1]
    rows = pl.ds(start, width)
    loads = [
        pltpu.make_async_copy(bands_ref.at[slot, part, rows, :], piece_buf.at[part], sems.at[0, part])
        for part in range(2)
    ]
    stores = [
        pltpu.make_async_copy(piece_buf.at[part], out_ref.at[part], sems.at[1, part])
        for part in range(2)
    ]
    for load in loads:
        load.start()
    for load, store in zip(loads, stores):
        load.wait()
        store.start()
    for store in stores:
        store.wait()


def piece_of(slot, start, width, bands, after):
    points = bands.shape[3]
    return pl.pallas_call(
        functools.partial(piece_kernel, slot, start),
        in_specs=[pl.BlockSpec(memory_space=pl.ANY)] * (1 + len(after)),
        out_specs=pl.BlockSpec(memory_space=pl.ANY),
        scratch_shapes=[
            pltpu.VMEM((2, width, points), bands.dtype),
            pltpu.SemaphoreType.DMA((2, 2)),
        ],
        out_shape=jax.ShapeDtypeStruct((2, width, points), bands.dtype),
        compiler_params=pltpu.CompilerParams(vmem_limit_bytes=VMEM_BYTES),
        cost_estimate=pl.CostEstimate(flops=1000, bytes_accessed=1000, transcendentals=0),
        name="piece_of",
    )(bands, *after)


def near_into(near_buf, there_ref, table_ref, base, planes):
    width, points = there_ref.shape[1:]

    @pl.loop(0, width // STRIP)
    def _(strip):
        rows = pl.ds(strip * STRIP, STRIP)
        mirror = pl.ds(width + strip * STRIP, STRIP)
        for start in range(0, points, DEPTH):
            plane = start // PLANE
            cosine = table_ref[base + 1 + plane]
            sine = table_ref[base + 1 + planes + plane]
            columns = pl.ds(start, DEPTH)
            real_part = there_ref[0, rows, columns].astype(jnp.float32)
            imag_part = there_ref[1, rows, columns].astype(jnp.float32)
            near_re = real_part * cosine + imag_part * sine
            near_im = imag_part * cosine - real_part * sine
            near_buf[rows, columns] = near_re.astype(jnp.bfloat16)
            near_buf[mirror, columns] = near_im.astype(jnp.bfloat16)


def put_sum(sum_buf, lane, total):
    width = total.shape[1] // 2
    sum_buf[:, 0, lane : lane + width] = total[:, :width]
    sum_buf[:, 1, lane : lane + width] = total[:, width:]


def step_kernel(plan, table_ref, *refs):
    rows, k_dev, _, nbands = plan.shape
    fold, depth = plan.fold, plan.depth
    refs = list(refs)

    def take(count):
        taken = refs[:count]
        del refs[:count]
        return taken

    stride = (table_ref.shape[0] - 1) // k_dev
    planes = (stride - 1) // 2
    me = table_ref[k_dev * stride].astype(jnp.int32)
    place, outer = lax.rem(me, fold), lax.div(me, fold)
    if plan.part:
        bands_ref, phased_ref = take(2)
    sources = [take(count) for count in plan.takes]
    arrived = [take(count) for count in plan.adds]
    if plan.adding and plan.placed:
        take(1)
    given_ref = take(1)[0] if plan.near == "give" else None
    outs = take(len(plan.ways))
    targets = [take(task.count) for task in plan.tasks]
    result_ref = take(1)[0] if plan.adding else None
    piece_ref = take(1)[0] if plan.later else None
    if plan.part:
        own_buf, own_sems = take(2)
        slot, _, width = plan.part
        base = slot * stride
        point = table_ref[base].astype(jnp.int32)
        own = []
        for way, distance in enumerate(plan.ways):
            target = lax.rem(place + distance, fold)
            own.append([])
            for part in range(2):
                for level in range(depth):
                    first = pl.multiple_of((level * fold + target) * rows, rows)
                    copy = pltpu.make_async_copy(
                        bands_ref.at[point, part, pl.ds(first, rows), :],
                        own_buf.at[way, part, pl.ds(level * rows, rows), :],
                        own_sems.at[way, part, level],
                    )
                    copy.start()
                    own[way].append(copy)
    if plan.later:
        piece_buf, piece_sems = take(2)
        later_slot, later_start, later_width = plan.later
        loads = [
            pltpu.make_async_copy(
                bands_ref.at[later_slot, part, pl.ds(later_start, later_width), :],
                piece_buf.at[part],
                piece_sems.at[0, part],
            )
            for part in range(2)
        ]
        stores = [
            pltpu.make_async_copy(piece_buf.at[part], piece_ref.at[part], piece_sems.at[1, part])
            for part in range(2)
        ]
        for copy in loads:
            copy.start()
    if plan.adding:
        sum_buf, placed_sem = take(2)
        add_slot, add_start, pieces = plan.adding
        for index, column, start, span in pieces:
            total = summed(arrived[index], 0, slice(column, column + 2 * span))
            put_sum(sum_buf, start - add_start, total)
        add_point = table_ref[add_slot * stride].astype(jnp.int32)
        columns = pl.ds(add_start, sum_buf.shape[2])
        placing = pltpu.make_async_copy(
            sum_buf, result_ref.at[:, add_point, :, columns], placed_sem
        )
        placing.start()
    for task, arrays, outputs in zip(plan.tasks, sources, targets):
        groups = [arrays[i : i + task.each] for i in range(0, len(arrays), task.each)]
        bit = lax.rem(lax.div(outer, 1 << task.stage), 2)
        for index, out_ref in enumerate(outputs):
            for level in range(out_ref.shape[0]):
                if task.direct:
                    source = partner(outer, index)
                else:
                    source = 2 * level + (1 - bit if index else bit)
                column = 0
                for group in groups:
                    total = summed(group, source)
                    columns = slice(column, column + total.shape[1])
                    out_ref[level, :, columns] = total.astype(out_ref.dtype)
                    column += total.shape[1]
    if plan.part:
        near_ref = phased_ref
        if plan.near != "use":
            near_ref = given_ref if plan.near == "give" else take(1)[0]
            near_into(near_ref, phased_ref, table_ref, base, planes)
        dims = (((1,), (1,)), ((), ()))
        points = own_buf.shape[3]
        run = points // 2 if width <= SPLIT else points
        for way, out_ref in enumerate(outs):
            of_both = []
            for part in range(2):
                for copy in own[way][part * depth : (part + 1) * depth]:
                    copy.wait()
                products = [
                    lax.dot_general(
                        own_buf[way, part, :, pl.ds(first, run)],
                        near_ref[:, pl.ds(first, run)],
                        dims,
                        preferred_element_type=jnp.float32,
                    )
                    for first in range(0, points, run)
                ]
                of_both.append(sum(products[1:], products[0]))
            of_re, of_im = of_both
            real_part = (of_re[:, :width] + of_im[:, width:]).astype(out_ref.dtype)
            imag_part = (of_re[:, width:] - of_im[:, :width]).astype(out_ref.dtype)
            for level in range(depth):
                lines = slice(level * rows, (level + 1) * rows)
                out_ref[level, :, :width] = real_part[lines]
                out_ref[level, :, width:] = imag_part[lines]
            if plan.later and way == 0:
                for load, store in zip(loads, stores):
                    load.wait()
                    store.start()
    if plan.adding:
        placing.wait()
    if plan.later:
        for store in stores:
            store.wait()


def partner(outer, distance):
    low, high = lax.rem(outer, 2), lax.rem(lax.div(outer, 2), 2)
    low = 1 - low if distance % 2 else low
    high = 1 - high if distance // 2 else high
    return outer - lax.rem(outer, 4) + 2 * high + low


def summed(arrays, level, columns=slice(None)):
    total = arrays[0][level, :, columns]
    for array in arrays[1:]:
        total = total + array[level, :, columns].astype(jnp.float32)
    return total


class Task(NamedTuple):
    batch: tuple
    stage: int
    direct: bool
    each: int
    count: int


class Plan(NamedTuple):
    shape: tuple
    fold: int
    depth: int
    part: tuple
    ways: tuple
    near: str
    tasks: tuple
    takes: tuple
    adding: tuple
    adds: tuple
    placed: bool
    later: tuple


def step(plan, table, bands, phased, sources, arrived, result):
    rows, _, _, nbands = plan.shape
    fold, depth = plan.fold, plan.depth
    points = bands.shape[3]
    vmem = pl.BlockSpec(memory_space=pltpu.VMEM)
    hbm = pl.BlockSpec(memory_space=pltpu.HBM)
    operands, in_specs = [table], [pl.BlockSpec(memory_space=pltpu.SMEM)]
    out_shape, out_specs, scratch, aliases = [], [], [], {}

    def kind(index):
        return jnp.bfloat16 if index else jnp.float32

    if plan.part:
        width = plan.part[2]
        operands += [bands, phased]
        in_specs += [hbm, vmem]
        if plan.near == "give":
            out_shape.append(jax.ShapeDtypeStruct((2 * width, points), jnp.bfloat16))
        out_shape += [
            jax.ShapeDtypeStruct((depth, rows, 2 * width), kind(way)) for way in plan.ways
        ]
        scratch += [
            pltpu.VMEM((len(plan.ways), 2, depth * rows, points), jnp.bfloat16),
            pltpu.SemaphoreType.DMA((len(plan.ways), 2, depth)),
        ]
    for arrays in sources + arrived:
        operands += arrays
        in_specs += [vmem] * len(arrays)
    for task in plan.tasks:
        wide = sum(2 * width for _, _, width in task.batch)
        levels = 1 if task.direct else depth >> (task.stage + 1)
        out_shape += [
            jax.ShapeDtypeStruct((levels, rows, wide), kind(i)) for i in range(task.count)
        ]
    out_specs += [vmem] * len(out_shape)
    if plan.later:
        scratch += [
            pltpu.VMEM((2, plan.later[2], points), bands.dtype),
            pltpu.SemaphoreType.DMA((2, 2)),
        ]
    if plan.adding:
        if plan.placed:
            aliases = {len(operands): len(out_shape)}
            operands.append(result)
            in_specs.append(hbm)
        out_shape.append(jax.ShapeDtypeStruct(plan.shape, jnp.float32))
        out_specs.append(hbm)
        lanes = sum(span for _, _, _, span in plan.adding[2])
        scratch += [pltpu.VMEM((rows, 2, lanes), jnp.float32), pltpu.SemaphoreType.DMA]
    if plan.later:
        out_shape.append(jax.ShapeDtypeStruct((2, plan.later[2], points), bands.dtype))
        out_specs.append(hbm)
    if plan.near == "make":
        scratch.append(pltpu.VMEM((2 * width, points), jnp.bfloat16))
    outs = list(
        pl.pallas_call(
            functools.partial(step_kernel, plan),
            in_specs=in_specs,
            out_specs=out_specs,
            scratch_shapes=scratch,
            out_shape=out_shape,
            input_output_aliases=aliases,
            compiler_params=pltpu.CompilerParams(vmem_limit_bytes=VMEM_BYTES),
            cost_estimate=pl.CostEstimate(flops=1000, bytes_accessed=1000, transcendentals=0),
            name="step",
        )(*operands)
    )
    piece = outs.pop() if plan.later else None
    result = outs.pop() if plan.adding else result
    near = outs.pop(0) if plan.near == "give" else None
    terms = outs[: len(plan.ways)]
    handed = outs[len(plan.ways) :]
    sends = []
    for task in plan.tasks:
        sends.append(handed[: task.count])
        handed = handed[task.count :]
    return terms, near, sends, result, piece


def cuts(nbands, first):
    eighth = nbands // 8
    widths = [4 * eighth, 4 * eighth] if first else [3 * eighth, 3 * eighth, 2 * eighth]
    starts = [sum(widths[:i]) for i in range(len(widths))]
    return list(zip(starts, widths))


def schedule(parts, fold, depth):
    every, others = tuple(range(fold)), tuple(range(1, fold))
    count = len(parts)
    kernels = []
    waiting, halved, crossed = [], [], []
    for index, part in enumerate(parts):
        ready = ready_parts(waiting)
        waiting = waiting[len(ready) :]
        tasks = []
        if halved:
            tasks.append(Task(tuple(halved), 1, False, 2, 2))
        if crossed:
            tasks.append(Task(tuple(crossed), 0, False, fold, 2))
        waiting += halved
        if index == count - 1:
            kernels.append((part, others, "give", tuple(tasks), ready))
            kernels.append((part, every[:1], "use", (), ()))
        else:
            kernels.append((part, every, "make", tuple(tasks), ready))
        halved, crossed = crossed, [part] if index < count - 2 else []
        if index == count - 3:
            kernels.append((None, (), "", (Task((part,), 0, False, fold, 2),), ()))
            halved, crossed = halved + crossed, []
    last = tuple(parts[-2:])
    kernels.append((None, (), "", (Task(last, 0, True, fold, depth),), ()))
    kernels.append((None, (), "", (), tuple(waiting) + last))
    return kernels


def ready_parts(waiting):
    total = 0
    for count, (slot, _, width) in enumerate(waiting, 1):
        total += width
        if slot != waiting[0][0]:
            break
        if total % LANES == 0:
            return tuple(waiting[:count])
    return ()


def body(bands, nbr_slot, gshift):
    grid_index = lax.axis_index("ga")
    grid_count = lax.axis_size("ga")
    k_dev, _, nbands, points = bands.shape
    rows = nbands // grid_count
    own_planes = points // PLANE
    total_planes = own_planes * grid_count
    planes = grid_index * own_planes + jnp.arange(own_planes, dtype=jnp.int32)
    slots = jnp.arange(k_dev, dtype=jnp.int32)
    chosen = nbr_slot[None, :] == slots[:, None]
    order = jnp.sum(jnp.where(chosen, slots[None, :], 0), axis=1)
    shifts = jnp.sum(jnp.where(chosen, gshift[None, :], 0), axis=1)
    turns = (1 + NKB * shifts[:, None]) * planes[None, :] % (NKB * total_planes)
    angle = 2.0 * math.pi / (NKB * total_planes) * turns.astype(jnp.float32)
    columns = [order[:, None].astype(jnp.float32), jnp.cos(angle), jnp.sin(angle)]
    table = jnp.concatenate(columns, axis=1).reshape(-1)
    table = jnp.append(table, grid_index.astype(jnp.float32))
    parts = []
    for slot in range(k_dev):
        for start, width in cuts(nbands, slot == 0):
            parts.append((slot, start, width))
    theres = []
    piece = None
    for slot, start, width in parts[:AHEAD]:
        piece = piece_of(slot, start, width, bands, [] if piece is None else [piece])
        theres.append(shifted(piece, "ka", -1))
    shape = (rows, k_dev, 2, nbands)
    depth = min(OUTER, grid_count)
    fold = grid_count // depth
    held = {}
    near, result = None, None
    for part, ways, phase, tasks, adds in schedule(parts, fold, depth):
        place = parts.index(part) if part else len(parts)
        later = parts[place + AHEAD] if place + AHEAD < len(parts) else None
        sources = [[array for done in task.batch for array in held[(done,)]] for task in tasks]
        batches, pieces = [], []
        for done in adds:
            batch = max((key for key in held if done in key), key=len)
            if batch not in batches:
                batches.append(batch)
            column = sum(2 * width for _, _, width in batch[: batch.index(done)])
            pieces.append((batches.index(batch), column, done[1], done[2]))
        arrived = [held[batch] for batch in batches]
        adding = (adds[0][0], adds[0][1], tuple(pieces)) if adds else ()
        plan = Plan(
            shape,
            fold,
            depth,
            part,
            ways,
            phase,
            tasks,
            tuple(len(arrays) for arrays in sources),
            adding,
            tuple(len(arrays) for arrays in arrived),
            result is not None,
            later,
        )
        phased = near if phase == "use" else theres[place] if part else None
        terms, near, sends, result, piece = step(
            plan, table, bands, phased, sources, arrived, result
        )
        if later:
            theres.append(shifted(piece, "ka", -1))
        for way, array in zip(ways, terms):
            array = shifted(array, "ga", way, fold, True) if way else array
            held.setdefault((part,), []).insert(0 if way == 0 else fold, array)
        for task, arrays in zip(tasks, sends):
            steps = range(1, depth) if task.direct else [1 << task.stage]
            held[task.batch] = [arrays[0]] + [
                swapped(array, "ga", fold * i) for array, i in zip(arrays[1:], steps)
            ]
    return result


def solution(mesh):
    placed = (P("ka", None, None, "ga"), P("ka"), P("ka"))
    return jax.shard_map(
        body, mesh=mesh, in_specs=placed, out_specs=P("ga", "ka", None, None), check_vma=False
    )
```

```python
import functools
import math
from typing import NamedTuple

import jax
import jax.numpy as jnp
from jax import lax
from jax.experimental import pallas as pl
from jax.experimental.pallas import tpu as pltpu
from jax.sharding import PartitionSpec as P

NKB = 4
PLANE = 1024
STRIP = 32
DEPTH = 512
AHEAD = 2
OUTER = 4
SPLIT = 128
LANES = 128
BLOCK = 256
VMEM_BYTES = 48 * 1024 * 1024


def shifted(block, axis, distance, fold=1, inner=False):
    count = lax.axis_size(axis)
    route = []
    for i in range(count):
        outer, place = divmod(i, fold)
        if inner:
            route.append((i, outer * fold + (place + distance) % fold))
        else:
            route.append((i, (outer + distance) % (count // fold) * fold + place))
    return lax.ppermute(block, axis, route)


def swapped(block, axis, distance):
    count = lax.axis_size(axis)
    return lax.ppermute(block, axis, [(i, i ^ distance) for i in range(count)])


def piece_kernel(slot, start, bands_ref, *rest):
    out_ref, piece_buf, sems = rest[-3:]
    width = piece_buf.shape[1]
    rows = pl.ds(start, width)
    loads = [
        pltpu.make_async_copy(bands_ref.at[slot, part, rows, :], piece_buf.at[part], sems.at[0, part])
        for part in range(2)
    ]
    stores = [
        pltpu.make_async_copy(piece_buf.at[part], out_ref.at[part], sems.at[1, part])
        for part in range(2)
    ]
    for load in loads:
        load.start()
    for load, store in zip(loads, stores):
        load.wait()
        store.start()
    for store in stores:
        store.wait()


def piece_of(slot, start, width, bands, after):
    points = bands.shape[3]
    return pl.pallas_call(
        functools.partial(piece_kernel, slot, start),
        in_specs=[pl.BlockSpec(memory_space=pl.ANY)] * (1 + len(after)),
        out_specs=pl.BlockSpec(memory_space=pl.ANY),
        scratch_shapes=[
            pltpu.VMEM((2, width, points), bands.dtype),
            pltpu.SemaphoreType.DMA((2, 2)),
        ],
        out_shape=jax.ShapeDtypeStruct((2, width, points), bands.dtype),
        compiler_params=pltpu.CompilerParams(vmem_limit_bytes=VMEM_BYTES),
        cost_estimate=pl.CostEstimate(flops=1000, bytes_accessed=1000, transcendentals=0),
        name="piece_of",
    )(bands, *after)


def near_into(near_buf, there_ref, table_ref, base, planes):
    width, points = there_ref.shape[1:]

    @pl.loop(0, width // STRIP)
    def _(strip):
        rows = pl.ds(strip * STRIP, STRIP)
        mirror = pl.ds(width + strip * STRIP, STRIP)
        for start in range(0, points, DEPTH):
            plane = start // PLANE
            cosine = table_ref[base + 1 + plane]
            sine = table_ref[base + 1 + planes + plane]
            columns = pl.ds(start, DEPTH)
            real_part = there_ref[0, rows, columns].astype(jnp.float32)
            imag_part = there_ref[1, rows, columns].astype(jnp.float32)
            near_re = real_part * cosine + imag_part * sine
            near_im = imag_part * cosine - real_part * sine
            near_buf[rows, columns] = near_re.astype(jnp.bfloat16)
            near_buf[mirror, columns] = near_im.astype(jnp.bfloat16)


def put_sum(sum_buf, lane, total):
    width = total.shape[1] // 2
    sum_buf[:, 0, lane : lane + width] = total[:, :width]
    sum_buf[:, 1, lane : lane + width] = total[:, width:]


def step_kernel(plan, table_ref, *refs):
    rows, k_dev, _, nbands = plan.shape
    fold, depth = plan.fold, plan.depth
    refs = list(refs)

    def take(count):
        taken = refs[:count]
        del refs[:count]
        return taken

    stride = (table_ref.shape[0] - 1) // k_dev
    planes = (stride - 1) // 2
    me = table_ref[k_dev * stride].astype(jnp.int32)
    place, outer = lax.rem(me, fold), lax.div(me, fold)
    if plan.part:
        bands_ref, phased_ref = take(2)
    sources = [take(count) for count in plan.takes]
    arrived = [take(count) for count in plan.adds]
    if plan.adding and plan.placed:
        take(1)
    given_ref, kept_ref = take(2) if plan.near == "give" else (None, None)
    outs = take(len(plan.ways))
    targets = [take(task.count) for task in plan.tasks]
    result_ref = take(1)[0] if plan.adding else None
    piece_ref = take(1)[0] if plan.later else None
    if plan.part:
        if plan.near != "use":
            own_buf, own_sems = take(2)
        slot, _, width = plan.part
        base = slot * stride
        point = table_ref[base].astype(jnp.int32)
        own = []
        loads_of = plan.ways + (0,) if plan.near == "give" else plan.ways
        for way, distance in enumerate(loads_of if plan.near != "use" else ()):
            target = lax.rem(place + distance, fold)
            rows_ref = own_buf.at[way] if way < len(plan.ways) else kept_ref
            own.append([])
            for part in range(2):
                for level in range(depth):
                    first = pl.multiple_of((level * fold + target) * rows, rows)
                    copy = pltpu.make_async_copy(
                        bands_ref.at[point, part, pl.ds(first, rows), :],
                        rows_ref.at[part, pl.ds(level * rows, rows), :],
                        own_sems.at[way, part, level],
                    )
                    copy.start()
                    own[way].append(copy)
    if plan.later:
        piece_buf, piece_sems = take(2)
        later_slot, later_start, later_width = plan.later
        loads = [
            pltpu.make_async_copy(
                bands_ref.at[later_slot, part, pl.ds(later_start, later_width), :],
                piece_buf.at[part],
                piece_sems.at[0, part],
            )
            for part in range(2)
        ]
        stores = [
            pltpu.make_async_copy(piece_buf.at[part], piece_ref.at[part], piece_sems.at[1, part])
            for part in range(2)
        ]
        for copy in loads:
            copy.start()
    if plan.adding:
        sum_buf, placed_sem = take(2)
        add_slot, add_start, pieces = plan.adding
        for index, column, start, span in pieces:
            total = summed(arrived[index], 0, slice(column, column + 2 * span))
            put_sum(sum_buf, start - add_start, total)
        add_point = table_ref[add_slot * stride].astype(jnp.int32)
        columns = pl.ds(add_start, sum_buf.shape[2])
        placing = pltpu.make_async_copy(
            sum_buf, result_ref.at[:, add_point, :, columns], placed_sem
        )
        placing.start()
    for task, arrays, outputs in zip(plan.tasks, sources, targets):
        groups = [arrays[i : i + task.each] for i in range(0, len(arrays), task.each)]
        bit = lax.rem(lax.div(outer, 1 << task.stage), 2)
        for index, out_ref in enumerate(outputs):
            for level in range(out_ref.shape[0]):
                if task.direct:
                    source = partner(outer, index)
                else:
                    source = 2 * level + (1 - bit if index else bit)
                column = 0
                for group in groups:
                    total = summed(group, source)
                    columns = slice(column, column + total.shape[1])
                    out_ref[level, :, columns] = total.astype(out_ref.dtype)
                    column += total.shape[1]
    if plan.part:
        near_ref = phased_ref
        if plan.near != "use":
            near_ref = given_ref if plan.near == "give" else take(1)[0]
            near_into(near_ref, phased_ref, table_ref, base, planes)
        dims = (((1,), (1,)), ((), ()))
        points = near_ref.shape[1]
        run = points // 2 if width <= SPLIT else points
        for way, out_ref in enumerate(outs):
            of_both = []
            for part in range(2):
                for copy in own[way][part * depth : (part + 1) * depth] if own else ():
                    copy.wait()
                rows_ref = bands_ref if plan.near == "use" else own_buf.at[way]
                products = [
                    lax.dot_general(
                        rows_ref[part, :, pl.ds(first, run)],
                        near_ref[:, pl.ds(first, run)],
                        dims,
                        preferred_element_type=jnp.float32,
                    )
                    for first in range(0, points, run)
                ]
                of_both.append(sum(products[1:], products[0]))
            of_re, of_im = of_both
            real_part = (of_re[:, :width] + of_im[:, width:]).astype(out_ref.dtype)
            imag_part = (of_re[:, width:] - of_im[:, :width]).astype(out_ref.dtype)
            for level in range(depth):
                lines = slice(level * rows, (level + 1) * rows)
                out_ref[level, :, :width] = real_part[lines]
                out_ref[level, :, width:] = imag_part[lines]
            if plan.near == "give" and way + 1 == len(outs):
                for copy in own[-1]:
                    copy.wait()
            if plan.later and way == 0:
                for load, store in zip(loads, stores):
                    load.wait()
                    store.start()
    if plan.adding:
        placing.wait()
    if plan.later:
        for store in stores:
            store.wait()


def partner(outer, distance):
    low, high = lax.rem(outer, 2), lax.rem(lax.div(outer, 2), 2)
    low = 1 - low if distance % 2 else low
    high = 1 - high if distance // 2 else high
    return outer - lax.rem(outer, 4) + 2 * high + low


def summed(arrays, level, columns=slice(None)):
    total = arrays[0][level, :, columns]
    for array in arrays[1:]:
        total = total + array[level, :, columns].astype(jnp.float32)
    return total


class Task(NamedTuple):
    batch: tuple
    stage: int
    direct: bool
    each: int
    count: int


class Plan(NamedTuple):
    shape: tuple
    fold: int
    depth: int
    part: tuple
    ways: tuple
    near: str
    tasks: tuple
    takes: tuple
    adding: tuple
    adds: tuple
    placed: bool
    later: tuple


def step(plan, table, bands, phased, sources, arrived, result):
    rows, _, _, nbands = plan.shape
    fold, depth = plan.fold, plan.depth
    points = bands.shape[-1]
    vmem = pl.BlockSpec(memory_space=pltpu.VMEM)
    hbm = pl.BlockSpec(memory_space=pltpu.HBM)
    operands, in_specs = [table], [pl.BlockSpec(memory_space=pltpu.SMEM)]
    out_shape, out_specs, scratch, aliases = [], [], [], {}

    def kind(index):
        return jnp.bfloat16 if index else jnp.float32

    if plan.part:
        width = plan.part[2]
        operands += [bands, phased]
        in_specs += [vmem if plan.near == "use" else hbm, vmem]
        if plan.near == "give":
            out_shape.append(jax.ShapeDtypeStruct((2 * width, points), jnp.bfloat16))
            out_shape.append(jax.ShapeDtypeStruct((2, depth * rows, points), jnp.bfloat16))
        out_shape += [
            jax.ShapeDtypeStruct((depth, rows, 2 * width), kind(way)) for way in plan.ways
        ]
        if plan.near != "use":
            scratch += [
                pltpu.VMEM((len(plan.ways), 2, depth * rows, points), jnp.bfloat16),
                pltpu.SemaphoreType.DMA((fold, 2, depth)),
            ]
    for arrays in sources + arrived:
        operands += arrays
        in_specs += [vmem] * len(arrays)
    for task in plan.tasks:
        wide = sum(2 * width for _, _, width in task.batch)
        levels = 1 if task.direct else depth >> (task.stage + 1)
        out_shape += [
            jax.ShapeDtypeStruct((levels, rows, wide), kind(i)) for i in range(task.count)
        ]
    out_specs += [vmem] * len(out_shape)
    if plan.later:
        scratch += [
            pltpu.VMEM((2, plan.later[2], points), bands.dtype),
            pltpu.SemaphoreType.DMA((2, 2)),
        ]
    if plan.adding:
        if plan.placed:
            aliases = {len(operands): len(out_shape)}
            operands.append(result)
            in_specs.append(hbm)
        out_shape.append(jax.ShapeDtypeStruct(plan.shape, jnp.float32))
        out_specs.append(hbm)
        lanes = sum(span for _, _, _, span in plan.adding[2])
        scratch += [pltpu.VMEM((rows, 2, lanes), jnp.float32), pltpu.SemaphoreType.DMA]
    if plan.later:
        out_shape.append(jax.ShapeDtypeStruct((2, plan.later[2], points), bands.dtype))
        out_specs.append(hbm)
    if plan.near == "make":
        scratch.append(pltpu.VMEM((2 * width, points), jnp.bfloat16))
    outs = list(
        pl.pallas_call(
            functools.partial(step_kernel, plan),
            in_specs=in_specs,
            out_specs=out_specs,
            scratch_shapes=scratch,
            out_shape=out_shape,
            input_output_aliases=aliases,
            compiler_params=pltpu.CompilerParams(vmem_limit_bytes=VMEM_BYTES),
            cost_estimate=pl.CostEstimate(flops=1000, bytes_accessed=1000, transcendentals=0),
            name="step",
        )(*operands)
    )
    piece = outs.pop() if plan.later else None
    result = outs.pop() if plan.adding else result
    near = [outs.pop(0), outs.pop(0)] if plan.near == "give" else None
    terms = outs[: len(plan.ways)]
    handed = outs[len(plan.ways) :]
    sends = []
    for task in plan.tasks:
        sends.append(handed[: task.count])
        handed = handed[task.count :]
    return terms, near, sends, result, piece


def cuts(nbands, first):
    eighth = nbands // 8
    widths = [4 * eighth, 4 * eighth] if first else [3 * eighth, 3 * eighth, 2 * eighth]
    starts = [sum(widths[:i]) for i in range(len(widths))]
    return list(zip(starts, widths))


def schedule(parts, fold, depth):
    every, others = tuple(range(fold)), tuple(range(1, fold))
    count = len(parts)
    kernels = []
    waiting, halved, crossed = [], [], []
    for index, part in enumerate(parts):
        ready = ready_parts(waiting)
        waiting = waiting[len(ready) :]
        tasks = []
        if halved:
            tasks.append(Task(tuple(halved), 1, False, 2, 2))
        if crossed:
            tasks.append(Task(tuple(crossed), 0, False, fold, 2))
        waiting += halved
        if index == count - 1:
            kernels.append((part, others, "give", tuple(tasks), ready))
            kernels.append((part, every[:1], "use", (), ()))
        else:
            kernels.append((part, every, "make", tuple(tasks), ready))
        halved, crossed = crossed, [part] if index < count - 2 else []
        if index in (0, count - 3):
            kernels.append((None, (), "", (Task((part,), 0, False, fold, 2),), ()))
            halved, crossed = halved + crossed, []
    last = tuple(parts[-2:])
    kernels.append((None, (), "", (Task(last, 0, True, fold, depth),), ()))
    kernels.append((None, (), "", (), tuple(waiting) + last))
    return kernels


def ready_parts(waiting):
    total = 0
    for count, (slot, _, width) in enumerate(waiting, 1):
        total += width
        if slot != waiting[0][0]:
            break
        if total % LANES == 0:
            return tuple(waiting[:count])
    return ()


def body(bands, nbr_slot, gshift):
    grid_index = lax.axis_index("ga")
    grid_count = lax.axis_size("ga")
    k_dev, _, nbands, points = bands.shape
    rows = nbands // grid_count
    own_planes = points // PLANE
    total_planes = own_planes * grid_count
    planes = grid_index * own_planes + jnp.arange(own_planes, dtype=jnp.int32)
    slots = jnp.arange(k_dev, dtype=jnp.int32)
    chosen = nbr_slot[None, :] == slots[:, None]
    order = jnp.sum(jnp.where(chosen, slots[None, :], 0), axis=1)
    shifts = jnp.sum(jnp.where(chosen, gshift[None, :], 0), axis=1)
    turns = (1 + NKB * shifts[:, None]) * planes[None, :] % (NKB * total_planes)
    angle = 2.0 * math.pi / (NKB * total_planes) * turns.astype(jnp.float32)
    columns = [order[:, None].astype(jnp.float32), jnp.cos(angle), jnp.sin(angle)]
    table = jnp.concatenate(columns, axis=1).reshape(-1)
    table = jnp.append(table, grid_index.astype(jnp.float32))
    parts = []
    for slot in range(k_dev):
        for start, width in cuts(nbands, slot == 0):
            parts.append((slot, start, width))
    theres = []
    piece = None
    for slot, start, width in parts[:AHEAD]:
        piece = piece_of(slot, start, width, bands, [] if piece is None else [piece])
        theres.append(shifted(piece, "ka", -1))
    shape = (rows, k_dev, 2, nbands)
    depth = min(OUTER, grid_count)
    fold = grid_count // depth
    held = {}
    near, result = None, None
    for part, ways, phase, tasks, adds in schedule(parts, fold, depth):
        place = parts.index(part) if part else len(parts)
        later = parts[place + AHEAD] if place + AHEAD < len(parts) else None
        sources = [[array for done in task.batch for array in held[(done,)]] for task in tasks]
        batches, pieces = [], []
        for done in adds:
            batch = max((key for key in held if done in key), key=len)
            if batch not in batches:
                batches.append(batch)
            column = sum(2 * width for _, _, width in batch[: batch.index(done)])
            pieces.append((batches.index(batch), column, done[1], done[2]))
        arrived = [held[batch] for batch in batches]
        adding = (adds[0][0], adds[0][1], tuple(pieces)) if adds else ()
        plan = Plan(
            shape,
            fold,
            depth,
            part,
            ways,
            phase,
            tasks,
            tuple(len(arrays) for arrays in sources),
            adding,
            tuple(len(arrays) for arrays in arrived),
            result is not None,
            later,
        )
        phased, own = theres[place] if part else None, bands
        if phase == "use":
            phased, own = near
        terms, near, sends, result, piece = step(
            plan, table, own, phased, sources, arrived, result
        )
        if later:
            theres.append(shifted(piece, "ka", -1))
        for way, array in zip(ways, terms):
            array = shifted(array, "ga", way, fold, True) if way else array
            held.setdefault((part,), []).insert(0 if way == 0 else fold, array)
        for task, arrays in zip(tasks, sends):
            steps = range(1, depth) if task.direct else [1 << task.stage]
            held[task.batch] = [arrays[0]] + [
                swapped(array, "ga", fold * i) for array, i in zip(arrays[1:], steps)
            ]
    return result


def solution(mesh):
    placed = (P("ka", None, None, "ga"), P("ka"), P("ka"))
    return jax.shard_map(
        body, mesh=mesh, in_specs=placed, out_specs=P("ga", "ka", None, None), check_vma=False
    )
```

```python
import functools
import math
from typing import NamedTuple

import jax
import jax.numpy as jnp
from jax import lax
from jax.experimental import pallas as pl
from jax.experimental.pallas import tpu as pltpu
from jax.sharding import PartitionSpec as P

NKB = 4
PLANE = 1024
STRIP = 32
DEPTH = 512
AHEAD = 2
OUTER = 4
SPLIT = 128
LANES = 128
BLOCK = 256
VMEM_BYTES = 48 * 1024 * 1024


def sent(block, step, parity):
    ka, ga = lax.axis_size("ka"), lax.axis_size("ga")
    route = [(i, step(i)) for i in range(ga)]
    if parity is None:
        return lax.ppermute(block, "ga", route)
    groups = range(parity, ka, 2)
    pairs = [(j * ga + source, j * ga + target) for j in groups for source, target in route]
    return lax.ppermute(block, ("ka", "ga"), pairs)


def crossed_over(block, distance, fold, parity):
    return sent(block, lambda i: i // fold * fold + (i + distance) % fold, parity)


def swapped(block, distance, parity):
    return sent(block, lambda i: i ^ distance, parity)


def from_next(block, parity):
    count = lax.axis_size("ka")
    targets = range(count) if parity is None else range(parity, count, 2)
    return lax.ppermute(block, "ka", [((i + 1) % count, i) for i in targets])


def piece_kernel(slot, start, bands_ref, *rest):
    out_ref, piece_buf, sems = rest[-3:]
    width = piece_buf.shape[1]
    rows = pl.ds(start, width)
    loads = [
        pltpu.make_async_copy(bands_ref.at[slot, part, rows, :], piece_buf.at[part], sems.at[0, part])
        for part in range(2)
    ]
    stores = [
        pltpu.make_async_copy(piece_buf.at[part], out_ref.at[part], sems.at[1, part])
        for part in range(2)
    ]
    for load in loads:
        load.start()
    for load, store in zip(loads, stores):
        load.wait()
        store.start()
    for store in stores:
        store.wait()


def piece_of(slot, start, width, bands, after):
    points = bands.shape[3]
    return pl.pallas_call(
        functools.partial(piece_kernel, slot, start),
        in_specs=[pl.BlockSpec(memory_space=pl.ANY)] * (1 + len(after)),
        out_specs=pl.BlockSpec(memory_space=pl.ANY),
        scratch_shapes=[
            pltpu.VMEM((2, width, points), bands.dtype),
            pltpu.SemaphoreType.DMA((2, 2)),
        ],
        out_shape=jax.ShapeDtypeStruct((2, width, points), bands.dtype),
        compiler_params=pltpu.CompilerParams(vmem_limit_bytes=VMEM_BYTES),
        cost_estimate=pl.CostEstimate(flops=1000, bytes_accessed=1000, transcendentals=0),
        name="piece_of",
    )(bands, *after)


def near_into(near_buf, there_ref, table_ref, base, planes):
    width, points = there_ref.shape[1:]

    @pl.loop(0, width // STRIP)
    def _(strip):
        rows = pl.ds(strip * STRIP, STRIP)
        mirror = pl.ds(width + strip * STRIP, STRIP)
        for start in range(0, points, DEPTH):
            plane = start // PLANE
            cosine = table_ref[base + 1 + plane]
            sine = table_ref[base + 1 + planes + plane]
            columns = pl.ds(start, DEPTH)
            real_part = there_ref[0, rows, columns].astype(jnp.float32)
            imag_part = there_ref[1, rows, columns].astype(jnp.float32)
            near_re = real_part * cosine + imag_part * sine
            near_im = imag_part * cosine - real_part * sine
            near_buf[rows, columns] = near_re.astype(jnp.bfloat16)
            near_buf[mirror, columns] = near_im.astype(jnp.bfloat16)


def put_sum(sum_buf, lane, total, again):
    width = total.shape[1] // 2
    for side in range(2):
        half = total[:, side * width : (side + 1) * width]
        if again:
            half = half + sum_buf[:, side, lane : lane + width]
        sum_buf[:, side, lane : lane + width] = half


def step_kernel(plan, table_ref, *refs):
    rows, k_dev, _, nbands = plan.shape
    fold, depth = plan.fold, plan.depth
    refs = list(refs)

    def take(count):
        taken = refs[:count]
        del refs[:count]
        return taken

    stride = (table_ref.shape[0] - 1) // k_dev
    planes = (stride - 1) // 2
    me = table_ref[k_dev * stride].astype(jnp.int32)
    place, outer = lax.rem(me, fold), lax.div(me, fold)
    if plan.part:
        bands_ref, phased_ref = take(2)
    sources = [take(count) for count in plan.takes]
    arrived = [take(count) for count in plan.adds]
    if plan.adding and plan.placed:
        take(1)
    take(plan.after)
    given_ref, kept_ref = take(2) if plan.near == "give" else (None, None)
    outs = take(len(plan.ways))
    targets = [take(task.count) for task in plan.tasks]
    result_ref = take(1)[0] if plan.adding else None
    piece_ref = take(1)[0] if plan.later else None
    if plan.part:
        if plan.near != "use":
            own_buf, own_sems = take(2)
        slot, _, width, _ = plan.part
        base = slot * stride
        point = table_ref[base].astype(jnp.int32)
        if plan.far:
            far_buf, far_sems = take(2)
            far = [
                pltpu.make_async_copy(
                    phased_ref.at[slot, part, pl.ds(plan.part[1], width), :],
                    far_buf.at[part],
                    far_sems.at[part],
                )
                for part in range(2)
            ]
            for copy in far:
                copy.start()
        own = []
        loads_of = plan.ways + (0,) if plan.near == "give" else plan.ways
        for way, distance in enumerate(loads_of if plan.near != "use" else ()):
            target = lax.rem(place + distance, fold)
            rows_ref = own_buf.at[way] if way < len(plan.ways) else kept_ref
            own.append([])
            for part in range(2):
                for level in range(depth):
                    first = pl.multiple_of((level * fold + target) * rows, rows)
                    copy = pltpu.make_async_copy(
                        bands_ref.at[point, part, pl.ds(first, rows), :],
                        rows_ref.at[part, pl.ds(level * rows, rows), :],
                        own_sems.at[way, part, level],
                    )
                    copy.start()
                    own[way].append(copy)
    if plan.later:
        piece_buf, piece_sems = take(2)
        later_slot, later_start, later_width, _ = plan.later
        loads = [
            pltpu.make_async_copy(
                bands_ref.at[later_slot, part, pl.ds(later_start, later_width), :],
                piece_buf.at[part],
                piece_sems.at[0, part],
            )
            for part in range(2)
        ]
        stores = [
            pltpu.make_async_copy(piece_buf.at[part], piece_ref.at[part], piece_sems.at[1, part])
            for part in range(2)
        ]
        for copy in loads:
            copy.start()
    if plan.adding:
        sum_buf, placed_sem = take(2)
        add_slot, add_start, pieces = plan.adding
        for index, column, start, span, again in pieces:
            total = summed(arrived[index], 0, slice(column, column + 2 * span))
            put_sum(sum_buf, start - add_start, total, again)
        add_point = table_ref[add_slot * stride].astype(jnp.int32)
        columns = pl.ds(add_start, sum_buf.shape[2])
        placing = pltpu.make_async_copy(
            sum_buf, result_ref.at[:, add_point, :, columns], placed_sem
        )
        placing.start()
    for task, arrays, outputs in zip(plan.tasks, sources, targets):
        groups = [arrays[i : i + task.each] for i in range(0, len(arrays), task.each)]
        bit = lax.rem(lax.div(outer, 1 << task.stage), 2)
        for index, out_ref in enumerate(outputs):
            for level in range(out_ref.shape[0]):
                if task.count == 1:
                    source = 0
                elif task.direct:
                    source = partner(outer, index)
                else:
                    source = 2 * level + (1 - bit if index else bit)
                column = 0
                for group in groups:
                    total = summed(group, source)
                    columns = slice(column, column + total.shape[1])
                    out_ref[level, :, columns] = total.astype(out_ref.dtype)
                    column += total.shape[1]
    if plan.part:
        near_ref = phased_ref
        if plan.far:
            for copy in far:
                copy.wait()
            phased_ref = far_buf
        if plan.near != "use":
            near_ref = given_ref if plan.near == "give" else take(1)[0]
            near_into(near_ref, phased_ref, table_ref, base, planes)
        dims = (((1,), (1,)), ((), ()))
        points = near_ref.shape[1]
        run = points // 2 if width <= SPLIT else points
        for way, out_ref in enumerate(outs):
            of_both = []
            for part in range(2):
                for copy in own[way][part * depth : (part + 1) * depth] if own else ():
                    copy.wait()
                rows_ref = bands_ref if plan.near == "use" else own_buf.at[way]
                products = [
                    lax.dot_general(
                        rows_ref[part, :, pl.ds(first, run)],
                        near_ref[:, pl.ds(first, run)],
                        dims,
                        preferred_element_type=jnp.float32,
                    )
                    for first in range(0, points, run)
                ]
                of_both.append(sum(products[1:], products[0]))
            of_re, of_im = of_both
            real_part = (of_re[:, :width] + of_im[:, width:]).astype(out_ref.dtype)
            imag_part = (of_re[:, width:] - of_im[:, :width]).astype(out_ref.dtype)
            for level in range(depth):
                lines = slice(level * rows, (level + 1) * rows)
                out_ref[level, :, :width] = real_part[lines]
                out_ref[level, :, width:] = imag_part[lines]
            if plan.near == "give" and way + 1 == len(outs):
                for copy in own[-1]:
                    copy.wait()
            if plan.later and way == 0:
                for load, store in zip(loads, stores):
                    load.wait()
                    store.start()
    if plan.adding:
        placing.wait()
    if plan.later:
        for store in stores:
            store.wait()


def partner(outer, distance):
    low, high = lax.rem(outer, 2), lax.rem(lax.div(outer, 2), 2)
    low = 1 - low if distance % 2 else low
    high = 1 - high if distance // 2 else high
    return outer - lax.rem(outer, 4) + 2 * high + low


def summed(arrays, level, columns=slice(None)):
    total = arrays[0][level, :, columns]
    for array in arrays[1:]:
        total = total + array[level, :, columns].astype(jnp.float32)
    return total


class Task(NamedTuple):
    keys: tuple
    stage: int
    direct: bool
    each: int
    count: int

    @property
    def batch(self):
        return sum(self.keys, ())


class Plan(NamedTuple):
    shape: tuple
    fold: int
    depth: int
    part: tuple
    ways: tuple
    near: str
    far: bool
    tasks: tuple
    takes: tuple
    adding: tuple
    adds: tuple
    placed: bool
    later: tuple
    after: int


def step(plan, table, bands, phased, sources, arrived, result, after):
    rows, _, _, nbands = plan.shape
    fold, depth = plan.fold, plan.depth
    points = bands.shape[-1]
    vmem = pl.BlockSpec(memory_space=pltpu.VMEM)
    hbm = pl.BlockSpec(memory_space=pltpu.HBM)
    operands, in_specs = [table], [pl.BlockSpec(memory_space=pltpu.SMEM)]
    out_shape, out_specs, scratch, aliases = [], [], [], {}

    def kind(index):
        return jnp.bfloat16 if index else jnp.float32

    if plan.part:
        width = plan.part[2]
        operands += [bands, phased]
        in_specs += [vmem if plan.near == "use" else hbm, hbm if plan.far else vmem]
        if plan.near == "give":
            out_shape.append(jax.ShapeDtypeStruct((2 * width, points), jnp.bfloat16))
            out_shape.append(jax.ShapeDtypeStruct((2, depth * rows, points), jnp.bfloat16))
        out_shape += [
            jax.ShapeDtypeStruct((depth, rows, 2 * width), kind(way)) for way in plan.ways
        ]
        if plan.near != "use":
            scratch += [
                pltpu.VMEM((len(plan.ways), 2, depth * rows, points), jnp.bfloat16),
                pltpu.SemaphoreType.DMA((fold, 2, depth)),
            ]
        if plan.far:
            scratch += [
                pltpu.VMEM((2, width, points), jnp.bfloat16),
                pltpu.SemaphoreType.DMA((2,)),
            ]
    for arrays in sources + arrived:
        operands += arrays
        in_specs += [vmem] * len(arrays)
    for task in plan.tasks:
        wide = sum(2 * part[2] for part in task.batch)
        levels = 1 if task.direct else depth >> (task.stage + 1)
        out_shape += [
            jax.ShapeDtypeStruct((levels, rows, wide), kind(i)) for i in range(task.count)
        ]
    out_specs += [vmem] * len(out_shape)
    if plan.later:
        scratch += [
            pltpu.VMEM((2, plan.later[2], points), bands.dtype),
            pltpu.SemaphoreType.DMA((2, 2)),
        ]
    if plan.adding:
        if plan.placed:
            aliases = {len(operands): len(out_shape)}
            operands.append(result)
            in_specs.append(hbm)
        out_shape.append(jax.ShapeDtypeStruct(plan.shape, jnp.float32))
        out_specs.append(hbm)
        lanes = sum(span for _, _, _, span, again in plan.adding[2] if not again)
        scratch += [pltpu.VMEM((rows, 2, lanes), jnp.float32), pltpu.SemaphoreType.DMA]
    if plan.later:
        out_shape.append(jax.ShapeDtypeStruct((2, plan.later[2], points), bands.dtype))
        out_specs.append(hbm)
    operands += after
    in_specs += [pl.BlockSpec(memory_space=pl.ANY)] * len(after)
    if plan.near == "make":
        scratch.append(pltpu.VMEM((2 * width, points), jnp.bfloat16))
    outs = list(
        pl.pallas_call(
            functools.partial(step_kernel, plan),
            in_specs=in_specs,
            out_specs=out_specs,
            scratch_shapes=scratch,
            out_shape=out_shape,
            input_output_aliases=aliases,
            compiler_params=pltpu.CompilerParams(vmem_limit_bytes=VMEM_BYTES),
            cost_estimate=pl.CostEstimate(flops=1000, bytes_accessed=1000, transcendentals=0),
            name="step",
        )(*operands)
    )
    piece = outs.pop() if plan.later else None
    result = outs.pop() if plan.adding else result
    near = [outs.pop(0), outs.pop(0)] if plan.near == "give" else None
    terms = outs[: len(plan.ways)]
    handed = outs[len(plan.ways) :]
    sends = []
    for task in plan.tasks:
        sends.append(handed[: task.count])
        handed = handed[task.count :]
    return terms, near, sends, result, piece


def cuts(nbands, k_dev):
    half, eighth = nbands // 2, nbands // 8
    last = k_dev - 1
    wide = [(slot, start, half, None) for slot in range(last) for start in (0, half)]
    early = [(last, start, half, 0) for start in (0, half)]
    widths = (3 * eighth, 3 * eighth, 2 * eighth)
    late = [(last, sum(widths[:i]), width, 1) for i, width in enumerate(widths)]
    return wide, early, late


def schedule(wide, early, late, fold, depth):
    every, others = tuple(range(fold)), tuple(range(1, fold))
    parts = wide + late
    count = len(parts)
    kernels = [(early[0], every, "make", (), ())]

    def cross(*done):
        return Task(tuple((part,) for part in done), 0, False, fold, 2)

    def halve(*keys):
        return Task(keys, 1, False, 2, 2)

    waiting, halved, crossed = [], [], []
    aside = [
        (),
        (cross(*early),),
        (halve(tuple(early)),),
        (Task((tuple(early),), 2, True, 2, 1),),
    ]
    for index, part in enumerate(parts):
        ready = tuple(waiting[:1])
        waiting = waiting[1:]
        tasks = []
        if halved:
            tasks.append(halve(*((done,) for done in halved)))
        if crossed:
            tasks.append(cross(*crossed))
        if index < len(aside):
            tasks += aside[index]
        waiting += [done for done in halved if done in wide]
        if index == count - 1:
            kernels.append((part, others, "give", tuple(tasks), ready))
            kernels.append((part, every[:1], "use", (), ()))
        else:
            kernels.append((part, every, "make", tuple(tasks), ready))
        halved, crossed = crossed, [part] if index < count - 2 else []
        if index == 0:
            kernels += [(other, every, "make", (), ()) for other in early[1:]]
        if index in (0, count - 3):
            kernels.append((None, (), "", (cross(part),), ()))
            halved, crossed = halved + crossed, []
    last = tuple((part,) for part in late[-2:])
    kernels.append((None, (), "", (Task(last, 0, True, fold, depth),), ()))
    kernels.append((None, (), "", (), tuple(early) + tuple(late)))
    return kernels


def body(bands, nbr_slot, gshift):
    grid_index = lax.axis_index("ga")
    grid_count = lax.axis_size("ga")
    k_dev, _, nbands, points = bands.shape
    rows = nbands // grid_count
    own_planes = points // PLANE
    total_planes = own_planes * grid_count
    planes = grid_index * own_planes + jnp.arange(own_planes, dtype=jnp.int32)
    slots = jnp.arange(k_dev, dtype=jnp.int32)
    chosen = nbr_slot[None, :] == slots[:, None]
    order = jnp.sum(jnp.where(chosen, slots[None, :], 0), axis=1)
    shifts = jnp.sum(jnp.where(chosen, gshift[None, :], 0), axis=1)
    turns = (1 + NKB * shifts[:, None]) * planes[None, :] % (NKB * total_planes)
    angle = 2.0 * math.pi / (NKB * total_planes) * turns.astype(jnp.float32)
    columns = [order[:, None].astype(jnp.float32), jnp.cos(angle), jnp.sin(angle)]
    table = jnp.concatenate(columns, axis=1).reshape(-1)
    table = jnp.append(table, grid_index.astype(jnp.float32))
    wide, early, late = cuts(nbands, k_dev)
    parts = wide + late
    theres = {}
    piece = None
    beside = from_next(bands, early[0][3])
    for part in parts[:AHEAD]:
        piece = piece_of(*part[:3], bands, [] if piece is None else [piece])
        theres[part] = from_next(piece, part[3])
    shape = (rows, k_dev, 2, nbands)
    depth = min(OUTER, grid_count)
    fold = grid_count // depth
    held = {}
    near, result = None, None
    after = []
    for part, ways, phase, tasks, adds in schedule(wide, early, late, fold, depth):
        later = None
        if part in parts and phase != "use" and parts.index(part) + AHEAD < len(parts):
            later = parts[parts.index(part) + AHEAD]
        sources = [[array for key in task.keys for array in held[key]] for task in tasks]
        batches, pieces = [], []
        for done in adds:
            batch = max((key for key in held if done in key), key=len)
            if batch not in batches:
                batches.append(batch)
            column = sum(2 * other[2] for other in batch[: batch.index(done)])
            again = done in late
            pieces.append((batches.index(batch), column, done[1], done[2], again))
        arrived = [held[batch] for batch in batches]
        adding = (adds[0][0], adds[0][1], tuple(pieces)) if adds else ()
        plan = Plan(
            shape,
            fold,
            depth,
            part,
            ways,
            phase,
            part in early,
            tasks,
            tuple(len(arrays) for arrays in sources),
            adding,
            tuple(len(arrays) for arrays in arrived),
            result is not None,
            later,
            len(after),
        )
        phased, own = beside if part in early else theres.get(part), bands
        if phase == "use":
            phased, own = near
        terms, near, sends, result, piece = step(
            plan, table, own, phased, sources, arrived, result, after
        )
        after = terms[:1]
        if later:
            theres[later] = from_next(piece, later[3])
        for way, array in zip(ways, terms):
            if way:
                array = crossed_over(array, way, fold, part[3])
            held.setdefault((part,), []).insert(0 if way == 0 else fold, array)
        for task, arrays in zip(tasks, sends):
            steps = range(1, depth) if task.direct else [1 << task.stage]
            parities = {done[3] for done in task.batch}
            parity = parities.pop() if len(parities) == 1 else None
            held[task.batch] = [arrays[0]] + [
                swapped(array, fold * i, parity) for array, i in zip(arrays[1:], steps)
            ]
    return result


def solution(mesh):
    placed = (P("ka", None, None, "ga"), P("ka"), P("ka"))
    return jax.shard_map(
        body, mesh=mesh, in_specs=placed, out_specs=P("ga", "ka", None, None), check_vma=False
    )
```

```python
import functools
import math
from typing import NamedTuple

import jax
import jax.numpy as jnp
from jax import lax
from jax.experimental import pallas as pl
from jax.experimental.pallas import tpu as pltpu
from jax.sharding import PartitionSpec as P

NKB = 4
PLANE = 1024
STRIP = 32
DEPTH = 512
AHEAD = 3
OUTER = 4
SPLIT = 128
LANES = 128
BLOCK = 256
VMEM_BYTES = 48 * 1024 * 1024


def shifted(block, axis, distance, fold=1, inner=False):
    count = lax.axis_size(axis)
    route = []
    for i in range(count):
        outer, place = divmod(i, fold)
        if inner:
            route.append((i, outer * fold + (place + distance) % fold))
        else:
            route.append((i, (outer + distance) % (count // fold) * fold + place))
    return lax.ppermute(block, axis, route)


def swapped(block, axis, distance):
    count = lax.axis_size(axis)
    return lax.ppermute(block, axis, [(i, i ^ distance) for i in range(count)])


def piece_kernel(slot, start, bands_ref, *rest):
    out_ref, piece_buf, sems = rest[-3:]
    width = piece_buf.shape[1]
    rows = pl.ds(start, width)
    loads = [
        pltpu.make_async_copy(bands_ref.at[slot, part, rows, :], piece_buf.at[part], sems.at[0, part])
        for part in range(2)
    ]
    stores = [
        pltpu.make_async_copy(piece_buf.at[part], out_ref.at[part], sems.at[1, part])
        for part in range(2)
    ]
    for load in loads:
        load.start()
    for load, store in zip(loads, stores):
        load.wait()
        store.start()
    for store in stores:
        store.wait()


def piece_of(slot, start, width, bands, after):
    points = bands.shape[3]
    return pl.pallas_call(
        functools.partial(piece_kernel, slot, start),
        in_specs=[pl.BlockSpec(memory_space=pl.ANY)] * (1 + len(after)),
        out_specs=pl.BlockSpec(memory_space=pl.ANY),
        scratch_shapes=[
            pltpu.VMEM((2, width, points), bands.dtype),
            pltpu.SemaphoreType.DMA((2, 2)),
        ],
        out_shape=jax.ShapeDtypeStruct((2, width, points), bands.dtype),
        compiler_params=pltpu.CompilerParams(vmem_limit_bytes=VMEM_BYTES),
        cost_estimate=pl.CostEstimate(flops=1000, bytes_accessed=1000, transcendentals=0),
        name="piece_of",
    )(bands, *after)


def near_into(near_buf, there_ref, table_ref, base, planes):
    width, points = there_ref.shape[1:]

    @pl.loop(0, width // STRIP)
    def _(strip):
        rows = pl.ds(strip * STRIP, STRIP)
        mirror = pl.ds(width + strip * STRIP, STRIP)
        for start in range(0, points, DEPTH):
            plane = start // PLANE
            cosine = table_ref[base + 1 + plane]
            sine = table_ref[base + 1 + planes + plane]
            columns = pl.ds(start, DEPTH)
            real_part = there_ref[0, rows, columns].astype(jnp.float32)
            imag_part = there_ref[1, rows, columns].astype(jnp.float32)
            near_re = real_part * cosine + imag_part * sine
            near_im = imag_part * cosine - real_part * sine
            near_buf[rows, columns] = near_re.astype(jnp.bfloat16)
            near_buf[mirror, columns] = near_im.astype(jnp.bfloat16)


def put_sum(sum_buf, lane, total):
    width = total.shape[1] // 2
    sum_buf[:, 0, lane : lane + width] = total[:, :width]
    sum_buf[:, 1, lane : lane + width] = total[:, width:]


def step_kernel(plan, table_ref, *refs):
    rows, k_dev, _, nbands = plan.shape
    fold, depth = plan.fold, plan.depth
    refs = list(refs)

    def take(count):
        taken = refs[:count]
        del refs[:count]
        return taken

    stride = (table_ref.shape[0] - 1) // k_dev
    planes = (stride - 1) // 2
    me = table_ref[k_dev * stride].astype(jnp.int32)
    place, outer = lax.rem(me, fold), lax.div(me, fold)
    if plan.part:
        bands_ref, phased_ref = take(2)
    sources = [take(count) for count in plan.takes]
    arrived = [take(count) for count in plan.adds]
    if plan.adding and plan.placed:
        take(1)
    given_ref, kept_ref = take(2) if plan.near == "give" else (None, None)
    outs = take(len(plan.ways))
    targets = [take(task.count) for task in plan.tasks]
    result_ref = take(1)[0] if plan.adding else None
    piece_ref = take(1)[0] if plan.later else None
    if plan.part:
        if plan.near != "use":
            own_buf, own_sems = take(2)
        slot, _, width = plan.part
        base = slot * stride
        point = table_ref[base].astype(jnp.int32)
        own = []
        loads_of = plan.ways + (0,) if plan.near == "give" else plan.ways
        for way, distance in enumerate(loads_of if plan.near != "use" else ()):
            target = lax.rem(place + distance, fold)
            rows_ref = own_buf.at[way] if way < len(plan.ways) else kept_ref
            own.append([])
            for part in range(2):
                for level in range(depth):
                    first = pl.multiple_of((level * fold + target) * rows, rows)
                    copy = pltpu.make_async_copy(
                        bands_ref.at[point, part, pl.ds(first, rows), :],
                        rows_ref.at[part, pl.ds(level * rows, rows), :],
                        own_sems.at[way, part, level],
                    )
                    copy.start()
                    own[way].append(copy)
    if plan.later:
        piece_buf, piece_sems = take(2)
        later_slot, later_start, later_width = plan.later
        loads = [
            pltpu.make_async_copy(
                bands_ref.at[later_slot, part, pl.ds(later_start, later_width), :],
                piece_buf.at[part],
                piece_sems.at[0, part],
            )
            for part in range(2)
        ]
        stores = [
            pltpu.make_async_copy(piece_buf.at[part], piece_ref.at[part], piece_sems.at[1, part])
            for part in range(2)
        ]
        for copy in loads:
            copy.start()
    if plan.adding:
        sum_buf, placed_sem = take(2)
        add_slot, add_start, pieces = plan.adding
        for index, column, start, span in pieces:
            total = summed(arrived[index], 0, slice(column, column + 2 * span))
            put_sum(sum_buf, start - add_start, total)
        add_point = table_ref[add_slot * stride].astype(jnp.int32)
        columns = pl.ds(add_start, sum_buf.shape[2])
        placing = pltpu.make_async_copy(
            sum_buf, result_ref.at[:, add_point, :, columns], placed_sem
        )
        placing.start()
    for task, arrays, outputs in zip(plan.tasks, sources, targets):
        groups = [arrays[i : i + task.each] for i in range(0, len(arrays), task.each)]
        bit = lax.rem(lax.div(outer, 1 << task.stage), 2)
        for index, out_ref in enumerate(outputs):
            for level in range(out_ref.shape[0]):
                if task.direct:
                    source = partner(outer, index)
                else:
                    source = 2 * level + (1 - bit if index else bit)
                column = 0
                for group in groups:
                    total = summed(group, source)
                    columns = slice(column, column + total.shape[1])
                    out_ref[level, :, columns] = total.astype(out_ref.dtype)
                    column += total.shape[1]
    if plan.part:
        near_ref = phased_ref
        if plan.near != "use":
            near_ref = given_ref if plan.near == "give" else take(1)[0]
            near_into(near_ref, phased_ref, table_ref, base, planes)
        dims = (((1,), (1,)), ((), ()))
        points = near_ref.shape[1]
        run = points // 2 if width <= SPLIT else points
        for way, out_ref in enumerate(outs):
            of_both = []
            for part in range(2):
                for copy in own[way][part * depth : (part + 1) * depth] if own else ():
                    copy.wait()
                rows_ref = bands_ref if plan.near == "use" else own_buf.at[way]
                products = [
                    lax.dot_general(
                        rows_ref[part, :, pl.ds(first, run)],
                        near_ref[:, pl.ds(first, run)],
                        dims,
                        preferred_element_type=jnp.float32,
                    )
                    for first in range(0, points, run)
                ]
                of_both.append(sum(products[1:], products[0]))
            of_re, of_im = of_both
            real_part = (of_re[:, :width] + of_im[:, width:]).astype(out_ref.dtype)
            imag_part = (of_re[:, width:] - of_im[:, :width]).astype(out_ref.dtype)
            for level in range(depth):
                lines = slice(level * rows, (level + 1) * rows)
                out_ref[level, :, :width] = real_part[lines]
                out_ref[level, :, width:] = imag_part[lines]
            if plan.near == "give" and way + 1 == len(outs):
                for copy in own[-1]:
                    copy.wait()
            if plan.later and way == 0:
                for load, store in zip(loads, stores):
                    load.wait()
                    store.start()
    if plan.adding:
        placing.wait()
    if plan.later:
        for store in stores:
            store.wait()


def partner(outer, distance):
    low, high = lax.rem(outer, 2), lax.rem(lax.div(outer, 2), 2)
    low = 1 - low if distance % 2 else low
    high = 1 - high if distance // 2 else high
    return outer - lax.rem(outer, 4) + 2 * high + low


def summed(arrays, level, columns=slice(None)):
    total = arrays[0][level, :, columns]
    for array in arrays[1:]:
        total = total + array[level, :, columns].astype(jnp.float32)
    return total


class Task(NamedTuple):
    batch: tuple
    stage: int
    direct: bool
    each: int
    count: int


class Plan(NamedTuple):
    shape: tuple
    fold: int
    depth: int
    part: tuple
    ways: tuple
    near: str
    tasks: tuple
    takes: tuple
    adding: tuple
    adds: tuple
    placed: bool
    later: tuple


def step(plan, table, bands, phased, sources, arrived, result):
    rows, _, _, nbands = plan.shape
    fold, depth = plan.fold, plan.depth
    points = bands.shape[-1]
    vmem = pl.BlockSpec(memory_space=pltpu.VMEM)
    hbm = pl.BlockSpec(memory_space=pltpu.HBM)
    operands, in_specs = [table], [pl.BlockSpec(memory_space=pltpu.SMEM)]
    out_shape, out_specs, scratch, aliases = [], [], [], {}

    def kind(index):
        return jnp.bfloat16 if index else jnp.float32

    if plan.part:
        width = plan.part[2]
        operands += [bands, phased]
        in_specs += [vmem if plan.near == "use" else hbm, vmem]
        if plan.near == "give":
            out_shape.append(jax.ShapeDtypeStruct((2 * width, points), jnp.bfloat16))
            out_shape.append(jax.ShapeDtypeStruct((2, depth * rows, points), jnp.bfloat16))
        out_shape += [
            jax.ShapeDtypeStruct((depth, rows, 2 * width), kind(way)) for way in plan.ways
        ]
        if plan.near != "use":
            scratch += [
                pltpu.VMEM((len(plan.ways), 2, depth * rows, points), jnp.bfloat16),
                pltpu.SemaphoreType.DMA((fold, 2, depth)),
            ]
    for arrays in sources + arrived:
        operands += arrays
        in_specs += [vmem] * len(arrays)
    for task in plan.tasks:
        wide = sum(2 * width for _, _, width in task.batch)
        levels = 1 if task.direct else depth >> (task.stage + 1)
        out_shape += [
            jax.ShapeDtypeStruct((levels, rows, wide), kind(i)) for i in range(task.count)
        ]
    out_specs += [vmem] * len(out_shape)
    if plan.later:
        scratch += [
            pltpu.VMEM((2, plan.later[2], points), bands.dtype),
            pltpu.SemaphoreType.DMA((2, 2)),
        ]
    if plan.adding:
        if plan.placed:
            aliases = {len(operands): len(out_shape)}
            operands.append(result)
            in_specs.append(hbm)
        out_shape.append(jax.ShapeDtypeStruct(plan.shape, jnp.float32))
        out_specs.append(hbm)
        lanes = sum(span for _, _, _, span in plan.adding[2])
        scratch += [pltpu.VMEM((rows, 2, lanes), jnp.float32), pltpu.SemaphoreType.DMA]
    if plan.later:
        out_shape.append(jax.ShapeDtypeStruct((2, plan.later[2], points), bands.dtype))
        out_specs.append(hbm)
    if plan.near == "make":
        scratch.append(pltpu.VMEM((2 * width, points), jnp.bfloat16))
    outs = list(
        pl.pallas_call(
            functools.partial(step_kernel, plan),
            in_specs=in_specs,
            out_specs=out_specs,
            scratch_shapes=scratch,
            out_shape=out_shape,
            input_output_aliases=aliases,
            compiler_params=pltpu.CompilerParams(vmem_limit_bytes=VMEM_BYTES),
            cost_estimate=pl.CostEstimate(flops=1000, bytes_accessed=1000, transcendentals=0),
            name="step",
        )(*operands)
    )
    piece = outs.pop() if plan.later else None
    result = outs.pop() if plan.adding else result
    near = [outs.pop(0), outs.pop(0)] if plan.near == "give" else None
    terms = outs[: len(plan.ways)]
    handed = outs[len(plan.ways) :]
    sends = []
    for task in plan.tasks:
        sends.append(handed[: task.count])
        handed = handed[task.count :]
    return terms, near, sends, result, piece


def cuts(nbands, first):
    eighth = nbands // 8
    widths = [4 * eighth, 4 * eighth] if first else [3 * eighth, 3 * eighth, 2 * eighth]
    starts = [sum(widths[:i]) for i in range(len(widths))]
    return list(zip(starts, widths))


def schedule(parts, fold, depth):
    every, others = tuple(range(fold)), tuple(range(1, fold))
    count = len(parts)
    kernels = []
    waiting, halved, crossed = [], [], []
    for index, part in enumerate(parts):
        ready = ready_parts(waiting)
        waiting = waiting[len(ready) :]
        tasks = []
        if halved:
            tasks.append(Task(tuple(halved), 1, False, 2, 2))
        if crossed:
            tasks.append(Task(tuple(crossed), 0, False, fold, 2))
        waiting += halved
        if index == count - 1:
            kernels.append((part, others, "give", tuple(tasks), ready))
            kernels.append((part, every[:1], "use", (), ()))
        else:
            kernels.append((part, every, "make", tuple(tasks), ready))
        halved, crossed = crossed, [part] if index < count - 2 else []
        if index in (0, count - 3):
            kernels.append((None, (), "", (Task((part,), 0, False, fold, 2),), ()))
            halved, crossed = halved + crossed, []
    last = tuple(parts[-2:])
    kernels.append((None, (), "", (Task(last, 0, True, fold, depth),), ()))
    kernels.append((None, (), "", (), tuple(waiting) + last))
    return kernels


def ready_parts(waiting):
    total = 0
    for count, (slot, _, width) in enumerate(waiting, 1):
        total += width
        if slot != waiting[0][0]:
            break
        if total % LANES == 0:
            return tuple(waiting[:count])
    return ()


def body(bands, nbr_slot, gshift):
    grid_index = lax.axis_index("ga")
    grid_count = lax.axis_size("ga")
    k_dev, _, nbands, points = bands.shape
    rows = nbands // grid_count
    own_planes = points // PLANE
    total_planes = own_planes * grid_count
    planes = grid_index * own_planes + jnp.arange(own_planes, dtype=jnp.int32)
    slots = jnp.arange(k_dev, dtype=jnp.int32)
    chosen = nbr_slot[None, :] == slots[:, None]
    order = jnp.sum(jnp.where(chosen, slots[None, :], 0), axis=1)
    shifts = jnp.sum(jnp.where(chosen, gshift[None, :], 0), axis=1)
    turns = (1 + NKB * shifts[:, None]) * planes[None, :] % (NKB * total_planes)
    angle = 2.0 * math.pi / (NKB * total_planes) * turns.astype(jnp.float32)
    columns = [order[:, None].astype(jnp.float32), jnp.cos(angle), jnp.sin(angle)]
    table = jnp.concatenate(columns, axis=1).reshape(-1)
    table = jnp.append(table, grid_index.astype(jnp.float32))
    parts = []
    for slot in range(k_dev):
        for start, width in cuts(nbands, slot == 0):
            parts.append((slot, start, width))
    theres = []
    piece = None
    for slot, start, width in parts[:AHEAD]:
        piece = piece_of(slot, start, width, bands, [] if piece is None else [piece])
        theres.append(shifted(piece, "ka", -1))
    shape = (rows, k_dev, 2, nbands)
    depth = min(OUTER, grid_count)
    fold = grid_count // depth
    held = {}
    near, result = None, None
    for part, ways, phase, tasks, adds in schedule(parts, fold, depth):
        place = parts.index(part) if part else len(parts)
        later = parts[place + AHEAD] if place + AHEAD < len(parts) else None
        sources = [[array for done in task.batch for array in held[(done,)]] for task in tasks]
        batches, pieces = [], []
        for done in adds:
            batch = max((key for key in held if done in key), key=len)
            if batch not in batches:
                batches.append(batch)
            column = sum(2 * width for _, _, width in batch[: batch.index(done)])
            pieces.append((batches.index(batch), column, done[1], done[2]))
        arrived = [held[batch] for batch in batches]
        adding = (adds[0][0], adds[0][1], tuple(pieces)) if adds else ()
        plan = Plan(
            shape,
            fold,
            depth,
            part,
            ways,
            phase,
            tasks,
            tuple(len(arrays) for arrays in sources),
            adding,
            tuple(len(arrays) for arrays in arrived),
            result is not None,
            later,
        )
        phased, own = theres[place] if part else None, bands
        if phase == "use":
            phased, own = near
        terms, near, sends, result, piece = step(
            plan, table, own, phased, sources, arrived, result
        )
        if later:
            theres.append(shifted(piece, "ka", -1))
        for way, array in zip(ways, terms):
            array = shifted(array, "ga", way, fold, True) if way else array
            held.setdefault((part,), []).insert(0 if way == 0 else fold, array)
        for task, arrays in zip(tasks, sends):
            steps = range(1, depth) if task.direct else [1 << task.stage]
            held[task.batch] = [arrays[0]] + [
                swapped(array, "ga", fold * i) for array, i in zip(arrays[1:], steps)
            ]
    return result


def solution(mesh):
    placed = (P("ka", None, None, "ga"), P("ka"), P("ka"))
    return jax.shard_map(
        body, mesh=mesh, in_specs=placed, out_specs=P("ga", "ka", None, None), check_vma=False
    )
```

```python
import functools
import math
from typing import NamedTuple

import jax
import jax.numpy as jnp
from jax import lax
from jax.experimental import pallas as pl
from jax.experimental.pallas import tpu as pltpu
from jax.sharding import PartitionSpec as P

NKB = 4
PLANE = 1024
STRIP = 32
DEPTH = 512
AHEAD = 3
OUTER = 4
SPLIT = 128
LANES = 128
BLOCK = 256
VMEM_BYTES = 46 * 1024 * 1024


def shifted(block, axis, distance, fold=1, inner=False):
    count = lax.axis_size(axis)
    route = []
    for i in range(count):
        outer, place = divmod(i, fold)
        if inner:
            route.append((i, outer * fold + (place + distance) % fold))
        else:
            route.append((i, (outer + distance) % (count // fold) * fold + place))
    return lax.ppermute(block, axis, route)


def swapped(block, axis, distance):
    count = lax.axis_size(axis)
    return lax.ppermute(block, axis, [(i, i ^ distance) for i in range(count)])


def piece_kernel(slot, start, bands_ref, *rest):
    out_ref, piece_buf, sems = rest[-3:]
    width = piece_buf.shape[1]
    rows = pl.ds(start, width)
    loads = [
        pltpu.make_async_copy(bands_ref.at[slot, part, rows, :], piece_buf.at[part], sems.at[0, part])
        for part in range(2)
    ]
    stores = [
        pltpu.make_async_copy(piece_buf.at[part], out_ref.at[part], sems.at[1, part])
        for part in range(2)
    ]
    for load in loads:
        load.start()
    for load, store in zip(loads, stores):
        load.wait()
        store.start()
    for store in stores:
        store.wait()


def piece_of(slot, start, width, bands, after):
    points = bands.shape[3]
    return pl.pallas_call(
        functools.partial(piece_kernel, slot, start),
        in_specs=[pl.BlockSpec(memory_space=pl.ANY)] * (1 + len(after)),
        out_specs=pl.BlockSpec(memory_space=pl.ANY),
        scratch_shapes=[
            pltpu.VMEM((2, width, points), bands.dtype),
            pltpu.SemaphoreType.DMA((2, 2)),
        ],
        out_shape=jax.ShapeDtypeStruct((2, width, points), bands.dtype),
        compiler_params=pltpu.CompilerParams(vmem_limit_bytes=VMEM_BYTES),
        cost_estimate=pl.CostEstimate(flops=1000, bytes_accessed=1000, transcendentals=0),
        name="piece_of",
    )(bands, *after)


def near_into(near_buf, there_ref, table_ref, base, planes):
    width, points = there_ref.shape[1:]

    @pl.loop(0, width // STRIP)
    def _(strip):
        rows = pl.ds(strip * STRIP, STRIP)
        mirror = pl.ds(width + strip * STRIP, STRIP)
        for start in range(0, points, DEPTH):
            plane = start // PLANE
            cosine = table_ref[base + 1 + plane]
            sine = table_ref[base + 1 + planes + plane]
            columns = pl.ds(start, DEPTH)
            real_part = there_ref[0, rows, columns].astype(jnp.float32)
            imag_part = there_ref[1, rows, columns].astype(jnp.float32)
            near_re = real_part * cosine + imag_part * sine
            near_im = imag_part * cosine - real_part * sine
            near_buf[rows, columns] = near_re.astype(jnp.bfloat16)
            near_buf[mirror, columns] = near_im.astype(jnp.bfloat16)


def put_sum(sum_buf, lane, total):
    width = total.shape[1] // 2
    sum_buf[:, 0, lane : lane + width] = total[:, :width]
    sum_buf[:, 1, lane : lane + width] = total[:, width:]


def step_kernel(plan, table_ref, *refs):
    rows, k_dev, _, nbands = plan.shape
    fold, depth = plan.fold, plan.depth
    refs = list(refs)

    def take(count):
        taken = refs[:count]
        del refs[:count]
        return taken

    stride = (table_ref.shape[0] - 1) // k_dev
    planes = (stride - 1) // 2
    me = table_ref[k_dev * stride].astype(jnp.int32)
    place, outer = lax.rem(me, fold), lax.div(me, fold)
    if plan.part:
        bands_ref, phased_ref = take(2)
    sources = [take(count) for count in plan.takes]
    arrived = [take(count) for count in plan.adds]
    if plan.adding and plan.placed:
        take(1)
    given_ref, kept_ref = take(2) if plan.near == "give" else (None, None)
    outs = take(len(plan.ways))
    targets = [take(task.count) for task in plan.tasks]
    result_ref = take(1)[0] if plan.adding else None
    piece_ref = take(1)[0] if plan.later else None
    if plan.part:
        if plan.near != "use":
            own_buf, own_sems = take(2)
        slot, _, width = plan.part
        base = slot * stride
        point = table_ref[base].astype(jnp.int32)
        own = []
        loads_of = plan.ways + (0,) if plan.near == "give" else plan.ways
        for way, distance in enumerate(loads_of if plan.near != "use" else ()):
            target = lax.rem(place + distance, fold)
            rows_ref = own_buf.at[way] if way < len(plan.ways) else kept_ref
            own.append([])
            for part in range(2):
                for level in range(depth):
                    first = pl.multiple_of((level * fold + target) * rows, rows)
                    copy = pltpu.make_async_copy(
                        bands_ref.at[point, part, pl.ds(first, rows), :],
                        rows_ref.at[part, pl.ds(level * rows, rows), :],
                        own_sems.at[way, part, level],
                    )
                    copy.start()
                    own[way].append(copy)
    if plan.later:
        piece_buf, piece_sems = take(2)
        later_slot, later_start, later_width = plan.later
        loads = [
            pltpu.make_async_copy(
                bands_ref.at[later_slot, part, pl.ds(later_start, later_width), :],
                piece_buf.at[part],
                piece_sems.at[0, part],
            )
            for part in range(2)
        ]
        stores = [
            pltpu.make_async_copy(piece_buf.at[part], piece_ref.at[part], piece_sems.at[1, part])
            for part in range(2)
        ]
        for copy in loads:
            copy.start()
    if plan.adding:
        sum_buf, placed_sem = take(2)
        add_slot, add_start, pieces = plan.adding
        for index, column, start, span in pieces:
            total = summed(arrived[index], 0, slice(column, column + 2 * span))
            put_sum(sum_buf, start - add_start, total)
        add_point = table_ref[add_slot * stride].astype(jnp.int32)
        columns = pl.ds(add_start, sum_buf.shape[2])
        placing = pltpu.make_async_copy(
            sum_buf, result_ref.at[:, add_point, :, columns], placed_sem
        )
        placing.start()
    for task, arrays, outputs in zip(plan.tasks, sources, targets):
        groups = [arrays[i : i + task.each] for i in range(0, len(arrays), task.each)]
        bit = lax.rem(lax.div(outer, 1 << task.stage), 2)
        for index, out_ref in enumerate(outputs):
            for level in range(out_ref.shape[0]):
                if task.direct:
                    source = partner(outer, index)
                else:
                    source = 2 * level + (1 - bit if index else bit)
                column = 0
                for group in groups:
                    total = summed(group, source)
                    columns = slice(column, column + total.shape[1])
                    out_ref[level, :, columns] = total.astype(out_ref.dtype)
                    column += total.shape[1]
    if plan.part:
        near_ref = phased_ref
        if plan.near != "use":
            near_ref = given_ref if plan.near == "give" else take(1)[0]
            near_into(near_ref, phased_ref, table_ref, base, planes)
        dims = (((1,), (1,)), ((), ()))
        points = near_ref.shape[1]
        run = points // 2 if width <= SPLIT else points
        for way, out_ref in enumerate(outs):
            of_both = []
            for part in range(2):
                for copy in own[way][part * depth : (part + 1) * depth] if own else ():
                    copy.wait()
                rows_ref = bands_ref if plan.near == "use" else own_buf.at[way]
                products = [
                    lax.dot_general(
                        rows_ref[part, :, pl.ds(first, run)],
                        near_ref[:, pl.ds(first, run)],
                        dims,
                        preferred_element_type=jnp.float32,
                    )
                    for first in range(0, points, run)
                ]
                of_both.append(sum(products[1:], products[0]))
            of_re, of_im = of_both
            real_part = (of_re[:, :width] + of_im[:, width:]).astype(out_ref.dtype)
            imag_part = (of_re[:, width:] - of_im[:, :width]).astype(out_ref.dtype)
            for level in range(depth):
                lines = slice(level * rows, (level + 1) * rows)
                out_ref[level, :, :width] = real_part[lines]
                out_ref[level, :, width:] = imag_part[lines]
            if plan.near == "give" and way + 1 == len(outs):
                for copy in own[-1]:
                    copy.wait()
            if plan.later and way == 0:
                for load, store in zip(loads, stores):
                    load.wait()
                    store.start()
    if plan.adding:
        placing.wait()
    if plan.later:
        for store in stores:
            store.wait()


def partner(outer, distance):
    low, high = lax.rem(outer, 2), lax.rem(lax.div(outer, 2), 2)
    low = 1 - low if distance % 2 else low
    high = 1 - high if distance // 2 else high
    return outer - lax.rem(outer, 4) + 2 * high + low


def summed(arrays, level, columns=slice(None)):
    total = arrays[0][level, :, columns]
    for array in arrays[1:]:
        total = total + array[level, :, columns].astype(jnp.float32)
    return total


class Task(NamedTuple):
    batch: tuple
    stage: int
    direct: bool
    each: int
    count: int


class Plan(NamedTuple):
    shape: tuple
    fold: int
    depth: int
    part: tuple
    ways: tuple
    near: str
    tasks: tuple
    takes: tuple
    adding: tuple
    adds: tuple
    placed: bool
    later: tuple


def step(plan, table, bands, phased, sources, arrived, result):
    rows, _, _, nbands = plan.shape
    fold, depth = plan.fold, plan.depth
    points = bands.shape[-1]
    vmem = pl.BlockSpec(memory_space=pltpu.VMEM)
    hbm = pl.BlockSpec(memory_space=pltpu.HBM)
    operands, in_specs = [table], [pl.BlockSpec(memory_space=pltpu.SMEM)]
    out_shape, out_specs, scratch, aliases = [], [], [], {}

    def kind(index):
        return jnp.bfloat16 if index else jnp.float32

    if plan.part:
        width = plan.part[2]
        operands += [bands, phased]
        in_specs += [vmem if plan.near == "use" else hbm, vmem]
        if plan.near == "give":
            out_shape.append(jax.ShapeDtypeStruct((2 * width, points), jnp.bfloat16))
            out_shape.append(jax.ShapeDtypeStruct((2, depth * rows, points), jnp.bfloat16))
        out_shape += [
            jax.ShapeDtypeStruct((depth, rows, 2 * width), kind(way)) for way in plan.ways
        ]
        if plan.near != "use":
            scratch += [
                pltpu.VMEM((len(plan.ways), 2, depth * rows, points), jnp.bfloat16),
                pltpu.SemaphoreType.DMA((fold, 2, depth)),
            ]
    for arrays in sources + arrived:
        operands += arrays
        in_specs += [vmem] * len(arrays)
    for task in plan.tasks:
        wide = sum(2 * width for _, _, width in task.batch)
        levels = 1 if task.direct else depth >> (task.stage + 1)
        out_shape += [
            jax.ShapeDtypeStruct((levels, rows, wide), kind(i)) for i in range(task.count)
        ]
    out_specs += [vmem] * len(out_shape)
    if plan.later:
        scratch += [
            pltpu.VMEM((2, plan.later[2], points), bands.dtype),
            pltpu.SemaphoreType.DMA((2, 2)),
        ]
    if plan.adding:
        if plan.placed:
            aliases = {len(operands): len(out_shape)}
            operands.append(result)
            in_specs.append(hbm)
        out_shape.append(jax.ShapeDtypeStruct(plan.shape, jnp.float32))
        out_specs.append(hbm)
        lanes = sum(span for _, _, _, span in plan.adding[2])
        scratch += [pltpu.VMEM((rows, 2, lanes), jnp.float32), pltpu.SemaphoreType.DMA]
    if plan.later:
        out_shape.append(jax.ShapeDtypeStruct((2, plan.later[2], points), bands.dtype))
        out_specs.append(hbm)
    if plan.near == "make":
        scratch.append(pltpu.VMEM((2 * width, points), jnp.bfloat16))
    outs = list(
        pl.pallas_call(
            functools.partial(step_kernel, plan),
            in_specs=in_specs,
            out_specs=out_specs,
            scratch_shapes=scratch,
            out_shape=out_shape,
            input_output_aliases=aliases,
            compiler_params=pltpu.CompilerParams(vmem_limit_bytes=VMEM_BYTES),
            cost_estimate=pl.CostEstimate(flops=1000, bytes_accessed=1000, transcendentals=0),
            name="step",
        )(*operands)
    )
    piece = outs.pop() if plan.later else None
    result = outs.pop() if plan.adding else result
    near = [outs.pop(0), outs.pop(0)] if plan.near == "give" else None
    terms = outs[: len(plan.ways)]
    handed = outs[len(plan.ways) :]
    sends = []
    for task in plan.tasks:
        sends.append(handed[: task.count])
        handed = handed[task.count :]
    return terms, near, sends, result, piece


def cuts(nbands, first):
    eighth = nbands // 8
    widths = [4 * eighth, 4 * eighth] if first else [3 * eighth, 3 * eighth, 2 * eighth]
    starts = [sum(widths[:i]) for i in range(len(widths))]
    return list(zip(starts, widths))


def schedule(parts, fold, depth):
    every, others = tuple(range(fold)), tuple(range(1, fold))
    count = len(parts)
    kernels = []
    waiting, halved, crossed = [], [], []
    for index, part in enumerate(parts):
        ready = ready_parts(waiting)
        waiting = waiting[len(ready) :]
        tasks = []
        if halved:
            tasks.append(Task(tuple(halved), 1, False, 2, 2))
        if crossed:
            tasks.append(Task(tuple(crossed), 0, False, fold, 2))
        waiting += halved
        if index >= count - 3:
            kernels.append((part, others, "give", tuple(tasks), ready))
            kernels.append((part, every[:1], "use", (), ()))
        else:
            kernels.append((part, every, "make", tuple(tasks), ready))
        halved, crossed = crossed, [part] if index < count - 1 else []
        if index in (0, count - 3):
            kernels.append((None, (), "", (Task((part,), 0, False, fold, 2),), ()))
            halved, crossed = halved + crossed, []
    tasks = (
        Task((parts[-1],), 0, True, fold, depth),
        Task(tuple(halved), 1, False, 2, 2),
    )
    kernels.append((None, (), "", tasks, ()))
    kernels.append((None, (), "", (), tuple(waiting) + tuple(halved) + (parts[-1],)))
    return kernels


def ready_parts(waiting):
    total = 0
    for count, (slot, _, width) in enumerate(waiting, 1):
        total += width
        if slot != waiting[0][0]:
            break
        if total % LANES == 0:
            return tuple(waiting[:count])
    return ()


def body(bands, nbr_slot, gshift):
    grid_index = lax.axis_index("ga")
    grid_count = lax.axis_size("ga")
    k_dev, _, nbands, points = bands.shape
    rows = nbands // grid_count
    own_planes = points // PLANE
    total_planes = own_planes * grid_count
    planes = grid_index * own_planes + jnp.arange(own_planes, dtype=jnp.int32)
    slots = jnp.arange(k_dev, dtype=jnp.int32)
    chosen = nbr_slot[None, :] == slots[:, None]
    order = jnp.sum(jnp.where(chosen, slots[None, :], 0), axis=1)
    shifts = jnp.sum(jnp.where(chosen, gshift[None, :], 0), axis=1)
    turns = (1 + NKB * shifts[:, None]) * planes[None, :] % (NKB * total_planes)
    angle = 2.0 * math.pi / (NKB * total_planes) * turns.astype(jnp.float32)
    columns = [order[:, None].astype(jnp.float32), jnp.cos(angle), jnp.sin(angle)]
    table = jnp.concatenate(columns, axis=1).reshape(-1)
    table = jnp.append(table, grid_index.astype(jnp.float32))
    parts = []
    for slot in range(k_dev):
        for start, width in cuts(nbands, slot == 0):
            parts.append((slot, start, width))
    theres = []
    piece = None
    for slot, start, width in parts[:AHEAD]:
        piece = piece_of(slot, start, width, bands, [] if piece is None else [piece])
        theres.append(shifted(piece, "ka", -1))
    shape = (rows, k_dev, 2, nbands)
    depth = min(OUTER, grid_count)
    fold = grid_count // depth
    held = {}
    near, result = None, None
    for part, ways, phase, tasks, adds in schedule(parts, fold, depth):
        place = parts.index(part) if part else len(parts)
        later = parts[place + AHEAD] if place + AHEAD < len(parts) and phase != "use" else None
        sources = [[array for done in task.batch for array in held[(done,)]] for task in tasks]
        batches, pieces = [], []
        for done in adds:
            batch = max((key for key in held if done in key), key=len)
            if batch not in batches:
                batches.append(batch)
            column = sum(2 * width for _, _, width in batch[: batch.index(done)])
            pieces.append((batches.index(batch), column, done[1], done[2]))
        arrived = [held[batch] for batch in batches]
        adding = (adds[0][0], adds[0][1], tuple(pieces)) if adds else ()
        plan = Plan(
            shape,
            fold,
            depth,
            part,
            ways,
            phase,
            tasks,
            tuple(len(arrays) for arrays in sources),
            adding,
            tuple(len(arrays) for arrays in arrived),
            result is not None,
            later,
        )
        phased, own = theres[place] if part else None, bands
        if phase == "use":
            phased, own = near
        terms, near, sends, result, piece = step(
            plan, table, own, phased, sources, arrived, result
        )
        if later:
            theres.append(shifted(piece, "ka", -1))
        for way, array in zip(ways, terms):
            array = shifted(array, "ga", way, fold, True) if way else array
            held.setdefault((part,), []).insert(0 if way == 0 else fold, array)
        for task, arrays in zip(tasks, sends):
            steps = range(1, depth) if task.direct else [1 << task.stage]
            held[task.batch] = [arrays[0]] + [
                swapped(array, "ga", fold * i) for array, i in zip(arrays[1:], steps)
            ]
    return result


def solution(mesh):
    placed = (P("ka", None, None, "ga"), P("ka"), P("ka"))
    return jax.shard_map(
        body, mesh=mesh, in_specs=placed, out_specs=P("ga", "ka", None, None), check_vma=False
    )
```

```python
import functools
import math
from typing import NamedTuple

import jax
import jax.numpy as jnp
from jax import lax
from jax.experimental import pallas as pl
from jax.experimental.pallas import tpu as pltpu
from jax.sharding import PartitionSpec as P

NKB = 4
PLANE = 1024
STRIP = 32
DEPTH = 512
AHEAD = 3
OUTER = 4
SPLIT = 128
JOINT = 2
LANES = 128
BLOCK = 256
VMEM_BYTES = 46 * 1024 * 1024


def shifted(block, axis, distance, fold=1, inner=False):
    count = lax.axis_size(axis)
    route = []
    for i in range(count):
        outer, place = divmod(i, fold)
        if inner:
            route.append((i, outer * fold + (place + distance) % fold))
        else:
            route.append((i, (outer + distance) % (count // fold) * fold + place))
    return lax.ppermute(block, axis, route)


def swapped(block, axis, distance):
    count = lax.axis_size(axis)
    return lax.ppermute(block, axis, [(i, i ^ distance) for i in range(count)])


def piece_kernel(slot, start, bands_ref, *rest):
    out_ref, piece_buf, sems = rest[-3:]
    width = piece_buf.shape[1]
    rows = pl.ds(start, width)
    loads = [
        pltpu.make_async_copy(bands_ref.at[slot, part, rows, :], piece_buf.at[part], sems.at[0, part])
        for part in range(2)
    ]
    stores = [
        pltpu.make_async_copy(piece_buf.at[part], out_ref.at[part], sems.at[1, part])
        for part in range(2)
    ]
    for load in loads:
        load.start()
    for load, store in zip(loads, stores):
        load.wait()
        store.start()
    for store in stores:
        store.wait()


def piece_of(slot, start, width, bands, after):
    points = bands.shape[3]
    return pl.pallas_call(
        functools.partial(piece_kernel, slot, start),
        in_specs=[pl.BlockSpec(memory_space=pl.ANY)] * (1 + len(after)),
        out_specs=pl.BlockSpec(memory_space=pl.ANY),
        scratch_shapes=[
            pltpu.VMEM((2, width, points), bands.dtype),
            pltpu.SemaphoreType.DMA((2, 2)),
        ],
        out_shape=jax.ShapeDtypeStruct((2, width, points), bands.dtype),
        compiler_params=pltpu.CompilerParams(vmem_limit_bytes=VMEM_BYTES),
        cost_estimate=pl.CostEstimate(flops=1000, bytes_accessed=1000, transcendentals=0),
        name="piece_of",
    )(bands, *after)


def near_into(near_buf, there_ref, table_ref, base, planes):
    width, points = there_ref.shape[1:]

    @pl.loop(0, width // STRIP)
    def _(strip):
        rows = pl.ds(strip * STRIP, STRIP)
        mirror = pl.ds(width + strip * STRIP, STRIP)
        for start in range(0, points, DEPTH):
            plane = start // PLANE
            cosine = table_ref[base + 1 + plane]
            sine = table_ref[base + 1 + planes + plane]
            columns = pl.ds(start, DEPTH)
            real_part = there_ref[0, rows, columns].astype(jnp.float32)
            imag_part = there_ref[1, rows, columns].astype(jnp.float32)
            near_re = real_part * cosine + imag_part * sine
            near_im = imag_part * cosine - real_part * sine
            near_buf[rows, columns] = near_re.astype(jnp.bfloat16)
            near_buf[mirror, columns] = near_im.astype(jnp.bfloat16)


def put_sum(sum_buf, lane, total):
    width = total.shape[1] // 2
    sum_buf[:, 0, lane : lane + width] = total[:, :width]
    sum_buf[:, 1, lane : lane + width] = total[:, width:]


def step_kernel(plan, table_ref, *refs):
    rows, k_dev, _, nbands = plan.shape
    fold, depth = plan.fold, plan.depth
    refs = list(refs)

    def take(count):
        taken = refs[:count]
        del refs[:count]
        return taken

    stride = (table_ref.shape[0] - 1) // k_dev
    planes = (stride - 1) // 2
    me = table_ref[k_dev * stride].astype(jnp.int32)
    place, outer = lax.rem(me, fold), lax.div(me, fold)
    if plan.part:
        bands_ref, phased_ref = take(2)
    sources = [take(count) for count in plan.takes]
    arrived = take(plan.adds)
    if plan.adding and plan.placed:
        take(1)
    given_ref, kept_ref = take(2) if plan.near == "give" else (None, None)
    outs = take(len(plan.ways))
    targets = [take(task.count) for task in plan.tasks]
    result_ref = take(1)[0] if plan.adding else None
    piece_ref = take(1)[0] if plan.later else None
    if plan.part:
        if plan.near != "use":
            own_buf, own_sems = take(2)
        slot, _, width = plan.part
        base = slot * stride
        point = table_ref[base].astype(jnp.int32)
        own = []
        loads_of = plan.ways + (0,) if plan.near == "give" else plan.ways
        for way, distance in enumerate(loads_of if plan.near != "use" else ()):
            target = lax.rem(place + distance, fold)
            rows_ref = own_buf.at[way] if way < len(plan.ways) else kept_ref
            own.append([])
            for part in range(2):
                for level in range(depth):
                    first = pl.multiple_of((level * fold + target) * rows, rows)
                    copy = pltpu.make_async_copy(
                        bands_ref.at[point, part, pl.ds(first, rows), :],
                        rows_ref.at[part, pl.ds(level * rows, rows), :],
                        own_sems.at[way, part, level],
                    )
                    copy.start()
                    own[way].append(copy)
    if plan.later:
        piece_buf, piece_sems = take(2)
        later_slot, later_start, later_width = plan.later
        loads = [
            pltpu.make_async_copy(
                bands_ref.at[later_slot, part, pl.ds(later_start, later_width), :],
                piece_buf.at[part],
                piece_sems.at[0, part],
            )
            for part in range(2)
        ]
        stores = [
            pltpu.make_async_copy(piece_buf.at[part], piece_ref.at[part], piece_sems.at[1, part])
            for part in range(2)
        ]
        for copy in loads:
            copy.start()
    if plan.adding:
        sum_buf, placed_sem = take(2)
        add_slot, add_start, pieces = plan.adding
        for start, span, terms in pieces:
            total = 0.0
            for index, column in terms:
                total += arrived[index][0, :, column : column + 2 * span].astype(jnp.float32)
            put_sum(sum_buf, start - add_start, total)
        add_point = table_ref[add_slot * stride].astype(jnp.int32)
        columns = pl.ds(add_start, sum_buf.shape[2])
        placing = pltpu.make_async_copy(
            sum_buf, result_ref.at[:, add_point, :, columns], placed_sem
        )
        placing.start()
    for task, arrays, outputs in zip(plan.tasks, sources, targets):
        groups = [arrays[i : i + task.each] for i in range(0, len(arrays), task.each)]
        bit = lax.rem(lax.div(outer, 1 << task.stage), 2)
        filled = [(out_ref, 0) for out_ref in outputs]
        if plan.joined and not task.direct:
            filled.append((targets[0][JOINT], 2 * plan.tasks[0].batch[0][2]))
        for index, (out_ref, shift) in enumerate(filled):
            for level in range(out_ref.shape[0]):
                if task.direct:
                    source = partner(outer, index)
                else:
                    source = 2 * level + (1 - bit if index else bit)
                column = shift
                for group in groups:
                    total = summed(group, source)
                    columns = slice(column, column + total.shape[1])
                    out_ref[level, :, columns] = total.astype(out_ref.dtype)
                    column += total.shape[1]
    if plan.part:
        near_ref = phased_ref
        if plan.near != "use":
            near_ref = given_ref if plan.near == "give" else take(1)[0]
            near_into(near_ref, phased_ref, table_ref, base, planes)
        dims = (((1,), (1,)), ((), ()))
        points = near_ref.shape[1]
        run = points // 2 if width <= SPLIT else points
        for way, out_ref in enumerate(outs):
            of_both = []
            for part in range(2):
                for copy in own[way][part * depth : (part + 1) * depth] if own else ():
                    copy.wait()
                rows_ref = bands_ref if plan.near == "use" else own_buf.at[way]
                products = [
                    lax.dot_general(
                        rows_ref[part, :, pl.ds(first, run)],
                        near_ref[:, pl.ds(first, run)],
                        dims,
                        preferred_element_type=jnp.float32,
                    )
                    for first in range(0, points, run)
                ]
                of_both.append(sum(products[1:], products[0]))
            of_re, of_im = of_both
            real_part = (of_re[:, :width] + of_im[:, width:]).astype(out_ref.dtype)
            imag_part = (of_re[:, width:] - of_im[:, :width]).astype(out_ref.dtype)
            for level in range(depth):
                lines = slice(level * rows, (level + 1) * rows)
                out_ref[level, :, :width] = real_part[lines]
                out_ref[level, :, width:] = imag_part[lines]
            if plan.near == "give" and way + 1 == len(outs):
                for copy in own[-1]:
                    copy.wait()
            if plan.later and way == 0:
                for load, store in zip(loads, stores):
                    load.wait()
                    store.start()
    if plan.adding:
        placing.wait()
    if plan.later:
        for store in stores:
            store.wait()


def partner(outer, distance):
    low, high = lax.rem(outer, 2), lax.rem(lax.div(outer, 2), 2)
    low = 1 - low if distance % 2 else low
    high = 1 - high if distance // 2 else high
    return outer - lax.rem(outer, 4) + 2 * high + low


def summed(arrays, level, columns=slice(None)):
    total = arrays[0][level, :, columns]
    for array in arrays[1:]:
        total = total + array[level, :, columns].astype(jnp.float32)
    return total


class Task(NamedTuple):
    batch: tuple
    stage: int
    direct: bool
    each: int
    count: int


class Plan(NamedTuple):
    shape: tuple
    fold: int
    depth: int
    part: tuple
    ways: tuple
    near: str
    tasks: tuple
    takes: tuple
    adding: tuple
    adds: int
    joined: bool
    placed: bool
    later: tuple


def step(plan, table, bands, phased, sources, arrived, result):
    rows, _, _, nbands = plan.shape
    fold, depth = plan.fold, plan.depth
    points = bands.shape[-1]
    vmem = pl.BlockSpec(memory_space=pltpu.VMEM)
    hbm = pl.BlockSpec(memory_space=pltpu.HBM)
    operands, in_specs = [table], [pl.BlockSpec(memory_space=pltpu.SMEM)]
    out_shape, out_specs, scratch, aliases = [], [], [], {}

    def kind(index):
        return jnp.bfloat16 if index else jnp.float32

    if plan.part:
        width = plan.part[2]
        operands += [bands, phased]
        in_specs += [vmem if plan.near == "use" else hbm, vmem]
        if plan.near == "give":
            out_shape.append(jax.ShapeDtypeStruct((2 * width, points), jnp.bfloat16))
            out_shape.append(jax.ShapeDtypeStruct((2, depth * rows, points), jnp.bfloat16))
        out_shape += [
            jax.ShapeDtypeStruct((depth, rows, 2 * width), kind(way)) for way in plan.ways
        ]
        if plan.near != "use":
            scratch += [
                pltpu.VMEM((len(plan.ways), 2, depth * rows, points), jnp.bfloat16),
                pltpu.SemaphoreType.DMA((fold, 2, depth)),
            ]
    for arrays in [*sources, arrived]:
        operands += arrays
        in_specs += [vmem] * len(arrays)
    for task in plan.tasks:
        wide = sum(2 * width for _, _, width in task.batch)
        levels = 1 if task.direct else depth >> (task.stage + 1)
        extra = 2 * plan.tasks[1].batch[0][2] if plan.joined and task.direct else 0
        for i in range(task.count):
            columns = wide + extra if i == JOINT else wide
            out_shape.append(jax.ShapeDtypeStruct((levels, rows, columns), kind(i)))
    out_specs += [vmem] * len(out_shape)
    if plan.later:
        scratch += [
            pltpu.VMEM((2, plan.later[2], points), bands.dtype),
            pltpu.SemaphoreType.DMA((2, 2)),
        ]
    if plan.adding:
        if plan.placed:
            aliases = {len(operands): len(out_shape)}
            operands.append(result)
            in_specs.append(hbm)
        out_shape.append(jax.ShapeDtypeStruct(plan.shape, jnp.float32))
        out_specs.append(hbm)
        lanes = sum(span for _, span, _ in plan.adding[2])
        scratch += [pltpu.VMEM((rows, 2, lanes), jnp.float32), pltpu.SemaphoreType.DMA]
    if plan.later:
        out_shape.append(jax.ShapeDtypeStruct((2, plan.later[2], points), bands.dtype))
        out_specs.append(hbm)
    if plan.near == "make":
        scratch.append(pltpu.VMEM((2 * width, points), jnp.bfloat16))
    outs = list(
        pl.pallas_call(
            functools.partial(step_kernel, plan),
            in_specs=in_specs,
            out_specs=out_specs,
            scratch_shapes=scratch,
            out_shape=out_shape,
            input_output_aliases=aliases,
            compiler_params=pltpu.CompilerParams(vmem_limit_bytes=VMEM_BYTES),
            cost_estimate=pl.CostEstimate(flops=1000, bytes_accessed=1000, transcendentals=0),
            name="step",
        )(*operands)
    )
    piece = outs.pop() if plan.later else None
    result = outs.pop() if plan.adding else result
    near = [outs.pop(0), outs.pop(0)] if plan.near == "give" else None
    terms = outs[: len(plan.ways)]
    handed = outs[len(plan.ways) :]
    sends = []
    for task in plan.tasks:
        sends.append(handed[: task.count])
        handed = handed[task.count :]
    return terms, near, sends, result, piece


def cuts(nbands, first):
    eighth = nbands // 8
    widths = [4 * eighth, 4 * eighth] if first else [3 * eighth, 3 * eighth, 2 * eighth]
    starts = [sum(widths[:i]) for i in range(len(widths))]
    return list(zip(starts, widths))


def schedule(parts, fold, depth):
    every, others = tuple(range(fold)), tuple(range(1, fold))
    count = len(parts)
    kernels = []
    waiting, halved, crossed = [], [], []
    for index, part in enumerate(parts):
        ready = ready_parts(waiting)
        waiting = waiting[len(ready) :]
        tasks = []
        if halved:
            tasks.append(Task(tuple(halved), 1, False, 2, 2))
        if crossed:
            tasks.append(Task(tuple(crossed), 0, False, fold, 2))
        waiting += halved
        if index >= count - 3:
            kernels.append((part, others, "give", tuple(tasks), ready))
            kernels.append((part, every[:1], "use", (), ()))
        else:
            kernels.append((part, every, "make", tuple(tasks), ready))
        halved, crossed = crossed, [part] if index < count - 1 else []
        if index in (0, count - 3):
            kernels.append((None, (), "", (Task((part,), 0, False, fold, 2),), ()))
            halved, crossed = halved + crossed, []
    tasks = (
        Task((parts[-1],), 0, True, fold, depth),
        Task(tuple(halved), 1, False, 2, 1),
    )
    kernels.append((None, (), "", tasks, ()))
    kernels.append((None, (), "", (), tuple(waiting) + tuple(halved) + (parts[-1],)))
    return kernels


def ready_parts(waiting):
    total = 0
    for count, (slot, _, width) in enumerate(waiting, 1):
        total += width
        if slot != waiting[0][0]:
            break
        if total % LANES == 0:
            return tuple(waiting[:count])
    return ()


def body(bands, nbr_slot, gshift):
    grid_index = lax.axis_index("ga")
    grid_count = lax.axis_size("ga")
    k_dev, _, nbands, points = bands.shape
    rows = nbands // grid_count
    own_planes = points // PLANE
    total_planes = own_planes * grid_count
    planes = grid_index * own_planes + jnp.arange(own_planes, dtype=jnp.int32)
    slots = jnp.arange(k_dev, dtype=jnp.int32)
    chosen = nbr_slot[None, :] == slots[:, None]
    order = jnp.sum(jnp.where(chosen, slots[None, :], 0), axis=1)
    shifts = jnp.sum(jnp.where(chosen, gshift[None, :], 0), axis=1)
    turns = (1 + NKB * shifts[:, None]) * planes[None, :] % (NKB * total_planes)
    angle = 2.0 * math.pi / (NKB * total_planes) * turns.astype(jnp.float32)
    columns = [order[:, None].astype(jnp.float32), jnp.cos(angle), jnp.sin(angle)]
    table = jnp.concatenate(columns, axis=1).reshape(-1)
    table = jnp.append(table, grid_index.astype(jnp.float32))
    parts = []
    for slot in range(k_dev):
        for start, width in cuts(nbands, slot == 0):
            parts.append((slot, start, width))
    theres = []
    piece = None
    for slot, start, width in parts[:AHEAD]:
        piece = piece_of(slot, start, width, bands, [] if piece is None else [piece])
        theres.append(shifted(piece, "ka", -1))
    shape = (rows, k_dev, 2, nbands)
    depth = min(OUTER, grid_count)
    fold = grid_count // depth
    held = {}
    near, result = None, None
    for part, ways, phase, tasks, adds in schedule(parts, fold, depth):
        place = parts.index(part) if part else len(parts)
        later = parts[place + AHEAD] if place + AHEAD < len(parts) and phase != "use" else None
        sources = [
            [array for done in task.batch for array, _ in held[(done,)]] for task in tasks
        ]
        arrived, pieces = [], []
        for done in adds:
            batch = max((key for key in held if done in key), key=len)
            column = sum(2 * width for _, _, width in batch[: batch.index(done)])
            terms = [(len(arrived) + i, first + column) for i, (_, first) in enumerate(held[batch])]
            arrived += [array for array, _ in held[batch]]
            pieces.append((done[1], done[2], tuple(terms)))
        adding = (adds[0][0], adds[0][1], tuple(pieces)) if adds else ()
        plan = Plan(
            shape,
            fold,
            depth,
            part,
            ways,
            phase,
            tasks,
            tuple(len(arrays) for arrays in sources),
            adding,
            len(arrived),
            len(tasks) > 1 and tasks[0].direct,
            result is not None,
            later,
        )
        phased, own = theres[place] if part else None, bands
        if phase == "use":
            phased, own = near
        terms, near, sends, result, piece = step(
            plan, table, own, phased, sources, arrived, result
        )
        if later:
            theres.append(shifted(piece, "ka", -1))
        for way, array in zip(ways, terms):
            array = shifted(array, "ga", way, fold, True) if way else array
            held.setdefault((part,), []).insert(0 if way == 0 else fold, (array, 0))
        for task, arrays in zip(tasks, sends):
            steps = range(1, depth) if task.direct else [1 << task.stage]
            held[task.batch] = [(arrays[0], 0)] + [
                (swapped(array, "ga", fold * i), 0) for array, i in zip(arrays[1:], steps)
            ]
        if plan.joined:
            joint = held[tasks[0].batch][JOINT][0]
            held[tasks[1].batch].append((joint, 2 * tasks[0].batch[0][2]))
    return result


def solution(mesh):
    placed = (P("ka", None, None, "ga"), P("ka"), P("ka"))
    return jax.shard_map(
        body, mesh=mesh, in_specs=placed, out_specs=P("ga", "ka", None, None), check_vma=False
    )
```

```python
import functools
import math
from typing import NamedTuple

import jax
import jax.numpy as jnp
from jax import lax
from jax.experimental import pallas as pl
from jax.experimental.pallas import tpu as pltpu
from jax.sharding import PartitionSpec as P

NKB = 4
PLANE = 1024
STRIP = 32
DEPTH = 512
AHEAD = 3
OUTER = 4
SPLIT = 128
JOINT = 2
CHUNKS = 4
LANES = 128
BLOCK = 256
VMEM_BYTES = 46 * 1024 * 1024


def shifted(block, axis, distance, fold=1, inner=False):
    count = lax.axis_size(axis)
    route = []
    for i in range(count):
        outer, place = divmod(i, fold)
        if inner:
            route.append((i, outer * fold + (place + distance) % fold))
        else:
            route.append((i, (outer + distance) % (count // fold) * fold + place))
    return lax.ppermute(block, axis, route)


def swapped(block, axis, distance):
    count = lax.axis_size(axis)
    return lax.ppermute(block, axis, [(i, i ^ distance) for i in range(count)])


def piece_kernel(slot, start, bands_ref, *rest):
    out_ref, piece_buf, sems = rest[-3:]
    width = piece_buf.shape[1] // CHUNKS
    loads, stores = [], []
    for index in range(2 * CHUNKS):
        part, chunk = divmod(index, CHUNKS)
        lines = pl.ds(chunk * width, width)
        source = bands_ref.at[slot, part, pl.ds(start + chunk * width, width), :]
        buf = piece_buf.at[part, lines, :]
        loads.append(pltpu.make_async_copy(source, buf, sems.at[0, index]))
        stores.append(pltpu.make_async_copy(buf, out_ref.at[part, lines, :], sems.at[1, index]))
    for load in loads:
        load.start()
    for load, store in zip(loads, stores):
        load.wait()
        store.start()
    for store in stores:
        store.wait()


def piece_of(slot, start, width, bands, after):
    points = bands.shape[3]
    return pl.pallas_call(
        functools.partial(piece_kernel, slot, start),
        in_specs=[pl.BlockSpec(memory_space=pl.ANY)] * (1 + len(after)),
        out_specs=pl.BlockSpec(memory_space=pl.ANY),
        scratch_shapes=[
            pltpu.VMEM((2, width, points), bands.dtype),
            pltpu.SemaphoreType.DMA((2, 2 * CHUNKS)),
        ],
        out_shape=jax.ShapeDtypeStruct((2, width, points), bands.dtype),
        compiler_params=pltpu.CompilerParams(vmem_limit_bytes=VMEM_BYTES),
        cost_estimate=pl.CostEstimate(flops=1000, bytes_accessed=1000, transcendentals=0),
        name="piece_of",
    )(bands, *after)


def near_into(near_buf, there_ref, table_ref, base, planes):
    width, points = there_ref.shape[1:]

    @pl.loop(0, width // STRIP)
    def _(strip):
        rows = pl.ds(strip * STRIP, STRIP)
        mirror = pl.ds(width + strip * STRIP, STRIP)
        for start in range(0, points, DEPTH):
            plane = start // PLANE
            cosine = table_ref[base + 1 + plane]
            sine = table_ref[base + 1 + planes + plane]
            columns = pl.ds(start, DEPTH)
            real_part = there_ref[0, rows, columns].astype(jnp.float32)
            imag_part = there_ref[1, rows, columns].astype(jnp.float32)
            near_re = real_part * cosine + imag_part * sine
            near_im = imag_part * cosine - real_part * sine
            near_buf[rows, columns] = near_re.astype(jnp.bfloat16)
            near_buf[mirror, columns] = near_im.astype(jnp.bfloat16)


def put_sum(sum_buf, lane, total):
    width = total.shape[1] // 2
    sum_buf[:, 0, lane : lane + width] = total[:, :width]
    sum_buf[:, 1, lane : lane + width] = total[:, width:]


def step_kernel(plan, table_ref, *refs):
    rows, k_dev, _, nbands = plan.shape
    fold, depth = plan.fold, plan.depth
    refs = list(refs)

    def take(count):
        taken = refs[:count]
        del refs[:count]
        return taken

    stride = (table_ref.shape[0] - 1) // k_dev
    planes = (stride - 1) // 2
    me = table_ref[k_dev * stride].astype(jnp.int32)
    place, outer = lax.rem(me, fold), lax.div(me, fold)
    if plan.part:
        bands_ref, phased_ref = take(2)
    sources = [take(count) for count in plan.takes]
    arrived = take(plan.adds)
    if plan.adding and plan.placed:
        take(1)
    given_ref, kept_ref = take(2) if plan.near == "give" else (None, None)
    outs = take(len(plan.ways))
    targets = [take(task.count) for task in plan.tasks]
    result_ref = take(1)[0] if plan.adding else None
    piece_ref = take(1)[0] if plan.later else None
    if plan.part:
        if plan.near != "use":
            own_buf, own_sems = take(2)
        slot, _, width = plan.part
        base = slot * stride
        point = table_ref[base].astype(jnp.int32)
        own = []
        loads_of = plan.ways + (0,) if plan.near == "give" else plan.ways
        for way, distance in enumerate(loads_of if plan.near != "use" else ()):
            target = lax.rem(place + distance, fold)
            rows_ref = own_buf.at[way] if way < len(plan.ways) else kept_ref
            own.append([])
            for part in range(2):
                for level in range(depth):
                    first = pl.multiple_of((level * fold + target) * rows, rows)
                    copy = pltpu.make_async_copy(
                        bands_ref.at[point, part, pl.ds(first, rows), :],
                        rows_ref.at[part, pl.ds(level * rows, rows), :],
                        own_sems.at[way, part, level],
                    )
                    copy.start()
                    own[way].append(copy)
    if plan.later:
        piece_buf, piece_sems = take(2)
        later_slot, later_start, later_width = plan.later
        loads = [
            pltpu.make_async_copy(
                bands_ref.at[later_slot, part, pl.ds(later_start, later_width), :],
                piece_buf.at[part],
                piece_sems.at[0, part],
            )
            for part in range(2)
        ]
        stores = [
            pltpu.make_async_copy(piece_buf.at[part], piece_ref.at[part], piece_sems.at[1, part])
            for part in range(2)
        ]
        for copy in loads:
            copy.start()
    if plan.adding:
        sum_buf, placed_sem = take(2)
        add_slot, add_start, pieces = plan.adding
        for start, span, terms in pieces:
            total = 0.0
            for index, column in terms:
                total += arrived[index][0, :, column : column + 2 * span].astype(jnp.float32)
            put_sum(sum_buf, start - add_start, total)
        add_point = table_ref[add_slot * stride].astype(jnp.int32)
        columns = pl.ds(add_start, sum_buf.shape[2])
        placing = pltpu.make_async_copy(
            sum_buf, result_ref.at[:, add_point, :, columns], placed_sem
        )
        placing.start()
    for task, arrays, outputs in zip(plan.tasks, sources, targets):
        groups = [arrays[i : i + task.each] for i in range(0, len(arrays), task.each)]
        bit = lax.rem(lax.div(outer, 1 << task.stage), 2)
        filled = [(out_ref, 0) for out_ref in outputs]
        if plan.joined and not task.direct:
            filled.append((targets[0][JOINT], 2 * plan.tasks[0].batch[0][2]))
        for index, (out_ref, shift) in enumerate(filled):
            for level in range(out_ref.shape[0]):
                if task.direct:
                    source = partner(outer, index)
                else:
                    source = 2 * level + (1 - bit if index else bit)
                column = shift
                for group in groups:
                    total = summed(group, source)
                    columns = slice(column, column + total.shape[1])
                    out_ref[level, :, columns] = total.astype(out_ref.dtype)
                    column += total.shape[1]
    if plan.part:
        near_ref = phased_ref
        if plan.near != "use":
            near_ref = given_ref if plan.near == "give" else take(1)[0]
            near_into(near_ref, phased_ref, table_ref, base, planes)
        dims = (((1,), (1,)), ((), ()))
        points = near_ref.shape[1]
        run = points // 2 if width <= SPLIT else points
        for way, out_ref in enumerate(outs):
            of_both = []
            for part in range(2):
                for copy in own[way][part * depth : (part + 1) * depth] if own else ():
                    copy.wait()
                rows_ref = bands_ref if plan.near == "use" else own_buf.at[way]
                products = [
                    lax.dot_general(
                        rows_ref[part, :, pl.ds(first, run)],
                        near_ref[:, pl.ds(first, run)],
                        dims,
                        preferred_element_type=jnp.float32,
                    )
                    for first in range(0, points, run)
                ]
                of_both.append(sum(products[1:], products[0]))
            of_re, of_im = of_both
            real_part = (of_re[:, :width] + of_im[:, width:]).astype(out_ref.dtype)
            imag_part = (of_re[:, width:] - of_im[:, :width]).astype(out_ref.dtype)
            for level in range(depth):
                lines = slice(level * rows, (level + 1) * rows)
                out_ref[level, :, :width] = real_part[lines]
                out_ref[level, :, width:] = imag_part[lines]
            if plan.near == "give" and way + 1 == len(outs):
                for copy in own[-1]:
                    copy.wait()
            if plan.later and way == 0:
                for load, store in zip(loads, stores):
                    load.wait()
                    store.start()
    if plan.adding:
        placing.wait()
    if plan.later:
        for store in stores:
            store.wait()


def partner(outer, distance):
    low, high = lax.rem(outer, 2), lax.rem(lax.div(outer, 2), 2)
    low = 1 - low if distance % 2 else low
    high = 1 - high if distance // 2 else high
    return outer - lax.rem(outer, 4) + 2 * high + low


def summed(arrays, level, columns=slice(None)):
    total = arrays[0][level, :, columns]
    for array in arrays[1:]:
        total = total + array[level, :, columns].astype(jnp.float32)
    return total


class Task(NamedTuple):
    batch: tuple
    stage: int
    direct: bool
    each: int
    count: int


class Plan(NamedTuple):
    shape: tuple
    fold: int
    depth: int
    part: tuple
    ways: tuple
    near: str
    tasks: tuple
    takes: tuple
    adding: tuple
    adds: int
    joined: bool
    placed: bool
    later: tuple


def step(plan, table, bands, phased, sources, arrived, result):
    rows, _, _, nbands = plan.shape
    fold, depth = plan.fold, plan.depth
    points = bands.shape[-1]
    vmem = pl.BlockSpec(memory_space=pltpu.VMEM)
    hbm = pl.BlockSpec(memory_space=pltpu.HBM)
    operands, in_specs = [table], [pl.BlockSpec(memory_space=pltpu.SMEM)]
    out_shape, out_specs, scratch, aliases = [], [], [], {}

    def kind(index):
        return jnp.bfloat16 if index else jnp.float32

    if plan.part:
        width = plan.part[2]
        operands += [bands, phased]
        in_specs += [vmem if plan.near == "use" else hbm, vmem]
        if plan.near == "give":
            out_shape.append(jax.ShapeDtypeStruct((2 * width, points), jnp.bfloat16))
            out_shape.append(jax.ShapeDtypeStruct((2, depth * rows, points), jnp.bfloat16))
        out_shape += [
            jax.ShapeDtypeStruct((depth, rows, 2 * width), kind(way)) for way in plan.ways
        ]
        if plan.near != "use":
            scratch += [
                pltpu.VMEM((len(plan.ways), 2, depth * rows, points), jnp.bfloat16),
                pltpu.SemaphoreType.DMA((fold, 2, depth)),
            ]
    for arrays in [*sources, arrived]:
        operands += arrays
        in_specs += [vmem] * len(arrays)
    for task in plan.tasks:
        wide = sum(2 * width for _, _, width in task.batch)
        levels = 1 if task.direct else depth >> (task.stage + 1)
        extra = 2 * plan.tasks[1].batch[0][2] if plan.joined and task.direct else 0
        for i in range(task.count):
            columns = wide + extra if i == JOINT else wide
            out_shape.append(jax.ShapeDtypeStruct((levels, rows, columns), kind(i)))
    out_specs += [vmem] * len(out_shape)
    if plan.later:
        scratch += [
            pltpu.VMEM((2, plan.later[2], points), bands.dtype),
            pltpu.SemaphoreType.DMA((2, 2)),
        ]
    if plan.adding:
        if plan.placed:
            aliases = {len(operands): len(out_shape)}
            operands.append(result)
            in_specs.append(hbm)
        out_shape.append(jax.ShapeDtypeStruct(plan.shape, jnp.float32))
        out_specs.append(hbm)
        lanes = sum(span for _, span, _ in plan.adding[2])
        scratch += [pltpu.VMEM((rows, 2, lanes), jnp.float32), pltpu.SemaphoreType.DMA]
    if plan.later:
        out_shape.append(jax.ShapeDtypeStruct((2, plan.later[2], points), bands.dtype))
        out_specs.append(hbm)
    if plan.near == "make":
        scratch.append(pltpu.VMEM((2 * width, points), jnp.bfloat16))
    outs = list(
        pl.pallas_call(
            functools.partial(step_kernel, plan),
            in_specs=in_specs,
            out_specs=out_specs,
            scratch_shapes=scratch,
            out_shape=out_shape,
            input_output_aliases=aliases,
            compiler_params=pltpu.CompilerParams(vmem_limit_bytes=VMEM_BYTES),
            cost_estimate=pl.CostEstimate(flops=1000, bytes_accessed=1000, transcendentals=0),
            name="step",
        )(*operands)
    )
    piece = outs.pop() if plan.later else None
    result = outs.pop() if plan.adding else result
    near = [outs.pop(0), outs.pop(0)] if plan.near == "give" else None
    terms = outs[: len(plan.ways)]
    handed = outs[len(plan.ways) :]
    sends = []
    for task in plan.tasks:
        sends.append(handed[: task.count])
        handed = handed[task.count :]
    return terms, near, sends, result, piece


def cuts(nbands, first):
    eighth = nbands // 8
    widths = [4 * eighth, 4 * eighth] if first else [3 * eighth, 3 * eighth, 2 * eighth]
    starts = [sum(widths[:i]) for i in range(len(widths))]
    return list(zip(starts, widths))


def schedule(parts, fold, depth):
    every, others = tuple(range(fold)), tuple(range(1, fold))
    count = len(parts)
    kernels = []
    waiting, halved, crossed = [], [], []
    for index, part in enumerate(parts):
        ready = ready_parts(waiting)
        waiting = waiting[len(ready) :]
        tasks = []
        if halved:
            tasks.append(Task(tuple(halved), 1, False, 2, 2))
        if crossed:
            tasks.append(Task(tuple(crossed), 0, False, fold, 2))
        waiting += halved
        if index >= count - 3:
            kernels.append((part, others, "give", tuple(tasks), ready))
            kernels.append((part, every[:1], "use", (), ()))
        else:
            kernels.append((part, every, "make", tuple(tasks), ready))
        halved, crossed = crossed, [part] if index < count - 1 else []
        if index in (0, count - 3):
            kernels.append((None, (), "", (Task((part,), 0, False, fold, 2),), ()))
            halved, crossed = halved + crossed, []
    tasks = (
        Task((parts[-1],), 0, True, fold, depth),
        Task(tuple(halved), 1, False, 2, 1),
    )
    kernels.append((None, (), "", tasks, ()))
    kernels.append((None, (), "", (), tuple(waiting) + tuple(halved) + (parts[-1],)))
    return kernels


def ready_parts(waiting):
    total = 0
    for count, (slot, _, width) in enumerate(waiting, 1):
        total += width
        if slot != waiting[0][0]:
            break
        if total % LANES == 0:
            return tuple(waiting[:count])
    return ()


def body(bands, nbr_slot, gshift):
    grid_index = lax.axis_index("ga")
    grid_count = lax.axis_size("ga")
    k_dev, _, nbands, points = bands.shape
    rows = nbands // grid_count
    own_planes = points // PLANE
    total_planes = own_planes * grid_count
    planes = grid_index * own_planes + jnp.arange(own_planes, dtype=jnp.int32)
    slots = jnp.arange(k_dev, dtype=jnp.int32)
    chosen = nbr_slot[None, :] == slots[:, None]
    order = jnp.sum(jnp.where(chosen, slots[None, :], 0), axis=1)
    shifts = jnp.sum(jnp.where(chosen, gshift[None, :], 0), axis=1)
    turns = (1 + NKB * shifts[:, None]) * planes[None, :] % (NKB * total_planes)
    angle = 2.0 * math.pi / (NKB * total_planes) * turns.astype(jnp.float32)
    columns = [order[:, None].astype(jnp.float32), jnp.cos(angle), jnp.sin(angle)]
    table = jnp.concatenate(columns, axis=1).reshape(-1)
    table = jnp.append(table, grid_index.astype(jnp.float32))
    parts = []
    for slot in range(k_dev):
        for start, width in cuts(nbands, slot == 0):
            parts.append((slot, start, width))
    theres = []
    piece = None
    for slot, start, width in parts[:AHEAD]:
        piece = piece_of(slot, start, width, bands, [] if piece is None else [piece])
        theres.append(shifted(piece, "ka", -1))
    shape = (rows, k_dev, 2, nbands)
    depth = min(OUTER, grid_count)
    fold = grid_count // depth
    held = {}
    near, result = None, None
    for part, ways, phase, tasks, adds in schedule(parts, fold, depth):
        place = parts.index(part) if part else len(parts)
        later = parts[place + AHEAD] if place + AHEAD < len(parts) and phase != "use" else None
        sources = [
            [array for done in task.batch for array, _ in held[(done,)]] for task in tasks
        ]
        arrived, pieces = [], []
        for done in adds:
            batch = max((key for key in held if done in key), key=len)
            column = sum(2 * width for _, _, width in batch[: batch.index(done)])
            terms = [(len(arrived) + i, first + column) for i, (_, first) in enumerate(held[batch])]
            arrived += [array for array, _ in held[batch]]
            pieces.append((done[1], done[2], tuple(terms)))
        adding = (adds[0][0], adds[0][1], tuple(pieces)) if adds else ()
        plan = Plan(
            shape,
            fold,
            depth,
            part,
            ways,
            phase,
            tasks,
            tuple(len(arrays) for arrays in sources),
            adding,
            len(arrived),
            len(tasks) > 1 and tasks[0].direct,
            result is not None,
            later,
        )
        phased, own = theres[place] if part else None, bands
        if phase == "use":
            phased, own = near
        terms, near, sends, result, piece = step(
            plan, table, own, phased, sources, arrived, result
        )
        if later:
            theres.append(shifted(piece, "ka", -1))
        for way, array in zip(ways, terms):
            array = shifted(array, "ga", way, fold, True) if way else array
            held.setdefault((part,), []).insert(0 if way == 0 else fold, (array, 0))
        for task, arrays in zip(tasks, sends):
            steps = range(1, depth) if task.direct else [1 << task.stage]
            moved = [swapped(array, "ga", fold * i) for array, i in zip(arrays[1:], steps)]
            held[task.batch] = [(array, 0) for array in [arrays[0], *reversed(moved)]]
        if plan.joined:
            joint = held[tasks[0].batch][JOINT][0]
            held[tasks[1].batch].append((joint, 2 * tasks[0].batch[0][2]))
    return result


def solution(mesh):
    placed = (P("ka", None, None, "ga"), P("ka"), P("ka"))
    return jax.shard_map(
        body, mesh=mesh, in_specs=placed, out_specs=P("ga", "ka", None, None), check_vma=False
    )
```

```python
import functools
import math
from typing import NamedTuple

import jax
import jax.numpy as jnp
from jax import lax
from jax.experimental import pallas as pl
from jax.experimental.pallas import tpu as pltpu
from jax.sharding import PartitionSpec as P

NKB = 4
PLANE = 1024
STRIP = 32
DEPTH = 512
AHEAD = 3
OUTER = 4
SPLIT = 128
JOINT = 2
CHUNKS = 4
LANES = 128
BLOCK = 256
VMEM_BYTES = 44 * 1024 * 1024
LEAN_BYTES = 32 * 1024 * 1024


def shifted(block, axis, distance, fold=1, inner=False):
    count = lax.axis_size(axis)
    route = []
    for i in range(count):
        outer, place = divmod(i, fold)
        if inner:
            route.append((i, outer * fold + (place + distance) % fold))
        else:
            route.append((i, (outer + distance) % (count // fold) * fold + place))
    return lax.ppermute(block, axis, route)


def swapped(block, axis, distance):
    count = lax.axis_size(axis)
    return lax.ppermute(block, axis, [(i, i ^ distance) for i in range(count)])


def piece_kernel(slot, start, bands_ref, *rest):
    out_ref, piece_buf, sems = rest[-3:]
    width = piece_buf.shape[1] // CHUNKS
    loads, stores = [], []
    for index in range(2 * CHUNKS):
        part, chunk = divmod(index, CHUNKS)
        lines = pl.ds(chunk * width, width)
        source = bands_ref.at[slot, part, pl.ds(start + chunk * width, width), :]
        buf = piece_buf.at[part, lines, :]
        loads.append(pltpu.make_async_copy(source, buf, sems.at[0, index]))
        stores.append(pltpu.make_async_copy(buf, out_ref.at[part, lines, :], sems.at[1, index]))
    for load in loads:
        load.start()
    for load, store in zip(loads, stores):
        load.wait()
        store.start()
    for store in stores:
        store.wait()


def piece_of(slot, start, width, bands, after):
    points = bands.shape[3]
    return pl.pallas_call(
        functools.partial(piece_kernel, slot, start),
        in_specs=[pl.BlockSpec(memory_space=pl.ANY)] * (1 + len(after)),
        out_specs=pl.BlockSpec(memory_space=pl.ANY),
        scratch_shapes=[
            pltpu.VMEM((2, width, points), bands.dtype),
            pltpu.SemaphoreType.DMA((2, 2 * CHUNKS)),
        ],
        out_shape=jax.ShapeDtypeStruct((2, width, points), bands.dtype),
        compiler_params=pltpu.CompilerParams(vmem_limit_bytes=VMEM_BYTES),
        cost_estimate=pl.CostEstimate(flops=1000, bytes_accessed=1000, transcendentals=0),
        name="piece_of",
    )(bands, *after)


def near_into(near_buf, there_ref, table_ref, base, planes):
    width, points = there_ref.shape[1:]

    @pl.loop(0, width // STRIP)
    def _(strip):
        rows = pl.ds(strip * STRIP, STRIP)
        mirror = pl.ds(width + strip * STRIP, STRIP)
        for start in range(0, points, DEPTH):
            plane = start // PLANE
            cosine = table_ref[base + 1 + plane]
            sine = table_ref[base + 1 + planes + plane]
            columns = pl.ds(start, DEPTH)
            real_part = there_ref[0, rows, columns].astype(jnp.float32)
            imag_part = there_ref[1, rows, columns].astype(jnp.float32)
            near_re = real_part * cosine + imag_part * sine
            near_im = imag_part * cosine - real_part * sine
            near_buf[rows, columns] = near_re.astype(jnp.bfloat16)
            near_buf[mirror, columns] = near_im.astype(jnp.bfloat16)


def put_sum(sum_buf, lane, total):
    width = total.shape[1] // 2
    sum_buf[:, 0, lane : lane + width] = total[:, :width]
    sum_buf[:, 1, lane : lane + width] = total[:, width:]


def step_kernel(plan, table_ref, *refs):
    rows, k_dev, _, nbands = plan.shape
    fold, depth = plan.fold, plan.depth
    refs = list(refs)

    def take(count):
        taken = refs[:count]
        del refs[:count]
        return taken

    stride = (table_ref.shape[0] - 1) // k_dev
    planes = (stride - 1) // 2
    me = table_ref[k_dev * stride].astype(jnp.int32)
    place, outer = lax.rem(me, fold), lax.div(me, fold)
    if plan.part:
        bands_ref, phased_ref = take(2)
    sources = [take(count) for count in plan.takes]
    arrived = take(plan.adds)
    if plan.adding and plan.placed:
        take(1)
    given_ref = take(1)[0] if plan.near == "give" else None
    kept_ref = take(1)[0] if plan.rows == "keep" else None
    outs = take(len(plan.ways))
    targets = [take(task.count) for task in plan.tasks]
    result_ref = take(1)[0] if plan.adding else None
    piece_ref = take(1)[0] if plan.later else None
    if plan.part:
        slot, _, width = plan.part
        base = slot * stride
        point = table_ref[base].astype(jnp.int32)
        own_ref = bands_ref
        own = []
        if plan.rows != "held":
            own_ref = take(1)[0] if plan.rows == "load" else kept_ref
            own_sems = take(1)[0]
            for distance in range(1, fold + 1):
                way = distance % fold
                target = lax.rem(place + way, fold)
                for part in range(2):
                    for level in range(depth):
                        first = pl.multiple_of((level * fold + target) * rows, rows)
                        copy = pltpu.make_async_copy(
                            bands_ref.at[point, part, pl.ds(first, rows), :],
                            own_ref.at[way, part, pl.ds(level * rows, rows), :],
                            own_sems.at[way, part, level],
                        )
                        copy.start()
                        own.append((way, part, copy))
    if plan.later:
        piece_buf, piece_sems = take(2)
        later_slot, later_start, later_width = plan.later
        loads = [
            pltpu.make_async_copy(
                bands_ref.at[later_slot, part, pl.ds(later_start, later_width), :],
                piece_buf.at[part],
                piece_sems.at[0, part],
            )
            for part in range(2)
        ]
        stores = [
            pltpu.make_async_copy(piece_buf.at[part], piece_ref.at[part], piece_sems.at[1, part])
            for part in range(2)
        ]
        for copy in loads:
            copy.start()
    if plan.adding:
        sum_buf, placed_sem = take(2)
        add_slot, add_start, pieces = plan.adding
        for start, span, terms in pieces:
            total = 0.0
            for index, column in terms:
                total += arrived[index][0, :, column : column + 2 * span].astype(jnp.float32)
            put_sum(sum_buf, start - add_start, total)
        add_point = table_ref[add_slot * stride].astype(jnp.int32)
        columns = pl.ds(add_start, sum_buf.shape[2])
        placing = pltpu.make_async_copy(
            sum_buf, result_ref.at[:, add_point, :, columns], placed_sem
        )
        placing.start()
    for task, arrays, outputs in zip(plan.tasks, sources, targets):
        groups = [arrays[i : i + task.each] for i in range(0, len(arrays), task.each)]
        bit = lax.rem(lax.div(outer, 1 << task.stage), 2)
        filled = [(out_ref, 0) for out_ref in outputs]
        if plan.joined and not task.direct:
            filled.append((targets[0][JOINT], 2 * plan.tasks[0].batch[0][2]))
        for index, (out_ref, shift) in enumerate(filled):
            for level in range(out_ref.shape[0]):
                if task.direct:
                    source = partner(outer, index)
                else:
                    source = 2 * level + (1 - bit if index else bit)
                column = shift
                for group in groups:
                    total = summed(group, source)
                    columns = slice(column, column + total.shape[1])
                    out_ref[level, :, columns] = total.astype(out_ref.dtype)
                    column += total.shape[1]
    if plan.part:
        near_ref = phased_ref
        if plan.near != "use":
            near_ref = given_ref if plan.near == "give" else take(1)[0]
            near_into(near_ref, phased_ref, table_ref, base, planes)
        dims = (((1,), (1,)), ((), ()))
        points = near_ref.shape[1]
        run = points // 2 if width <= SPLIT else points
        for way, out_ref in zip(plan.ways, outs):
            of_both = []
            for part in range(2):
                for copy in [copy for *which, copy in own if which == [way, part]]:
                    copy.wait()
                products = [
                    lax.dot_general(
                        own_ref[way, part, :, pl.ds(first, run)],
                        near_ref[:, pl.ds(first, run)],
                        dims,
                        preferred_element_type=jnp.float32,
                    )
                    for first in range(0, points, run)
                ]
                of_both.append(sum(products[1:], products[0]))
            of_re, of_im = of_both
            real_part = (of_re[:, :width] + of_im[:, width:]).astype(out_ref.dtype)
            imag_part = (of_re[:, width:] - of_im[:, :width]).astype(out_ref.dtype)
            for level in range(depth):
                lines = slice(level * rows, (level + 1) * rows)
                out_ref[level, :, :width] = real_part[lines]
                out_ref[level, :, width:] = imag_part[lines]
            if plan.later and way == plan.ways[0]:
                for load, store in zip(loads, stores):
                    load.wait()
                    store.start()
        for way, _, copy in own:
            if way not in plan.ways:
                copy.wait()
    if plan.adding:
        placing.wait()
    if plan.later:
        for store in stores:
            store.wait()


def partner(outer, distance):
    low, high = lax.rem(outer, 2), lax.rem(lax.div(outer, 2), 2)
    low = 1 - low if distance % 2 else low
    high = 1 - high if distance // 2 else high
    return outer - lax.rem(outer, 4) + 2 * high + low


def summed(arrays, level, columns=slice(None)):
    total = arrays[0][level, :, columns]
    for array in arrays[1:]:
        total = total + array[level, :, columns].astype(jnp.float32)
    return total


class Task(NamedTuple):
    batch: tuple
    stage: int
    direct: bool
    each: int
    count: int


class Plan(NamedTuple):
    shape: tuple
    fold: int
    depth: int
    part: tuple
    ways: tuple
    near: str
    rows: str
    tasks: tuple
    takes: tuple
    adding: tuple
    adds: int
    joined: bool
    placed: bool
    later: tuple


def step(plan, table, bands, phased, sources, arrived, result):
    rows, _, _, nbands = plan.shape
    fold, depth = plan.fold, plan.depth
    points = bands.shape[-1]
    vmem = pl.BlockSpec(memory_space=pltpu.VMEM)
    hbm = pl.BlockSpec(memory_space=pltpu.HBM)
    operands, in_specs = [table], [pl.BlockSpec(memory_space=pltpu.SMEM)]
    out_shape, out_specs, scratch, aliases = [], [], [], {}

    def kind(index):
        return jnp.bfloat16 if index else jnp.float32

    if plan.part:
        width = plan.part[2]
        operands += [bands, phased]
        in_specs += [vmem if plan.rows == "held" else hbm, vmem]
        kept = (fold, 2, depth * rows, points)
        if plan.near == "give":
            out_shape.append(jax.ShapeDtypeStruct((2 * width, points), jnp.bfloat16))
        if plan.rows == "keep":
            out_shape.append(jax.ShapeDtypeStruct(kept, jnp.bfloat16))
        out_shape += [
            jax.ShapeDtypeStruct((depth, rows, 2 * width), kind(way)) for way in plan.ways
        ]
        if plan.rows == "load":
            scratch.append(pltpu.VMEM(kept, jnp.bfloat16))
        if plan.rows != "held":
            scratch.append(pltpu.SemaphoreType.DMA((fold, 2, depth)))
    for arrays in [*sources, arrived]:
        operands += arrays
        in_specs += [vmem] * len(arrays)
    for task in plan.tasks:
        wide = sum(2 * width for _, _, width in task.batch)
        levels = 1 if task.direct else depth >> (task.stage + 1)
        extra = 2 * plan.tasks[1].batch[0][2] if plan.joined and task.direct else 0
        for i in range(task.count):
            columns = wide + extra if i == JOINT else wide
            out_shape.append(jax.ShapeDtypeStruct((levels, rows, columns), kind(i)))
    out_specs += [vmem] * len(out_shape)
    if plan.later:
        scratch += [
            pltpu.VMEM((2, plan.later[2], points), bands.dtype),
            pltpu.SemaphoreType.DMA((2, 2)),
        ]
    if plan.adding:
        if plan.placed:
            aliases = {len(operands): len(out_shape)}
            operands.append(result)
            in_specs.append(hbm)
        out_shape.append(jax.ShapeDtypeStruct(plan.shape, jnp.float32))
        out_specs.append(hbm)
        lanes = sum(span for _, span, _ in plan.adding[2])
        scratch += [pltpu.VMEM((rows, 2, lanes), jnp.float32), pltpu.SemaphoreType.DMA]
    if plan.later:
        out_shape.append(jax.ShapeDtypeStruct((2, plan.later[2], points), bands.dtype))
        out_specs.append(hbm)
    if plan.near == "make":
        scratch.append(pltpu.VMEM((2 * width, points), jnp.bfloat16))
    outs = list(
        pl.pallas_call(
            functools.partial(step_kernel, plan),
            in_specs=in_specs,
            out_specs=out_specs,
            scratch_shapes=scratch,
            out_shape=out_shape,
            input_output_aliases=aliases,
            compiler_params=pltpu.CompilerParams(
                vmem_limit_bytes=VMEM_BYTES if plan.part and plan.rows != "held" else LEAN_BYTES
            ),
            cost_estimate=pl.CostEstimate(flops=1000, bytes_accessed=1000, transcendentals=0),
            name="step",
        )(*operands)
    )
    piece = outs.pop() if plan.later else None
    result = outs.pop() if plan.adding else result
    near = outs.pop(0) if plan.near == "give" else None
    kept = outs.pop(0) if plan.rows == "keep" else None
    terms = outs[: len(plan.ways)]
    handed = outs[len(plan.ways) :]
    sends = []
    for task in plan.tasks:
        sends.append(handed[: task.count])
        handed = handed[task.count :]
    return terms, near, kept, sends, result, piece


def cuts(nbands, first):
    eighth = nbands // 8
    widths = [4 * eighth, 4 * eighth] if first else [3 * eighth, 3 * eighth, 2 * eighth]
    starts = [sum(widths[:i]) for i in range(len(widths))]
    return list(zip(starts, widths))


def schedule(parts, fold, depth):
    every, others = tuple(range(fold)), tuple(range(1, fold))
    count = len(parts)
    kernels = []
    waiting, halved, crossed = [], [], []
    for index, part in enumerate(parts):
        ready = ready_parts(waiting)
        waiting = waiting[len(ready) :]
        tasks = []
        if halved:
            tasks.append(Task(tuple(halved), 1, False, 2, 2))
        if crossed:
            tasks.append(Task(tuple(crossed), 0, False, fold, 2))
        waiting += halved
        if index >= count - 3:
            kernels.append((part, others, "give", tuple(tasks), ready))
            kernels.append((part, every[:1], "use", (), ()))
        else:
            kernels.append((part, every, "make", tuple(tasks), ready))
        halved, crossed = crossed, [part] if index < count - 1 else []
        if index in (0, count - 3):
            kernels.append((None, (), "", (Task((part,), 0, False, fold, 2),), ()))
            halved, crossed = halved + crossed, []
    tasks = (
        Task((parts[-1],), 0, True, fold, depth),
        Task(tuple(halved), 1, False, 2, 1),
    )
    kernels.append((None, (), "", tasks, ()))
    kernels.append((None, (), "", (), tuple(waiting) + tuple(halved) + (parts[-1],)))
    return kernels


def ready_parts(waiting):
    total = 0
    for count, (slot, _, width) in enumerate(waiting, 1):
        total += width
        if slot != waiting[0][0]:
            break
        if total % LANES == 0:
            return tuple(waiting[:count])
    return ()


def body(bands, nbr_slot, gshift):
    grid_index = lax.axis_index("ga")
    grid_count = lax.axis_size("ga")
    k_dev, _, nbands, points = bands.shape
    rows = nbands // grid_count
    own_planes = points // PLANE
    total_planes = own_planes * grid_count
    planes = grid_index * own_planes + jnp.arange(own_planes, dtype=jnp.int32)
    slots = jnp.arange(k_dev, dtype=jnp.int32)
    chosen = nbr_slot[None, :] == slots[:, None]
    order = jnp.sum(jnp.where(chosen, slots[None, :], 0), axis=1)
    shifts = jnp.sum(jnp.where(chosen, gshift[None, :], 0), axis=1)
    turns = (1 + NKB * shifts[:, None]) * planes[None, :] % (NKB * total_planes)
    angle = 2.0 * math.pi / (NKB * total_planes) * turns.astype(jnp.float32)
    columns = [order[:, None].astype(jnp.float32), jnp.cos(angle), jnp.sin(angle)]
    table = jnp.concatenate(columns, axis=1).reshape(-1)
    table = jnp.append(table, grid_index.astype(jnp.float32))
    parts = []
    for slot in range(k_dev):
        for start, width in cuts(nbands, slot == 0):
            parts.append((slot, start, width))
    theres = []
    piece = None
    for slot, start, width in parts[:AHEAD]:
        piece = piece_of(slot, start, width, bands, [] if piece is None else [piece])
        theres.append(shifted(piece, "ka", -1))
    shape = (rows, k_dev, 2, nbands)
    depth = min(OUTER, grid_count)
    fold = grid_count // depth
    held = {}
    near, kept, result = None, None, None
    for part, ways, phase, tasks, adds in schedule(parts, fold, depth):
        place = parts.index(part) if part else len(parts)
        later = parts[place + AHEAD] if place + AHEAD < len(parts) and phase != "use" else None
        sources = [
            [array for done in task.batch for array, _ in held[(done,)]] for task in tasks
        ]
        arrived, pieces = [], []
        for done in adds:
            batch = max((key for key in held if done in key), key=len)
            column = sum(2 * width for _, _, width in batch[: batch.index(done)])
            terms = [(len(arrived) + i, first + column) for i, (_, first) in enumerate(held[batch])]
            arrived += [array for array, _ in held[batch]]
            pieces.append((done[1], done[2], tuple(terms)))
        adding = (adds[0][0], adds[0][1], tuple(pieces)) if adds else ()
        plan = Plan(
            shape,
            fold,
            depth,
            part,
            ways,
            phase,
            "held" if kept is not None else "keep" if phase == "give" else "load",
            tasks,
            tuple(len(arrays) for arrays in sources),
            adding,
            len(arrived),
            len(tasks) > 1 and tasks[0].direct,
            result is not None,
            later,
        )
        phased = near if phase == "use" else theres[place] if part else None
        terms, near, found, sends, result, piece = step(
            plan,
            table,
            bands if kept is None else kept,
            phased,
            sources,
            arrived,
            result,
        )
        kept = found if kept is None else kept
        if later:
            theres.append(shifted(piece, "ka", -1))
        for way, array in zip(ways, terms):
            array = shifted(array, "ga", way, fold, True) if way else array
            held.setdefault((part,), []).insert(0 if way == 0 else fold, (array, 0))
        for task, arrays in zip(tasks, sends):
            steps = range(1, depth) if task.direct else [1 << task.stage]
            moved = [swapped(array, "ga", fold * i) for array, i in zip(arrays[1:], steps)]
            held[task.batch] = [(array, 0) for array in [arrays[0], *reversed(moved)]]
        if plan.joined:
            joint = held[tasks[0].batch][JOINT][0]
            held[tasks[1].batch].append((joint, 2 * tasks[0].batch[0][2]))
    return result


def solution(mesh):
    placed = (P("ka", None, None, "ga"), P("ka"), P("ka"))
    return jax.shard_map(
        body, mesh=mesh, in_specs=placed, out_specs=P("ga", "ka", None, None), check_vma=False
    )
```

```python
import functools
import math
from typing import NamedTuple

import jax
import jax.numpy as jnp
from jax import lax
from jax.experimental import pallas as pl
from jax.experimental.pallas import tpu as pltpu
from jax.sharding import PartitionSpec as P

NKB = 4
PLANE = 1024
STRIP = 32
DEPTH = 512
AHEAD = 3
OUTER = 4
SPLIT = 128
JOINT = 2
LANES = 128
BLOCK = 256
VMEM_BYTES = 44 * 1024 * 1024
LEAN_BYTES = 32 * 1024 * 1024


def shifted(block, axis, distance, fold=1, inner=False):
    count = lax.axis_size(axis)
    route = []
    for i in range(count):
        outer, place = divmod(i, fold)
        if inner:
            route.append((i, outer * fold + (place + distance) % fold))
        else:
            route.append((i, (outer + distance) % (count // fold) * fold + place))
    return lax.ppermute(block, axis, route)


def swapped(block, axis, distance):
    count = lax.axis_size(axis)
    return lax.ppermute(block, axis, [(i, i ^ distance) for i in range(count)])


def first_kernel(slot, start, bands_ref, out_ref, sems):
    width = out_ref.shape[1]
    loads = [
        pltpu.make_async_copy(
            bands_ref.at[slot, part, pl.ds(start, width), :], out_ref.at[part], sems.at[part]
        )
        for part in range(2)
    ]
    for load in loads:
        load.start()
    for load in loads:
        load.wait()


def piece_kernel(slot, start, bands_ref, *rest):
    out_ref, piece_buf, sems = rest[-3:]
    width = piece_buf.shape[1]
    rows = pl.ds(start, width)
    loads = [
        pltpu.make_async_copy(bands_ref.at[slot, part, rows, :], piece_buf.at[part], sems.at[0, part])
        for part in range(2)
    ]
    stores = [
        pltpu.make_async_copy(piece_buf.at[part], out_ref.at[part], sems.at[1, part])
        for part in range(2)
    ]
    for load in loads:
        load.start()
    for load, store in zip(loads, stores):
        load.wait()
        store.start()
    for store in stores:
        store.wait()


def piece_of(slot, start, width, bands, after):
    points = bands.shape[3]
    hbm = pl.BlockSpec(memory_space=pltpu.HBM)
    scratch = [pltpu.VMEM((2, width, points), bands.dtype), pltpu.SemaphoreType.DMA((2, 2))]
    return pl.pallas_call(
        functools.partial(piece_kernel if after else first_kernel, slot, start),
        in_specs=[hbm] * (1 + len(after)),
        out_specs=hbm if after else pl.BlockSpec(memory_space=pltpu.VMEM),
        scratch_shapes=scratch if after else [pltpu.SemaphoreType.DMA((2,))],
        out_shape=jax.ShapeDtypeStruct((2, width, points), bands.dtype),
        compiler_params=pltpu.CompilerParams(vmem_limit_bytes=VMEM_BYTES),
        cost_estimate=pl.CostEstimate(flops=1000, bytes_accessed=1000, transcendentals=0),
        name="piece_of",
    )(bands, *after)


def near_into(near_buf, there_ref, table_ref, base, planes):
    width, points = there_ref.shape[1:]

    @pl.loop(0, width // STRIP)
    def _(strip):
        rows = pl.ds(strip * STRIP, STRIP)
        mirror = pl.ds(width + strip * STRIP, STRIP)
        for start in range(0, points, DEPTH):
            plane = start // PLANE
            cosine = table_ref[base + 1 + plane]
            sine = table_ref[base + 1 + planes + plane]
            columns = pl.ds(start, DEPTH)
            real_part = there_ref[0, rows, columns].astype(jnp.float32)
            imag_part = there_ref[1, rows, columns].astype(jnp.float32)
            near_re = real_part * cosine + imag_part * sine
            near_im = imag_part * cosine - real_part * sine
            near_buf[rows, columns] = near_re.astype(jnp.bfloat16)
            near_buf[mirror, columns] = near_im.astype(jnp.bfloat16)


def put_sum(sum_buf, lane, total):
    width = total.shape[1] // 2
    sum_buf[:, 0, lane : lane + width] = total[:, :width]
    sum_buf[:, 1, lane : lane + width] = total[:, width:]


def step_kernel(plan, table_ref, *refs):
    rows, k_dev, _, nbands = plan.shape
    fold, depth = plan.fold, plan.depth
    refs = list(refs)

    def take(count):
        taken = refs[:count]
        del refs[:count]
        return taken

    stride = (table_ref.shape[0] - 1) // k_dev
    planes = (stride - 1) // 2
    me = table_ref[k_dev * stride].astype(jnp.int32)
    place, outer = lax.rem(me, fold), lax.div(me, fold)
    if plan.part:
        bands_ref, phased_ref = take(2)
    sources = [take(count) for count in plan.takes]
    arrived = take(plan.adds)
    if plan.adding and plan.placed:
        take(1)
    given_ref = take(1)[0] if plan.near == "give" else None
    kept_ref = take(1)[0] if plan.rows == "keep" else None
    outs = take(len(plan.ways))
    targets = [take(task.count) for task in plan.tasks]
    result_ref = take(1)[0] if plan.adding else None
    piece_ref = take(1)[0] if plan.later else None
    if plan.part:
        slot, _, width = plan.part
        base = slot * stride
        point = table_ref[base].astype(jnp.int32)
        own_ref = bands_ref
        own = []
        if plan.rows != "held":
            own_ref = take(1)[0] if plan.rows == "load" else kept_ref
            own_sems = take(1)[0]
            for distance in range(1, fold + 1):
                way = distance % fold
                target = lax.rem(place + way, fold)
                for part in range(2):
                    for level in range(depth):
                        first = pl.multiple_of((level * fold + target) * rows, rows)
                        copy = pltpu.make_async_copy(
                            bands_ref.at[point, part, pl.ds(first, rows), :],
                            own_ref.at[way, part, pl.ds(level * rows, rows), :],
                            own_sems.at[way, part, level],
                        )
                        copy.start()
                        own.append((way, part, copy))
    if plan.later:
        piece_buf, piece_sems = take(2)
        later_slot, later_start, later_width = plan.later
        loads = [
            pltpu.make_async_copy(
                bands_ref.at[later_slot, part, pl.ds(later_start, later_width), :],
                piece_buf.at[part],
                piece_sems.at[0, part],
            )
            for part in range(2)
        ]
        stores = [
            pltpu.make_async_copy(piece_buf.at[part], piece_ref.at[part], piece_sems.at[1, part])
            for part in range(2)
        ]
        for copy in loads:
            copy.start()
    if plan.adding:
        sum_buf, placed_sem = take(2)
        add_slot, add_start, pieces = plan.adding
        for start, span, terms in pieces:
            total = 0.0
            for index, column in terms:
                total += arrived[index][0, :, column : column + 2 * span].astype(jnp.float32)
            put_sum(sum_buf, start - add_start, total)
        add_point = table_ref[add_slot * stride].astype(jnp.int32)
        columns = pl.ds(add_start, sum_buf.shape[2])
        placing = pltpu.make_async_copy(
            sum_buf, result_ref.at[:, add_point, :, columns], placed_sem
        )
        placing.start()
    for task, arrays, outputs in zip(plan.tasks, sources, targets):
        groups = [arrays[i : i + task.each] for i in range(0, len(arrays), task.each)]
        bit = lax.rem(lax.div(outer, 1 << task.stage), 2)
        filled = [(out_ref, 0) for out_ref in outputs]
        if plan.joined and not task.direct:
            filled.append((targets[0][JOINT], 2 * plan.tasks[0].batch[0][2]))
        for index, (out_ref, shift) in enumerate(filled):
            for level in range(out_ref.shape[0]):
                if task.direct:
                    source = partner(outer, index)
                else:
                    source = 2 * level + (1 - bit if index else bit)
                column = shift
                for group in groups:
                    total = summed(group, source)
                    columns = slice(column, column + total.shape[1])
                    out_ref[level, :, columns] = total.astype(out_ref.dtype)
                    column += total.shape[1]
    if plan.part:
        near_ref = phased_ref
        if plan.near != "use":
            near_ref = given_ref if plan.near == "give" else take(1)[0]
            near_into(near_ref, phased_ref, table_ref, base, planes)
        dims = (((1,), (1,)), ((), ()))
        points = near_ref.shape[1]
        run = points // 2 if width <= SPLIT else points
        for way, out_ref in zip(plan.ways, outs):
            of_both = []
            for part in range(2):
                for copy in [copy for *which, copy in own if which == [way, part]]:
                    copy.wait()
                products = [
                    lax.dot_general(
                        own_ref[way, part, :, pl.ds(first, run)],
                        near_ref[:, pl.ds(first, run)],
                        dims,
                        preferred_element_type=jnp.float32,
                    )
                    for first in range(0, points, run)
                ]
                of_both.append(sum(products[1:], products[0]))
            of_re, of_im = of_both
            real_part = (of_re[:, :width] + of_im[:, width:]).astype(out_ref.dtype)
            imag_part = (of_re[:, width:] - of_im[:, :width]).astype(out_ref.dtype)
            for level in range(depth):
                lines = slice(level * rows, (level + 1) * rows)
                out_ref[level, :, :width] = real_part[lines]
                out_ref[level, :, width:] = imag_part[lines]
            if plan.later and way == plan.ways[0]:
                for load, store in zip(loads, stores):
                    load.wait()
                    store.start()
        for way, _, copy in own:
            if way not in plan.ways:
                copy.wait()
    if plan.adding:
        placing.wait()
    if plan.later:
        for store in stores:
            store.wait()


def partner(outer, distance):
    low, high = lax.rem(outer, 2), lax.rem(lax.div(outer, 2), 2)
    low = 1 - low if distance % 2 else low
    high = 1 - high if distance // 2 else high
    return outer - lax.rem(outer, 4) + 2 * high + low


def summed(arrays, level, columns=slice(None)):
    total = arrays[0][level, :, columns]
    for array in arrays[1:]:
        total = total + array[level, :, columns].astype(jnp.float32)
    return total


class Task(NamedTuple):
    batch: tuple
    stage: int
    direct: bool
    each: int
    count: int


class Plan(NamedTuple):
    shape: tuple
    fold: int
    depth: int
    part: tuple
    ways: tuple
    near: str
    rows: str
    tasks: tuple
    takes: tuple
    adding: tuple
    adds: int
    joined: bool
    placed: bool
    later: tuple


def step(plan, table, bands, phased, sources, arrived, result):
    rows, _, _, nbands = plan.shape
    fold, depth = plan.fold, plan.depth
    points = bands.shape[-1]
    vmem = pl.BlockSpec(memory_space=pltpu.VMEM)
    hbm = pl.BlockSpec(memory_space=pltpu.HBM)
    operands, in_specs = [table], [pl.BlockSpec(memory_space=pltpu.SMEM)]
    out_shape, out_specs, scratch, aliases = [], [], [], {}

    def kind(index):
        return jnp.bfloat16 if index else jnp.float32

    if plan.part:
        width = plan.part[2]
        operands += [bands, phased]
        in_specs += [vmem if plan.rows == "held" else hbm, vmem]
        kept = (fold, 2, depth * rows, points)
        if plan.near == "give":
            out_shape.append(jax.ShapeDtypeStruct((2 * width, points), jnp.bfloat16))
        if plan.rows == "keep":
            out_shape.append(jax.ShapeDtypeStruct(kept, jnp.bfloat16))
        out_shape += [
            jax.ShapeDtypeStruct((depth, rows, 2 * width), kind(way)) for way in plan.ways
        ]
        if plan.rows == "load":
            scratch.append(pltpu.VMEM(kept, jnp.bfloat16))
        if plan.rows != "held":
            scratch.append(pltpu.SemaphoreType.DMA((fold, 2, depth)))
    for arrays in [*sources, arrived]:
        operands += arrays
        in_specs += [vmem] * len(arrays)
    for task in plan.tasks:
        wide = sum(2 * width for _, _, width in task.batch)
        levels = 1 if task.direct else depth >> (task.stage + 1)
        extra = 2 * plan.tasks[1].batch[0][2] if plan.joined and task.direct else 0
        for i in range(task.count):
            columns = wide + extra if i == JOINT else wide
            out_shape.append(jax.ShapeDtypeStruct((levels, rows, columns), kind(i)))
    out_specs += [vmem] * len(out_shape)
    if plan.later:
        scratch += [
            pltpu.VMEM((2, plan.later[2], points), bands.dtype),
            pltpu.SemaphoreType.DMA((2, 2)),
        ]
    if plan.adding:
        if plan.placed:
            aliases = {len(operands): len(out_shape)}
            operands.append(result)
            in_specs.append(hbm)
        out_shape.append(jax.ShapeDtypeStruct(plan.shape, jnp.float32))
        out_specs.append(hbm)
        lanes = sum(span for _, span, _ in plan.adding[2])
        scratch += [pltpu.VMEM((rows, 2, lanes), jnp.float32), pltpu.SemaphoreType.DMA]
    if plan.later:
        out_shape.append(jax.ShapeDtypeStruct((2, plan.later[2], points), bands.dtype))
        out_specs.append(hbm)
    if plan.near == "make":
        scratch.append(pltpu.VMEM((2 * width, points), jnp.bfloat16))
    outs = list(
        pl.pallas_call(
            functools.partial(step_kernel, plan),
            in_specs=in_specs,
            out_specs=out_specs,
            scratch_shapes=scratch,
            out_shape=out_shape,
            input_output_aliases=aliases,
            compiler_params=pltpu.CompilerParams(
                vmem_limit_bytes=VMEM_BYTES if plan.part and plan.rows != "held" else LEAN_BYTES
            ),
            cost_estimate=pl.CostEstimate(flops=1000, bytes_accessed=1000, transcendentals=0),
            name="step",
        )(*operands)
    )
    piece = outs.pop() if plan.later else None
    result = outs.pop() if plan.adding else result
    near = outs.pop(0) if plan.near == "give" else None
    kept = outs.pop(0) if plan.rows == "keep" else None
    terms = outs[: len(plan.ways)]
    handed = outs[len(plan.ways) :]
    sends = []
    for task in plan.tasks:
        sends.append(handed[: task.count])
        handed = handed[task.count :]
    return terms, near, kept, sends, result, piece


def cuts(nbands, first):
    eighth = nbands // 8
    widths = [4 * eighth, 4 * eighth] if first else [3 * eighth, 3 * eighth, 2 * eighth]
    starts = [sum(widths[:i]) for i in range(len(widths))]
    return list(zip(starts, widths))


def schedule(parts, fold, depth):
    every, others = tuple(range(fold)), tuple(range(1, fold))
    count = len(parts)
    kernels = []
    waiting, halved, crossed = [], [], []
    for index, part in enumerate(parts):
        ready = ready_parts(waiting)
        waiting = waiting[len(ready) :]
        tasks = []
        if halved:
            tasks.append(Task(tuple(halved), 1, False, 2, 2))
        if crossed:
            tasks.append(Task(tuple(crossed), 0, False, fold, 2))
        waiting += halved
        if index >= count - 3:
            kernels.append((part, others, "give", tuple(tasks), ready))
            kernels.append((part, every[:1], "use", (), ()))
        else:
            kernels.append((part, every, "make", tuple(tasks), ready))
        halved, crossed = crossed, [part] if index < count - 1 else []
        if index in (0, count - 3):
            kernels.append((None, (), "", (Task((part,), 0, False, fold, 2),), ()))
            halved, crossed = halved + crossed, []
    tasks = (
        Task((parts[-1],), 0, True, fold, depth),
        Task(tuple(halved), 1, False, 2, 1),
    )
    kernels.append((None, (), "", tasks, ()))
    kernels.append((None, (), "", (), tuple(waiting) + tuple(halved) + (parts[-1],)))
    return kernels


def ready_parts(waiting):
    total = 0
    for count, (slot, _, width) in enumerate(waiting, 1):
        total += width
        if slot != waiting[0][0]:
            break
        if total % LANES == 0:
            return tuple(waiting[:count])
    return ()


def body(bands, nbr_slot, gshift):
    grid_index = lax.axis_index("ga")
    grid_count = lax.axis_size("ga")
    k_dev, _, nbands, points = bands.shape
    rows = nbands // grid_count
    own_planes = points // PLANE
    total_planes = own_planes * grid_count
    planes = grid_index * own_planes + jnp.arange(own_planes, dtype=jnp.int32)
    slots = jnp.arange(k_dev, dtype=jnp.int32)
    chosen = nbr_slot[None, :] == slots[:, None]
    order = jnp.sum(jnp.where(chosen, slots[None, :], 0), axis=1)
    shifts = jnp.sum(jnp.where(chosen, gshift[None, :], 0), axis=1)
    turns = (1 + NKB * shifts[:, None]) * planes[None, :] % (NKB * total_planes)
    angle = 2.0 * math.pi / (NKB * total_planes) * turns.astype(jnp.float32)
    columns = [order[:, None].astype(jnp.float32), jnp.cos(angle), jnp.sin(angle)]
    table = jnp.concatenate(columns, axis=1).reshape(-1)
    table = jnp.append(table, grid_index.astype(jnp.float32))
    parts = []
    for slot in range(k_dev):
        for start, width in cuts(nbands, slot == 0):
            parts.append((slot, start, width))
    theres = []
    piece = None
    for slot, start, width in parts[:AHEAD]:
        piece = piece_of(slot, start, width, bands, [] if piece is None else [piece])
        theres.append(shifted(piece, "ka", -1))
    shape = (rows, k_dev, 2, nbands)
    depth = min(OUTER, grid_count)
    fold = grid_count // depth
    held = {}
    near, kept, result = None, None, None
    for part, ways, phase, tasks, adds in schedule(parts, fold, depth):
        place = parts.index(part) if part else len(parts)
        later = parts[place + AHEAD] if place + AHEAD < len(parts) and phase != "use" else None
        sources = [
            [array for done in task.batch for array, _ in held[(done,)]] for task in tasks
        ]
        arrived, pieces = [], []
        for done in adds:
            batch = max((key for key in held if done in key), key=len)
            column = sum(2 * width for _, _, width in batch[: batch.index(done)])
            terms = [(len(arrived) + i, first + column) for i, (_, first) in enumerate(held[batch])]
            arrived += [array for array, _ in held[batch]]
            pieces.append((done[1], done[2], tuple(terms)))
        adding = (adds[0][0], adds[0][1], tuple(pieces)) if adds else ()
        plan = Plan(
            shape,
            fold,
            depth,
            part,
            ways,
            phase,
            "held" if kept is not None else "keep" if phase == "give" else "load",
            tasks,
            tuple(len(arrays) for arrays in sources),
            adding,
            len(arrived),
            len(tasks) > 1 and tasks[0].direct,
            result is not None,
            later,
        )
        phased = near if phase == "use" else theres[place] if part else None
        terms, near, found, sends, result, piece = step(
            plan,
            table,
            bands if kept is None else kept,
            phased,
            sources,
            arrived,
            result,
        )
        kept = found if kept is None else kept
        if later:
            theres.append(shifted(piece, "ka", -1))
        for way, array in zip(ways, terms):
            array = shifted(array, "ga", way, fold, True) if way else array
            held.setdefault((part,), []).insert(0 if way == 0 else fold, (array, 0))
        for task, arrays in zip(tasks, sends):
            steps = range(1, depth) if task.direct else [1 << task.stage]
            moved = [swapped(array, "ga", fold * i) for array, i in zip(arrays[1:], steps)]
            held[task.batch] = [(array, 0) for array in [arrays[0], *reversed(moved)]]
        if plan.joined:
            joint = held[tasks[0].batch][JOINT][0]
            held[tasks[1].batch].append((joint, 2 * tasks[0].batch[0][2]))
    return result


def solution(mesh):
    placed = (P("ka", None, None, "ga"), P("ka"), P("ka"))
    return jax.shard_map(
        body, mesh=mesh, in_specs=placed, out_specs=P("ga", "ka", None, None), check_vma=False
    )
```

```python
import functools
import math
from typing import NamedTuple

import jax
import jax.numpy as jnp
from jax import lax
from jax.experimental import pallas as pl
from jax.experimental.pallas import tpu as pltpu
from jax.sharding import PartitionSpec as P

NKB = 4
PLANE = 1024
STRIP = 32
DEPTH = 512
AHEAD = 3
OUTER = 4
SPLIT = 128
JOINT = 2
LANES = 128
BLOCK = 256
VMEM_BYTES = 44 * 1024 * 1024
LEAN_BYTES = 32 * 1024 * 1024


def shifted(block, axis, distance, fold=1, inner=False):
    count = lax.axis_size(axis)
    route = []
    for i in range(count):
        outer, place = divmod(i, fold)
        if inner:
            route.append((i, outer * fold + (place + distance) % fold))
        else:
            route.append((i, (outer + distance) % (count // fold) * fold + place))
    return lax.ppermute(block, axis, route)


def swapped(block, axis, distance):
    count = lax.axis_size(axis)
    return lax.ppermute(block, axis, [(i, i ^ distance) for i in range(count)])


def first_kernel(slot, start, bands_ref, out_ref, sems):
    width = out_ref.shape[1]
    loads = [
        pltpu.make_async_copy(
            bands_ref.at[slot, part, pl.ds(start, width), :], out_ref.at[part], sems.at[part]
        )
        for part in range(2)
    ]
    for load in loads:
        load.start()
    for load in loads:
        load.wait()


def piece_kernel(slot, start, bands_ref, *rest):
    out_ref, piece_buf, sems = rest[-3:]
    width = piece_buf.shape[1]
    rows = pl.ds(start, width)
    loads = [
        pltpu.make_async_copy(bands_ref.at[slot, part, rows, :], piece_buf.at[part], sems.at[0, part])
        for part in range(2)
    ]
    stores = [
        pltpu.make_async_copy(piece_buf.at[part], out_ref.at[part], sems.at[1, part])
        for part in range(2)
    ]
    for load in loads:
        load.start()
    for load, store in zip(loads, stores):
        load.wait()
        store.start()
    for store in stores:
        store.wait()


def piece_of(slot, start, width, bands, after):
    points = bands.shape[3]
    hbm = pl.BlockSpec(memory_space=pltpu.HBM)
    scratch = [pltpu.VMEM((2, width, points), bands.dtype), pltpu.SemaphoreType.DMA((2, 2))]
    return pl.pallas_call(
        functools.partial(piece_kernel if after else first_kernel, slot, start),
        in_specs=[hbm] * (1 + len(after)),
        out_specs=hbm if after else pl.BlockSpec(memory_space=pltpu.VMEM),
        scratch_shapes=scratch if after else [pltpu.SemaphoreType.DMA((2,))],
        out_shape=jax.ShapeDtypeStruct((2, width, points), bands.dtype),
        compiler_params=pltpu.CompilerParams(vmem_limit_bytes=VMEM_BYTES),
        cost_estimate=pl.CostEstimate(flops=1000, bytes_accessed=1000, transcendentals=0),
        name="piece_of",
    )(bands, *after)


def near_into(near_buf, there_ref, table_ref, base, planes):
    width, points = there_ref.shape[1:]

    @pl.loop(0, width // STRIP)
    def _(strip):
        rows = pl.ds(strip * STRIP, STRIP)
        mirror = pl.ds(width + strip * STRIP, STRIP)
        for start in range(0, points, DEPTH):
            plane = start // PLANE
            cosine = table_ref[base + 1 + plane]
            sine = table_ref[base + 1 + planes + plane]
            columns = pl.ds(start, DEPTH)
            real_part = there_ref[0, rows, columns].astype(jnp.float32)
            imag_part = there_ref[1, rows, columns].astype(jnp.float32)
            near_re = real_part * cosine + imag_part * sine
            near_im = imag_part * cosine - real_part * sine
            near_buf[rows, columns] = near_re.astype(jnp.bfloat16)
            near_buf[mirror, columns] = near_im.astype(jnp.bfloat16)


def put_sum(sum_buf, lane, total):
    width = total.shape[1] // 2
    sum_buf[:, 0, lane : lane + width] = total[:, :width]
    sum_buf[:, 1, lane : lane + width] = total[:, width:]


def step_kernel(plan, table_ref, *refs):
    rows, k_dev, _, nbands = plan.shape
    fold, depth = plan.fold, plan.depth
    refs = list(refs)

    def take(count):
        taken = refs[:count]
        del refs[:count]
        return taken

    stride = (table_ref.shape[0] - 1) // k_dev
    planes = (stride - 1) // 2
    me = table_ref[k_dev * stride].astype(jnp.int32)
    place, outer = lax.rem(me, fold), lax.div(me, fold)
    if plan.part:
        bands_ref, phased_ref = take(2)
    sources = [take(count) for count in plan.takes]
    arrived = take(plan.adds)
    if plan.adding and plan.placed:
        take(1)
    given_ref = take(1)[0] if plan.near == "give" else None
    kept_ref = take(1)[0] if plan.ahead else None
    outs = take(len(plan.ways))
    targets = [take(task.count) for task in plan.tasks]
    result_ref = take(1)[0] if plan.adding else None
    piece_ref = take(1)[0] if plan.later else None
    if plan.part:
        slot, _, width = plan.part
        base = slot * stride
        point = table_ref[base].astype(jnp.int32)

        def load_rows(point, into_ref, load_sems):
            copies = []
            for distance in range(1, fold + 1):
                way = distance % fold
                target = lax.rem(place + way, fold)
                for part in range(2):
                    for level in range(depth):
                        first = pl.multiple_of((level * fold + target) * rows, rows)
                        copy = pltpu.make_async_copy(
                            bands_ref.at[point, part, pl.ds(first, rows), :],
                            into_ref.at[way, part, pl.ds(level * rows, rows), :],
                            load_sems.at[way, part, level],
                        )
                        copy.start()
                        copies.append((way, part, copy))
            return copies

        own_ref = bands_ref
        own, ahead = [], []
        if plan.rows != "held":
            own_ref, own_sems = take(2)
            own = load_rows(point, own_ref, own_sems)
        if plan.ahead:
            next_point = table_ref[base + stride].astype(jnp.int32)
            ahead = load_rows(next_point, kept_ref, take(1)[0])
    if plan.later:
        piece_buf, piece_sems = take(2)
        later_slot, later_start, later_width = plan.later
        loads = [
            pltpu.make_async_copy(
                bands_ref.at[later_slot, part, pl.ds(later_start, later_width), :],
                piece_buf.at[part],
                piece_sems.at[0, part],
            )
            for part in range(2)
        ]
        stores = [
            pltpu.make_async_copy(piece_buf.at[part], piece_ref.at[part], piece_sems.at[1, part])
            for part in range(2)
        ]
        for copy in loads:
            copy.start()
    if plan.adding:
        sum_buf, placed_sem = take(2)
        add_slot, add_start, pieces = plan.adding
        for start, span, terms in pieces:
            total = 0.0
            for index, column in terms:
                total += arrived[index][0, :, column : column + 2 * span].astype(jnp.float32)
            put_sum(sum_buf, start - add_start, total)
        add_point = table_ref[add_slot * stride].astype(jnp.int32)
        columns = pl.ds(add_start, sum_buf.shape[2])
        placing = pltpu.make_async_copy(
            sum_buf, result_ref.at[:, add_point, :, columns], placed_sem
        )
        placing.start()
    for task, arrays, outputs in zip(plan.tasks, sources, targets):
        groups = [arrays[i : i + task.each] for i in range(0, len(arrays), task.each)]
        bit = lax.rem(lax.div(outer, 1 << task.stage), 2)
        filled = [(out_ref, 0) for out_ref in outputs]
        if plan.joined and not task.direct:
            filled.append((targets[0][JOINT], 2 * plan.tasks[0].batch[0][2]))
        for index, (out_ref, shift) in enumerate(filled):
            for level in range(out_ref.shape[0]):
                if task.direct:
                    source = partner(outer, index)
                else:
                    source = 2 * level + (1 - bit if index else bit)
                column = shift
                for group in groups:
                    total = summed(group, source)
                    columns = slice(column, column + total.shape[1])
                    out_ref[level, :, columns] = total.astype(out_ref.dtype)
                    column += total.shape[1]
    if plan.part:
        near_ref = phased_ref
        if plan.near != "use":
            near_ref = given_ref if plan.near == "give" else take(1)[0]
            near_into(near_ref, phased_ref, table_ref, base, planes)
        dims = (((1,), (1,)), ((), ()))
        points = near_ref.shape[1]
        run = points // 2 if width <= SPLIT else points
        for way, out_ref in zip(plan.ways, outs):
            of_both = []
            for part in range(2):
                for copy in [copy for *which, copy in own if which == [way, part]]:
                    copy.wait()
                products = [
                    lax.dot_general(
                        own_ref[way, part, :, pl.ds(first, run)],
                        near_ref[:, pl.ds(first, run)],
                        dims,
                        preferred_element_type=jnp.float32,
                    )
                    for first in range(0, points, run)
                ]
                of_both.append(sum(products[1:], products[0]))
            of_re, of_im = of_both
            real_part = (of_re[:, :width] + of_im[:, width:]).astype(out_ref.dtype)
            imag_part = (of_re[:, width:] - of_im[:, :width]).astype(out_ref.dtype)
            for level in range(depth):
                lines = slice(level * rows, (level + 1) * rows)
                out_ref[level, :, :width] = real_part[lines]
                out_ref[level, :, width:] = imag_part[lines]
            if plan.later and way == plan.ways[0]:
                for load, store in zip(loads, stores):
                    load.wait()
                    store.start()
        for _, _, copy in ahead:
            copy.wait()
    if plan.adding:
        placing.wait()
    if plan.later:
        for store in stores:
            store.wait()


def partner(outer, distance):
    low, high = lax.rem(outer, 2), lax.rem(lax.div(outer, 2), 2)
    low = 1 - low if distance % 2 else low
    high = 1 - high if distance // 2 else high
    return outer - lax.rem(outer, 4) + 2 * high + low


def summed(arrays, level, columns=slice(None)):
    total = arrays[0][level, :, columns]
    for array in arrays[1:]:
        total = total + array[level, :, columns].astype(jnp.float32)
    return total


class Task(NamedTuple):
    batch: tuple
    stage: int
    direct: bool
    each: int
    count: int


class Plan(NamedTuple):
    shape: tuple
    fold: int
    depth: int
    part: tuple
    ways: tuple
    near: str
    rows: str
    ahead: bool
    tasks: tuple
    takes: tuple
    adding: tuple
    adds: int
    joined: bool
    placed: bool
    later: tuple


def step(plan, table, bands, phased, sources, arrived, result):
    rows, _, _, nbands = plan.shape
    fold, depth = plan.fold, plan.depth
    points = bands.shape[-1]
    vmem = pl.BlockSpec(memory_space=pltpu.VMEM)
    hbm = pl.BlockSpec(memory_space=pltpu.HBM)
    operands, in_specs = [table], [pl.BlockSpec(memory_space=pltpu.SMEM)]
    out_shape, out_specs, scratch, aliases = [], [], [], {}

    def kind(index):
        return jnp.bfloat16 if index else jnp.float32

    if plan.part:
        width = plan.part[2]
        operands += [bands, phased]
        in_specs += [vmem if plan.rows == "held" else hbm, vmem]
        kept = (fold, 2, depth * rows, points)
        if plan.near == "give":
            out_shape.append(jax.ShapeDtypeStruct((2 * width, points), jnp.bfloat16))
        if plan.ahead:
            out_shape.append(jax.ShapeDtypeStruct(kept, jnp.bfloat16))
        out_shape += [
            jax.ShapeDtypeStruct((depth, rows, 2 * width), kind(way)) for way in plan.ways
        ]
        if plan.rows != "held":
            scratch.append(pltpu.VMEM(kept, jnp.bfloat16))
            scratch.append(pltpu.SemaphoreType.DMA((fold, 2, depth)))
        if plan.ahead:
            scratch.append(pltpu.SemaphoreType.DMA((fold, 2, depth)))
    for arrays in [*sources, arrived]:
        operands += arrays
        in_specs += [vmem] * len(arrays)
    for task in plan.tasks:
        wide = sum(2 * width for _, _, width in task.batch)
        levels = 1 if task.direct else depth >> (task.stage + 1)
        extra = 2 * plan.tasks[1].batch[0][2] if plan.joined and task.direct else 0
        for i in range(task.count):
            columns = wide + extra if i == JOINT else wide
            out_shape.append(jax.ShapeDtypeStruct((levels, rows, columns), kind(i)))
    out_specs += [vmem] * len(out_shape)
    if plan.later:
        scratch += [
            pltpu.VMEM((2, plan.later[2], points), bands.dtype),
            pltpu.SemaphoreType.DMA((2, 2)),
        ]
    if plan.adding:
        if plan.placed:
            aliases = {len(operands): len(out_shape)}
            operands.append(result)
            in_specs.append(hbm)
        out_shape.append(jax.ShapeDtypeStruct(plan.shape, jnp.float32))
        out_specs.append(hbm)
        lanes = sum(span for _, span, _ in plan.adding[2])
        scratch += [pltpu.VMEM((rows, 2, lanes), jnp.float32), pltpu.SemaphoreType.DMA]
    if plan.later:
        out_shape.append(jax.ShapeDtypeStruct((2, plan.later[2], points), bands.dtype))
        out_specs.append(hbm)
    if plan.near == "make":
        scratch.append(pltpu.VMEM((2 * width, points), jnp.bfloat16))
    outs = list(
        pl.pallas_call(
            functools.partial(step_kernel, plan),
            in_specs=in_specs,
            out_specs=out_specs,
            scratch_shapes=scratch,
            out_shape=out_shape,
            input_output_aliases=aliases,
            compiler_params=pltpu.CompilerParams(
                vmem_limit_bytes=VMEM_BYTES if plan.part and plan.rows != "held" else LEAN_BYTES
            ),
            cost_estimate=pl.CostEstimate(flops=1000, bytes_accessed=1000, transcendentals=0),
            name="step",
        )(*operands)
    )
    piece = outs.pop() if plan.later else None
    result = outs.pop() if plan.adding else result
    near = outs.pop(0) if plan.near == "give" else None
    kept = outs.pop(0) if plan.ahead else None
    terms = outs[: len(plan.ways)]
    handed = outs[len(plan.ways) :]
    sends = []
    for task in plan.tasks:
        sends.append(handed[: task.count])
        handed = handed[task.count :]
    return terms, near, kept, sends, result, piece


def cuts(nbands, first):
    eighth = nbands // 8
    widths = [4 * eighth, 4 * eighth] if first else [3 * eighth, 3 * eighth, 2 * eighth]
    starts = [sum(widths[:i]) for i in range(len(widths))]
    return list(zip(starts, widths))


def schedule(parts, fold, depth):
    every, others = tuple(range(fold)), tuple(range(1, fold))
    count = len(parts)
    kernels = []
    waiting, halved, crossed = [], [], []
    for index, part in enumerate(parts):
        ready = ready_parts(waiting)
        waiting = waiting[len(ready) :]
        tasks = []
        if halved:
            tasks.append(Task(tuple(halved), 1, False, 2, 2))
        if crossed:
            tasks.append(Task(tuple(crossed), 0, False, fold, 2))
        waiting += halved
        if index >= count - 3:
            kernels.append((part, others, "give", tuple(tasks), ready))
            kernels.append((part, every[:1], "use", (), ()))
        else:
            kernels.append((part, every, "make", tuple(tasks), ready))
        halved, crossed = crossed, [part] if index < count - 1 else []
        if index in (0, count - 3):
            kernels.append((None, (), "", (Task((part,), 0, False, fold, 2),), ()))
            halved, crossed = halved + crossed, []
    tasks = (
        Task((parts[-1],), 0, True, fold, depth),
        Task(tuple(halved), 1, False, 2, 1),
    )
    kernels.append((None, (), "", tasks, ()))
    kernels.append((None, (), "", (), tuple(waiting) + tuple(halved) + (parts[-1],)))
    return kernels


def ready_parts(waiting):
    total = 0
    for count, (slot, _, width) in enumerate(waiting, 1):
        total += width
        if slot != waiting[0][0]:
            break
        if total % LANES == 0:
            return tuple(waiting[:count])
    return ()


def body(bands, nbr_slot, gshift):
    grid_index = lax.axis_index("ga")
    grid_count = lax.axis_size("ga")
    k_dev, _, nbands, points = bands.shape
    rows = nbands // grid_count
    own_planes = points // PLANE
    total_planes = own_planes * grid_count
    planes = grid_index * own_planes + jnp.arange(own_planes, dtype=jnp.int32)
    slots = jnp.arange(k_dev, dtype=jnp.int32)
    chosen = nbr_slot[None, :] == slots[:, None]
    order = jnp.sum(jnp.where(chosen, slots[None, :], 0), axis=1)
    shifts = jnp.sum(jnp.where(chosen, gshift[None, :], 0), axis=1)
    turns = (1 + NKB * shifts[:, None]) * planes[None, :] % (NKB * total_planes)
    angle = 2.0 * math.pi / (NKB * total_planes) * turns.astype(jnp.float32)
    columns = [order[:, None].astype(jnp.float32), jnp.cos(angle), jnp.sin(angle)]
    table = jnp.concatenate(columns, axis=1).reshape(-1)
    table = jnp.append(table, grid_index.astype(jnp.float32))
    parts = []
    for slot in range(k_dev):
        for start, width in cuts(nbands, slot == 0):
            parts.append((slot, start, width))
    theres = []
    piece = None
    for slot, start, width in parts[:AHEAD]:
        piece = piece_of(slot, start, width, bands, [] if piece is None else [piece])
        theres.append(shifted(piece, "ka", -1))
    shape = (rows, k_dev, 2, nbands)
    depth = min(OUTER, grid_count)
    fold = grid_count // depth
    held = {}
    near, kept, result = None, None, None
    for part, ways, phase, tasks, adds in schedule(parts, fold, depth):
        place = parts.index(part) if part else len(parts)
        later = parts[place + AHEAD] if place + AHEAD < len(parts) and phase != "use" else None
        sources = [
            [array for done in task.batch for array, _ in held[(done,)]] for task in tasks
        ]
        arrived, pieces = [], []
        for done in adds:
            batch = max((key for key in held if done in key), key=len)
            column = sum(2 * width for _, _, width in batch[: batch.index(done)])
            terms = [(len(arrived) + i, first + column) for i, (_, first) in enumerate(held[batch])]
            arrived += [array for array, _ in held[batch]]
            pieces.append((done[1], done[2], tuple(terms)))
        adding = (adds[0][0], adds[0][1], tuple(pieces)) if adds else ()
        plan = Plan(
            shape,
            fold,
            depth,
            part,
            ways,
            phase,
            "load" if kept is None else "held",
            place == len(parts) - 4,
            tasks,
            tuple(len(arrays) for arrays in sources),
            adding,
            len(arrived),
            len(tasks) > 1 and tasks[0].direct,
            result is not None,
            later,
        )
        phased = near if phase == "use" else theres[place] if part else None
        terms, near, found, sends, result, piece = step(
            plan,
            table,
            bands if kept is None else kept,
            phased,
            sources,
            arrived,
            result,
        )
        kept = found if kept is None else kept
        if later:
            theres.append(shifted(piece, "ka", -1))
        for way, array in zip(ways, terms):
            array = shifted(array, "ga", way, fold, True) if way else array
            held.setdefault((part,), []).insert(0 if way == 0 else fold, (array, 0))
        for task, arrays in zip(tasks, sends):
            steps = range(1, depth) if task.direct else [1 << task.stage]
            moved = [swapped(array, "ga", fold * i) for array, i in zip(arrays[1:], steps)]
            held[task.batch] = [(array, 0) for array in [arrays[0], *reversed(moved)]]
        if plan.joined:
            joint = held[tasks[0].batch][JOINT][0]
            held[tasks[1].batch].append((joint, 2 * tasks[0].batch[0][2]))
    return result


def solution(mesh):
    placed = (P("ka", None, None, "ga"), P("ka"), P("ka"))
    return jax.shard_map(
        body, mesh=mesh, in_specs=placed, out_specs=P("ga", "ka", None, None), check_vma=False
    )
```

```python
import functools
import math
from typing import NamedTuple

import jax
import jax.numpy as jnp
from jax import lax
from jax.experimental import pallas as pl
from jax.experimental.pallas import tpu as pltpu
from jax.sharding import PartitionSpec as P

NKB = 4
PLANE = 1024
STRIP = 32
DEPTH = 512
AHEAD = 3
OUTER = 4
SPLIT = 128
JOINT = 2
LANES = 128
BLOCK = 256
VMEM_BYTES = 44 * 1024 * 1024
LEAN_BYTES = 32 * 1024 * 1024


def shifted(block, axis, distance, fold=1, inner=False):
    count = lax.axis_size(axis)
    route = []
    for i in range(count):
        outer, place = divmod(i, fold)
        if inner:
            route.append((i, outer * fold + (place + distance) % fold))
        else:
            route.append((i, (outer + distance) % (count // fold) * fold + place))
    return lax.ppermute(block, axis, route)


def swapped(block, axis, distance):
    count = lax.axis_size(axis)
    return lax.ppermute(block, axis, [(i, i ^ distance) for i in range(count)])


def first_kernel(slot, start, bands_ref, out_ref, sems):
    width = out_ref.shape[1]
    loads = [
        pltpu.make_async_copy(
            bands_ref.at[slot, part, pl.ds(start, width), :], out_ref.at[part], sems.at[part]
        )
        for part in range(2)
    ]
    for load in loads:
        load.start()
    for load in loads:
        load.wait()


def piece_kernel(slot, start, bands_ref, *rest):
    out_ref, piece_buf, sems = rest[-3:]
    width = piece_buf.shape[1]
    rows = pl.ds(start, width)
    loads = [
        pltpu.make_async_copy(bands_ref.at[slot, part, rows, :], piece_buf.at[part], sems.at[0, part])
        for part in range(2)
    ]
    stores = [
        pltpu.make_async_copy(piece_buf.at[part], out_ref.at[part], sems.at[1, part])
        for part in range(2)
    ]
    for load in loads:
        load.start()
    for load, store in zip(loads, stores):
        load.wait()
        store.start()
    for store in stores:
        store.wait()


def piece_of(slot, start, width, bands, after):
    points = bands.shape[3]
    hbm = pl.BlockSpec(memory_space=pltpu.HBM)
    scratch = [pltpu.VMEM((2, width, points), bands.dtype), pltpu.SemaphoreType.DMA((2, 2))]
    return pl.pallas_call(
        functools.partial(piece_kernel if after else first_kernel, slot, start),
        in_specs=[hbm] * (1 + len(after)),
        out_specs=hbm if after else pl.BlockSpec(memory_space=pltpu.VMEM),
        scratch_shapes=scratch if after else [pltpu.SemaphoreType.DMA((2,))],
        out_shape=jax.ShapeDtypeStruct((2, width, points), bands.dtype),
        compiler_params=pltpu.CompilerParams(vmem_limit_bytes=VMEM_BYTES),
        cost_estimate=pl.CostEstimate(flops=1000, bytes_accessed=1000, transcendentals=0),
        name="piece_of",
    )(bands, *after)


def near_into(near_buf, there_ref, table_ref, base, planes):
    width, points = there_ref.shape[1:]

    @pl.loop(0, width // STRIP)
    def _(strip):
        rows = pl.ds(strip * STRIP, STRIP)
        mirror = pl.ds(width + strip * STRIP, STRIP)
        for start in range(0, points, DEPTH):
            plane = start // PLANE
            cosine = table_ref[base + 1 + plane]
            sine = table_ref[base + 1 + planes + plane]
            columns = pl.ds(start, DEPTH)
            real_part = there_ref[0, rows, columns].astype(jnp.float32)
            imag_part = there_ref[1, rows, columns].astype(jnp.float32)
            near_re = real_part * cosine + imag_part * sine
            near_im = imag_part * cosine - real_part * sine
            near_buf[rows, columns] = near_re.astype(jnp.bfloat16)
            near_buf[mirror, columns] = near_im.astype(jnp.bfloat16)


def put_sum(sum_buf, lane, total):
    width = total.shape[1] // 2
    sum_buf[:, 0, lane : lane + width] = total[:, :width]
    sum_buf[:, 1, lane : lane + width] = total[:, width:]


def step_kernel(plan, table_ref, *refs):
    rows, k_dev, _, nbands = plan.shape
    fold, depth = plan.fold, plan.depth
    refs = list(refs)

    def take(count):
        taken = refs[:count]
        del refs[:count]
        return taken

    stride = (table_ref.shape[0] - 1) // k_dev
    planes = (stride - 1) // 2
    me = table_ref[k_dev * stride].astype(jnp.int32)
    place, outer = lax.rem(me, fold), lax.div(me, fold)
    if plan.part:
        bands_ref, phased_ref = take(2)
    sources = [take(count) for count in plan.takes]
    arrived = take(plan.adds)
    if plan.adding and plan.placed:
        take(1)
    take(plan.after)
    given_ref = take(1)[0] if plan.near == "give" else None
    kept_ref = take(1)[0] if plan.ahead else None
    outs = [take(2 if plan.split else 1) for _ in plan.ways]
    targets = [take(task.count) for task in plan.tasks]
    result_ref = take(1)[0] if plan.adding else None
    piece_ref = take(1)[0] if plan.later else None
    if plan.part:
        slot, _, width = plan.part
        base = slot * stride
        point = table_ref[base].astype(jnp.int32)

        def load_rows(point, into_ref, load_sems):
            copies = []
            for distance in range(1, fold + 1):
                way = distance % fold
                target = lax.rem(place + way, fold)
                for part in range(2):
                    for level in range(depth):
                        first = pl.multiple_of((level * fold + target) * rows, rows)
                        copy = pltpu.make_async_copy(
                            bands_ref.at[point, part, pl.ds(first, rows), :],
                            into_ref.at[way, part, pl.ds(level * rows, rows), :],
                            load_sems.at[way, part, level],
                        )
                        copy.start()
                        copies.append((way, part, copy))
            return copies

        own_ref = bands_ref
        own, ahead = [], []
        if plan.rows != "held":
            own_ref, own_sems = take(2)
            own = load_rows(point, own_ref, own_sems)
        if plan.ahead:
            next_point = table_ref[base + stride].astype(jnp.int32)
            ahead = load_rows(next_point, kept_ref, take(1)[0])
    if plan.later:
        piece_buf, piece_sems = take(2)
        later_slot, later_start, later_width = plan.later
        loads = [
            pltpu.make_async_copy(
                bands_ref.at[later_slot, part, pl.ds(later_start, later_width), :],
                piece_buf.at[part],
                piece_sems.at[0, part],
            )
            for part in range(2)
        ]
        stores = [
            pltpu.make_async_copy(piece_buf.at[part], piece_ref.at[part], piece_sems.at[1, part])
            for part in range(2)
        ]
        for copy in loads:
            copy.start()
    if plan.adding:
        sum_buf, placed_sem = take(2)
        add_slot, add_start, pieces = plan.adding
        for start, span, terms in pieces:
            total = 0.0
            for index, column in terms:
                total += arrived[index][0, :, column : column + 2 * span].astype(jnp.float32)
            put_sum(sum_buf, start - add_start, total)
        add_point = table_ref[add_slot * stride].astype(jnp.int32)
        columns = pl.ds(add_start, sum_buf.shape[2])
        placing = pltpu.make_async_copy(
            sum_buf, result_ref.at[:, add_point, :, columns], placed_sem
        )
        placing.start()
    for task, arrays, outputs in zip(plan.tasks, sources, targets):
        groups = [arrays[i : i + task.each] for i in range(0, len(arrays), task.each)]
        bit = lax.rem(lax.div(outer, 1 << task.stage), 2)
        filled = [(out_ref, 0) for out_ref in outputs]
        if plan.joined and not task.direct:
            filled.append((targets[0][JOINT], 2 * plan.tasks[0].batch[0][2]))
        for index, (out_ref, shift) in enumerate(filled):
            for level in range(out_ref.shape[0]):
                if task.direct:
                    source = partner(outer, index)
                else:
                    source = 2 * level + (1 - bit if index else bit)
                column = shift
                for group in groups:
                    total = summed(group, source)
                    columns = slice(column, column + total.shape[1])
                    out_ref[level, :, columns] = total.astype(out_ref.dtype)
                    column += total.shape[1]
    if plan.part:
        near_ref = phased_ref
        if plan.near != "use":
            near_ref = given_ref if plan.near == "give" else take(1)[0]
            near_into(near_ref, phased_ref, table_ref, base, planes)
        dims = (((1,), (1,)), ((), ()))
        points = near_ref.shape[1]
        run = points // 2 if width <= SPLIT else points
        for way, out_refs in zip(plan.ways, outs):
            kind = out_refs[0].dtype
            of_both = []
            for part in range(2):
                for copy in [copy for *which, copy in own if which == [way, part]]:
                    copy.wait()
                products = [
                    lax.dot_general(
                        own_ref[way, part, :, pl.ds(first, run)],
                        near_ref[:, pl.ds(first, run)],
                        dims,
                        preferred_element_type=jnp.float32,
                    )
                    for first in range(0, points, run)
                ]
                of_both.append(sum(products[1:], products[0]))
            of_re, of_im = of_both
            sides = (
                (of_re[:, :width] + of_im[:, width:]).astype(kind),
                (of_re[:, width:] - of_im[:, :width]).astype(kind),
            )
            for level in range(depth):
                lines = slice(level * rows, (level + 1) * rows)
                for side, values in enumerate(sides):
                    if plan.split:
                        out_refs[side][level] = values[lines]
                    else:
                        columns = slice(side * width, (side + 1) * width)
                        out_refs[0][level, :, columns] = values[lines]
            if plan.later and way == plan.ways[0]:
                for load, store in zip(loads, stores):
                    load.wait()
                    store.start()
        for _, _, copy in ahead:
            copy.wait()
    if plan.adding:
        placing.wait()
    if plan.later:
        for store in stores:
            store.wait()


def partner(outer, distance):
    low, high = lax.rem(outer, 2), lax.rem(lax.div(outer, 2), 2)
    low = 1 - low if distance % 2 else low
    high = 1 - high if distance // 2 else high
    return outer - lax.rem(outer, 4) + 2 * high + low


def summed(arrays, level):
    total = arrays[0][level].astype(jnp.float32)
    rest = [array[level].astype(jnp.float32) for array in arrays[1:]]
    while rest:
        more = rest.pop(0)
        if more.shape != total.shape:
            more = jnp.concatenate([more, rest.pop(0)], axis=1)
        total = total + more
    return total


class Task(NamedTuple):
    batch: tuple
    stage: int
    direct: bool
    each: int
    count: int


class Plan(NamedTuple):
    shape: tuple
    fold: int
    depth: int
    part: tuple
    ways: tuple
    near: str
    rows: str
    ahead: bool
    tasks: tuple
    takes: tuple
    adding: tuple
    adds: int
    joined: bool
    placed: bool
    later: tuple
    split: bool
    after: int


def step(plan, table, bands, phased, sources, arrived, result, after):
    rows, _, _, nbands = plan.shape
    fold, depth = plan.fold, plan.depth
    points = bands.shape[-1]
    vmem = pl.BlockSpec(memory_space=pltpu.VMEM)
    hbm = pl.BlockSpec(memory_space=pltpu.HBM)
    operands, in_specs = [table], [pl.BlockSpec(memory_space=pltpu.SMEM)]
    out_shape, out_specs, scratch, aliases = [], [], [], {}

    def kind(index):
        return jnp.bfloat16 if index else jnp.float32

    if plan.part:
        width = plan.part[2]
        operands += [bands, phased]
        in_specs += [vmem if plan.rows == "held" else hbm, vmem]
        kept = (fold, 2, depth * rows, points)
        if plan.near == "give":
            out_shape.append(jax.ShapeDtypeStruct((2 * width, points), jnp.bfloat16))
        if plan.ahead:
            out_shape.append(jax.ShapeDtypeStruct(kept, jnp.bfloat16))
        out_shape += [
            jax.ShapeDtypeStruct((depth, rows, width if plan.split else 2 * width), kind(way))
            for way in plan.ways
            for _ in range(2 if plan.split else 1)
        ]
        if plan.rows != "held":
            scratch.append(pltpu.VMEM(kept, jnp.bfloat16))
            scratch.append(pltpu.SemaphoreType.DMA((fold, 2, depth)))
        if plan.ahead:
            scratch.append(pltpu.SemaphoreType.DMA((fold, 2, depth)))
    for arrays in [*sources, arrived]:
        operands += arrays
        in_specs += [vmem] * len(arrays)
    for task in plan.tasks:
        wide = sum(2 * width for _, _, width in task.batch)
        levels = 1 if task.direct else depth >> (task.stage + 1)
        extra = 2 * plan.tasks[1].batch[0][2] if plan.joined and task.direct else 0
        for i in range(task.count):
            columns = wide + extra if i == JOINT else wide
            out_shape.append(jax.ShapeDtypeStruct((levels, rows, columns), kind(i)))
    out_specs += [vmem] * len(out_shape)
    if plan.later:
        scratch += [
            pltpu.VMEM((2, plan.later[2], points), bands.dtype),
            pltpu.SemaphoreType.DMA((2, 2)),
        ]
    if plan.adding:
        if plan.placed:
            aliases = {len(operands): len(out_shape)}
            operands.append(result)
            in_specs.append(hbm)
        out_shape.append(jax.ShapeDtypeStruct(plan.shape, jnp.float32))
        out_specs.append(hbm)
        lanes = sum(span for _, span, _ in plan.adding[2])
        scratch += [pltpu.VMEM((rows, 2, lanes), jnp.float32), pltpu.SemaphoreType.DMA]
    operands += after
    in_specs += [pl.BlockSpec(memory_space=pl.ANY)] * len(after)
    if plan.later:
        out_shape.append(jax.ShapeDtypeStruct((2, plan.later[2], points), bands.dtype))
        out_specs.append(hbm)
    if plan.near == "make":
        scratch.append(pltpu.VMEM((2 * width, points), jnp.bfloat16))
    outs = list(
        pl.pallas_call(
            functools.partial(step_kernel, plan),
            in_specs=in_specs,
            out_specs=out_specs,
            scratch_shapes=scratch,
            out_shape=out_shape,
            input_output_aliases=aliases,
            compiler_params=pltpu.CompilerParams(
                vmem_limit_bytes=VMEM_BYTES if plan.part and plan.rows != "held" else LEAN_BYTES
            ),
            cost_estimate=pl.CostEstimate(flops=1000, bytes_accessed=1000, transcendentals=0),
            name="step",
        )(*operands)
    )
    piece = outs.pop() if plan.later else None
    result = outs.pop() if plan.adding else result
    near = outs.pop(0) if plan.near == "give" else None
    kept = outs.pop(0) if plan.ahead else None
    count = len(plan.ways) * (2 if plan.split else 1)
    terms, handed = outs[:count], outs[count:]
    sends = []
    for task in plan.tasks:
        sends.append(handed[: task.count])
        handed = handed[task.count :]
    return terms, near, kept, sends, result, piece


def cuts(nbands, first):
    eighth = nbands // 8
    widths = [4 * eighth, 4 * eighth] if first else [3 * eighth, 3 * eighth, 2 * eighth]
    starts = [sum(widths[:i]) for i in range(len(widths))]
    return list(zip(starts, widths))


def schedule(parts, fold, depth):
    every, others = tuple(range(fold)), tuple(range(1, fold))
    count = len(parts)
    kernels = []
    waiting, halved, crossed = [], [], []
    for index, part in enumerate(parts):
        ready = ready_parts(waiting)
        waiting = waiting[len(ready) :]
        final = index == count - 1
        tasks = []
        if halved and not final:
            tasks.append(Task(tuple(halved), 1, False, 2, 2))
            waiting += halved
        if crossed:
            tasks.append(Task(tuple(crossed), 0, False, fold, 2))
        if index >= count - 3:
            kernels.append((part, others, "give", tuple(tasks), ready))
            kernels.append((part, every[:1], "use", (), ()))
        else:
            kernels.append((part, every, "make", tuple(tasks), ready))
        if final:
            break
        halved, crossed = crossed, [part]
        if index in (0, count - 3, count - 2):
            kernels.append((None, (), "", (Task((part,), 0, False, fold, 2),), ()))
            halved, crossed = halved + crossed, []
    tasks = (
        Task((parts[-1],), 0, True, 2 * fold - 1, depth),
        Task(tuple(halved), 1, False, 2, 1),
    )
    kernels.append((None, (), "", tasks, ()))
    kernels.append((None, (), "", (), tuple(waiting) + tuple(halved) + (parts[-1],)))
    return kernels


def ready_parts(waiting):
    total = 0
    for count, (slot, _, width) in enumerate(waiting, 1):
        total += width
        if slot != waiting[0][0]:
            break
        if total % LANES == 0:
            return tuple(waiting[:count])
    return ()


def body(bands, nbr_slot, gshift):
    grid_index = lax.axis_index("ga")
    grid_count = lax.axis_size("ga")
    k_dev, _, nbands, points = bands.shape
    rows = nbands // grid_count
    own_planes = points // PLANE
    total_planes = own_planes * grid_count
    planes = grid_index * own_planes + jnp.arange(own_planes, dtype=jnp.int32)
    slots = jnp.arange(k_dev, dtype=jnp.int32)
    chosen = nbr_slot[None, :] == slots[:, None]
    order = jnp.sum(jnp.where(chosen, slots[None, :], 0), axis=1)
    shifts = jnp.sum(jnp.where(chosen, gshift[None, :], 0), axis=1)
    turns = (1 + NKB * shifts[:, None]) * planes[None, :] % (NKB * total_planes)
    angle = 2.0 * math.pi / (NKB * total_planes) * turns.astype(jnp.float32)
    columns = [order[:, None].astype(jnp.float32), jnp.cos(angle), jnp.sin(angle)]
    table = jnp.concatenate(columns, axis=1).reshape(-1)
    table = jnp.append(table, grid_index.astype(jnp.float32))
    parts = []
    for slot in range(k_dev):
        for start, width in cuts(nbands, slot == 0):
            parts.append((slot, start, width))
    theres = []
    piece = None
    for slot, start, width in parts[:AHEAD]:
        piece = piece_of(slot, start, width, bands, [] if piece is None else [piece])
        theres.append(shifted(piece, "ka", -1))
    shape = (rows, k_dev, 2, nbands)
    depth = min(OUTER, grid_count)
    fold = grid_count // depth
    held = {}
    near, kept, result = None, None, None
    for part, ways, phase, tasks, adds in schedule(parts, fold, depth):
        place = parts.index(part) if part else len(parts)
        later = parts[place + AHEAD] if place + AHEAD < len(parts) and phase != "use" else None
        sources = [
            [array for done in task.batch for array, _ in held[(done,)]] for task in tasks
        ]
        arrived, pieces = [], []
        for done in adds:
            batch = max((key for key in held if done in key), key=len)
            column = sum(2 * width for _, _, width in batch[: batch.index(done)])
            terms = [(len(arrived) + i, first + column) for i, (_, first) in enumerate(held[batch])]
            arrived += [array for array, _ in held[batch]]
            pieces.append((done[1], done[2], tuple(terms)))
        adding = (adds[0][0], adds[0][1], tuple(pieces)) if adds else ()
        split = place == len(parts) - 1 and phase == "give"
        after = order_by if split else []
        plan = Plan(
            shape,
            fold,
            depth,
            part,
            ways,
            phase,
            "load" if kept is None else "held",
            place == len(parts) - 4,
            tasks,
            tuple(len(arrays) for arrays in sources),
            adding,
            len(arrived),
            len(tasks) > 1 and tasks[0].direct,
            result is not None,
            later,
            split,
            len(after),
        )
        phased = near if phase == "use" else theres[place] if part else None
        terms, near, found, sends, result, piece = step(
            plan,
            table,
            bands if kept is None else kept,
            phased,
            sources,
            arrived,
            result,
            after,
        )
        order_by = sends[0][:1] if sends else []
        kept = found if kept is None else kept
        if later:
            theres.append(shifted(piece, "ka", -1))
        for way, array in zip([way for way in ways for _ in range(1 + split)], terms):
            array = shifted(array, "ga", way, fold, True) if way else array
            entries = held.setdefault((part,), [])
            entries.insert(len(entries) if way else 0, (array, 0))
        for task, arrays in zip(tasks, sends):
            steps = range(1, depth) if task.direct else [1 << task.stage]
            moved = [swapped(array, "ga", fold * i) for array, i in zip(arrays[1:], steps)]
            held[task.batch] = [(array, 0) for array in [arrays[0], *reversed(moved)]]
        if plan.joined:
            joint = held[tasks[0].batch][JOINT][0]
            held[tasks[1].batch].append((joint, 2 * tasks[0].batch[0][2]))
    return result


def solution(mesh):
    placed = (P("ka", None, None, "ga"), P("ka"), P("ka"))
    return jax.shard_map(
        body, mesh=mesh, in_specs=placed, out_specs=P("ga", "ka", None, None), check_vma=False
    )
```

```python
import functools
import math
from typing import NamedTuple

import jax
import jax.numpy as jnp
from jax import lax
from jax.experimental import pallas as pl
from jax.experimental.pallas import tpu as pltpu
from jax.sharding import PartitionSpec as P

NKB = 4
PLANE = 1024
STRIP = 32
DEPTH = 512
AHEAD = 3
OUTER = 4
SPLIT = 128
JOINT = 1
LANES = 128
BLOCK = 256
VMEM_BYTES = 44 * 1024 * 1024
LEAN_BYTES = 32 * 1024 * 1024


def shifted(block, axis, distance, fold=1, inner=False):
    count = lax.axis_size(axis)
    route = []
    for i in range(count):
        outer, place = divmod(i, fold)
        if inner:
            route.append((i, outer * fold + (place + distance) % fold))
        else:
            route.append((i, (outer + distance) % (count // fold) * fold + place))
    return lax.ppermute(block, axis, route)


def swapped(block, axis, distance):
    count = lax.axis_size(axis)
    return lax.ppermute(block, axis, [(i, i ^ distance) for i in range(count)])


def first_kernel(slot, start, bands_ref, out_ref, sems):
    width = out_ref.shape[1]
    loads = [
        pltpu.make_async_copy(
            bands_ref.at[slot, part, pl.ds(start, width), :], out_ref.at[part], sems.at[part]
        )
        for part in range(2)
    ]
    for load in loads:
        load.start()
    for load in loads:
        load.wait()


def piece_kernel(slot, start, bands_ref, *rest):
    out_ref, piece_buf, sems = rest[-3:]
    width = piece_buf.shape[1]
    rows = pl.ds(start, width)
    loads = [
        pltpu.make_async_copy(bands_ref.at[slot, part, rows, :], piece_buf.at[part], sems.at[0, part])
        for part in range(2)
    ]
    stores = [
        pltpu.make_async_copy(piece_buf.at[part], out_ref.at[part], sems.at[1, part])
        for part in range(2)
    ]
    for load in loads:
        load.start()
    for load, store in zip(loads, stores):
        load.wait()
        store.start()
    for store in stores:
        store.wait()


def piece_of(slot, start, width, bands, after):
    points = bands.shape[3]
    hbm = pl.BlockSpec(memory_space=pltpu.HBM)
    scratch = [pltpu.VMEM((2, width, points), bands.dtype), pltpu.SemaphoreType.DMA((2, 2))]
    return pl.pallas_call(
        functools.partial(piece_kernel if after else first_kernel, slot, start),
        in_specs=[hbm] * (1 + len(after)),
        out_specs=hbm if after else pl.BlockSpec(memory_space=pltpu.VMEM),
        scratch_shapes=scratch if after else [pltpu.SemaphoreType.DMA((2,))],
        out_shape=jax.ShapeDtypeStruct((2, width, points), bands.dtype),
        compiler_params=pltpu.CompilerParams(vmem_limit_bytes=VMEM_BYTES),
        cost_estimate=pl.CostEstimate(flops=1000, bytes_accessed=1000, transcendentals=0),
        name="piece_of",
    )(bands, *after)


def near_into(near_buf, there_ref, table_ref, base, planes):
    width, points = there_ref.shape[1:]

    @pl.loop(0, width // STRIP)
    def _(strip):
        rows = pl.ds(strip * STRIP, STRIP)
        mirror = pl.ds(width + strip * STRIP, STRIP)
        for start in range(0, points, DEPTH):
            plane = start // PLANE
            cosine = table_ref[base + 1 + plane]
            sine = table_ref[base + 1 + planes + plane]
            columns = pl.ds(start, DEPTH)
            real_part = there_ref[0, rows, columns].astype(jnp.float32)
            imag_part = there_ref[1, rows, columns].astype(jnp.float32)
            near_re = real_part * cosine + imag_part * sine
            near_im = imag_part * cosine - real_part * sine
            near_buf[rows, columns] = near_re.astype(jnp.bfloat16)
            near_buf[mirror, columns] = near_im.astype(jnp.bfloat16)


def put_sum(sum_buf, lane, total):
    width = total.shape[1] // 2
    sum_buf[:, 0, lane : lane + width] = total[:, :width]
    sum_buf[:, 1, lane : lane + width] = total[:, width:]


def step_kernel(plan, table_ref, *refs):
    rows, k_dev, _, nbands = plan.shape
    fold, depth = plan.fold, plan.depth
    refs = list(refs)

    def take(count):
        taken = refs[:count]
        del refs[:count]
        return taken

    stride = (table_ref.shape[0] - 1) // k_dev
    planes = (stride - 1) // 2
    me = table_ref[k_dev * stride].astype(jnp.int32)
    place, outer = lax.rem(me, fold), lax.div(me, fold)
    if plan.part:
        bands_ref, phased_ref = take(2)
    sources = [take(count) for count in plan.takes]
    arrived = take(plan.adds)
    if plan.adding and plan.placed:
        take(1)
    take(plan.after)
    given_ref = take(1)[0] if plan.near == "give" else None
    kept_ref = take(1)[0] if plan.ahead else None
    outs = [take(2 if plan.split else 1) for _ in plan.ways]
    targets = [take(task.count) for task in plan.tasks]
    result_ref = take(1)[0] if plan.adding else None
    piece_ref = take(1)[0] if plan.later else None
    if plan.part:
        slot, _, width = plan.part
        base = slot * stride
        point = table_ref[base].astype(jnp.int32)

        def load_rows(point, into_ref, load_sems):
            copies = []
            for distance in range(1, fold + 1):
                way = distance % fold
                target = lax.rem(place + way, fold)
                for part in range(2):
                    for level in range(depth):
                        first = pl.multiple_of((level * fold + target) * rows, rows)
                        copy = pltpu.make_async_copy(
                            bands_ref.at[point, part, pl.ds(first, rows), :],
                            into_ref.at[way, part, pl.ds(level * rows, rows), :],
                            load_sems.at[way, part, level],
                        )
                        copy.start()
                        copies.append((way, part, copy))
            return copies

        own_ref = bands_ref
        own, ahead = [], []
        if plan.rows != "held":
            own_ref, own_sems = take(2)
            own = load_rows(point, own_ref, own_sems)
        if plan.ahead:
            next_point = table_ref[base + stride].astype(jnp.int32)
            ahead = load_rows(next_point, kept_ref, take(1)[0])
    if plan.later:
        piece_buf, piece_sems = take(2)
        later_slot, later_start, later_width = plan.later
        loads = [
            pltpu.make_async_copy(
                bands_ref.at[later_slot, part, pl.ds(later_start, later_width), :],
                piece_buf.at[part],
                piece_sems.at[0, part],
            )
            for part in range(2)
        ]
        stores = [
            pltpu.make_async_copy(piece_buf.at[part], piece_ref.at[part], piece_sems.at[1, part])
            for part in range(2)
        ]
        for copy in loads:
            copy.start()
    if plan.adding:
        sum_buf, placed_sem = take(2)
        add_slot, add_start, pieces = plan.adding
        for start, span, terms in pieces:
            total = 0.0
            for index, column in terms:
                total += arrived[index][0, :, column : column + 2 * span].astype(jnp.float32)
            put_sum(sum_buf, start - add_start, total)
        add_point = table_ref[add_slot * stride].astype(jnp.int32)
        columns = pl.ds(add_start, sum_buf.shape[2])
        placing = pltpu.make_async_copy(
            sum_buf, result_ref.at[:, add_point, :, columns], placed_sem
        )
        placing.start()
    for task, arrays, outputs in zip(plan.tasks, sources, targets):
        groups = [arrays[i : i + task.each] for i in range(0, len(arrays), task.each)]
        bit = lax.rem(lax.div(outer, 1 << task.bit(depth)), 2)
        filled = [(out_ref, 0) for out_ref in outputs]
        if plan.joined and not task.direct:
            filled.append((targets[0][JOINT], 2 * plan.tasks[0].batch[0][2]))
        for index, (out_ref, shift) in enumerate(filled):
            for level in range(out_ref.shape[0]):
                if task.direct:
                    source = partner(outer, index)
                elif task.far_first:
                    source = (1 - bit if index else bit) * out_ref.shape[0] + level
                else:
                    source = 2 * level + (1 - bit if index else bit)
                column = shift
                for group in groups:
                    total = summed(group, source)
                    columns = slice(column, column + total.shape[1])
                    out_ref[level, :, columns] = total.astype(out_ref.dtype)
                    column += total.shape[1]
    if plan.part:
        near_ref = phased_ref
        if plan.near != "use":
            near_ref = given_ref if plan.near == "give" else take(1)[0]
            near_into(near_ref, phased_ref, table_ref, base, planes)
        dims = (((1,), (1,)), ((), ()))
        points = near_ref.shape[1]
        run = points // 2 if width <= SPLIT else points
        for way, out_refs in zip(plan.ways, outs):
            kind = out_refs[0].dtype
            of_both = []
            for part in range(2):
                for copy in [copy for *which, copy in own if which == [way, part]]:
                    copy.wait()
                products = [
                    lax.dot_general(
                        own_ref[way, part, :, pl.ds(first, run)],
                        near_ref[:, pl.ds(first, run)],
                        dims,
                        preferred_element_type=jnp.float32,
                    )
                    for first in range(0, points, run)
                ]
                of_both.append(sum(products[1:], products[0]))
            of_re, of_im = of_both
            sides = (
                (of_re[:, :width] + of_im[:, width:]).astype(kind),
                (of_re[:, width:] - of_im[:, :width]).astype(kind),
            )
            for level in range(depth):
                lines = slice(level * rows, (level + 1) * rows)
                for side, values in enumerate(sides):
                    if plan.split:
                        out_refs[side][level] = values[lines]
                    else:
                        columns = slice(side * width, (side + 1) * width)
                        out_refs[0][level, :, columns] = values[lines]
            if plan.later and way == plan.ways[0]:
                for load, store in zip(loads, stores):
                    load.wait()
                    store.start()
        for _, _, copy in ahead:
            copy.wait()
    if plan.adding:
        placing.wait()
    if plan.later:
        for store in stores:
            store.wait()


def partner(outer, distance):
    low, high = lax.rem(outer, 2), lax.rem(lax.div(outer, 2), 2)
    low = 1 - low if distance % 2 else low
    high = 1 - high if distance // 2 else high
    return outer - lax.rem(outer, 4) + 2 * high + low


def summed(arrays, level):
    total = arrays[0][level].astype(jnp.float32)
    rest = [array[level].astype(jnp.float32) for array in arrays[1:]]
    while rest:
        more = rest.pop(0)
        if more.shape != total.shape:
            more = jnp.concatenate([more, rest.pop(0)], axis=1)
        total = total + more
    return total


class Task(NamedTuple):
    batch: tuple
    stage: int
    direct: bool
    each: int
    count: int
    far_first: bool = False

    def bit(self, depth):
        last = depth.bit_length() - 2
        return last - self.stage if self.far_first else self.stage


class Plan(NamedTuple):
    shape: tuple
    fold: int
    depth: int
    part: tuple
    ways: tuple
    near: str
    rows: str
    ahead: bool
    tasks: tuple
    takes: tuple
    adding: tuple
    adds: int
    joined: bool
    placed: bool
    later: tuple
    split: bool
    after: int


def step(plan, table, bands, phased, sources, arrived, result, after):
    rows, _, _, nbands = plan.shape
    fold, depth = plan.fold, plan.depth
    points = bands.shape[-1]
    vmem = pl.BlockSpec(memory_space=pltpu.VMEM)
    hbm = pl.BlockSpec(memory_space=pltpu.HBM)
    operands, in_specs = [table], [pl.BlockSpec(memory_space=pltpu.SMEM)]
    out_shape, out_specs, scratch, aliases = [], [], [], {}

    def kind(index):
        return jnp.bfloat16 if index else jnp.float32

    if plan.part:
        width = plan.part[2]
        operands += [bands, phased]
        in_specs += [vmem if plan.rows == "held" else hbm, vmem]
        kept = (fold, 2, depth * rows, points)
        if plan.near == "give":
            out_shape.append(jax.ShapeDtypeStruct((2 * width, points), jnp.bfloat16))
        if plan.ahead:
            out_shape.append(jax.ShapeDtypeStruct(kept, jnp.bfloat16))
        out_shape += [
            jax.ShapeDtypeStruct((depth, rows, width if plan.split else 2 * width), kind(way))
            for way in plan.ways
            for _ in range(2 if plan.split else 1)
        ]
        if plan.rows != "held":
            scratch.append(pltpu.VMEM(kept, jnp.bfloat16))
            scratch.append(pltpu.SemaphoreType.DMA((fold, 2, depth)))
        if plan.ahead:
            scratch.append(pltpu.SemaphoreType.DMA((fold, 2, depth)))
    for arrays in [*sources, arrived]:
        operands += arrays
        in_specs += [vmem] * len(arrays)
    for task in plan.tasks:
        wide = sum(2 * width for _, _, width in task.batch)
        levels = 1 if task.direct else depth >> (task.stage + 1)
        extra = 2 * plan.tasks[1].batch[0][2] if plan.joined and task.direct else 0
        for i in range(task.count):
            columns = wide + extra if i == JOINT else wide
            out_shape.append(jax.ShapeDtypeStruct((levels, rows, columns), kind(i)))
    out_specs += [vmem] * len(out_shape)
    if plan.later:
        scratch += [
            pltpu.VMEM((2, plan.later[2], points), bands.dtype),
            pltpu.SemaphoreType.DMA((2, 2)),
        ]
    if plan.adding:
        if plan.placed:
            aliases = {len(operands): len(out_shape)}
            operands.append(result)
            in_specs.append(hbm)
        out_shape.append(jax.ShapeDtypeStruct(plan.shape, jnp.float32))
        out_specs.append(hbm)
        lanes = sum(span for _, span, _ in plan.adding[2])
        scratch += [pltpu.VMEM((rows, 2, lanes), jnp.float32), pltpu.SemaphoreType.DMA]
    operands += after
    in_specs += [pl.BlockSpec(memory_space=pl.ANY)] * len(after)
    if plan.later:
        out_shape.append(jax.ShapeDtypeStruct((2, plan.later[2], points), bands.dtype))
        out_specs.append(hbm)
    if plan.near == "make":
        scratch.append(pltpu.VMEM((2 * width, points), jnp.bfloat16))
    outs = list(
        pl.pallas_call(
            functools.partial(step_kernel, plan),
            in_specs=in_specs,
            out_specs=out_specs,
            scratch_shapes=scratch,
            out_shape=out_shape,
            input_output_aliases=aliases,
            compiler_params=pltpu.CompilerParams(
                vmem_limit_bytes=VMEM_BYTES if plan.part and plan.rows != "held" else LEAN_BYTES
            ),
            cost_estimate=pl.CostEstimate(flops=1000, bytes_accessed=1000, transcendentals=0),
            name="step",
        )(*operands)
    )
    piece = outs.pop() if plan.later else None
    result = outs.pop() if plan.adding else result
    near = outs.pop(0) if plan.near == "give" else None
    kept = outs.pop(0) if plan.ahead else None
    count = len(plan.ways) * (2 if plan.split else 1)
    terms, handed = outs[:count], outs[count:]
    sends = []
    for task in plan.tasks:
        sends.append(handed[: task.count])
        handed = handed[task.count :]
    return terms, near, kept, sends, result, piece


def cuts(nbands, first):
    eighth = nbands // 8
    widths = [4 * eighth, 4 * eighth] if first else [3 * eighth, 3 * eighth, 2 * eighth]
    starts = [sum(widths[:i]) for i in range(len(widths))]
    return list(zip(starts, widths))


def schedule(parts, fold, depth):
    every, others = tuple(range(fold)), tuple(range(1, fold))
    count = len(parts)
    kernels = []
    waiting, halved, crossed = [], [], []
    for index, part in enumerate(parts):
        ready = ready_parts(waiting)
        waiting = waiting[len(ready) :]
        final = index == count - 1
        tasks = []
        if halved and not final:
            tasks.append(Task(tuple(halved), 1, False, 2, 2))
            waiting += halved
        if crossed:
            tasks.append(Task(tuple(crossed), 0, False, fold, 2))
        if index >= count - 3:
            kernels.append((part, others, "give", tuple(tasks), ready))
            kernels.append((part, every[:1], "use", (), ()))
        else:
            kernels.append((part, every, "make", tuple(tasks), ready))
        if final:
            break
        halved, crossed = crossed, [part]
        if index in (0, count - 3, count - 2):
            task = Task((part,), 0, False, fold, 2, index == count - 2)
            kernels.append((None, (), "", (task,), ()))
            halved, crossed = halved + crossed, []
    tasks = (
        Task((parts[-1],), 0, True, 2 * fold - 1, depth),
        Task(tuple(halved), 1, False, 2, 1, True),
    )
    kernels.append((None, (), "", tasks, ()))
    kernels.append((None, (), "", (), tuple(waiting) + tuple(halved) + (parts[-1],)))
    return kernels


def ready_parts(waiting):
    total = 0
    for count, (slot, _, width) in enumerate(waiting, 1):
        total += width
        if slot != waiting[0][0]:
            break
        if total % LANES == 0:
            return tuple(waiting[:count])
    return ()


def body(bands, nbr_slot, gshift):
    grid_index = lax.axis_index("ga")
    grid_count = lax.axis_size("ga")
    k_dev, _, nbands, points = bands.shape
    rows = nbands // grid_count
    own_planes = points // PLANE
    total_planes = own_planes * grid_count
    planes = grid_index * own_planes + jnp.arange(own_planes, dtype=jnp.int32)
    slots = jnp.arange(k_dev, dtype=jnp.int32)
    chosen = nbr_slot[None, :] == slots[:, None]
    order = jnp.sum(jnp.where(chosen, slots[None, :], 0), axis=1)
    shifts = jnp.sum(jnp.where(chosen, gshift[None, :], 0), axis=1)
    turns = (1 + NKB * shifts[:, None]) * planes[None, :] % (NKB * total_planes)
    angle = 2.0 * math.pi / (NKB * total_planes) * turns.astype(jnp.float32)
    columns = [order[:, None].astype(jnp.float32), jnp.cos(angle), jnp.sin(angle)]
    table = jnp.concatenate(columns, axis=1).reshape(-1)
    table = jnp.append(table, grid_index.astype(jnp.float32))
    parts = []
    for slot in range(k_dev):
        for start, width in cuts(nbands, slot == 0):
            parts.append((slot, start, width))
    theres = []
    piece = None
    for slot, start, width in parts[:AHEAD]:
        piece = piece_of(slot, start, width, bands, [] if piece is None else [piece])
        theres.append(shifted(piece, "ka", -1))
    shape = (rows, k_dev, 2, nbands)
    depth = min(OUTER, grid_count)
    fold = grid_count // depth
    held = {}
    near, kept, result = None, None, None
    for part, ways, phase, tasks, adds in schedule(parts, fold, depth):
        place = parts.index(part) if part else len(parts)
        later = parts[place + AHEAD] if place + AHEAD < len(parts) and phase != "use" else None
        sources = [
            [array for done in task.batch for array, _ in held[(done,)]] for task in tasks
        ]
        arrived, pieces = [], []
        for done in adds:
            batch = max((key for key in held if done in key), key=len)
            column = sum(2 * width for _, _, width in batch[: batch.index(done)])
            terms = [(len(arrived) + i, first + column) for i, (_, first) in enumerate(held[batch])]
            arrived += [array for array, _ in held[batch]]
            pieces.append((done[1], done[2], tuple(terms)))
        adding = (adds[0][0], adds[0][1], tuple(pieces)) if adds else ()
        split = place == len(parts) - 1 and phase == "give"
        after = order_by if split else []
        plan = Plan(
            shape,
            fold,
            depth,
            part,
            ways,
            phase,
            "load" if kept is None else "held",
            place == len(parts) - 4,
            tasks,
            tuple(len(arrays) for arrays in sources),
            adding,
            len(arrived),
            len(tasks) > 1 and tasks[0].direct,
            result is not None,
            later,
            split,
            len(after),
        )
        phased = near if phase == "use" else theres[place] if part else None
        terms, near, found, sends, result, piece = step(
            plan,
            table,
            bands if kept is None else kept,
            phased,
            sources,
            arrived,
            result,
            after,
        )
        order_by = sends[0][:1] if sends else []
        kept = found if kept is None else kept
        if later:
            theres.append(shifted(piece, "ka", -1))
        for way, array in zip([way for way in ways for _ in range(1 + split)], terms):
            array = shifted(array, "ga", way, fold, True) if way else array
            entries = held.setdefault((part,), [])
            entries.insert(len(entries) if way else 0, (array, 0))
        for task, arrays in zip(tasks, sends):
            steps = range(1, depth) if task.direct else [1 << task.bit(depth)]
            moved = [swapped(array, "ga", fold * i) for array, i in zip(arrays[1:], steps)]
            held[task.batch] = [(array, 0) for array in [arrays[0], *reversed(moved)]]
        if plan.joined:
            joint = held[tasks[0].batch][depth - JOINT][0]
            held[tasks[1].batch].append((joint, 2 * tasks[0].batch[0][2]))
    return result


def solution(mesh):
    placed = (P("ka", None, None, "ga"), P("ka"), P("ka"))
    return jax.shard_map(
        body, mesh=mesh, in_specs=placed, out_specs=P("ga", "ka", None, None), check_vma=False
    )
```

```python
import functools
import math
from typing import NamedTuple

import jax
import jax.numpy as jnp
from jax import lax
from jax.experimental import pallas as pl
from jax.experimental.pallas import tpu as pltpu
from jax.sharding import PartitionSpec as P

NKB = 4
PLANE = 1024
STRIP = 32
DEPTH = 512
AHEAD = 4
OUTER = 4
SPLIT = 128
JOINT = 2
LANES = 128
BLOCK = 256
VMEM_BYTES = 44 * 1024 * 1024
LEAN_BYTES = 32 * 1024 * 1024


def shifted(block, axis, distance, fold=1, inner=False):
    count = lax.axis_size(axis)
    route = []
    for i in range(count):
        outer, place = divmod(i, fold)
        if inner:
            route.append((i, outer * fold + (place + distance) % fold))
        else:
            route.append((i, (outer + distance) % (count // fold) * fold + place))
    return lax.ppermute(block, axis, route)


def swapped(block, axis, distance):
    count = lax.axis_size(axis)
    return lax.ppermute(block, axis, [(i, i ^ distance) for i in range(count)])


def first_kernel(slot, start, bands_ref, out_ref, sems):
    width = out_ref.shape[1]
    loads = [
        pltpu.make_async_copy(
            bands_ref.at[slot, part, pl.ds(start, width), :], out_ref.at[part], sems.at[part]
        )
        for part in range(2)
    ]
    for load in loads:
        load.start()
    for load in loads:
        load.wait()


def piece_kernel(slot, start, bands_ref, *rest):
    out_ref, piece_buf, sems = rest[-3:]
    width = piece_buf.shape[1]
    rows = pl.ds(start, width)
    loads = [
        pltpu.make_async_copy(bands_ref.at[slot, part, rows, :], piece_buf.at[part], sems.at[0, part])
        for part in range(2)
    ]
    stores = [
        pltpu.make_async_copy(piece_buf.at[part], out_ref.at[part], sems.at[1, part])
        for part in range(2)
    ]
    for load in loads:
        load.start()
    for load, store in zip(loads, stores):
        load.wait()
        store.start()
    for store in stores:
        store.wait()


def piece_of(slot, start, width, bands, after):
    points = bands.shape[3]
    hbm = pl.BlockSpec(memory_space=pltpu.HBM)
    scratch = [pltpu.VMEM((2, width, points), bands.dtype), pltpu.SemaphoreType.DMA((2, 2))]
    return pl.pallas_call(
        functools.partial(piece_kernel if after else first_kernel, slot, start),
        in_specs=[hbm] * (1 + len(after)),
        out_specs=hbm if after else pl.BlockSpec(memory_space=pltpu.VMEM),
        scratch_shapes=scratch if after else [pltpu.SemaphoreType.DMA((2,))],
        out_shape=jax.ShapeDtypeStruct((2, width, points), bands.dtype),
        compiler_params=pltpu.CompilerParams(vmem_limit_bytes=VMEM_BYTES),
        cost_estimate=pl.CostEstimate(flops=1000, bytes_accessed=1000, transcendentals=0),
        name="piece_of",
    )(bands, *after)


def near_into(near_buf, there_ref, table_ref, base, planes):
    width, points = there_ref.shape[1:]

    @pl.loop(0, width // STRIP)
    def _(strip):
        rows = pl.ds(strip * STRIP, STRIP)
        mirror = pl.ds(width + strip * STRIP, STRIP)
        for start in range(0, points, DEPTH):
            plane = start // PLANE
            cosine = table_ref[base + 1 + plane]
            sine = table_ref[base + 1 + planes + plane]
            columns = pl.ds(start, DEPTH)
            real_part = there_ref[0, rows, columns].astype(jnp.float32)
            imag_part = there_ref[1, rows, columns].astype(jnp.float32)
            near_re = real_part * cosine + imag_part * sine
            near_im = imag_part * cosine - real_part * sine
            near_buf[rows, columns] = near_re.astype(jnp.bfloat16)
            near_buf[mirror, columns] = near_im.astype(jnp.bfloat16)


def put_sum(sum_buf, lane, total):
    width = total.shape[1] // 2
    sum_buf[:, 0, lane : lane + width] = total[:, :width]
    sum_buf[:, 1, lane : lane + width] = total[:, width:]


def step_kernel(plan, table_ref, *refs):
    rows, k_dev, _, nbands = plan.shape
    fold, depth = plan.fold, plan.depth
    refs = list(refs)

    def take(count):
        taken = refs[:count]
        del refs[:count]
        return taken

    stride = (table_ref.shape[0] - 1) // k_dev
    planes = (stride - 1) // 2
    me = table_ref[k_dev * stride].astype(jnp.int32)
    place, outer = lax.rem(me, fold), lax.div(me, fold)
    if plan.part:
        bands_ref, phased_ref = take(2)
    sources = [take(count) for count in plan.takes]
    arrived = take(plan.adds)
    if plan.adding and plan.placed:
        take(1)
    take(plan.after)
    given_ref = take(1)[0] if plan.near == "give" else None
    kept_ref = take(1)[0] if plan.ahead else None
    outs = [take(2 if plan.split else 1) for _ in plan.ways]
    targets = [take(task.count) for task in plan.tasks]
    result_ref = take(1)[0] if plan.adding else None
    piece_ref = take(1)[0] if plan.later else None
    if plan.part:
        slot, _, width = plan.part
        base = slot * stride
        point = table_ref[base].astype(jnp.int32)

        def load_rows(point, into_ref, load_sems):
            copies = []
            for distance in range(1, fold + 1):
                way = distance % fold
                target = lax.rem(place + way, fold)
                for part in range(2):
                    for level in range(depth):
                        first = pl.multiple_of((level * fold + target) * rows, rows)
                        copy = pltpu.make_async_copy(
                            bands_ref.at[point, part, pl.ds(first, rows), :],
                            into_ref.at[way, part, pl.ds(level * rows, rows), :],
                            load_sems.at[way, part, level],
                        )
                        copy.start()
                        copies.append((way, part, copy))
            return copies

        own_ref = bands_ref
        own, ahead = [], []
        if plan.rows != "held":
            own_ref, own_sems = take(2)
            own = load_rows(point, own_ref, own_sems)
        if plan.ahead:
            next_point = table_ref[base + stride].astype(jnp.int32)
            ahead = load_rows(next_point, kept_ref, take(1)[0])
    if plan.later:
        piece_buf, piece_sems = take(2)
        later_slot, later_start, later_width = plan.later
        loads = [
            pltpu.make_async_copy(
                bands_ref.at[later_slot, part, pl.ds(later_start, later_width), :],
                piece_buf.at[part],
                piece_sems.at[0, part],
            )
            for part in range(2)
        ]
        stores = [
            pltpu.make_async_copy(piece_buf.at[part], piece_ref.at[part], piece_sems.at[1, part])
            for part in range(2)
        ]
        for copy in loads:
            copy.start()
    if plan.adding:
        sum_buf, placed_sem = take(2)
        add_slot, add_start, pieces = plan.adding
        for start, span, terms in pieces:
            total = 0.0
            for index, column in terms:
                total += arrived[index][0, :, column : column + 2 * span].astype(jnp.float32)
            put_sum(sum_buf, start - add_start, total)
        add_point = table_ref[add_slot * stride].astype(jnp.int32)
        columns = pl.ds(add_start, sum_buf.shape[2])
        placing = pltpu.make_async_copy(
            sum_buf, result_ref.at[:, add_point, :, columns], placed_sem
        )
        placing.start()
    for task, arrays, outputs in zip(plan.tasks, sources, targets):
        groups = [arrays[i : i + task.each] for i in range(0, len(arrays), task.each)]
        bit = lax.rem(lax.div(outer, 1 << task.stage), 2)
        filled = [(out_ref, 0) for out_ref in outputs]
        if plan.joined and not task.direct:
            filled.append((targets[0][JOINT], 2 * plan.tasks[0].batch[0][2]))
        for index, (out_ref, shift) in enumerate(filled):
            for level in range(out_ref.shape[0]):
                if task.direct:
                    source = partner(outer, index)
                else:
                    source = 2 * level + (1 - bit if index else bit)
                column = shift
                for group in groups:
                    total = summed(group, source)
                    columns = slice(column, column + total.shape[1])
                    out_ref[level, :, columns] = total.astype(out_ref.dtype)
                    column += total.shape[1]
    if plan.part:
        near_ref = phased_ref
        if plan.near != "use":
            near_ref = given_ref if plan.near == "give" else take(1)[0]
            near_into(near_ref, phased_ref, table_ref, base, planes)
        dims = (((1,), (1,)), ((), ()))
        points = near_ref.shape[1]
        run = points // 2 if width <= SPLIT else points
        for way, out_refs in zip(plan.ways, outs):
            kind = out_refs[0].dtype
            of_both = []
            for part in range(2):
                for copy in [copy for *which, copy in own if which == [way, part]]:
                    copy.wait()
                products = [
                    lax.dot_general(
                        own_ref[way, part, :, pl.ds(first, run)],
                        near_ref[:, pl.ds(first, run)],
                        dims,
                        preferred_element_type=jnp.float32,
                    )
                    for first in range(0, points, run)
                ]
                of_both.append(sum(products[1:], products[0]))
            of_re, of_im = of_both
            sides = (
                (of_re[:, :width] + of_im[:, width:]).astype(kind),
                (of_re[:, width:] - of_im[:, :width]).astype(kind),
            )
            for level in range(depth):
                lines = slice(level * rows, (level + 1) * rows)
                for side, values in enumerate(sides):
                    if plan.split:
                        out_refs[side][level] = values[lines]
                    else:
                        columns = slice(side * width, (side + 1) * width)
                        out_refs[0][level, :, columns] = values[lines]
            if plan.later and way == plan.ways[0]:
                for load, store in zip(loads, stores):
                    load.wait()
                    store.start()
        for _, _, copy in ahead:
            copy.wait()
    if plan.adding:
        placing.wait()
    if plan.later:
        for store in stores:
            store.wait()


def partner(outer, distance):
    low, high = lax.rem(outer, 2), lax.rem(lax.div(outer, 2), 2)
    low = 1 - low if distance % 2 else low
    high = 1 - high if distance // 2 else high
    return outer - lax.rem(outer, 4) + 2 * high + low


def summed(arrays, level):
    total = arrays[0][level].astype(jnp.float32)
    rest = [array[level].astype(jnp.float32) for array in arrays[1:]]
    while rest:
        more = rest.pop(0)
        if more.shape != total.shape:
            more = jnp.concatenate([more, rest.pop(0)], axis=1)
        total = total + more
    return total


class Task(NamedTuple):
    batch: tuple
    stage: int
    direct: bool
    each: int
    count: int


class Plan(NamedTuple):
    shape: tuple
    fold: int
    depth: int
    part: tuple
    ways: tuple
    near: str
    rows: str
    ahead: bool
    tasks: tuple
    takes: tuple
    adding: tuple
    adds: int
    joined: bool
    placed: bool
    later: tuple
    split: bool
    after: int


def step(plan, table, bands, phased, sources, arrived, result, after):
    rows, _, _, nbands = plan.shape
    fold, depth = plan.fold, plan.depth
    points = bands.shape[-1]
    vmem = pl.BlockSpec(memory_space=pltpu.VMEM)
    hbm = pl.BlockSpec(memory_space=pltpu.HBM)
    operands, in_specs = [table], [pl.BlockSpec(memory_space=pltpu.SMEM)]
    out_shape, out_specs, scratch, aliases = [], [], [], {}

    def kind(index):
        return jnp.bfloat16 if index else jnp.float32

    if plan.part:
        width = plan.part[2]
        operands += [bands, phased]
        in_specs += [vmem if plan.rows == "held" else hbm, vmem]
        kept = (fold, 2, depth * rows, points)
        if plan.near == "give":
            out_shape.append(jax.ShapeDtypeStruct((2 * width, points), jnp.bfloat16))
        if plan.ahead:
            out_shape.append(jax.ShapeDtypeStruct(kept, jnp.bfloat16))
        out_shape += [
            jax.ShapeDtypeStruct((depth, rows, width if plan.split else 2 * width), kind(way))
            for way in plan.ways
            for _ in range(2 if plan.split else 1)
        ]
        if plan.rows != "held":
            scratch.append(pltpu.VMEM(kept, jnp.bfloat16))
            scratch.append(pltpu.SemaphoreType.DMA((fold, 2, depth)))
        if plan.ahead:
            scratch.append(pltpu.SemaphoreType.DMA((fold, 2, depth)))
    for arrays in [*sources, arrived]:
        operands += arrays
        in_specs += [vmem] * len(arrays)
    for task in plan.tasks:
        wide = sum(2 * width for _, _, width in task.batch)
        levels = 1 if task.direct else depth >> (task.stage + 1)
        extra = 2 * plan.tasks[1].batch[0][2] if plan.joined and task.direct else 0
        for i in range(task.count):
            columns = wide + extra if i == JOINT else wide
            out_shape.append(jax.ShapeDtypeStruct((levels, rows, columns), kind(i)))
    out_specs += [vmem] * len(out_shape)
    if plan.later:
        scratch += [
            pltpu.VMEM((2, plan.later[2], points), bands.dtype),
            pltpu.SemaphoreType.DMA((2, 2)),
        ]
    if plan.adding:
        if plan.placed:
            aliases = {len(operands): len(out_shape)}
            operands.append(result)
            in_specs.append(hbm)
        out_shape.append(jax.ShapeDtypeStruct(plan.shape, jnp.float32))
        out_specs.append(hbm)
        lanes = sum(span for _, span, _ in plan.adding[2])
        scratch += [pltpu.VMEM((rows, 2, lanes), jnp.float32), pltpu.SemaphoreType.DMA]
    operands += after
    in_specs += [pl.BlockSpec(memory_space=pl.ANY)] * len(after)
    if plan.later:
        out_shape.append(jax.ShapeDtypeStruct((2, plan.later[2], points), bands.dtype))
        out_specs.append(hbm)
    if plan.near == "make":
        scratch.append(pltpu.VMEM((2 * width, points), jnp.bfloat16))
    outs = list(
        pl.pallas_call(
            functools.partial(step_kernel, plan),
            in_specs=in_specs,
            out_specs=out_specs,
            scratch_shapes=scratch,
            out_shape=out_shape,
            input_output_aliases=aliases,
            compiler_params=pltpu.CompilerParams(
                vmem_limit_bytes=VMEM_BYTES if plan.part and plan.rows != "held" else LEAN_BYTES
            ),
            cost_estimate=pl.CostEstimate(flops=1000, bytes_accessed=1000, transcendentals=0),
            name="step",
        )(*operands)
    )
    piece = outs.pop() if plan.later else None
    result = outs.pop() if plan.adding else result
    near = outs.pop(0) if plan.near == "give" else None
    kept = outs.pop(0) if plan.ahead else None
    count = len(plan.ways) * (2 if plan.split else 1)
    terms, handed = outs[:count], outs[count:]
    sends = []
    for task in plan.tasks:
        sends.append(handed[: task.count])
        handed = handed[task.count :]
    return terms, near, kept, sends, result, piece


def cuts(nbands, first):
    eighth = nbands // 8
    widths = [4 * eighth, 4 * eighth] if first else [3 * eighth, 3 * eighth, 2 * eighth]
    starts = [sum(widths[:i]) for i in range(len(widths))]
    return list(zip(starts, widths))


def schedule(parts, fold, depth):
    every, others = tuple(range(fold)), tuple(range(1, fold))
    count = len(parts)
    kernels = []
    waiting, halved, crossed = [], [], []
    for index, part in enumerate(parts):
        ready = ready_parts(waiting)
        waiting = waiting[len(ready) :]
        final = index == count - 1
        tasks = []
        if halved and not final:
            tasks.append(Task(tuple(halved), 1, False, 2, 2))
            waiting += halved
        if crossed:
            tasks.append(Task(tuple(crossed), 0, False, fold, 2))
        if index >= count - 3:
            kernels.append((part, others, "give", tuple(tasks), ready))
            kernels.append((part, every[:1], "use", (), ()))
        else:
            kernels.append((part, every, "make", tuple(tasks), ready))
        if final:
            break
        halved, crossed = crossed, [part]
        if index in (0, count - 3, count - 2):
            kernels.append((None, (), "", (Task((part,), 0, False, fold, 2),), ()))
            halved, crossed = halved + crossed, []
    tasks = (
        Task((parts[-1],), 0, True, 2 * fold - 1, depth),
        Task(tuple(halved), 1, False, 2, 1),
    )
    kernels.append((None, (), "", tasks, ()))
    kernels.append((None, (), "", (), tuple(waiting) + tuple(halved) + (parts[-1],)))
    return kernels


def ready_parts(waiting):
    total = 0
    for count, (slot, _, width) in enumerate(waiting, 1):
        total += width
        if slot != waiting[0][0]:
            break
        if total % LANES == 0:
            return tuple(waiting[:count])
    return ()


def body(bands, nbr_slot, gshift):
    grid_index = lax.axis_index("ga")
    grid_count = lax.axis_size("ga")
    k_dev, _, nbands, points = bands.shape
    rows = nbands // grid_count
    own_planes = points // PLANE
    total_planes = own_planes * grid_count
    planes = grid_index * own_planes + jnp.arange(own_planes, dtype=jnp.int32)
    slots = jnp.arange(k_dev, dtype=jnp.int32)
    chosen = nbr_slot[None, :] == slots[:, None]
    order = jnp.sum(jnp.where(chosen, slots[None, :], 0), axis=1)
    shifts = jnp.sum(jnp.where(chosen, gshift[None, :], 0), axis=1)
    turns = (1 + NKB * shifts[:, None]) * planes[None, :] % (NKB * total_planes)
    angle = 2.0 * math.pi / (NKB * total_planes) * turns.astype(jnp.float32)
    columns = [order[:, None].astype(jnp.float32), jnp.cos(angle), jnp.sin(angle)]
    table = jnp.concatenate(columns, axis=1).reshape(-1)
    table = jnp.append(table, grid_index.astype(jnp.float32))
    parts = []
    for slot in range(k_dev):
        for start, width in cuts(nbands, slot == 0):
            parts.append((slot, start, width))
    theres = []
    piece = None
    for slot, start, width in parts[:AHEAD]:
        piece = piece_of(slot, start, width, bands, [] if piece is None else [piece])
        theres.append(shifted(piece, "ka", -1))
    shape = (rows, k_dev, 2, nbands)
    depth = min(OUTER, grid_count)
    fold = grid_count // depth
    held = {}
    near, kept, result = None, None, None
    for part, ways, phase, tasks, adds in schedule(parts, fold, depth):
        place = parts.index(part) if part else len(parts)
        later = parts[place + AHEAD] if place + AHEAD < len(parts) and phase != "use" else None
        sources = [
            [array for done in task.batch for array, _ in held[(done,)]] for task in tasks
        ]
        arrived, pieces = [], []
        for done in adds:
            batch = max((key for key in held if done in key), key=len)
            column = sum(2 * width for _, _, width in batch[: batch.index(done)])
            terms = [(len(arrived) + i, first + column) for i, (_, first) in enumerate(held[batch])]
            arrived += [array for array, _ in held[batch]]
            pieces.append((done[1], done[2], tuple(terms)))
        adding = (adds[0][0], adds[0][1], tuple(pieces)) if adds else ()
        split = place == len(parts) - 1 and phase == "give"
        after = order_by if split else []
        plan = Plan(
            shape,
            fold,
            depth,
            part,
            ways,
            phase,
            "load" if kept is None else "held",
            place == len(parts) - 4,
            tasks,
            tuple(len(arrays) for arrays in sources),
            adding,
            len(arrived),
            len(tasks) > 1 and tasks[0].direct,
            result is not None,
            later,
            split,
            len(after),
        )
        phased = near if phase == "use" else theres[place] if part else None
        terms, near, found, sends, result, piece = step(
            plan,
            table,
            bands if kept is None else kept,
            phased,
            sources,
            arrived,
            result,
            after,
        )
        order_by = sends[0][:1] if sends else []
        kept = found if kept is None else kept
        if later:
            theres.append(shifted(piece, "ka", -1))
        for way, array in zip([way for way in ways for _ in range(1 + split)], terms):
            array = shifted(array, "ga", way, fold, True) if way else array
            entries = held.setdefault((part,), [])
            entries.insert(len(entries) if way else 0, (array, 0))
        for task, arrays in zip(tasks, sends):
            steps = range(1, depth) if task.direct else [1 << task.stage]
            moved = [swapped(array, "ga", fold * i) for array, i in zip(arrays[1:], steps)]
            held[task.batch] = [(array, 0) for array in [arrays[0], *reversed(moved)]]
        if plan.joined:
            joint = held[tasks[0].batch][JOINT][0]
            held[tasks[1].batch].append((joint, 2 * tasks[0].batch[0][2]))
    return result


def solution(mesh):
    placed = (P("ka", None, None, "ga"), P("ka"), P("ka"))
    return jax.shard_map(
        body, mesh=mesh, in_specs=placed, out_specs=P("ga", "ka", None, None), check_vma=False
    )
```

```python
import functools
import math
from typing import NamedTuple

import jax
import jax.numpy as jnp
from jax import lax
from jax.experimental import pallas as pl
from jax.experimental.pallas import tpu as pltpu
from jax.sharding import PartitionSpec as P

NKB = 4
PLANE = 1024
STRIP = 32
DEPTH = 512
AHEAD = 3
OUTER = 4
SPLIT = 128
JOINT = 2
LANES = 128
BLOCK = 256
VMEM_BYTES = 45 * 1024 * 1024
LEAN_BYTES = 32 * 1024 * 1024


def shifted(block, axis, distance, fold=1, inner=False):
    count = lax.axis_size(axis)
    route = []
    for i in range(count):
        outer, place = divmod(i, fold)
        if inner:
            route.append((i, outer * fold + (place + distance) % fold))
        else:
            route.append((i, (outer + distance) % (count // fold) * fold + place))
    return lax.ppermute(block, axis, route)


def swapped(block, axis, distance):
    count = lax.axis_size(axis)
    return lax.ppermute(block, axis, [(i, i ^ distance) for i in range(count)])


def first_kernel(slot, start, bands_ref, out_ref, sems):
    width = out_ref.shape[1]
    loads = [
        pltpu.make_async_copy(
            bands_ref.at[slot, part, pl.ds(start, width), :], out_ref.at[part], sems.at[part]
        )
        for part in range(2)
    ]
    for load in loads:
        load.start()
    for load in loads:
        load.wait()


def piece_kernel(slot, start, bands_ref, *rest):
    out_ref, piece_buf, sems = rest[-3:]
    width = piece_buf.shape[1]
    rows = pl.ds(start, width)
    loads = [
        pltpu.make_async_copy(bands_ref.at[slot, part, rows, :], piece_buf.at[part], sems.at[0, part])
        for part in range(2)
    ]
    stores = [
        pltpu.make_async_copy(piece_buf.at[part], out_ref.at[part], sems.at[1, part])
        for part in range(2)
    ]
    for load in loads:
        load.start()
    for load, store in zip(loads, stores):
        load.wait()
        store.start()
    for store in stores:
        store.wait()


def piece_of(slot, start, width, bands, after):
    points = bands.shape[3]
    hbm = pl.BlockSpec(memory_space=pltpu.HBM)
    scratch = [pltpu.VMEM((2, width, points), bands.dtype), pltpu.SemaphoreType.DMA((2, 2))]
    return pl.pallas_call(
        functools.partial(piece_kernel if after else first_kernel, slot, start),
        in_specs=[hbm] * (1 + len(after)),
        out_specs=hbm if after else pl.BlockSpec(memory_space=pltpu.VMEM),
        scratch_shapes=scratch if after else [pltpu.SemaphoreType.DMA((2,))],
        out_shape=jax.ShapeDtypeStruct((2, width, points), bands.dtype),
        compiler_params=pltpu.CompilerParams(vmem_limit_bytes=VMEM_BYTES),
        cost_estimate=pl.CostEstimate(flops=1000, bytes_accessed=1000, transcendentals=0),
        name="piece_of",
    )(bands, *after)


def near_into(near_buf, there_ref, table_ref, base, planes):
    width, points = there_ref.shape[1:]

    @pl.loop(0, width // STRIP)
    def _(strip):
        rows = pl.ds(strip * STRIP, STRIP)
        mirror = pl.ds(width + strip * STRIP, STRIP)
        for start in range(0, points, DEPTH):
            plane = start // PLANE
            cosine = table_ref[base + 1 + plane]
            sine = table_ref[base + 1 + planes + plane]
            columns = pl.ds(start, DEPTH)
            real_part = there_ref[0, rows, columns].astype(jnp.float32)
            imag_part = there_ref[1, rows, columns].astype(jnp.float32)
            near_re = real_part * cosine + imag_part * sine
            near_im = imag_part * cosine - real_part * sine
            near_buf[rows, columns] = near_re.astype(jnp.bfloat16)
            near_buf[mirror, columns] = near_im.astype(jnp.bfloat16)


def put_sum(sum_buf, lane, total):
    width = total.shape[1] // 2
    sum_buf[:, 0, lane : lane + width] = total[:, :width]
    sum_buf[:, 1, lane : lane + width] = total[:, width:]


def step_kernel(plan, table_ref, *refs):
    rows, k_dev, _, nbands = plan.shape
    fold, depth = plan.fold, plan.depth
    refs = list(refs)

    def take(count):
        taken = refs[:count]
        del refs[:count]
        return taken

    stride = (table_ref.shape[0] - 1) // k_dev
    planes = (stride - 1) // 2
    me = table_ref[k_dev * stride].astype(jnp.int32)
    place, outer = lax.rem(me, fold), lax.div(me, fold)
    if plan.part:
        bands_ref, phased_ref = take(2)
    sources = [take(count) for count in plan.takes]
    arrived = take(plan.adds)
    if plan.adding and plan.placed:
        take(1)
    take(plan.after)
    given_ref = take(1)[0] if plan.near == "give" else None
    kept_ref = take(1)[0] if plan.ahead else None
    outs = [take(2 if plan.split else 1) for _ in plan.ways]
    targets = [take(task.count) for task in plan.tasks]
    result_ref = take(1)[0] if plan.adding else None
    piece_ref = take(1)[0] if plan.later else None
    if plan.part:
        slot, _, width = plan.part
        base = slot * stride
        point = table_ref[base].astype(jnp.int32)

        def load_rows(point, into_ref, load_sems):
            copies = []
            for distance in range(1, fold + 1):
                way = distance % fold
                target = lax.rem(place + way, fold)
                for part in range(2):
                    for level in range(depth):
                        first = pl.multiple_of((level * fold + target) * rows, rows)
                        copy = pltpu.make_async_copy(
                            bands_ref.at[point, part, pl.ds(first, rows), :],
                            into_ref.at[way, part, pl.ds(level * rows, rows), :],
                            load_sems.at[way, part, level],
                        )
                        copy.start()
                        copies.append((way, part, copy))
            return copies

        own_ref = bands_ref
        own, ahead = [], []
        if plan.rows != "held":
            own_ref, own_sems = take(2)
            own = load_rows(point, own_ref, own_sems)
        if plan.ahead:
            next_point = table_ref[base + stride].astype(jnp.int32)
            ahead = load_rows(next_point, kept_ref, take(1)[0])
    if plan.later:
        piece_buf, piece_sems = take(2)
        later_slot, later_start, later_width = plan.later
        loads = [
            pltpu.make_async_copy(
                bands_ref.at[later_slot, part, pl.ds(later_start, later_width), :],
                piece_buf.at[part],
                piece_sems.at[0, part],
            )
            for part in range(2)
        ]
        stores = [
            pltpu.make_async_copy(piece_buf.at[part], piece_ref.at[part], piece_sems.at[1, part])
            for part in range(2)
        ]
        for copy in loads:
            copy.start()
    if plan.adding:
        sum_buf, placed_sem = take(2)
        add_slot, add_start, pieces = plan.adding
        for start, span, terms in pieces:
            total = 0.0
            for index, column in terms:
                total += arrived[index][0, :, column : column + 2 * span].astype(jnp.float32)
            put_sum(sum_buf, start - add_start, total)
        add_point = table_ref[add_slot * stride].astype(jnp.int32)
        columns = pl.ds(add_start, sum_buf.shape[2])
        placing = pltpu.make_async_copy(
            sum_buf, result_ref.at[:, add_point, :, columns], placed_sem
        )
        placing.start()
    for task, arrays, outputs in zip(plan.tasks, sources, targets):
        groups = [arrays[i : i + task.each] for i in range(0, len(arrays), task.each)]
        bit = lax.rem(lax.div(outer, 1 << task.stage), 2)
        filled = [(out_ref, 0) for out_ref in outputs]
        if plan.joined and not task.direct:
            filled.append((targets[0][JOINT], 2 * plan.tasks[0].batch[0][2]))
        for index, (out_ref, shift) in enumerate(filled):
            for level in range(out_ref.shape[0]):
                if task.direct:
                    source = partner(outer, index)
                else:
                    source = 2 * level + (1 - bit if index else bit)
                column = shift
                for group in groups:
                    total = summed(group, source)
                    columns = slice(column, column + total.shape[1])
                    out_ref[level, :, columns] = total.astype(out_ref.dtype)
                    column += total.shape[1]
    if plan.part:
        near_ref = phased_ref
        if plan.near != "use":
            near_ref = given_ref if plan.near == "give" else take(1)[0]
            near_into(near_ref, phased_ref, table_ref, base, planes)
        dims = (((1,), (1,)), ((), ()))
        points = near_ref.shape[1]
        run = points // 2 if width <= SPLIT else points
        for way, out_refs in zip(plan.ways, outs):
            kind = out_refs[0].dtype
            of_both = []
            for part in range(2):
                for copy in [copy for *which, copy in own if which == [way, part]]:
                    copy.wait()
                products = [
                    lax.dot_general(
                        own_ref[way, part, :, pl.ds(first, run)],
                        near_ref[:, pl.ds(first, run)],
                        dims,
                        preferred_element_type=jnp.float32,
                    )
                    for first in range(0, points, run)
                ]
                of_both.append(sum(products[1:], products[0]))
            of_re, of_im = of_both
            sides = (
                (of_re[:, :width] + of_im[:, width:]).astype(kind),
                (of_re[:, width:] - of_im[:, :width]).astype(kind),
            )
            for level in range(depth):
                lines = slice(level * rows, (level + 1) * rows)
                for side, values in enumerate(sides):
                    if plan.split:
                        out_refs[side][level] = values[lines]
                    else:
                        columns = slice(side * width, (side + 1) * width)
                        out_refs[0][level, :, columns] = values[lines]
            if plan.later and way == plan.ways[0]:
                for load, store in zip(loads, stores):
                    load.wait()
                    store.start()
        for _, _, copy in ahead:
            copy.wait()
    if plan.adding:
        placing.wait()
    if plan.later:
        for store in stores:
            store.wait()


def partner(outer, distance):
    low, high = lax.rem(outer, 2), lax.rem(lax.div(outer, 2), 2)
    low = 1 - low if distance % 2 else low
    high = 1 - high if distance // 2 else high
    return outer - lax.rem(outer, 4) + 2 * high + low


def summed(arrays, level):
    total = arrays[0][level].astype(jnp.float32)
    rest = [array[level].astype(jnp.float32) for array in arrays[1:]]
    while rest:
        more = rest.pop(0)
        if more.shape != total.shape:
            more = jnp.concatenate([more, rest.pop(0)], axis=1)
        total = total + more
    return total


class Task(NamedTuple):
    batch: tuple
    stage: int
    direct: bool
    each: int
    count: int


class Plan(NamedTuple):
    shape: tuple
    fold: int
    depth: int
    part: tuple
    ways: tuple
    near: str
    rows: str
    ahead: bool
    tasks: tuple
    takes: tuple
    adding: tuple
    adds: int
    joined: bool
    placed: bool
    later: tuple
    split: bool
    after: int


def step(plan, table, bands, phased, sources, arrived, result, after):
    rows, _, _, nbands = plan.shape
    fold, depth = plan.fold, plan.depth
    points = bands.shape[-1]
    vmem = pl.BlockSpec(memory_space=pltpu.VMEM)
    hbm = pl.BlockSpec(memory_space=pltpu.HBM)
    operands, in_specs = [table], [pl.BlockSpec(memory_space=pltpu.SMEM)]
    out_shape, out_specs, scratch, aliases = [], [], [], {}

    def kind(index):
        return jnp.bfloat16 if index else jnp.float32

    if plan.part:
        width = plan.part[2]
        operands += [bands, phased]
        in_specs += [vmem if plan.rows == "held" else hbm, vmem]
        kept = (fold, 2, depth * rows, points)
        if plan.near == "give":
            out_shape.append(jax.ShapeDtypeStruct((2 * width, points), jnp.bfloat16))
        if plan.ahead:
            out_shape.append(jax.ShapeDtypeStruct(kept, jnp.bfloat16))
        out_shape += [
            jax.ShapeDtypeStruct((depth, rows, width if plan.split else 2 * width), kind(way))
            for way in plan.ways
            for _ in range(2 if plan.split else 1)
        ]
        if plan.rows != "held":
            scratch.append(pltpu.VMEM(kept, jnp.bfloat16))
            scratch.append(pltpu.SemaphoreType.DMA((fold, 2, depth)))
        if plan.ahead:
            scratch.append(pltpu.SemaphoreType.DMA((fold, 2, depth)))
    for arrays in [*sources, arrived]:
        operands += arrays
        in_specs += [vmem] * len(arrays)
    for task in plan.tasks:
        wide = sum(2 * width for _, _, width in task.batch)
        levels = 1 if task.direct else depth >> (task.stage + 1)
        extra = 2 * plan.tasks[1].batch[0][2] if plan.joined and task.direct else 0
        for i in range(task.count):
            columns = wide + extra if i == JOINT else wide
            out_shape.append(jax.ShapeDtypeStruct((levels, rows, columns), kind(i)))
    out_specs += [vmem] * len(out_shape)
    if plan.later:
        scratch += [
            pltpu.VMEM((2, plan.later[2], points), bands.dtype),
            pltpu.SemaphoreType.DMA((2, 2)),
        ]
    if plan.adding:
        if plan.placed:
            aliases = {len(operands): len(out_shape)}
            operands.append(result)
            in_specs.append(hbm)
        out_shape.append(jax.ShapeDtypeStruct(plan.shape, jnp.float32))
        out_specs.append(hbm)
        lanes = sum(span for _, span, _ in plan.adding[2])
        scratch += [pltpu.VMEM((rows, 2, lanes), jnp.float32), pltpu.SemaphoreType.DMA]
    operands += after
    in_specs += [pl.BlockSpec(memory_space=pl.ANY)] * len(after)
    if plan.later:
        out_shape.append(jax.ShapeDtypeStruct((2, plan.later[2], points), bands.dtype))
        out_specs.append(hbm)
    if plan.near == "make":
        scratch.append(pltpu.VMEM((2 * width, points), jnp.bfloat16))
    outs = list(
        pl.pallas_call(
            functools.partial(step_kernel, plan),
            in_specs=in_specs,
            out_specs=out_specs,
            scratch_shapes=scratch,
            out_shape=out_shape,
            input_output_aliases=aliases,
            compiler_params=pltpu.CompilerParams(
                vmem_limit_bytes=VMEM_BYTES if plan.part and plan.rows != "held" else LEAN_BYTES
            ),
            cost_estimate=pl.CostEstimate(flops=1000, bytes_accessed=1000, transcendentals=0),
            name="step",
        )(*operands)
    )
    piece = outs.pop() if plan.later else None
    result = outs.pop() if plan.adding else result
    near = outs.pop(0) if plan.near == "give" else None
    kept = outs.pop(0) if plan.ahead else None
    count = len(plan.ways) * (2 if plan.split else 1)
    terms, handed = outs[:count], outs[count:]
    sends = []
    for task in plan.tasks:
        sends.append(handed[: task.count])
        handed = handed[task.count :]
    return terms, near, kept, sends, result, piece


def cuts(nbands, first):
    eighth = nbands // 8
    widths = [4 * eighth, 4 * eighth] if first else [3 * eighth, 3 * eighth, 2 * eighth]
    starts = [sum(widths[:i]) for i in range(len(widths))]
    return list(zip(starts, widths))


def schedule(parts, fold, depth):
    every, others = tuple(range(fold)), tuple(range(1, fold))
    count = len(parts)
    kernels = []
    waiting, halved, crossed = [], [], []
    for index, part in enumerate(parts):
        ready = ready_parts(waiting)
        waiting = waiting[len(ready) :]
        final = index == count - 1
        tasks = []
        if halved and not final:
            tasks.append(Task(tuple(halved), 1, False, 2, 2))
            waiting += halved
        if crossed:
            tasks.append(Task(tuple(crossed), 0, False, fold, 2))
        if index >= count - 3:
            kernels.append((part, others, "give", tuple(tasks), ready))
            kernels.append((part, every[:1], "use", (), ()))
        else:
            kernels.append((part, every, "make", tuple(tasks), ready))
        if final:
            break
        halved, crossed = crossed, [part]
        if index in (0, count - 3, count - 2):
            kernels.append((None, (), "", (Task((part,), 0, False, fold, 2),), ()))
            halved, crossed = halved + crossed, []
    tasks = (
        Task((parts[-1],), 0, True, 2 * fold - 1, depth),
        Task(tuple(halved), 1, False, 2, 1),
    )
    kernels.append((None, (), "", tasks, ()))
    kernels.append((None, (), "", (), tuple(waiting) + tuple(halved) + (parts[-1],)))
    return kernels


def ready_parts(waiting):
    total = 0
    for count, (slot, _, width) in enumerate(waiting, 1):
        total += width
        if slot != waiting[0][0]:
            break
        if total % LANES == 0:
            return tuple(waiting[:count])
    return ()


def body(bands, nbr_slot, gshift):
    grid_index = lax.axis_index("ga")
    grid_count = lax.axis_size("ga")
    k_dev, _, nbands, points = bands.shape
    rows = nbands // grid_count
    own_planes = points // PLANE
    total_planes = own_planes * grid_count
    planes = grid_index * own_planes + jnp.arange(own_planes, dtype=jnp.int32)
    slots = jnp.arange(k_dev, dtype=jnp.int32)
    chosen = nbr_slot[None, :] == slots[:, None]
    order = jnp.sum(jnp.where(chosen, slots[None, :], 0), axis=1)
    shifts = jnp.sum(jnp.where(chosen, gshift[None, :], 0), axis=1)
    turns = (1 + NKB * shifts[:, None]) * planes[None, :] % (NKB * total_planes)
    angle = 2.0 * math.pi / (NKB * total_planes) * turns.astype(jnp.float32)
    columns = [order[:, None].astype(jnp.float32), jnp.cos(angle), jnp.sin(angle)]
    table = jnp.concatenate(columns, axis=1).reshape(-1)
    table = jnp.append(table, grid_index.astype(jnp.float32))
    parts = []
    for slot in range(k_dev):
        for start, width in cuts(nbands, slot == 0):
            parts.append((slot, start, width))
    theres = []
    piece = None
    for slot, start, width in parts[:AHEAD]:
        piece = piece_of(slot, start, width, bands, [] if piece is None else [piece])
        theres.append(shifted(piece, "ka", -1))
    shape = (rows, k_dev, 2, nbands)
    depth = min(OUTER, grid_count)
    fold = grid_count // depth
    held = {}
    near, kept, result = None, None, None
    for part, ways, phase, tasks, adds in schedule(parts, fold, depth):
        place = parts.index(part) if part else len(parts)
        later = parts[place + AHEAD] if place + AHEAD < len(parts) and phase != "use" else None
        sources = [
            [array for done in task.batch for array, _ in held[(done,)]] for task in tasks
        ]
        arrived, pieces = [], []
        for done in adds:
            batch = max((key for key in held if done in key), key=len)
            column = sum(2 * width for _, _, width in batch[: batch.index(done)])
            terms = [(len(arrived) + i, first + column) for i, (_, first) in enumerate(held[batch])]
            arrived += [array for array, _ in held[batch]]
            pieces.append((done[1], done[2], tuple(terms)))
        adding = (adds[0][0], adds[0][1], tuple(pieces)) if adds else ()
        split = place == len(parts) - 1 and phase == "give"
        after = order_by if split else []
        plan = Plan(
            shape,
            fold,
            depth,
            part,
            ways,
            phase,
            "held" if part and part[0] == k_dev - 1 else "load",
            place == len(parts) - 5,
            tasks,
            tuple(len(arrays) for arrays in sources),
            adding,
            len(arrived),
            len(tasks) > 1 and tasks[0].direct,
            result is not None,
            later,
            split,
            len(after),
        )
        phased = near if phase == "use" else theres[place] if part else None
        terms, near, found, sends, result, piece = step(
            plan,
            table,
            kept if part and part[0] == k_dev - 1 else bands,
            phased,
            sources,
            arrived,
            result,
            after,
        )
        order_by = sends[0][:1] if sends else []
        kept = found if kept is None else kept
        if later:
            theres.append(shifted(piece, "ka", -1))
        for way, array in zip([way for way in ways for _ in range(1 + split)], terms):
            array = shifted(array, "ga", way, fold, True) if way else array
            entries = held.setdefault((part,), [])
            entries.insert(len(entries) if way else 0, (array, 0))
        for task, arrays in zip(tasks, sends):
            steps = range(1, depth) if task.direct else [1 << task.stage]
            moved = [swapped(array, "ga", fold * i) for array, i in zip(arrays[1:], steps)]
            held[task.batch] = [(array, 0) for array in [arrays[0], *reversed(moved)]]
        if plan.joined:
            joint = held[tasks[0].batch][JOINT][0]
            held[tasks[1].batch].append((joint, 2 * tasks[0].batch[0][2]))
    return result


def solution(mesh):
    placed = (P("ka", None, None, "ga"), P("ka"), P("ka"))
    return jax.shard_map(
        body, mesh=mesh, in_specs=placed, out_specs=P("ga", "ka", None, None), check_vma=False
    )
```

```python
import functools
import math
from typing import NamedTuple

import jax
import jax.numpy as jnp
from jax import lax
from jax.experimental import pallas as pl
from jax.experimental.pallas import tpu as pltpu
from jax.sharding import PartitionSpec as P

NKB = 4
PLANE = 1024
STRIP = 32
DEPTH = 512
AHEAD = 3
OUTER = 4
SPLIT = 0
JOINT = 2
LANES = 128
BLOCK = 256
VMEM_BYTES = 44 * 1024 * 1024
LEAN_BYTES = 32 * 1024 * 1024


def shifted(block, axis, distance, fold=1, inner=False):
    count = lax.axis_size(axis)
    route = []
    for i in range(count):
        outer, place = divmod(i, fold)
        if inner:
            route.append((i, outer * fold + (place + distance) % fold))
        else:
            route.append((i, (outer + distance) % (count // fold) * fold + place))
    return lax.ppermute(block, axis, route)


def swapped(block, axis, distance):
    count = lax.axis_size(axis)
    return lax.ppermute(block, axis, [(i, i ^ distance) for i in range(count)])


def first_kernel(slot, start, bands_ref, out_ref, sems):
    width = out_ref.shape[1]
    loads = [
        pltpu.make_async_copy(
            bands_ref.at[slot, part, pl.ds(start, width), :], out_ref.at[part], sems.at[part]
        )
        for part in range(2)
    ]
    for load in loads:
        load.start()
    for load in loads:
        load.wait()


def piece_kernel(slot, start, bands_ref, *rest):
    out_ref, piece_buf, sems = rest[-3:]
    width = piece_buf.shape[1]
    rows = pl.ds(start, width)
    loads = [
        pltpu.make_async_copy(bands_ref.at[slot, part, rows, :], piece_buf.at[part], sems.at[0, part])
        for part in range(2)
    ]
    stores = [
        pltpu.make_async_copy(piece_buf.at[part], out_ref.at[part], sems.at[1, part])
        for part in range(2)
    ]
    for load in loads:
        load.start()
    for load, store in zip(loads, stores):
        load.wait()
        store.start()
    for store in stores:
        store.wait()


def piece_of(slot, start, width, bands, after):
    points = bands.shape[3]
    hbm = pl.BlockSpec(memory_space=pltpu.HBM)
    scratch = [pltpu.VMEM((2, width, points), bands.dtype), pltpu.SemaphoreType.DMA((2, 2))]
    return pl.pallas_call(
        functools.partial(piece_kernel if after else first_kernel, slot, start),
        in_specs=[hbm] * (1 + len(after)),
        out_specs=hbm if after else pl.BlockSpec(memory_space=pltpu.VMEM),
        scratch_shapes=scratch if after else [pltpu.SemaphoreType.DMA((2,))],
        out_shape=jax.ShapeDtypeStruct((2, width, points), bands.dtype),
        compiler_params=pltpu.CompilerParams(vmem_limit_bytes=VMEM_BYTES),
        cost_estimate=pl.CostEstimate(flops=1000, bytes_accessed=1000, transcendentals=0),
        name="piece_of",
    )(bands, *after)


def near_into(near_buf, there_ref, table_ref, base, planes):
    width, points = there_ref.shape[1:]

    @pl.loop(0, width // STRIP)
    def _(strip):
        rows = pl.ds(strip * STRIP, STRIP)
        mirror = pl.ds(width + strip * STRIP, STRIP)
        for start in range(0, points, DEPTH):
            plane = start // PLANE
            cosine = table_ref[base + 1 + plane]
            sine = table_ref[base + 1 + planes + plane]
            columns = pl.ds(start, DEPTH)
            real_part = there_ref[0, rows, columns].astype(jnp.float32)
            imag_part = there_ref[1, rows, columns].astype(jnp.float32)
            near_re = real_part * cosine + imag_part * sine
            near_im = imag_part * cosine - real_part * sine
            near_buf[rows, columns] = near_re.astype(jnp.bfloat16)
            near_buf[mirror, columns] = near_im.astype(jnp.bfloat16)


def put_sum(sum_buf, lane, total):
    width = total.shape[1] // 2
    sum_buf[:, 0, lane : lane + width] = total[:, :width]
    sum_buf[:, 1, lane : lane + width] = total[:, width:]


def step_kernel(plan, table_ref, *refs):
    rows, k_dev, _, nbands = plan.shape
    fold, depth = plan.fold, plan.depth
    refs = list(refs)

    def take(count):
        taken = refs[:count]
        del refs[:count]
        return taken

    stride = (table_ref.shape[0] - 1) // k_dev
    planes = (stride - 1) // 2
    me = table_ref[k_dev * stride].astype(jnp.int32)
    place, outer = lax.rem(me, fold), lax.div(me, fold)
    if plan.part:
        bands_ref, phased_ref = take(2)
    sources = [take(count) for count in plan.takes]
    arrived = take(plan.adds)
    if plan.adding and plan.placed:
        take(1)
    given_ref = take(1)[0] if plan.near == "give" else None
    kept_ref = take(1)[0] if plan.rows == "keep" else None
    outs = take(len(plan.ways))
    targets = [take(task.count) for task in plan.tasks]
    result_ref = take(1)[0] if plan.adding else None
    piece_ref = take(1)[0] if plan.later else None
    if plan.part:
        slot, _, width = plan.part
        base = slot * stride
        point = table_ref[base].astype(jnp.int32)
        own_ref = bands_ref
        own = []
        if plan.rows != "held":
            own_ref = take(1)[0] if plan.rows == "load" else kept_ref
            own_sems = take(1)[0]
            for distance in range(1, fold + 1):
                way = distance % fold
                target = lax.rem(place + way, fold)
                for part in range(2):
                    for level in range(depth):
                        first = pl.multiple_of((level * fold + target) * rows, rows)
                        copy = pltpu.make_async_copy(
                            bands_ref.at[point, part, pl.ds(first, rows), :],
                            own_ref.at[way, part, pl.ds(level * rows, rows), :],
                            own_sems.at[way, part, level],
                        )
                        copy.start()
                        own.append((way, part, copy))
    if plan.later:
        piece_buf, piece_sems = take(2)
        later_slot, later_start, later_width = plan.later
        loads = [
            pltpu.make_async_copy(
                bands_ref.at[later_slot, part, pl.ds(later_start, later_width), :],
                piece_buf.at[part],
                piece_sems.at[0, part],
            )
            for part in range(2)
        ]
        stores = [
            pltpu.make_async_copy(piece_buf.at[part], piece_ref.at[part], piece_sems.at[1, part])
            for part in range(2)
        ]
        for copy in loads:
            copy.start()
    if plan.adding:
        sum_buf, placed_sem = take(2)
        add_slot, add_start, pieces = plan.adding
        for start, span, terms in pieces:
            total = 0.0
            for index, column in terms:
                total += arrived[index][0, :, column : column + 2 * span].astype(jnp.float32)
            put_sum(sum_buf, start - add_start, total)
        add_point = table_ref[add_slot * stride].astype(jnp.int32)
        columns = pl.ds(add_start, sum_buf.shape[2])
        placing = pltpu.make_async_copy(
            sum_buf, result_ref.at[:, add_point, :, columns], placed_sem
        )
        placing.start()
    for task, arrays, outputs in zip(plan.tasks, sources, targets):
        groups = [arrays[i : i + task.each] for i in range(0, len(arrays), task.each)]
        bit = lax.rem(lax.div(outer, 1 << task.stage), 2)
        filled = [(out_ref, 0) for out_ref in outputs]
        if plan.joined and not task.direct:
            filled.append((targets[0][JOINT], 2 * plan.tasks[0].batch[0][2]))
        for index, (out_ref, shift) in enumerate(filled):
            for level in range(out_ref.shape[0]):
                if task.direct:
                    source = partner(outer, index)
                else:
                    source = 2 * level + (1 - bit if index else bit)
                column = shift
                for group in groups:
                    total = summed(group, source)
                    columns = slice(column, column + total.shape[1])
                    out_ref[level, :, columns] = total.astype(out_ref.dtype)
                    column += total.shape[1]
    if plan.part:
        near_ref = phased_ref
        if plan.near != "use":
            near_ref = given_ref if plan.near == "give" else take(1)[0]
            near_into(near_ref, phased_ref, table_ref, base, planes)
        dims = (((1,), (1,)), ((), ()))
        points = near_ref.shape[1]
        run = points // 2 if width <= SPLIT else points
        for way, out_ref in zip(plan.ways, outs):
            of_both = []
            for part in range(2):
                for copy in [copy for *which, copy in own if which == [way, part]]:
                    copy.wait()
                products = [
                    lax.dot_general(
                        own_ref[way, part, :, pl.ds(first, run)],
                        near_ref[:, pl.ds(first, run)],
                        dims,
                        preferred_element_type=jnp.float32,
                    )
                    for first in range(0, points, run)
                ]
                of_both.append(sum(products[1:], products[0]))
            of_re, of_im = of_both
            real_part = (of_re[:, :width] + of_im[:, width:]).astype(out_ref.dtype)
            imag_part = (of_re[:, width:] - of_im[:, :width]).astype(out_ref.dtype)
            for level in range(depth):
                lines = slice(level * rows, (level + 1) * rows)
                out_ref[level, :, :width] = real_part[lines]
                out_ref[level, :, width:] = imag_part[lines]
            if plan.later and way == plan.ways[0]:
                for load, store in zip(loads, stores):
                    load.wait()
                    store.start()
        for way, _, copy in own:
            if way not in plan.ways:
                copy.wait()
    if plan.adding:
        placing.wait()
    if plan.later:
        for store in stores:
            store.wait()


def partner(outer, distance):
    low, high = lax.rem(outer, 2), lax.rem(lax.div(outer, 2), 2)
    low = 1 - low if distance % 2 else low
    high = 1 - high if distance // 2 else high
    return outer - lax.rem(outer, 4) + 2 * high + low


def summed(arrays, level, columns=slice(None)):
    total = arrays[0][level, :, columns]
    for array in arrays[1:]:
        total = total + array[level, :, columns].astype(jnp.float32)
    return total


class Task(NamedTuple):
    batch: tuple
    stage: int
    direct: bool
    each: int
    count: int


class Plan(NamedTuple):
    shape: tuple
    fold: int
    depth: int
    part: tuple
    ways: tuple
    near: str
    rows: str
    tasks: tuple
    takes: tuple
    adding: tuple
    adds: int
    joined: bool
    placed: bool
    later: tuple


def step(plan, table, bands, phased, sources, arrived, result):
    rows, _, _, nbands = plan.shape
    fold, depth = plan.fold, plan.depth
    points = bands.shape[-1]
    vmem = pl.BlockSpec(memory_space=pltpu.VMEM)
    hbm = pl.BlockSpec(memory_space=pltpu.HBM)
    operands, in_specs = [table], [pl.BlockSpec(memory_space=pltpu.SMEM)]
    out_shape, out_specs, scratch, aliases = [], [], [], {}

    def kind(index):
        return jnp.bfloat16 if index else jnp.float32

    if plan.part:
        width = plan.part[2]
        operands += [bands, phased]
        in_specs += [vmem if plan.rows == "held" else hbm, vmem]
        kept = (fold, 2, depth * rows, points)
        if plan.near == "give":
            out_shape.append(jax.ShapeDtypeStruct((2 * width, points), jnp.bfloat16))
        if plan.rows == "keep":
            out_shape.append(jax.ShapeDtypeStruct(kept, jnp.bfloat16))
        out_shape += [
            jax.ShapeDtypeStruct((depth, rows, 2 * width), kind(way)) for way in plan.ways
        ]
        if plan.rows == "load":
            scratch.append(pltpu.VMEM(kept, jnp.bfloat16))
        if plan.rows != "held":
            scratch.append(pltpu.SemaphoreType.DMA((fold, 2, depth)))
    for arrays in [*sources, arrived]:
        operands += arrays
        in_specs += [vmem] * len(arrays)
    for task in plan.tasks:
        wide = sum(2 * width for _, _, width in task.batch)
        levels = 1 if task.direct else depth >> (task.stage + 1)
        extra = 2 * plan.tasks[1].batch[0][2] if plan.joined and task.direct else 0
        for i in range(task.count):
            columns = wide + extra if i == JOINT else wide
            out_shape.append(jax.ShapeDtypeStruct((levels, rows, columns), kind(i)))
    out_specs += [vmem] * len(out_shape)
    if plan.later:
        scratch += [
            pltpu.VMEM((2, plan.later[2], points), bands.dtype),
            pltpu.SemaphoreType.DMA((2, 2)),
        ]
    if plan.adding:
        if plan.placed:
            aliases = {len(operands): len(out_shape)}
            operands.append(result)
            in_specs.append(hbm)
        out_shape.append(jax.ShapeDtypeStruct(plan.shape, jnp.float32))
        out_specs.append(hbm)
        lanes = sum(span for _, span, _ in plan.adding[2])
        scratch += [pltpu.VMEM((rows, 2, lanes), jnp.float32), pltpu.SemaphoreType.DMA]
    if plan.later:
        out_shape.append(jax.ShapeDtypeStruct((2, plan.later[2], points), bands.dtype))
        out_specs.append(hbm)
    if plan.near == "make":
        scratch.append(pltpu.VMEM((2 * width, points), jnp.bfloat16))
    outs = list(
        pl.pallas_call(
            functools.partial(step_kernel, plan),
            in_specs=in_specs,
            out_specs=out_specs,
            scratch_shapes=scratch,
            out_shape=out_shape,
            input_output_aliases=aliases,
            compiler_params=pltpu.CompilerParams(
                vmem_limit_bytes=VMEM_BYTES if plan.part and plan.rows != "held" else LEAN_BYTES
            ),
            cost_estimate=pl.CostEstimate(flops=1000, bytes_accessed=1000, transcendentals=0),
            name="step",
        )(*operands)
    )
    piece = outs.pop() if plan.later else None
    result = outs.pop() if plan.adding else result
    near = outs.pop(0) if plan.near == "give" else None
    kept = outs.pop(0) if plan.rows == "keep" else None
    terms = outs[: len(plan.ways)]
    handed = outs[len(plan.ways) :]
    sends = []
    for task in plan.tasks:
        sends.append(handed[: task.count])
        handed = handed[task.count :]
    return terms, near, kept, sends, result, piece


def cuts(nbands, first):
    eighth = nbands // 8
    widths = [4 * eighth, 4 * eighth] if first else [3 * eighth, 3 * eighth, 2 * eighth]
    starts = [sum(widths[:i]) for i in range(len(widths))]
    return list(zip(starts, widths))


def schedule(parts, fold, depth):
    every, others = tuple(range(fold)), tuple(range(1, fold))
    count = len(parts)
    kernels = []
    waiting, halved, crossed = [], [], []
    for index, part in enumerate(parts):
        ready = ready_parts(waiting)
        waiting = waiting[len(ready) :]
        tasks = []
        if halved:
            tasks.append(Task(tuple(halved), 1, False, 2, 2))
        if crossed:
            tasks.append(Task(tuple(crossed), 0, False, fold, 2))
        waiting += halved
        if index >= count - 3:
            kernels.append((part, others, "give", tuple(tasks), ready))
            kernels.append((part, every[:1], "use", (), ()))
        else:
            kernels.append((part, every, "make", tuple(tasks), ready))
        halved, crossed = crossed, [part] if index < count - 1 else []
        if index in (0, count - 3):
            kernels.append((None, (), "", (Task((part,), 0, False, fold, 2),), ()))
            halved, crossed = halved + crossed, []
    tasks = (
        Task((parts[-1],), 0, True, fold, depth),
        Task(tuple(halved), 1, False, 2, 1),
    )
    kernels.append((None, (), "", tasks, ()))
    kernels.append((None, (), "", (), tuple(waiting) + tuple(halved) + (parts[-1],)))
    return kernels


def ready_parts(waiting):
    total = 0
    for count, (slot, _, width) in enumerate(waiting, 1):
        total += width
        if slot != waiting[0][0]:
            break
        if total % LANES == 0:
            return tuple(waiting[:count])
    return ()


def body(bands, nbr_slot, gshift):
    grid_index = lax.axis_index("ga")
    grid_count = lax.axis_size("ga")
    k_dev, _, nbands, points = bands.shape
    rows = nbands // grid_count
    own_planes = points // PLANE
    total_planes = own_planes * grid_count
    planes = grid_index * own_planes + jnp.arange(own_planes, dtype=jnp.int32)
    slots = jnp.arange(k_dev, dtype=jnp.int32)
    chosen = nbr_slot[None, :] == slots[:, None]
    order = jnp.sum(jnp.where(chosen, slots[None, :], 0), axis=1)
    shifts = jnp.sum(jnp.where(chosen, gshift[None, :], 0), axis=1)
    turns = (1 + NKB * shifts[:, None]) * planes[None, :] % (NKB * total_planes)
    angle = 2.0 * math.pi / (NKB * total_planes) * turns.astype(jnp.float32)
    columns = [order[:, None].astype(jnp.float32), jnp.cos(angle), jnp.sin(angle)]
    table = jnp.concatenate(columns, axis=1).reshape(-1)
    table = jnp.append(table, grid_index.astype(jnp.float32))
    parts = []
    for slot in range(k_dev):
        for start, width in cuts(nbands, slot == 0):
            parts.append((slot, start, width))
    theres = []
    piece = None
    for slot, start, width in parts[:AHEAD]:
        piece = piece_of(slot, start, width, bands, [] if piece is None else [piece])
        theres.append(shifted(piece, "ka", -1))
    shape = (rows, k_dev, 2, nbands)
    depth = min(OUTER, grid_count)
    fold = grid_count // depth
    held = {}
    near, kept, result = None, None, None
    for part, ways, phase, tasks, adds in schedule(parts, fold, depth):
        place = parts.index(part) if part else len(parts)
        later = parts[place + AHEAD] if place + AHEAD < len(parts) and phase != "use" else None
        sources = [
            [array for done in task.batch for array, _ in held[(done,)]] for task in tasks
        ]
        arrived, pieces = [], []
        for done in adds:
            batch = max((key for key in held if done in key), key=len)
            column = sum(2 * width for _, _, width in batch[: batch.index(done)])
            terms = [(len(arrived) + i, first + column) for i, (_, first) in enumerate(held[batch])]
            arrived += [array for array, _ in held[batch]]
            pieces.append((done[1], done[2], tuple(terms)))
        adding = (adds[0][0], adds[0][1], tuple(pieces)) if adds else ()
        plan = Plan(
            shape,
            fold,
            depth,
            part,
            ways,
            phase,
            "held" if kept is not None else "keep" if phase == "give" else "load",
            tasks,
            tuple(len(arrays) for arrays in sources),
            adding,
            len(arrived),
            len(tasks) > 1 and tasks[0].direct,
            result is not None,
            later,
        )
        phased = near if phase == "use" else theres[place] if part else None
        terms, near, found, sends, result, piece = step(
            plan,
            table,
            bands if kept is None else kept,
            phased,
            sources,
            arrived,
            result,
        )
        kept = found if kept is None else kept
        if later:
            theres.append(shifted(piece, "ka", -1))
        for way, array in zip(ways, terms):
            array = shifted(array, "ga", way, fold, True) if way else array
            held.setdefault((part,), []).insert(0 if way == 0 else fold, (array, 0))
        for task, arrays in zip(tasks, sends):
            steps = range(1, depth) if task.direct else [1 << task.stage]
            moved = [swapped(array, "ga", fold * i) for array, i in zip(arrays[1:], steps)]
            held[task.batch] = [(array, 0) for array in [arrays[0], *reversed(moved)]]
        if plan.joined:
            joint = held[tasks[0].batch][JOINT][0]
            held[tasks[1].batch].append((joint, 2 * tasks[0].batch[0][2]))
    return result


def solution(mesh):
    placed = (P("ka", None, None, "ga"), P("ka"), P("ka"))
    return jax.shard_map(
        body, mesh=mesh, in_specs=placed, out_specs=P("ga", "ka", None, None), check_vma=False
    )
```

```python
import functools
import math
from typing import NamedTuple

import jax
import jax.numpy as jnp
from jax import lax
from jax.experimental import pallas as pl
from jax.experimental.pallas import tpu as pltpu
from jax.sharding import PartitionSpec as P

NKB = 4
PLANE = 1024
STRIP = 32
DEPTH = 512
AHEAD = 3
OUTER = 4
SPLIT = 0
JOINT = 2
LANES = 128
BLOCK = 256
VMEM_BYTES = 44 * 1024 * 1024
LEAN_BYTES = 32 * 1024 * 1024


def shifted(block, axis, distance, fold=1, inner=False):
    count = lax.axis_size(axis)
    route = []
    for i in range(count):
        outer, place = divmod(i, fold)
        if inner:
            route.append((i, outer * fold + (place + distance) % fold))
        else:
            route.append((i, (outer + distance) % (count // fold) * fold + place))
    return lax.ppermute(block, axis, route)


def swapped(block, axis, distance):
    count = lax.axis_size(axis)
    return lax.ppermute(block, axis, [(i, i ^ distance) for i in range(count)])


def first_kernel(slot, start, bands_ref, out_ref, sems):
    width = out_ref.shape[1]
    loads = [
        pltpu.make_async_copy(
            bands_ref.at[slot, part, pl.ds(start, width), :], out_ref.at[part], sems.at[part]
        )
        for part in range(2)
    ]
    for load in loads:
        load.start()
    for load in loads:
        load.wait()


def piece_kernel(slot, start, bands_ref, *rest):
    out_ref, piece_buf, sems = rest[-3:]
    width = piece_buf.shape[1]
    rows = pl.ds(start, width)
    loads = [
        pltpu.make_async_copy(bands_ref.at[slot, part, rows, :], piece_buf.at[part], sems.at[0, part])
        for part in range(2)
    ]
    stores = [
        pltpu.make_async_copy(piece_buf.at[part], out_ref.at[part], sems.at[1, part])
        for part in range(2)
    ]
    for load in loads:
        load.start()
    for load, store in zip(loads, stores):
        load.wait()
        store.start()
    for store in stores:
        store.wait()


def piece_of(slot, start, width, bands, after):
    points = bands.shape[3]
    hbm = pl.BlockSpec(memory_space=pltpu.HBM)
    scratch = [pltpu.VMEM((2, width, points), bands.dtype), pltpu.SemaphoreType.DMA((2, 2))]
    return pl.pallas_call(
        functools.partial(piece_kernel if after else first_kernel, slot, start),
        in_specs=[hbm] * (1 + len(after)),
        out_specs=hbm if after else pl.BlockSpec(memory_space=pltpu.VMEM),
        scratch_shapes=scratch if after else [pltpu.SemaphoreType.DMA((2,))],
        out_shape=jax.ShapeDtypeStruct((2, width, points), bands.dtype),
        compiler_params=pltpu.CompilerParams(vmem_limit_bytes=VMEM_BYTES),
        cost_estimate=pl.CostEstimate(flops=1000, bytes_accessed=1000, transcendentals=0),
        name="piece_of",
    )(bands, *after)


def near_into(near_buf, there_ref, table_ref, base, planes):
    width, points = there_ref.shape[1:]

    @pl.loop(0, width // STRIP)
    def _(strip):
        rows = pl.ds(strip * STRIP, STRIP)
        mirror = pl.ds(width + strip * STRIP, STRIP)
        for start in range(0, points, DEPTH):
            plane = start // PLANE
            cosine = table_ref[base + 1 + plane]
            sine = table_ref[base + 1 + planes + plane]
            columns = pl.ds(start, DEPTH)
            real_part = there_ref[0, rows, columns].astype(jnp.float32)
            imag_part = there_ref[1, rows, columns].astype(jnp.float32)
            near_re = real_part * cosine + imag_part * sine
            near_im = imag_part * cosine - real_part * sine
            near_buf[rows, columns] = near_re.astype(jnp.bfloat16)
            near_buf[mirror, columns] = near_im.astype(jnp.bfloat16)


def put_sum(sum_buf, lane, total):
    width = total.shape[1] // 2
    sum_buf[:, 0, lane : lane + width] = total[:, :width]
    sum_buf[:, 1, lane : lane + width] = total[:, width:]


def step_kernel(plan, table_ref, *refs):
    rows, k_dev, _, nbands = plan.shape
    fold, depth = plan.fold, plan.depth
    refs = list(refs)

    def take(count):
        taken = refs[:count]
        del refs[:count]
        return taken

    stride = (table_ref.shape[0] - 1) // k_dev
    planes = (stride - 1) // 2
    me = table_ref[k_dev * stride].astype(jnp.int32)
    place, outer = lax.rem(me, fold), lax.div(me, fold)
    if plan.part:
        bands_ref, phased_ref = take(2)
    sources = [take(count) for count in plan.takes]
    arrived = take(plan.adds)
    if plan.adding and plan.placed:
        take(1)
    given_ref = take(1)[0] if plan.near == "give" else None
    kept_ref = take(1)[0] if plan.rows == "keep" else None
    outs = take(len(plan.ways))
    targets = [take(task.count) for task in plan.tasks]
    result_ref = take(1)[0] if plan.adding else None
    piece_ref = take(1)[0] if plan.later else None
    if plan.part:
        slot, _, width = plan.part
        base = slot * stride
        point = table_ref[base].astype(jnp.int32)
        own_ref = bands_ref
        own = []
        if plan.rows != "held":
            own_ref = take(1)[0] if plan.rows == "load" else kept_ref
            own_sems = take(1)[0]
            for distance in range(1, fold + 1):
                way = distance % fold
                target = lax.rem(place + way, fold)
                for part in range(2):
                    for level in range(depth):
                        first = pl.multiple_of((level * fold + target) * rows, rows)
                        copy = pltpu.make_async_copy(
                            bands_ref.at[point, part, pl.ds(first, rows), :],
                            own_ref.at[way, part, pl.ds(level * rows, rows), :],
                            own_sems.at[way, part, level],
                        )
                        copy.start()
                        own.append((way, part, copy))
    if plan.later:
        piece_buf, piece_sems = take(2)
        later_slot, later_start, later_width = plan.later
        loads = [
            pltpu.make_async_copy(
                bands_ref.at[later_slot, part, pl.ds(later_start, later_width), :],
                piece_buf.at[part],
                piece_sems.at[0, part],
            )
            for part in range(2)
        ]
        stores = [
            pltpu.make_async_copy(piece_buf.at[part], piece_ref.at[part], piece_sems.at[1, part])
            for part in range(2)
        ]
        for copy in loads:
            copy.start()
    if plan.adding:
        sum_buf, placed_sem = take(2)
        add_slot, add_start, pieces = plan.adding
        add_point = table_ref[add_slot * stride].astype(jnp.int32)
        placing = []
        placed = 0
        for start, span, terms in pieces:
            total = 0.0
            for index, column in terms:
                total += arrived[index][0, :, column : column + 2 * span].astype(jnp.float32)
            put_sum(sum_buf, start - add_start, total)
            filled_to = start - add_start + span
            if filled_to % LANES == 0:
                columns = pl.ds(add_start + placed, filled_to - placed)
                copy = pltpu.make_async_copy(
                    sum_buf.at[:, :, pl.ds(placed, filled_to - placed)],
                    result_ref.at[:, add_point, :, columns],
                    placed_sem.at[len(placing)],
                )
                copy.start()
                placing.append(copy)
                placed = filled_to
    for task, arrays, outputs in zip(plan.tasks, sources, targets):
        groups = [arrays[i : i + task.each] for i in range(0, len(arrays), task.each)]
        bit = lax.rem(lax.div(outer, 1 << task.stage), 2)
        filled = [(out_ref, 0) for out_ref in outputs]
        if plan.joined and not task.direct:
            filled.append((targets[0][JOINT], 2 * plan.tasks[0].batch[0][2]))
        for index, (out_ref, shift) in enumerate(filled):
            for level in range(out_ref.shape[0]):
                if task.direct:
                    source = partner(outer, index)
                else:
                    source = 2 * level + (1 - bit if index else bit)
                column = shift
                for group in groups:
                    total = summed(group, source)
                    columns = slice(column, column + total.shape[1])
                    out_ref[level, :, columns] = total.astype(out_ref.dtype)
                    column += total.shape[1]
    if plan.part:
        near_ref = phased_ref
        if plan.near != "use":
            near_ref = given_ref if plan.near == "give" else take(1)[0]
            near_into(near_ref, phased_ref, table_ref, base, planes)
        dims = (((1,), (1,)), ((), ()))
        points = near_ref.shape[1]
        run = points // 2 if width <= SPLIT else points
        for way, out_ref in zip(plan.ways, outs):
            of_both = []
            for part in range(2):
                for copy in [copy for *which, copy in own if which == [way, part]]:
                    copy.wait()
                products = [
                    lax.dot_general(
                        own_ref[way, part, :, pl.ds(first, run)],
                        near_ref[:, pl.ds(first, run)],
                        dims,
                        preferred_element_type=jnp.float32,
                    )
                    for first in range(0, points, run)
                ]
                of_both.append(sum(products[1:], products[0]))
            of_re, of_im = of_both
            real_part = (of_re[:, :width] + of_im[:, width:]).astype(out_ref.dtype)
            imag_part = (of_re[:, width:] - of_im[:, :width]).astype(out_ref.dtype)
            for level in range(depth):
                lines = slice(level * rows, (level + 1) * rows)
                out_ref[level, :, :width] = real_part[lines]
                out_ref[level, :, width:] = imag_part[lines]
            if plan.later and way == plan.ways[0]:
                for load, store in zip(loads, stores):
                    load.wait()
                    store.start()
        for way, _, copy in own:
            if way not in plan.ways:
                copy.wait()
    if plan.adding:
        for copy in placing:
            copy.wait()
    if plan.later:
        for store in stores:
            store.wait()


def partner(outer, distance):
    low, high = lax.rem(outer, 2), lax.rem(lax.div(outer, 2), 2)
    low = 1 - low if distance % 2 else low
    high = 1 - high if distance // 2 else high
    return outer - lax.rem(outer, 4) + 2 * high + low


def summed(arrays, level, columns=slice(None)):
    total = arrays[0][level, :, columns]
    for array in arrays[1:]:
        total = total + array[level, :, columns].astype(jnp.float32)
    return total


class Task(NamedTuple):
    batch: tuple
    stage: int
    direct: bool
    each: int
    count: int


class Plan(NamedTuple):
    shape: tuple
    fold: int
    depth: int
    part: tuple
    ways: tuple
    near: str
    rows: str
    tasks: tuple
    takes: tuple
    adding: tuple
    adds: int
    joined: bool
    placed: bool
    later: tuple


def step(plan, table, bands, phased, sources, arrived, result):
    rows, _, _, nbands = plan.shape
    fold, depth = plan.fold, plan.depth
    points = bands.shape[-1]
    vmem = pl.BlockSpec(memory_space=pltpu.VMEM)
    hbm = pl.BlockSpec(memory_space=pltpu.HBM)
    operands, in_specs = [table], [pl.BlockSpec(memory_space=pltpu.SMEM)]
    out_shape, out_specs, scratch, aliases = [], [], [], {}

    def kind(index):
        return jnp.bfloat16 if index else jnp.float32

    if plan.part:
        width = plan.part[2]
        operands += [bands, phased]
        in_specs += [vmem if plan.rows == "held" else hbm, vmem]
        kept = (fold, 2, depth * rows, points)
        if plan.near == "give":
            out_shape.append(jax.ShapeDtypeStruct((2 * width, points), jnp.bfloat16))
        if plan.rows == "keep":
            out_shape.append(jax.ShapeDtypeStruct(kept, jnp.bfloat16))
        out_shape += [
            jax.ShapeDtypeStruct((depth, rows, 2 * width), kind(way)) for way in plan.ways
        ]
        if plan.rows == "load":
            scratch.append(pltpu.VMEM(kept, jnp.bfloat16))
        if plan.rows != "held":
            scratch.append(pltpu.SemaphoreType.DMA((fold, 2, depth)))
    for arrays in [*sources, arrived]:
        operands += arrays
        in_specs += [vmem] * len(arrays)
    for task in plan.tasks:
        wide = sum(2 * width for _, _, width in task.batch)
        levels = 1 if task.direct else depth >> (task.stage + 1)
        extra = 2 * plan.tasks[1].batch[0][2] if plan.joined and task.direct else 0
        for i in range(task.count):
            columns = wide + extra if i == JOINT else wide
            out_shape.append(jax.ShapeDtypeStruct((levels, rows, columns), kind(i)))
    out_specs += [vmem] * len(out_shape)
    if plan.later:
        scratch += [
            pltpu.VMEM((2, plan.later[2], points), bands.dtype),
            pltpu.SemaphoreType.DMA((2, 2)),
        ]
    if plan.adding:
        if plan.placed:
            aliases = {len(operands): len(out_shape)}
            operands.append(result)
            in_specs.append(hbm)
        out_shape.append(jax.ShapeDtypeStruct(plan.shape, jnp.float32))
        out_specs.append(hbm)
        lanes = sum(span for _, span, _ in plan.adding[2])
        stores = pltpu.SemaphoreType.DMA((len(plan.adding[2]),))
        scratch += [pltpu.VMEM((rows, 2, lanes), jnp.float32), stores]
    if plan.later:
        out_shape.append(jax.ShapeDtypeStruct((2, plan.later[2], points), bands.dtype))
        out_specs.append(hbm)
    if plan.near == "make":
        scratch.append(pltpu.VMEM((2 * width, points), jnp.bfloat16))
    outs = list(
        pl.pallas_call(
            functools.partial(step_kernel, plan),
            in_specs=in_specs,
            out_specs=out_specs,
            scratch_shapes=scratch,
            out_shape=out_shape,
            input_output_aliases=aliases,
            compiler_params=pltpu.CompilerParams(
                vmem_limit_bytes=VMEM_BYTES if plan.part and plan.rows != "held" else LEAN_BYTES
            ),
            cost_estimate=pl.CostEstimate(flops=1000, bytes_accessed=1000, transcendentals=0),
            name="step",
        )(*operands)
    )
    piece = outs.pop() if plan.later else None
    result = outs.pop() if plan.adding else result
    near = outs.pop(0) if plan.near == "give" else None
    kept = outs.pop(0) if plan.rows == "keep" else None
    terms = outs[: len(plan.ways)]
    handed = outs[len(plan.ways) :]
    sends = []
    for task in plan.tasks:
        sends.append(handed[: task.count])
        handed = handed[task.count :]
    return terms, near, kept, sends, result, piece


def cuts(nbands, first):
    eighth = nbands // 8
    widths = [4 * eighth, 4 * eighth] if first else [3 * eighth, 3 * eighth, 2 * eighth]
    starts = [sum(widths[:i]) for i in range(len(widths))]
    return list(zip(starts, widths))


def schedule(parts, fold, depth):
    every, others = tuple(range(fold)), tuple(range(1, fold))
    count = len(parts)
    kernels = []
    waiting, halved, crossed = [], [], []
    for index, part in enumerate(parts):
        ready = ready_parts(waiting)
        waiting = waiting[len(ready) :]
        tasks = []
        if halved:
            tasks.append(Task(tuple(halved), 1, False, 2, 2))
        if crossed:
            tasks.append(Task(tuple(crossed), 0, False, fold, 2))
        waiting += halved
        if index >= count - 3:
            kernels.append((part, others, "give", tuple(tasks), ready))
            kernels.append((part, every[:1], "use", (), ()))
        else:
            kernels.append((part, every, "make", tuple(tasks), ready))
        halved, crossed = crossed, [part] if index < count - 1 else []
        if index in (0, count - 3):
            kernels.append((None, (), "", (Task((part,), 0, False, fold, 2),), ()))
            halved, crossed = halved + crossed, []
    tasks = (
        Task((parts[-1],), 0, True, fold, depth),
        Task(tuple(halved), 1, False, 2, 1),
    )
    kernels.append((None, (), "", tasks, ()))
    kernels.append((None, (), "", (), tuple(waiting) + tuple(halved) + (parts[-1],)))
    return kernels


def ready_parts(waiting):
    total = 0
    for count, (slot, _, width) in enumerate(waiting, 1):
        total += width
        if slot != waiting[0][0]:
            break
        if total % LANES == 0:
            return tuple(waiting[:count])
    return ()


def body(bands, nbr_slot, gshift):
    grid_index = lax.axis_index("ga")
    grid_count = lax.axis_size("ga")
    k_dev, _, nbands, points = bands.shape
    rows = nbands // grid_count
    own_planes = points // PLANE
    total_planes = own_planes * grid_count
    planes = grid_index * own_planes + jnp.arange(own_planes, dtype=jnp.int32)
    slots = jnp.arange(k_dev, dtype=jnp.int32)
    chosen = nbr_slot[None, :] == slots[:, None]
    order = jnp.sum(jnp.where(chosen, slots[None, :], 0), axis=1)
    shifts = jnp.sum(jnp.where(chosen, gshift[None, :], 0), axis=1)
    turns = (1 + NKB * shifts[:, None]) * planes[None, :] % (NKB * total_planes)
    angle = 2.0 * math.pi / (NKB * total_planes) * turns.astype(jnp.float32)
    columns = [order[:, None].astype(jnp.float32), jnp.cos(angle), jnp.sin(angle)]
    table = jnp.concatenate(columns, axis=1).reshape(-1)
    table = jnp.append(table, grid_index.astype(jnp.float32))
    parts = []
    for slot in range(k_dev):
        for start, width in cuts(nbands, slot == 0):
            parts.append((slot, start, width))
    theres = []
    piece = None
    for slot, start, width in parts[:AHEAD]:
        piece = piece_of(slot, start, width, bands, [] if piece is None else [piece])
        theres.append(shifted(piece, "ka", -1))
    shape = (rows, k_dev, 2, nbands)
    depth = min(OUTER, grid_count)
    fold = grid_count // depth
    held = {}
    near, kept, result = None, None, None
    for part, ways, phase, tasks, adds in schedule(parts, fold, depth):
        place = parts.index(part) if part else len(parts)
        later = parts[place + AHEAD] if place + AHEAD < len(parts) and phase != "use" else None
        sources = [
            [array for done in task.batch for array, _ in held[(done,)]] for task in tasks
        ]
        arrived, pieces = [], []
        for done in adds:
            batch = max((key for key in held if done in key), key=len)
            column = sum(2 * width for _, _, width in batch[: batch.index(done)])
            terms = [(len(arrived) + i, first + column) for i, (_, first) in enumerate(held[batch])]
            arrived += [array for array, _ in held[batch]]
            pieces.append((done[1], done[2], tuple(terms)))
        adding = (adds[0][0], adds[0][1], tuple(pieces)) if adds else ()
        plan = Plan(
            shape,
            fold,
            depth,
            part,
            ways,
            phase,
            "held" if kept is not None else "keep" if phase == "give" else "load",
            tasks,
            tuple(len(arrays) for arrays in sources),
            adding,
            len(arrived),
            len(tasks) > 1 and tasks[0].direct,
            result is not None,
            later,
        )
        phased = near if phase == "use" else theres[place] if part else None
        terms, near, found, sends, result, piece = step(
            plan,
            table,
            bands if kept is None else kept,
            phased,
            sources,
            arrived,
            result,
        )
        kept = found if kept is None else kept
        if later:
            theres.append(shifted(piece, "ka", -1))
        for way, array in zip(ways, terms):
            array = shifted(array, "ga", way, fold, True) if way else array
            held.setdefault((part,), []).insert(0 if way == 0 else fold, (array, 0))
        for task, arrays in zip(tasks, sends):
            steps = range(1, depth) if task.direct else [1 << task.stage]
            moved = [swapped(array, "ga", fold * i) for array, i in zip(arrays[1:], steps)]
            held[task.batch] = [(array, 0) for array in [arrays[0], *reversed(moved)]]
        if plan.joined:
            joint = held[tasks[0].batch][JOINT][0]
            held[tasks[1].batch].append((joint, 2 * tasks[0].batch[0][2]))
    return result


def solution(mesh):
    placed = (P("ka", None, None, "ga"), P("ka"), P("ka"))
    return jax.shard_map(
        body, mesh=mesh, in_specs=placed, out_specs=P("ga", "ka", None, None), check_vma=False
    )
```

```python
import functools
import math
from typing import NamedTuple

import jax
import jax.numpy as jnp
from jax import lax
from jax.experimental import pallas as pl
from jax.experimental.pallas import tpu as pltpu
from jax.sharding import PartitionSpec as P

NKB = 4
PLANE = 1024
STRIP = 32
DEPTH = 512
AHEAD = 3
OUTER = 4
SPLIT = 0
JOINT = 2
LANES = 128
BLOCK = 256
VMEM_BYTES = 44 * 1024 * 1024
LEAN_BYTES = 32 * 1024 * 1024


def shifted(block, axis, distance, fold=1, inner=False):
    count = lax.axis_size(axis)
    route = []
    for i in range(count):
        outer, place = divmod(i, fold)
        if inner:
            route.append((i, outer * fold + (place + distance) % fold))
        else:
            route.append((i, (outer + distance) % (count // fold) * fold + place))
    return lax.ppermute(block, axis, route)


def swapped(block, axis, distance):
    count = lax.axis_size(axis)
    return lax.ppermute(block, axis, [(i, i ^ distance) for i in range(count)])


def first_kernel(slot, start, bands_ref, out_ref, sems):
    width = out_ref.shape[1]
    loads = [
        pltpu.make_async_copy(
            bands_ref.at[slot, part, pl.ds(start, width), :], out_ref.at[part], sems.at[part]
        )
        for part in range(2)
    ]
    for load in loads:
        load.start()
    for load in loads:
        load.wait()


def piece_kernel(slot, start, bands_ref, *rest):
    out_ref, piece_buf, sems = rest[-3:]
    width = piece_buf.shape[1]
    rows = pl.ds(start, width)
    loads = [
        pltpu.make_async_copy(bands_ref.at[slot, part, rows, :], piece_buf.at[part], sems.at[0, part])
        for part in range(2)
    ]
    stores = [
        pltpu.make_async_copy(piece_buf.at[part], out_ref.at[part], sems.at[1, part])
        for part in range(2)
    ]
    for load in loads:
        load.start()
    for load, store in zip(loads, stores):
        load.wait()
        store.start()
    for store in stores:
        store.wait()


def piece_of(slot, start, width, bands, after):
    points = bands.shape[3]
    hbm = pl.BlockSpec(memory_space=pltpu.HBM)
    scratch = [pltpu.VMEM((2, width, points), bands.dtype), pltpu.SemaphoreType.DMA((2, 2))]
    return pl.pallas_call(
        functools.partial(piece_kernel if after else first_kernel, slot, start),
        in_specs=[hbm] * (1 + len(after)),
        out_specs=hbm if after else pl.BlockSpec(memory_space=pltpu.VMEM),
        scratch_shapes=scratch if after else [pltpu.SemaphoreType.DMA((2,))],
        out_shape=jax.ShapeDtypeStruct((2, width, points), bands.dtype),
        compiler_params=pltpu.CompilerParams(vmem_limit_bytes=VMEM_BYTES),
        cost_estimate=pl.CostEstimate(flops=1000, bytes_accessed=1000, transcendentals=0),
        name="piece_of",
    )(bands, *after)


def near_into(near_buf, there_ref, table_ref, base, planes):
    width, points = there_ref.shape[1:]

    @pl.loop(0, width // STRIP)
    def _(strip):
        rows = pl.ds(strip * STRIP, STRIP)
        mirror = pl.ds(width + strip * STRIP, STRIP)
        for start in range(0, points, DEPTH):
            plane = start // PLANE
            cosine = table_ref[base + 1 + plane]
            sine = table_ref[base + 1 + planes + plane]
            columns = pl.ds(start, DEPTH)
            real_part = there_ref[0, rows, columns].astype(jnp.float32)
            imag_part = there_ref[1, rows, columns].astype(jnp.float32)
            near_re = real_part * cosine + imag_part * sine
            near_im = imag_part * cosine - real_part * sine
            near_buf[rows, columns] = near_re.astype(jnp.bfloat16)
            near_buf[mirror, columns] = near_im.astype(jnp.bfloat16)


def put_sum(sum_buf, lane, total):
    width = total.shape[1] // 2
    sum_buf[:, 0, lane : lane + width] = total[:, :width]
    sum_buf[:, 1, lane : lane + width] = total[:, width:]


def step_kernel(plan, table_ref, *refs):
    rows, k_dev, _, nbands = plan.shape
    fold, depth = plan.fold, plan.depth
    refs = list(refs)

    def take(count):
        taken = refs[:count]
        del refs[:count]
        return taken

    stride = (table_ref.shape[0] - 1) // k_dev
    planes = (stride - 1) // 2
    me = table_ref[k_dev * stride].astype(jnp.int32)
    place, outer = lax.rem(me, fold), lax.div(me, fold)
    if plan.part:
        bands_ref, phased_ref = take(2)
    sources = [take(count) for count in plan.takes]
    arrived = take(plan.adds)
    if plan.adding and plan.placed:
        take(1)
    take(plan.after)
    given_ref = take(1)[0] if plan.near == "give" else None
    kept_ref = take(1)[0] if plan.ahead else None
    outs = [take(2 if plan.split else 1) for _ in plan.ways]
    targets = [take(task.count) for task in plan.tasks]
    result_ref = take(1)[0] if plan.adding else None
    piece_ref = take(1)[0] if plan.later else None
    if plan.part:
        slot, _, width = plan.part
        base = slot * stride
        point = table_ref[base].astype(jnp.int32)

        def load_rows(point, into_ref, load_sems):
            copies = []
            for distance in range(1, fold + 1):
                way = distance % fold
                target = lax.rem(place + way, fold)
                for part in range(2):
                    for level in range(depth):
                        first = pl.multiple_of((level * fold + target) * rows, rows)
                        copy = pltpu.make_async_copy(
                            bands_ref.at[point, part, pl.ds(first, rows), :],
                            into_ref.at[way, part, pl.ds(level * rows, rows), :],
                            load_sems.at[way, part, level],
                        )
                        copy.start()
                        copies.append((way, part, copy))
            return copies

        own_ref = bands_ref
        own, ahead = [], []
        if plan.rows != "held":
            own_ref, own_sems = take(2)
            own = load_rows(point, own_ref, own_sems)
        if plan.ahead:
            next_point = table_ref[base + stride].astype(jnp.int32)
            ahead = load_rows(next_point, kept_ref, take(1)[0])
    if plan.later:
        piece_buf, piece_sems = take(2)
        later_slot, later_start, later_width = plan.later
        loads = [
            pltpu.make_async_copy(
                bands_ref.at[later_slot, part, pl.ds(later_start, later_width), :],
                piece_buf.at[part],
                piece_sems.at[0, part],
            )
            for part in range(2)
        ]
        stores = [
            pltpu.make_async_copy(piece_buf.at[part], piece_ref.at[part], piece_sems.at[1, part])
            for part in range(2)
        ]
        for copy in loads:
            copy.start()
    if plan.adding:
        sum_buf, placed_sem = take(2)
        add_slot, add_start, pieces = plan.adding
        for start, span, terms in pieces:
            total = 0.0
            for index, column in terms:
                total += arrived[index][0, :, column : column + 2 * span].astype(jnp.float32)
            put_sum(sum_buf, start - add_start, total)
        add_point = table_ref[add_slot * stride].astype(jnp.int32)
        columns = pl.ds(add_start, sum_buf.shape[2])
        placing = pltpu.make_async_copy(
            sum_buf, result_ref.at[:, add_point, :, columns], placed_sem
        )
        placing.start()
    for task, arrays, outputs in zip(plan.tasks, sources, targets):
        groups = [arrays[i : i + task.each] for i in range(0, len(arrays), task.each)]
        bit = lax.rem(lax.div(outer, 1 << task.stage), 2)
        filled = [(out_ref, 0) for out_ref in outputs]
        if plan.joined and not task.direct:
            filled.append((targets[0][JOINT], 2 * plan.tasks[0].batch[0][2]))
        for index, (out_ref, shift) in enumerate(filled):
            for level in range(out_ref.shape[0]):
                if task.direct:
                    source = partner(outer, index)
                else:
                    source = 2 * level + (1 - bit if index else bit)
                column = shift
                for group in groups:
                    total = summed(group, source)
                    columns = slice(column, column + total.shape[1])
                    out_ref[level, :, columns] = total.astype(out_ref.dtype)
                    column += total.shape[1]
    if plan.part:
        near_ref = phased_ref
        if plan.near != "use":
            near_ref = given_ref if plan.near == "give" else take(1)[0]
            near_into(near_ref, phased_ref, table_ref, base, planes)
        dims = (((1,), (1,)), ((), ()))
        points = near_ref.shape[1]
        run = points // 2 if width <= SPLIT else points
        for way, out_refs in zip(plan.ways, outs):
            kind = out_refs[0].dtype
            of_both = []
            for part in range(2):
                for copy in [copy for *which, copy in own if which == [way, part]]:
                    copy.wait()
                products = [
                    lax.dot_general(
                        own_ref[way, part, :, pl.ds(first, run)],
                        near_ref[:, pl.ds(first, run)],
                        dims,
                        preferred_element_type=jnp.float32,
                    )
                    for first in range(0, points, run)
                ]
                of_both.append(sum(products[1:], products[0]))
            of_re, of_im = of_both
            sides = (
                (of_re[:, :width] + of_im[:, width:]).astype(kind),
                (of_re[:, width:] - of_im[:, :width]).astype(kind),
            )
            for level in range(depth):
                lines = slice(level * rows, (level + 1) * rows)
                for side, values in enumerate(sides):
                    if plan.split:
                        out_refs[side][level] = values[lines]
                    else:
                        columns = slice(side * width, (side + 1) * width)
                        out_refs[0][level, :, columns] = values[lines]
            if plan.later and way == plan.ways[0]:
                for load, store in zip(loads, stores):
                    load.wait()
                    store.start()
        for _, _, copy in ahead:
            copy.wait()
    if plan.adding:
        placing.wait()
    if plan.later:
        for store in stores:
            store.wait()


def partner(outer, distance):
    low, high = lax.rem(outer, 2), lax.rem(lax.div(outer, 2), 2)
    low = 1 - low if distance % 2 else low
    high = 1 - high if distance // 2 else high
    return outer - lax.rem(outer, 4) + 2 * high + low


def summed(arrays, level):
    total = arrays[0][level].astype(jnp.float32)
    rest = [array[level].astype(jnp.float32) for array in arrays[1:]]
    while rest:
        more = rest.pop(0)
        if more.shape != total.shape:
            more = jnp.concatenate([more, rest.pop(0)], axis=1)
        total = total + more
    return total


class Task(NamedTuple):
    batch: tuple
    stage: int
    direct: bool
    each: int
    count: int


class Plan(NamedTuple):
    shape: tuple
    fold: int
    depth: int
    part: tuple
    ways: tuple
    near: str
    rows: str
    ahead: bool
    tasks: tuple
    takes: tuple
    adding: tuple
    adds: int
    joined: bool
    placed: bool
    later: tuple
    split: bool
    after: int


def step(plan, table, bands, phased, sources, arrived, result, after):
    rows, _, _, nbands = plan.shape
    fold, depth = plan.fold, plan.depth
    points = bands.shape[-1]
    vmem = pl.BlockSpec(memory_space=pltpu.VMEM)
    hbm = pl.BlockSpec(memory_space=pltpu.HBM)
    operands, in_specs = [table], [pl.BlockSpec(memory_space=pltpu.SMEM)]
    out_shape, out_specs, scratch, aliases = [], [], [], {}

    def kind(index):
        return jnp.bfloat16 if index else jnp.float32

    if plan.part:
        width = plan.part[2]
        operands += [bands, phased]
        in_specs += [vmem if plan.rows == "held" else hbm, vmem]
        kept = (fold, 2, depth * rows, points)
        if plan.near == "give":
            out_shape.append(jax.ShapeDtypeStruct((2 * width, points), jnp.bfloat16))
        if plan.ahead:
            out_shape.append(jax.ShapeDtypeStruct(kept, jnp.bfloat16))
        out_shape += [
            jax.ShapeDtypeStruct((depth, rows, width if plan.split else 2 * width), kind(way))
            for way in plan.ways
            for _ in range(2 if plan.split else 1)
        ]
        if plan.rows != "held":
            scratch.append(pltpu.VMEM(kept, jnp.bfloat16))
            scratch.append(pltpu.SemaphoreType.DMA((fold, 2, depth)))
        if plan.ahead:
            scratch.append(pltpu.SemaphoreType.DMA((fold, 2, depth)))
    for arrays in [*sources, arrived]:
        operands += arrays
        in_specs += [vmem] * len(arrays)
    for task in plan.tasks:
        wide = sum(2 * width for _, _, width in task.batch)
        levels = 1 if task.direct else depth >> (task.stage + 1)
        extra = 2 * plan.tasks[1].batch[0][2] if plan.joined and task.direct else 0
        for i in range(task.count):
            columns = wide + extra if i == JOINT else wide
            out_shape.append(jax.ShapeDtypeStruct((levels, rows, columns), kind(i)))
    out_specs += [vmem] * len(out_shape)
    if plan.later:
        scratch += [
            pltpu.VMEM((2, plan.later[2], points), bands.dtype),
            pltpu.SemaphoreType.DMA((2, 2)),
        ]
    if plan.adding:
        if plan.placed:
            aliases = {len(operands): len(out_shape)}
            operands.append(result)
            in_specs.append(hbm)
        out_shape.append(jax.ShapeDtypeStruct(plan.shape, jnp.float32))
        out_specs.append(hbm)
        lanes = sum(span for _, span, _ in plan.adding[2])
        scratch += [pltpu.VMEM((rows, 2, lanes), jnp.float32), pltpu.SemaphoreType.DMA]
    operands += after
    in_specs += [pl.BlockSpec(memory_space=pl.ANY)] * len(after)
    if plan.later:
        out_shape.append(jax.ShapeDtypeStruct((2, plan.later[2], points), bands.dtype))
        out_specs.append(hbm)
    if plan.near == "make":
        scratch.append(pltpu.VMEM((2 * width, points), jnp.bfloat16))
    outs = list(
        pl.pallas_call(
            functools.partial(step_kernel, plan),
            in_specs=in_specs,
            out_specs=out_specs,
            scratch_shapes=scratch,
            out_shape=out_shape,
            input_output_aliases=aliases,
            compiler_params=pltpu.CompilerParams(
                vmem_limit_bytes=VMEM_BYTES if plan.part and plan.rows != "held" else LEAN_BYTES
            ),
            cost_estimate=pl.CostEstimate(flops=1000, bytes_accessed=1000, transcendentals=0),
            name="step",
        )(*operands)
    )
    piece = outs.pop() if plan.later else None
    result = outs.pop() if plan.adding else result
    near = outs.pop(0) if plan.near == "give" else None
    kept = outs.pop(0) if plan.ahead else None
    count = len(plan.ways) * (2 if plan.split else 1)
    terms, handed = outs[:count], outs[count:]
    sends = []
    for task in plan.tasks:
        sends.append(handed[: task.count])
        handed = handed[task.count :]
    return terms, near, kept, sends, result, piece


def cuts(nbands, first):
    eighth = nbands // 8
    widths = [4 * eighth, 4 * eighth] if first else [3 * eighth, 3 * eighth, 2 * eighth]
    starts = [sum(widths[:i]) for i in range(len(widths))]
    return list(zip(starts, widths))


def schedule(parts, fold, depth):
    every, others = tuple(range(fold)), tuple(range(1, fold))
    count = len(parts)
    kernels = []
    waiting, halved, crossed = [], [], []
    for index, part in enumerate(parts):
        ready = ready_parts(waiting)
        waiting = waiting[len(ready) :]
        final = index == count - 1
        tasks = []
        if halved and not final:
            tasks.append(Task(tuple(halved), 1, False, 2, 2))
            waiting += halved
        if crossed:
            tasks.append(Task(tuple(crossed), 0, False, fold, 2))
        if index >= count - 3:
            kernels.append((part, others, "give", tuple(tasks), ready))
            kernels.append((part, every[:1], "use", (), ()))
        else:
            kernels.append((part, every, "make", tuple(tasks), ready))
        if final:
            break
        halved, crossed = crossed, [part]
        if index in (0, count - 3, count - 2):
            kernels.append((None, (), "", (Task((part,), 0, False, fold, 2),), ()))
            halved, crossed = halved + crossed, []
    tasks = (
        Task((parts[-1],), 0, True, 2 * fold - 1, depth),
        Task(tuple(halved), 1, False, 2, 1),
    )
    kernels.append((None, (), "", tasks, ()))
    kernels.append((None, (), "", (), tuple(waiting) + tuple(halved) + (parts[-1],)))
    return kernels


def ready_parts(waiting):
    total = 0
    for count, (slot, _, width) in enumerate(waiting, 1):
        total += width
        if slot != waiting[0][0]:
            break
        if total % LANES == 0:
            return tuple(waiting[:count])
    return ()


def body(bands, nbr_slot, gshift):
    grid_index = lax.axis_index("ga")
    grid_count = lax.axis_size("ga")
    k_dev, _, nbands, points = bands.shape
    rows = nbands // grid_count
    own_planes = points // PLANE
    total_planes = own_planes * grid_count
    planes = grid_index * own_planes + jnp.arange(own_planes, dtype=jnp.int32)
    slots = jnp.arange(k_dev, dtype=jnp.int32)
    chosen = nbr_slot[None, :] == slots[:, None]
    order = jnp.sum(jnp.where(chosen, slots[None, :], 0), axis=1)
    shifts = jnp.sum(jnp.where(chosen, gshift[None, :], 0), axis=1)
    turns = (1 + NKB * shifts[:, None]) * planes[None, :] % (NKB * total_planes)
    angle = 2.0 * math.pi / (NKB * total_planes) * turns.astype(jnp.float32)
    columns = [order[:, None].astype(jnp.float32), jnp.cos(angle), jnp.sin(angle)]
    table = jnp.concatenate(columns, axis=1).reshape(-1)
    table = jnp.append(table, grid_index.astype(jnp.float32))
    parts = []
    for slot in range(k_dev):
        for start, width in cuts(nbands, slot == 0):
            parts.append((slot, start, width))
    theres = []
    piece = None
    for slot, start, width in parts[:AHEAD]:
        piece = piece_of(slot, start, width, bands, [] if piece is None else [piece])
        theres.append(shifted(piece, "ka", -1))
    shape = (rows, k_dev, 2, nbands)
    depth = min(OUTER, grid_count)
    fold = grid_count // depth
    held = {}
    near, kept, result = None, None, None
    for part, ways, phase, tasks, adds in schedule(parts, fold, depth):
        place = parts.index(part) if part else len(parts)
        later = parts[place + AHEAD] if place + AHEAD < len(parts) and phase != "use" else None
        sources = [
            [array for done in task.batch for array, _ in held[(done,)]] for task in tasks
        ]
        arrived, pieces = [], []
        for done in adds:
            batch = max((key for key in held if done in key), key=len)
            column = sum(2 * width for _, _, width in batch[: batch.index(done)])
            terms = [(len(arrived) + i, first + column) for i, (_, first) in enumerate(held[batch])]
            arrived += [array for array, _ in held[batch]]
            pieces.append((done[1], done[2], tuple(terms)))
        adding = (adds[0][0], adds[0][1], tuple(pieces)) if adds else ()
        split = place == len(parts) - 1 and phase == "give"
        after = order_by if split else []
        plan = Plan(
            shape,
            fold,
            depth,
            part,
            ways,
            phase,
            "load" if kept is None else "held",
            place == len(parts) - 4,
            tasks,
            tuple(len(arrays) for arrays in sources),
            adding,
            len(arrived),
            len(tasks) > 1 and tasks[0].direct,
            result is not None,
            later,
            split,
            len(after),
        )
        phased = near if phase == "use" else theres[place] if part else None
        terms, near, found, sends, result, piece = step(
            plan,
            table,
            bands if kept is None else kept,
            phased,
            sources,
            arrived,
            result,
            after,
        )
        order_by = sends[0][:1] if sends else []
        kept = found if kept is None else kept
        if later:
            theres.append(shifted(piece, "ka", -1))
        for way, array in zip([way for way in ways for _ in range(1 + split)], terms):
            array = shifted(array, "ga", way, fold, True) if way else array
            entries = held.setdefault((part,), [])
            entries.insert(len(entries) if way else 0, (array, 0))
        for task, arrays in zip(tasks, sends):
            steps = range(1, depth) if task.direct else [1 << task.stage]
            moved = [swapped(array, "ga", fold * i) for array, i in zip(arrays[1:], steps)]
            held[task.batch] = [(array, 0) for array in [arrays[0], *reversed(moved)]]
        if plan.joined:
            joint = held[tasks[0].batch][JOINT][0]
            held[tasks[1].batch].append((joint, 2 * tasks[0].batch[0][2]))
    return result


def solution(mesh):
    placed = (P("ka", None, None, "ga"), P("ka"), P("ka"))
    return jax.shard_map(
        body, mesh=mesh, in_specs=placed, out_specs=P("ga", "ka", None, None), check_vma=False
    )
```
